32 devices in a mesh: parts: 2 (over y), adapter: 4 (over z), tensor: 4 (over x, core).
Axes of the slice: x: 2, y: 2, z: 4, core: 2. Of those that a mesh axis runs over, the one named last changes fastest.
Arguments:
- tokens: bfloat16 [3072, 8192], P(('parts', 'adapter'), 'tensor'), parts along dimension 0, may hold values from -6 to 6
- tenant: int32 [3072, 1], P(('parts', 'adapter')), parts along dimension 0, may hold values from 0 to 3; in each aligned block of 384 rows (0 to 383, 384 to 767, ...) at most 128 rows name the same one
- placement: int32 [4], replicated, may hold values from 0 to 3, each once
- frozen_projection_weight: bfloat16 [8192, 2048], P(None, 'tensor'), may hold values from -0.0625 to 0.0625
- lowrank_down_weight: bfloat16 [4, 8192, 64], P('adapter', None, 'tensor'), may hold values from -0.0625 to 0.0625
- lowrank_up_weight: bfloat16 [4, 64, 2048], P('adapter', None, 'tensor'), may hold values from -0.75 to 0.75
Outputs:
- projected: bfloat16 [3072, 2048], P(('parts', 'adapter'), 'tensor'), parts along dimension 0
The draws below stay inside these ranges and needn't reach their ends.
There are 2 independent parts, one for each index of `parts`. The reference program is written for one: setup_inputs(seed, part) draws one part's arguments, and reference() takes and returns one part's arrays. A program takes and returns all parts, laid end to end along the dimension named above; an argument that names none is the same for every part. Nothing has to cross between parts.
Inputs may be any that keep to these rules, and one draw needn't show every extreme that they name: Within each aligned block of 384 rows (the rows of one device) no tenant is named more than 128 times; in at least one block some tenant is named exactly 128 times; every tenant is named somewhere. `placement`: each storage slot holds exactly one tenant.
All inputs are finite; a program needn't handle non-finite values.
Results may differ from the reference program's by a relative error of at most 0.0054.
Values may be sent and summed in bfloat16 or wider, within the bound.
No kernel may reach another device: no remote copies, remote signals or barrier semaphores. Data moves between devices by JAX's collectives and lax.ppermute only.
A program may use at most 128 MiB of HBM per device.

```python
import math
import jax
import jax.numpy as jnp
import numpy as np
from jax import lax

MODEL_WIDTH = 8192
KEY_VALUE_WIDTH = 2048
ADAPTER_RANK = 64
TOK_DEV = 384
TENANT_ADAPTERS = 4
CAP = 128
TOKENS = 1536
N_ADAPTER = 4


def steps_of(rng, extent, shards, smallest, largest):
    loudness, own = 1.0, jax.random.fold_in(rng, 6)
    for dim, blocks in shards:
        steps = jnp.exp(jax.random.uniform(jax.random.fold_in(own, dim), (blocks,), jnp.float32, smallest / len(shards), largest / len(shards)))
        loudness = loudness * jnp.repeat(steps, extent[dim] // blocks).reshape([-1 if axis == dim else 1 for axis in range(len(extent))])
    return loudness


def assign_block(stream_key, own, number, rows, count, top, bound, slope):
    order = jax.random.permutation(stream_key, count)
    heavy_load, usual = shares(count, rows * top, bound, slope, True), shares(count, rows * top, bound, slope, False)
    places = jnp.arange(count)

    def named(lengths, rotation):
        used = int((lengths > 0).sum())
        fixed = max(1, used // 4)
        moved = fixed + (places - fixed + rotation * (used - fixed)) % max(1, count - fixed)
        return jnp.zeros((count,), jnp.int32).at[order[jnp.where(places < fixed, places, moved)]].set(jnp.asarray(lengths, jnp.int32))

    lengths = jnp.where(number % 4 == 0, named(heavy_load, number // 4), named(usual, number - number // 4 - 1))
    mixed = jax.random.permutation(jax.random.fold_in(own, 3), count)
    donor, receiver = mixed[0:count // 2 * 2:2], mixed[1:count // 2 * 2:2]
    margin = jnp.minimum(lengths[donor] - 1, bound - lengths[receiver]) // 2
    margin = jnp.where((donor == order[0]) | (receiver == order[0]) | (lengths[receiver] == 0), 0, jnp.maximum(margin, 0))
    moved = jax.random.randint(jax.random.fold_in(own, 4), (count // 2,), 0, 1 << 20) % (margin + 1)
    lengths = lengths.at[donor].add(-moved).at[receiver].add(moved)
    members = jnp.searchsorted(jnp.cumsum(lengths), jnp.arange(rows * top), side="right").astype(jnp.int32)
    grid = members.reshape(top, rows).T
    grid = grid[jax.random.permutation(jax.random.fold_in(own, 1), rows)]
    rotation = jax.random.randint(jax.random.fold_in(own, 2), (rows, 1), 0, top)
    return jnp.take_along_axis(grid, (jnp.arange(top)[None, :] + rotation) % top, axis=1)


def shares(count, total, limit, slope, full):
    weights = [(1 << 20) // math.isqrt(rank ** slope) + 1 for rank in range(1, count + 1)]
    largest = limit if full else min(limit, max(-(-total // count), total * weights[0] // sum(weights)))
    least = 1 if total - largest >= count - 1 else 0
    counts, surplus = [largest] + [least] * (count - 1), total - largest - least * (count - 1)
    while surplus > 0:
        movable = [i for i in range(1, count) if counts[i] < largest] or [i for i in range(1, count) if counts[i] < limit]
        mass, left = sum([weights[i] for i in movable]), surplus
        for i in movable:
            more = min(limit - counts[i], max(1, left * weights[i] // mass), surplus)
            counts[i] = counts[i] + more
            surplus = surplus - more
    return np.array(counts)


def bell_draw(stream_key, extent, width, most, pieces=(), kind=jnp.bfloat16):
    drawn = width * jax.random.normal(stream_key, extent, jnp.float32)
    if pieces:
        drawn = drawn * steps_of(stream_key, extent, pieces, -0.22, 0.18)
    return jnp.clip(drawn, -most, most).astype(kind)


def setup_inputs(seed: int = 0, part: int = 0) -> dict:
    keys = jax.random.split(jax.random.key(seed), 7)
    own_keys = jax.random.split(jax.random.fold_in(keys[6], part), 7)
    tokens = bell_draw(own_keys[0], (TOKENS, MODEL_WIDTH), 1.0, 6.0, ((0, 4), (1, 4)))
    tenant_keys = jax.random.split(jax.random.fold_in(own_keys[1], 1), TOKENS // TOK_DEV)
    tenant_turns = jax.random.permutation(jax.random.fold_in(own_keys[1], 3), TOKENS // TOK_DEV)
    tenant = jax.vmap(lambda own, number: assign_block(jax.random.fold_in(own_keys[1], 2), own, number, TOK_DEV, TENANT_ADAPTERS, 1, CAP, 2))(tenant_keys, tenant_turns).reshape((TOKENS, 1))
    placement = jax.random.permutation(keys[2], TENANT_ADAPTERS).astype(jnp.int32)
    frozen_projection_weight = bell_draw(keys[3], (MODEL_WIDTH, KEY_VALUE_WIDTH), MODEL_WIDTH ** -0.5, 0.0625, ((1, 4),))
    lowrank_down_weight = bell_draw(keys[4], (TENANT_ADAPTERS, MODEL_WIDTH, ADAPTER_RANK), MODEL_WIDTH ** -0.5, 0.0625, ((0, 4), (2, 4)))
    lowrank_up_weight = bell_draw(keys[5], (TENANT_ADAPTERS, ADAPTER_RANK, KEY_VALUE_WIDTH), ADAPTER_RANK ** -0.5, 0.75, ((0, 4), (2, 4)))
    return dict(tokens=tokens, tenant=tenant, placement=placement, frozen_projection_weight=frozen_projection_weight, lowrank_down_weight=lowrank_down_weight, lowrank_up_weight=lowrank_up_weight)


LOWRANK_SCALE = 2.0


def reference(tokens, tenant, placement, frozen_projection_weight, lowrank_down_weight, lowrank_up_weight):
    slot_ids = jnp.arange(TENANT_ADAPTERS, dtype=jnp.int32)
    labels = tenant[:, 0].astype(jnp.int32)
    stored = jnp.sum(jnp.where(labels[:, None] == slot_ids[None, :], placement[None, :], 0), axis=1).astype(jnp.int32)
    hot_marks = (stored[:, None] == slot_ids[None, :]).astype(jnp.int32).reshape(N_ADAPTER, TOK_DEV, TENANT_ADAPTERS)
    earlier = jnp.cumsum(hot_marks, axis=1) - hot_marks
    position = jnp.sum(earlier * hot_marks, axis=2).reshape(-1).astype(jnp.int32)
    block_id = (jnp.arange(TOKENS, dtype=jnp.int32) // TOK_DEV).astype(jnp.int32)
    storage_depth = N_ADAPTER * CAP
    target = (stored * storage_depth + block_id * CAP + position).astype(jnp.int32)
    input_rows = jnp.zeros((TENANT_ADAPTERS * storage_depth,), jnp.int32).at[target].set(jnp.arange(TOKENS, dtype=jnp.int32) + 1)

    def single_tenant_update(packed):
        row_index, down_part, up_part = packed
        occupied = row_index > 0
        gathered = jnp.take(tokens, jnp.maximum(row_index - 1, 0).astype(jnp.int32), axis=0)
        row_data = jnp.where(occupied[:, None], gathered, jnp.zeros((), tokens.dtype))
        shrunk = jnp.dot(row_data, down_part, preferred_element_type=jnp.float32).astype(jnp.bfloat16)
        return jnp.dot(shrunk, up_part, preferred_element_type=jnp.float32).astype(jnp.bfloat16)

    widened_update = lax.map(single_tenant_update, (input_rows.reshape(TENANT_ADAPTERS, storage_depth), lowrank_down_weight, lowrank_up_weight))
    update_rows = jnp.take(widened_update.reshape(TENANT_ADAPTERS * storage_depth, KEY_VALUE_WIDTH), target, axis=0)
    update_rows = lax.optimization_barrier(update_rows)
    frozen_output = jnp.dot(tokens, frozen_projection_weight, preferred_element_type=jnp.float32)
    return (frozen_output + LOWRANK_SCALE * update_rows.astype(jnp.float32)).astype(jnp.bfloat16)
```

```python
import jax
import jax.numpy as jnp
from jax import lax
from jax.sharding import PartitionSpec as P

LOWRANK_SCALE = 2.0
CORES = 2
CHUNKS = 4


def pair_up(axis_count, flip):
    return [(i, i ^ flip) for i in range(axis_count)]


def in_order(pieces, me):
    bit = 1
    while bit < len(pieces):
        swap = (me & bit) != 0
        pieces = [jnp.where(swap, pieces[j ^ bit], pieces[j]) for j in range(len(pieces))]
        bit *= 2
    return pieces


def sum_over_tensor(value, count):
    flip = 1
    while flip < count:
        value = value + lax.ppermute(value, "tensor", pair_up(count, flip))
        flip *= 2
    return value


def body(
    tokens, tenant, placement, frozen_projection_weight, lowrank_down_weight, lowrank_up_weight
):
    rows, depth = tokens.shape
    slots = placement.shape[0]
    count = lax.axis_size("tensor")
    me = lax.axis_index("tensor")
    rank_part = lowrank_down_weight.shape[2]
    rank = rank_part * count
    step = depth // CHUNKS

    down = lowrank_down_weight[0].T
    pieces = [lax.dynamic_slice_in_dim(down, me * depth, depth, axis=1)]
    for flip in range(1, count):
        piece = lax.dynamic_slice_in_dim(down, (me ^ flip) * depth, depth, axis=1)
        pieces.append(lax.ppermute(piece, "tensor", pair_up(count, flip)))
    down_slice = jnp.concatenate(in_order(pieces, me), axis=0)
    stored_here = jnp.concatenate([down_slice, lowrank_up_weight[0]], axis=1)
    adapters = lax.all_gather(stored_here, "adapter", axis=0, tiled=True)

    local = [(me, 0, tokens), (me ^ 1, 0, lax.ppermute(tokens, "tensor", pair_up(count, 1)))]
    arrived = []
    for m in range(CHUNKS):
        chunk = tokens[:, m * step : (m + 1) * step]
        for flip in range(CORES, count, CORES):
            far = lax.ppermute(chunk, "tensor", pair_up(count, flip))
            arrived.append((me ^ flip, m, far))
            arrived.append((me ^ flip ^ 1, m, lax.ppermute(far, "tensor", pair_up(count, 1))))

    labels = tenant[:, 0]
    slot_ids = jnp.arange(slots, dtype=jnp.int32)
    stored = jnp.sum(jnp.where(labels[:, None] == slot_ids[None, :], placement[None, :], 0), axis=1)
    all_slots = lax.dot_general(
        tokens, adapters[:, :depth], (((1,), (1,)), ((), ())), preferred_element_type=jnp.float32
    )
    partial = jnp.zeros((rows, rank), jnp.float32)
    for s in range(slots):
        partial += jnp.where((stored == s)[:, None], all_slots[:, s * rank : (s + 1) * rank], 0.0)
    shrunk = sum_over_tensor(partial, count).astype(jnp.bfloat16)
    spread = jnp.concatenate(
        [jnp.where((stored == s)[:, None], shrunk, jnp.zeros((), shrunk.dtype)) for s in range(slots)],
        axis=1,
    )
    expanded = jnp.dot(spread, adapters[:, depth:], preferred_element_type=jnp.float32)
    total = LOWRANK_SCALE * expanded.astype(jnp.bfloat16).astype(jnp.float32)

    for owner, m, features in local + arrived:
        part = lax.dynamic_slice_in_dim(
            frozen_projection_weight, owner * depth + m * step, features.shape[1], axis=0
        )
        total += jnp.dot(features, part, preferred_element_type=jnp.float32)
    return total.astype(jnp.bfloat16)


def solution(mesh):
    placed = (
        P(("parts", "adapter"), "tensor"),
        P(("parts", "adapter"), None),
        P(),
        P(None, "tensor"),
        P("adapter", None, "tensor"),
        P("adapter", None, "tensor"),
    )
    return jax.shard_map(
        body,
        mesh=mesh,
        in_specs=placed,
        out_specs=P(("parts", "adapter"), "tensor"),
        check_vma=False,
    )
```

```python
import jax
import jax.numpy as jnp
from jax import lax
from jax.sharding import PartitionSpec as P

LOWRANK_SCALE = 2.0
CORES = 2
CHUNKS = 4


def pair_up(axis_count, flip):
    return [(i, i ^ flip) for i in range(axis_count)]


def in_order(pieces, me):
    bit = 1
    while bit < len(pieces):
        swap = (me & bit) != 0
        pieces = [jnp.where(swap, pieces[j ^ bit], pieces[j]) for j in range(len(pieces))]
        bit *= 2
    return pieces


def sum_over_tensor(value, count):
    flip = 1
    while flip < count:
        value = value + lax.ppermute(value, "tensor", pair_up(count, flip))
        flip *= 2
    return value


def body(
    tokens, tenant, placement, frozen_projection_weight, lowrank_down_weight, lowrank_up_weight
):
    rows, depth = tokens.shape
    slots = placement.shape[0]
    count = lax.axis_size("tensor")
    me = lax.axis_index("tensor")
    rank_part = lowrank_down_weight.shape[2]
    rank = rank_part * count
    step = depth // CHUNKS

    parts = lax.axis_size("parts")
    half = depth // parts
    mine = lax.axis_index("parts") * half

    chunks = [tokens[:, m * step : (m + 1) * step] for m in range(CHUNKS)]

    down = lowrank_down_weight[0].T
    pieces = [
        lax.dynamic_slice_in_dim(down, (me ^ flip) * depth + mine, half, axis=1)
        for flip in range(count)
    ]
    chunks[0], pieces = lax.optimization_barrier((chunks[0], pieces))
    pieces = [pieces[0]] + [
        lax.ppermute(pieces[flip], "tensor", pair_up(count, flip)) for flip in range(1, count)
    ]
    down_slice = jnp.concatenate(in_order(pieces, me), axis=0)
    columns = lowrank_up_weight.shape[2]
    up_share = lax.dynamic_slice_in_dim(
        lowrank_up_weight[0], lax.axis_index("parts") * (rank // parts), rank // parts, axis=0
    )
    up = lax.all_gather(up_share, ("adapter", "parts"), axis=0, tiled=True)
    down_all = lax.all_gather(down_slice, ("parts", "adapter"), axis=0, tiled=True)

    arrived = []
    neighbour = lax.ppermute(tokens, "tensor", pair_up(count, 1))
    for m in range(CHUNKS):
        for flip in range(CORES, count, CORES):
            far = lax.ppermute(chunks[m], "tensor", pair_up(count, flip))
            arrived.append((me ^ flip, m, far))
            arrived.append((me ^ flip ^ 1, m, lax.ppermute(far, "tensor", pair_up(count, 1))))

    def weight_rows(owner, m, width):
        return lax.dynamic_slice_in_dim(
            frozen_projection_weight, owner * depth + m * step, width, axis=0
        )

    total = jnp.dot(tokens, weight_rows(me, 0, depth), preferred_element_type=jnp.float32)
    total += jnp.dot(neighbour, weight_rows(me ^ 1, 0, depth), preferred_element_type=jnp.float32)

    labels = tenant[:, 0]
    slot_ids = jnp.arange(slots, dtype=jnp.int32)
    stored = jnp.sum(jnp.where(labels[:, None] == slot_ids[None, :], placement[None, :], 0), axis=1)
    all_slots = jnp.zeros((rows, slots * rank), jnp.float32)
    for p in range(parts):
        all_slots += lax.dot_general(
            tokens[:, p * half : (p + 1) * half],
            down_all[p * slots * rank : (p + 1) * slots * rank],
            (((1,), (1,)), ((), ())),
            preferred_element_type=jnp.float32,
        )
    partial = jnp.zeros((rows, rank), jnp.float32)
    for s in range(slots):
        partial += jnp.where((stored == s)[:, None], all_slots[:, s * rank : (s + 1) * rank], 0.0)
    shrunk = sum_over_tensor(partial, count).astype(jnp.bfloat16)
    spread = jnp.concatenate(
        [jnp.where((stored == s)[:, None], shrunk, jnp.zeros((), shrunk.dtype)) for s in range(slots)],
        axis=1,
    )
    expanded = jnp.dot(spread, up, preferred_element_type=jnp.float32)
    for owner, m, features in arrived:
        total += jnp.dot(features, weight_rows(owner, m, step), preferred_element_type=jnp.float32)
    total += LOWRANK_SCALE * expanded.astype(jnp.bfloat16).astype(jnp.float32)
    return total.astype(jnp.bfloat16)


def solution(mesh):
    placed = (
        P(("parts", "adapter"), "tensor"),
        P(("parts", "adapter"), None),
        P(),
        P(None, "tensor"),
        P("adapter", None, "tensor"),
        P("adapter", None, "tensor"),
    )
    return jax.shard_map(
        body,
        mesh=mesh,
        in_specs=placed,
        out_specs=P(("parts", "adapter"), "tensor"),
        check_vma=False,
    )
```

```python
import jax
import jax.numpy as jnp
from jax import lax
from jax.sharding import PartitionSpec as P

LOWRANK_SCALE = 2.0
CORES = 2
SHARES = (2, 6, 5, 3)


def flipped(value, axis, flip):
    count = lax.axis_size(axis)
    return lax.ppermute(value, axis, [(i, i ^ flip) for i in range(count)])


def by_device(pieces, me):
    bit = 1
    while bit < len(pieces):
        swap = (me & bit) != 0
        pieces = [jnp.where(swap, pieces[j ^ bit], pieces[j]) for j in range(len(pieces))]
        bit *= 2
    return pieces


def chained(*values):
    return lax.optimization_barrier(values)


def body(
    tokens, tenant, placement, frozen_projection_weight, lowrank_down_weight, lowrank_up_weight
):
    rows, depth = tokens.shape
    slots = placement.shape[0]
    tensors = lax.axis_size("tensor")
    groups = lax.axis_size("adapter")
    parts = lax.axis_size("parts")
    me = lax.axis_index("tensor")
    group = lax.axis_index("adapter")
    part = lax.axis_index("parts")
    rank = lowrank_up_weight.shape[1]
    share = depth // parts
    unit = depth // sum(SHARES)
    edges = [unit * sum(SHARES[:m]) for m in range(len(SHARES) + 1)]
    columns = lowrank_up_weight.shape[2]

    down = lowrank_down_weight[0].T
    pieces = [
        lax.dynamic_slice_in_dim(down, (me ^ flip) * depth + part * share, share, axis=1)
        for flip in range(tensors)
    ]
    chunks = [tokens[:, edges[m] : edges[m + 1]] for m in range(len(SHARES))]
    pieces = [pieces[0]] + [flipped(pieces[f], "tensor", f) for f in range(1, tensors)]
    hops = range(CORES, tensors, CORES)
    far = [[flipped(chunk, "tensor", hop) for hop in hops] for chunk in chunks]
    ups = [lowrank_up_weight[0]] + [
        flipped(lowrank_up_weight[0], "adapter", f) for f in range(1, groups)
    ]
    neighbour = flipped(tokens, "tensor", 1)

    def weight_rows(owner, start, width):
        return lax.dynamic_slice_in_dim(
            frozen_projection_weight, owner * depth + start, width, axis=0
        )

    def times_weight(features, owner, start):
        return jnp.dot(
            features,
            weight_rows(owner, start, features.shape[1]),
            preferred_element_type=jnp.float32,
        )

    pieces, far[0] = chained(pieces, far[0])
    own = jnp.concatenate(by_device(pieces, me), axis=0)
    downs = [own] + [flipped(own, "adapter", f) for f in range(1, groups)]
    shares = [[piece] + [flipped(piece, "parts", f) for f in range(1, parts)] for piece in downs]

    total = times_weight(tokens, me, 0)
    total, neighbour = chained(total, neighbour)
    total += times_weight(neighbour, me ^ 1, 0)
    for m in range(len(SHARES) - 1):
        total, far[m] = chained(total, far[m])
        for hop, value in zip(hops, far[m]):
            near = flipped(value, "tensor", 1)
            total += times_weight(value, me ^ hop, edges[m])
            total, near = chained(total, near)
            total += times_weight(near, me ^ hop ^ 1, edges[m])

    labels = tenant[:, 0]
    slot_ids = jnp.arange(slots, dtype=jnp.int32)
    stored = jnp.sum(jnp.where(labels[:, None] == slot_ids[None, :], placement[None, :], 0), axis=1)
    masks = [(stored == (group ^ f))[:, None] for f in range(groups)]
    partial = jnp.zeros((rows, rank), jnp.float32)
    for f in range(groups):
        for p in range(parts):
            mine = lax.dynamic_slice_in_dim(tokens, (part ^ p) * share, share, axis=1)
            partial += jnp.where(
                masks[f],
                lax.dot_general(
                    mine,
                    shares[f][p],
                    (((1,), (1,)), ((), ())),
                    preferred_element_type=jnp.float32,
                ),
                0.0,
            )
    flip = 1
    while flip < tensors:
        partial += flipped(partial, "tensor", flip)
        flip *= 2
    shrunk = partial.astype(jnp.bfloat16)
    spread = jnp.concatenate(
        [jnp.where(mask, shrunk, jnp.zeros((), shrunk.dtype)) for mask in masks], axis=1
    )
    expanded = jnp.dot(
        spread, jnp.concatenate(ups, axis=0), preferred_element_type=jnp.float32
    ).astype(jnp.bfloat16)
    total += LOWRANK_SCALE * expanded.astype(jnp.float32)

    for hop, value in zip(hops, far[-1]):
        near = flipped(value, "tensor", 1)
        total += times_weight(value, me ^ hop, edges[-2])
        total, near = chained(total, near)
        total += times_weight(near, me ^ hop ^ 1, edges[-2])
    return total.astype(jnp.bfloat16)


def solution(mesh):
    placed = (
        P(("parts", "adapter"), "tensor"),
        P(("parts", "adapter"), None),
        P(),
        P(None, "tensor"),
        P("adapter", None, "tensor"),
        P("adapter", None, "tensor"),
    )
    return jax.shard_map(
        body,
        mesh=mesh,
        in_specs=placed,
        out_specs=P(("parts", "adapter"), "tensor"),
        check_vma=False,
    )
```

```python
import functools

import jax
import jax.numpy as jnp
from jax import lax
from jax.experimental import pallas as pl
from jax.experimental.pallas import tpu as pltpu
from jax.sharding import PartitionSpec as P

LOWRANK_SCALE = 2.0
CORES = 2
LANES = 128
CUTS = (0.1875, 0.75)
VMEM_BYTES = 24 * 1024 * 1024
FREE = pl.CostEstimate(flops=0, bytes_accessed=0, transcendentals=0)
LONG = pl.CostEstimate(flops=10**10, bytes_accessed=0, transcendentals=0)
ANYWHERE = pl.BlockSpec(memory_space=pl.ANY)
IN_HBM = pl.BlockSpec(memory_space=pltpu.HBM)
VECTOR = pl.BlockSpec(memory_space=pltpu.VMEM)
SCALAR = pl.BlockSpec(memory_space=pltpu.SMEM)


def flipped(value, axis, flip):
    count = lax.axis_size(axis)
    return lax.ppermute(value, axis, [(i, i ^ flip) for i in range(count)])


def chained(*values):
    return lax.optimization_barrier(values)


def tile_of(width):
    return max(t for t in range(1, width + 1) if width % t == 0 and (t == width or t % LANES == 0) and t <= 768)


def call(kernel, out_shape, in_specs, scratch, out_specs=VECTOR, cost=FREE):
    return pl.pallas_call(
        kernel,
        out_shape=out_shape,
        in_specs=in_specs,
        out_specs=out_specs,
        scratch_shapes=scratch,
        cost_estimate=cost,
        compiler_params=pltpu.CompilerParams(vmem_limit_bytes=VMEM_BYTES),
    )


def row_masks(tenant, placement_ref, slots, wanted):
    stored = jnp.zeros(tenant.shape, jnp.int32)
    for slot in range(slots):
        stored = jnp.where(tenant == slot, placement_ref[slot], stored)
    return [stored == slot for slot in wanted]


def add_products(starts_ref, features, weight_ref, held_ref, sems, total_ref, begun=False):
    copies, base = [], 0
    for i, part in enumerate(features):
        width = part.shape[1]
        start = pl.multiple_of(starts_ref[i], LANES)
        copies.append(
            pltpu.make_async_copy(
                weight_ref.at[pl.ds(start, width)], held_ref.at[pl.ds(base, width)], sems.at[i]
            )
        )
        copies[-1].start()
        base += width

    def finish():
        base = 0
        for i, part in enumerate(features):
            width = part.shape[1]
            tile = tile_of(width)
            copies[i].wait()
            for k in range(0, width, tile):
                total_ref[...] += jnp.dot(
                    part[:, k : k + tile],
                    held_ref[base + k : base + k + tile],
                    preferred_element_type=jnp.float32,
                )
            base += width

    return finish


def products_kernel(count, has_total, starts_ref, weight_ref, *refs):
    features = refs[:count]
    given = refs[count] if has_total else None
    out_ref, held_ref, sems = refs[count + has_total :]
    finish = add_products(starts_ref, features, weight_ref, held_ref, sems, out_ref)
    out_ref[...] = given[...] if has_total else jnp.zeros_like(out_ref)
    finish()


def products(starts, features, weight, total=None, cost=FREE):
    rows, columns = features[0].shape[0], weight.shape[1]
    count = len(features)
    given = [] if total is None else [total]
    return call(
        functools.partial(products_kernel, count, len(given)),
        jax.ShapeDtypeStruct((rows, columns), jnp.float32),
        [SCALAR, IN_HBM] + [VECTOR] * (count + len(given)),
        [
            pltpu.VMEM((sum(f.shape[1] for f in features), columns), weight.dtype),
            pltpu.SemaphoreType.DMA((count,)),
        ],
        cost=cost,
    )(jnp.stack(starts), weight, *features, *given)


def last_kernel(count, offsets, slots, starts_ref, ids_ref, placement_ref, weight_ref, *refs):
    features = refs[:count]
    given, tenant_ref, sum_ref, more_ref, ups_ref = refs[count : count + 5]
    out_ref, held_ref, total_ref, sems = refs[count + 5 :]
    finish = add_products(starts_ref, features, weight_ref, held_ref, sems, total_ref)
    shrunk = (sum_ref[...] + more_ref[...]).astype(jnp.bfloat16)
    masks = row_masks(
        tenant_ref[...], placement_ref, slots, [ids_ref[0] ^ offset for offset in offsets]
    )
    spread = jnp.concatenate(
        [jnp.where(mask, shrunk, jnp.zeros((), shrunk.dtype)) for mask in masks], axis=1
    )
    expanded = jnp.dot(spread, ups_ref[...], preferred_element_type=jnp.float32)
    expanded = expanded.astype(jnp.bfloat16).astype(jnp.float32)
    total_ref[...] = given[...] + LOWRANK_SCALE * expanded
    finish()
    out_ref[...] = total_ref[...].astype(out_ref.dtype)


def shrink_kernel(offsets, slots, rank, shares, ids_ref, placement_ref, tokens_ref, tenant_ref, *refs):
    downs, out_ref = refs[:-1], refs[-1]
    share = downs[0].shape[1]
    masks = row_masks(
        tenant_ref[...], placement_ref, slots, [ids_ref[0] ^ offset for offset in offsets]
    )
    total = jnp.zeros(out_ref.shape, jnp.float32)
    per_share = len(downs) // shares
    for p in range(shares):
        start = pl.multiple_of((ids_ref[1] ^ p) * share, LANES)
        own = tokens_ref[:, pl.ds(start, share)]
        slot = 0
        for down in downs[p * per_share : (p + 1) * per_share]:
            sums = lax.dot_general(
                own, down[...], (((1,), (1,)), ((), ())), preferred_element_type=jnp.float32
            )
            for b in range(down.shape[0] // rank):
                total += jnp.where(masks[slot], sums[:, b * rank : (b + 1) * rank], 0.0)
                slot += 1
    out_ref[...] = total


def order_kernel(rank_part, ids_ref, *refs):
    pieces, out_ref, sems = refs[:-2], refs[-2], refs[-1]
    copies = [
        pltpu.make_async_copy(
            piece,
            out_ref.at[pl.ds(pl.multiple_of((ids_ref[2] ^ flip) * rank_part, rank_part), rank_part)],
            sems.at[flip],
        )
        for flip, piece in enumerate(pieces)
    ]
    for copy in copies:
        copy.start()
    for copy in copies:
        copy.wait()


def body(
    tokens, tenant, placement, frozen_projection_weight, lowrank_down_weight, lowrank_up_weight
):
    rows, depth = tokens.shape
    slots = placement.shape[0]
    tensors = lax.axis_size("tensor")
    groups = lax.axis_size("adapter")
    parts = lax.axis_size("parts")
    me = lax.axis_index("tensor")
    part = lax.axis_index("parts")
    ids = jnp.stack([lax.axis_index("adapter"), part, me])
    rank, columns = lowrank_up_weight.shape[1:]
    share = depth // parts
    edges = [0] + [int(depth * cut) // LANES * LANES for cut in CUTS] + [depth]

    down = lowrank_down_weight[0].T
    pieces = [
        lax.dynamic_slice_in_dim(down, (me ^ flip) * depth + part * share, share, axis=1)
        for flip in range(tensors)
    ]
    chunks = [tokens[:, a:b] for a, b in zip(edges, edges[1:])]
    pieces = [pieces[0]] + [flipped(pieces[f], "tensor", f) for f in range(1, tensors)]
    hops = range(CORES, tensors, CORES)
    neighbour = flipped(tokens, "tensor", 1)
    if lowrank_down_weight.shape[2] % 16 == 0:
        own = call(
            functools.partial(order_kernel, lowrank_down_weight.shape[2]),
            jax.ShapeDtypeStruct((rank, share), down.dtype),
            [SCALAR] + [ANYWHERE] * tensors,
            [pltpu.SemaphoreType.DMA((tensors,))],
            ANYWHERE,
        )(ids, *pieces)
    else:
        own = jnp.concatenate(
            [
                sum(jnp.where((me ^ f) == j, pieces[f], jnp.zeros((), down.dtype)) for f in range(tensors))
                for j in range(tensors)
            ],
            axis=0,
        )

    def send(m):
        return [flipped(chunks[m], "tensor", hop) for hop in hops]

    def spread_out(m, far):
        starts, features = [], []
        for hop, value in zip(hops, far):
            features += [value, flipped(value, "tensor", 1)]
            starts += [(me ^ hop) * depth + edges[m], (me ^ hop ^ 1) * depth + edges[m]]
        return starts, features

    first = send(0)
    own, chunks[1], chunks[2] = chained(own, chunks[1], chunks[2])
    second, third = send(1), send(2)
    total = products([me * depth, (me ^ 1) * depth], [tokens, neighbour], frozen_projection_weight)
    first, total = chained(first, total)

    offsets, held = [0], own
    mask = groups - 1
    while mask:
        arriving = flipped(held, "adapter", mask)
        if mask == groups - 1:
            arriving, total, up = chained(arriving, total, lowrank_up_weight[0])
        offsets = offsets + [offset ^ mask for offset in offsets]
        mask //= 2
        if mask:
            held = jnp.concatenate([held, arriving], axis=0)
    starts, features = spread_out(0, first)
    downs = [held, arriving]
    downs = downs + [flipped(value, "parts", p) for p in range(1, parts) for value in downs]
    ups = [up] + [flipped(up, "adapter", offset) for offset in offsets[1:]]
    ups, downs = chained(ups, downs)
    ups = jnp.concatenate(ups, axis=0)

    partial = call(
        functools.partial(shrink_kernel, offsets, slots, rank, parts),
        jax.ShapeDtypeStruct((rows, rank), jnp.float32),
        [SCALAR, SCALAR] + [VECTOR] * (2 + len(downs)),
        [],
    )(ids, placement, tokens, tenant, *downs)
    second, partial = chained(second, partial)
    more_starts, more_features = spread_out(1, second)
    flip = 1
    while flip < tensors // 2:
        partial += flipped(partial, "tensor", flip)
        flip *= 2
    more_features, partial = chained(more_features, partial)
    more = flipped(partial, "tensor", flip)
    total = products(
        starts + more_starts, features + more_features, frozen_projection_weight, total, LONG
    )
    third, total = chained(third, total)
    starts, features = spread_out(2, third)

    return call(
        functools.partial(last_kernel, len(features), offsets, slots),
        jax.ShapeDtypeStruct((rows, columns), jnp.bfloat16),
        [SCALAR, SCALAR, SCALAR, IN_HBM] + [VECTOR] * (len(features) + 5),
        [
            pltpu.VMEM((sum(f.shape[1] for f in features), columns), jnp.bfloat16),
            pltpu.VMEM((rows, columns), jnp.float32),
            pltpu.SemaphoreType.DMA((len(features),)),
        ],
    )(
        jnp.stack(starts), ids, placement, frozen_projection_weight, *features, total, tenant,
        partial, more, ups,
    )


def solution(mesh):
    placed = (
        P(("parts", "adapter"), "tensor"),
        P(("parts", "adapter"), None),
        P(),
        P(None, "tensor"),
        P("adapter", None, "tensor"),
        P("adapter", None, "tensor"),
    )
    return jax.shard_map(
        body,
        mesh=mesh,
        in_specs=placed,
        out_specs=P(("parts", "adapter"), "tensor"),
        check_vma=False,
    )
```

```python
import functools

import jax
import jax.numpy as jnp
from jax import lax
from jax.experimental import pallas as pl
from jax.experimental.pallas import tpu as pltpu
from jax.sharding import PartitionSpec as P

LOWRANK_SCALE = 2.0
CORES = 2
LANES = 128
CUTS = (0.1875, 0.75)
VMEM_BYTES = 48 * 1024 * 1024
FREE = pl.CostEstimate(flops=0, bytes_accessed=0, transcendentals=0)
LONG = pl.CostEstimate(flops=10**10, bytes_accessed=0, transcendentals=0)
ANYWHERE = pl.BlockSpec(memory_space=pl.ANY)
IN_HBM = pl.BlockSpec(memory_space=pltpu.HBM)
VECTOR = pl.BlockSpec(memory_space=pltpu.VMEM)
SCALAR = pl.BlockSpec(memory_space=pltpu.SMEM)


def flipped(value, axis, flip):
    count = lax.axis_size(axis)
    return lax.ppermute(value, axis, [(i, i ^ flip) for i in range(count)])


def chained(*values):
    return lax.optimization_barrier(values)


def tile_of(width):
    return max(t for t in range(1, width + 1) if width % t == 0 and (t == width or t % LANES == 0) and t <= 768)


def call(kernel, out_shape, in_specs, scratch, out_specs=VECTOR, cost=FREE):
    return pl.pallas_call(
        kernel,
        out_shape=out_shape,
        in_specs=in_specs,
        out_specs=out_specs,
        scratch_shapes=scratch,
        cost_estimate=cost,
        compiler_params=pltpu.CompilerParams(vmem_limit_bytes=VMEM_BYTES),
    )


def slot_masks(tenant, placement_ref, slots, wanted):
    stored = jnp.zeros(tenant.shape, jnp.int32)
    for slot in range(slots):
        stored = jnp.where(tenant == slot, placement_ref[slot], stored)
    return [stored == slot for slot in wanted]


def add_products(starts_ref, features, weight_ref, held_ref, sems, total_ref, begun=False):
    copies, base = [], 0
    for i, part in enumerate(features):
        width = part.shape[1]
        start = pl.multiple_of(starts_ref[i], LANES)
        copies.append(
            pltpu.make_async_copy(
                weight_ref.at[pl.ds(start, width)], held_ref.at[pl.ds(base, width)], sems.at[i]
            )
        )
        copies[-1].start()
        base += width

    def finish():
        base = 0
        for i, part in enumerate(features):
            width = part.shape[1]
            tile = tile_of(width)
            copies[i].wait()
            for k in range(0, width, tile):
                total_ref[...] += jnp.dot(
                    part[:, k : k + tile],
                    held_ref[base + k : base + k + tile],
                    preferred_element_type=jnp.float32,
                )
            base += width

    return finish


def products_kernel(count, has_total, starts_ref, weight_ref, *refs):
    features = refs[:count]
    given = refs[count] if has_total else None
    out_ref, held_ref, sems = refs[count + has_total :]
    finish = add_products(starts_ref, features, weight_ref, held_ref, sems, out_ref)
    out_ref[...] = given[...] if has_total else jnp.zeros_like(out_ref)
    finish()


def products(starts, features, weight, total=None, cost=FREE):
    rows, columns = features[0].shape[0], weight.shape[1]
    count = len(features)
    given = [] if total is None else [total]
    return call(
        functools.partial(products_kernel, count, len(given)),
        jax.ShapeDtypeStruct((rows, columns), jnp.float32),
        [SCALAR, IN_HBM] + [VECTOR] * (count + len(given)),
        [
            pltpu.VMEM((sum(f.shape[1] for f in features), columns), weight.dtype),
            pltpu.SemaphoreType.DMA((count,)),
        ],
        cost=cost,
    )(jnp.stack(starts), weight, *features, *given)


def last_kernel(count, offsets, slots, starts_ref, ids_ref, placement_ref, weight_ref, *refs):
    features = refs[:count]
    given, tenant_ref, sum_ref, more_ref = refs[count : count + 4]
    ups = refs[count + 4 : count + 4 + len(offsets)]
    out_ref, held_ref, total_ref, sems = refs[count + 4 + len(offsets) :]
    finish = add_products(starts_ref, features, weight_ref, held_ref, sems, total_ref)
    shrunk = (sum_ref[...] + more_ref[...]).astype(jnp.bfloat16).astype(jnp.float32)
    masks = slot_masks(
        tenant_ref[...], placement_ref, slots, [ids_ref[0] ^ offset for offset in offsets]
    )
    spread = jnp.concatenate([jnp.where(mask, shrunk, 0.0) for mask in masks], axis=0)
    spread = spread.T.astype(jnp.bfloat16)
    stacked = jnp.concatenate([up[...] for up in ups], axis=0)
    expanded = jnp.dot(spread, stacked, preferred_element_type=jnp.float32)
    expanded = expanded.astype(jnp.bfloat16).astype(jnp.float32)
    total_ref[...] = given[...] + LOWRANK_SCALE * expanded
    finish()
    out_ref[...] = total_ref[...].astype(out_ref.dtype)


def shrink_kernel(offsets, slots, rank, shares, ids_ref, placement_ref, tokens_ref, tenant_ref, *refs):
    downs, out_ref = refs[:-1], refs[-1]
    share = downs[0].shape[1]
    masks = slot_masks(
        tenant_ref[...], placement_ref, slots, [ids_ref[0] ^ offset for offset in offsets]
    )
    total = jnp.zeros(out_ref.shape, jnp.float32)
    per_share = len(downs) // shares
    for p in range(shares):
        start = pl.multiple_of((ids_ref[1] ^ p) * share, LANES)
        own = tokens_ref[:, pl.ds(start, share)]
        slot = 0
        for down in downs[p * per_share : (p + 1) * per_share]:
            sums = lax.dot_general(
                down[...], own, (((1,), (1,)), ((), ())), preferred_element_type=jnp.float32
            )
            for b in range(down.shape[0] // rank):
                total += jnp.where(masks[slot], sums[b * rank : (b + 1) * rank], 0.0)
                slot += 1
    out_ref[...] = total


def cut_kernel(edges, share, ids_ref, tokens_ref, down_ref, *refs):
    outs, sems = refs[:-1], refs[-1]
    depth = tokens_ref.shape[1]
    chunks, pieces = outs[: len(edges) - 1], outs[len(edges) - 1 :]
    copies = []
    for flip, piece in enumerate(pieces):
        start = pl.multiple_of((ids_ref[2] ^ flip) * depth + ids_ref[1] * share, LANES)
        copies.append((down_ref.at[:, pl.ds(start, share)], piece))
    for a, b, chunk in zip(edges, edges[1:], chunks):
        copies.append((tokens_ref.at[:, a:b], chunk))
    copies = [
        pltpu.make_async_copy(source, target, sems.at[i])
        for i, (source, target) in enumerate(copies)
    ]
    for copy in copies:
        copy.start()
    for copy in copies:
        copy.wait()


def order_kernel(rank_part, ids_ref, *refs):
    pieces, out_ref, sems = refs[:-2], refs[-2], refs[-1]
    copies = [
        pltpu.make_async_copy(
            piece,
            out_ref.at[pl.ds(pl.multiple_of((ids_ref[2] ^ flip) * rank_part, rank_part), rank_part)],
            sems.at[flip],
        )
        for flip, piece in enumerate(pieces)
    ]
    for copy in copies:
        copy.start()
    for copy in copies:
        copy.wait()


def body(
    tokens, tenant, placement, frozen_projection_weight, lowrank_down_weight, lowrank_up_weight
):
    rows, depth = tokens.shape
    slots = placement.shape[0]
    tensors = lax.axis_size("tensor")
    groups = lax.axis_size("adapter")
    parts = lax.axis_size("parts")
    me = lax.axis_index("tensor")
    part = lax.axis_index("parts")
    ids = jnp.stack([lax.axis_index("adapter"), part, me])
    rank, columns = lowrank_up_weight.shape[1:]
    share = depth // parts
    tenant_row = tenant.reshape(1, rows)
    edges = [0] + [int(depth * cut) // LANES * LANES for cut in CUTS] + [depth]

    down = lowrank_down_weight[0].T
    whole_tiles = down.shape[0] % 16 == 0
    if whole_tiles:
        cut = call(
            functools.partial(cut_kernel, edges, share),
            [jax.ShapeDtypeStruct((rows, b - a), tokens.dtype) for a, b in zip(edges, edges[1:])]
            + [jax.ShapeDtypeStruct((down.shape[0], share), down.dtype)] * tensors,
            [SCALAR, ANYWHERE, ANYWHERE],
            [pltpu.SemaphoreType.DMA((len(edges) - 1 + tensors,))],
            [ANYWHERE] * (len(edges) - 1 + tensors),
        )(ids, tokens, down)
        chunks, pieces = list(cut[: len(edges) - 1]), list(cut[len(edges) - 1 :])
    else:
        chunks = [tokens[:, a:b] for a, b in zip(edges, edges[1:])]
        pieces = [
            lax.dynamic_slice_in_dim(down, (me ^ flip) * depth + part * share, share, axis=1)
            for flip in range(tensors)
        ]
    pieces = [pieces[0]] + [flipped(pieces[f], "tensor", f) for f in range(1, tensors)]
    hops = range(CORES, tensors, CORES)
    neighbour = flipped(tokens, "tensor", 1)
    if whole_tiles:
        own = call(
            functools.partial(order_kernel, lowrank_down_weight.shape[2]),
            jax.ShapeDtypeStruct((rank, share), down.dtype),
            [SCALAR] + [ANYWHERE] * tensors,
            [pltpu.SemaphoreType.DMA((tensors,))],
            ANYWHERE,
        )(ids, *pieces)
    else:
        own = jnp.concatenate(
            [
                sum(jnp.where((me ^ f) == j, pieces[f], jnp.zeros((), down.dtype)) for f in range(tensors))
                for j in range(tensors)
            ],
            axis=0,
        )

    def send(m):
        return [flipped(chunks[m], "tensor", hop) for hop in hops]

    def spread_out(m, far):
        starts, features = [], []
        for hop, value in zip(hops, far):
            features += [value, flipped(value, "tensor", 1)]
            starts += [(me ^ hop) * depth + edges[m], (me ^ hop ^ 1) * depth + edges[m]]
        return starts, features

    far = [send(m) for m in range(len(chunks))]

    offsets = list(range(groups))
    up = lowrank_up_weight[0]
    ups = [up] + [flipped(up, "adapter", offset) for offset in offsets[1:]]
    arriving = [own] + [flipped(own, "adapter", offset) for offset in offsets[1:]]
    own, neighbour, ups = chained(own, neighbour, ups)
    total = products(
        [me * depth, (me ^ 1) * depth], [tokens, neighbour], frozen_projection_weight, cost=LONG
    )
    for offset in offsets[1:]:
        arriving[offset], total = chained(arriving[offset], total)
    exchanged = [
        [flipped(value, "parts", p) for value in arriving] for p in range(1, parts)
    ]
    starts, features = spread_out(0, far[0])
    total = products(starts, features, frozen_projection_weight, total, LONG)
    exchanged, total = chained(exchanged, total)
    downs = arriving + [value for values in exchanged for value in values]
    far[1], downs = chained(far[1], downs)

    partial = call(
        functools.partial(shrink_kernel, offsets, slots, rank, parts),
        jax.ShapeDtypeStruct((rank, rows), jnp.float32),
        [SCALAR, SCALAR] + [VECTOR] * (2 + len(downs)),
        [],
        cost=LONG,
    )(ids, placement, tokens, tenant_row, *downs)
    starts, features = spread_out(1, far[1])
    total = products(starts, features, frozen_projection_weight, total, LONG)
    flip = 1
    while flip < tensors // 2:
        received = flipped(partial, "tensor", flip)
        if flip == 1:
            received, total = chained(received, total)
        partial += received
        flip *= 2
    more = flipped(partial, "tensor", flip)
    far[2], total, partial = chained(far[2], total, partial)
    starts, features = spread_out(2, far[2])

    return call(
        functools.partial(last_kernel, len(features), offsets, slots),
        jax.ShapeDtypeStruct((rows, columns), jnp.bfloat16),
        [SCALAR, SCALAR, SCALAR, IN_HBM] + [VECTOR] * (len(features) + 4 + groups),
        [
            pltpu.VMEM((sum(f.shape[1] for f in features), columns), jnp.bfloat16),
            pltpu.VMEM((rows, columns), jnp.float32),
            pltpu.SemaphoreType.DMA((len(features),)),
        ],
    )(
        jnp.stack(starts), ids, placement, frozen_projection_weight, *features, total, tenant_row,
        partial, more, *ups,
    )


def solution(mesh):
    placed = (
        P(("parts", "adapter"), "tensor"),
        P(("parts", "adapter"), None),
        P(),
        P(None, "tensor"),
        P("adapter", None, "tensor"),
        P("adapter", None, "tensor"),
    )
    return jax.shard_map(
        body,
        mesh=mesh,
        in_specs=placed,
        out_specs=P(("parts", "adapter"), "tensor"),
        check_vma=False,
    )
```

```python
import functools
import math

import jax
import jax.numpy as jnp
from jax import lax
from jax.experimental import pallas as pl
from jax.experimental.pallas import tpu as pltpu
from jax.sharding import PartitionSpec as P

LOWRANK_SCALE = 2.0
CORES = 2
LANES = 128
CUTS = (0.75,)
MIB = 1024 * 1024
FREE = pl.CostEstimate(flops=0, bytes_accessed=0, transcendentals=0)
LONG = pl.CostEstimate(flops=10**11, bytes_accessed=0, transcendentals=0)
ANYWHERE = pl.BlockSpec(memory_space=pl.ANY)
VECTOR = pl.BlockSpec(memory_space=pltpu.VMEM)
SCALAR = pl.BlockSpec(memory_space=pltpu.SMEM)


def flipped(value, axis, flip):
    count = lax.axis_size(axis)
    return lax.ppermute(value, axis, [(i, i ^ flip) for i in range(count)])


def chained(*values):
    return lax.optimization_barrier(values)


def call(kernel, out_shape, in_specs, scratch, out_specs=VECTOR, cost=LONG, mib=48):
    return pl.pallas_call(
        kernel,
        out_shape=out_shape,
        in_specs=in_specs,
        out_specs=out_specs,
        scratch_shapes=scratch,
        cost_estimate=cost,
        compiler_params=pltpu.CompilerParams(vmem_limit_bytes=mib * MIB),
    )


def run_copies(pairs, sems):
    copies = [
        pltpu.make_async_copy(source, target, sems.at[i]) for i, (source, target) in enumerate(pairs)
    ]
    for copy in copies:
        copy.start()
    for copy in copies:
        copy.wait()


def cut_kernel(edges, source_ref, *refs):
    run_copies(
        [(source_ref.at[:, a:b], out) for a, b, out in zip(edges, edges[1:], refs[:-1])], refs[-1]
    )


def slice_kernel(ids_ref, down_ref, *refs):
    outs, sems = refs[:-1], refs[-1]
    depth = outs[0].shape[1]
    run_copies(
        [
            (down_ref.at[:, pl.ds(pl.multiple_of((ids_ref[0] ^ flip) * depth, LANES), depth)], out)
            for flip, out in enumerate(outs)
        ],
        sems,
    )


def order_kernel(rank_part, ids_ref, *refs):
    pieces, out_ref, sems = refs[:-2], refs[-2], refs[-1]
    run_copies(
        [
            (piece, out_ref.at[pl.ds(pl.multiple_of((ids_ref[0] ^ f) * rank_part, rank_part), rank_part)])
            for f, piece in enumerate(pieces)
        ],
        sems,
    )


def slot_of_row(tenant, placement_ref, slots):
    stored = jnp.zeros(tenant.shape, jnp.int32)
    for slot in range(slots):
        stored = jnp.where(tenant == slot, placement_ref[slot], stored)
    return stored


def start_tiles(tile, starts_ref, features, weight_ref, held_ref, rows_ref, sems):
    t = 0
    for i, part in enumerate(features):
        for k in range(0, part.shape[1], tile):
            start = pl.multiple_of(starts_ref[i] + k, LANES)
            pltpu.make_async_copy(part.at[:, pl.ds(k, tile)], held_ref.at[t], sems.at[0, t]).start()
            pltpu.make_async_copy(
                weight_ref.at[pl.ds(start, tile)], rows_ref.at[t], sems.at[1, t]
            ).start()
            t += 1


def add_tiles(held_ref, rows_ref, sems, total_ref):
    @pl.loop(0, held_ref.shape[0])
    def _(t):
        pltpu.make_async_copy(held_ref.at[t], held_ref.at[t], sems.at[0, t]).wait()
        pltpu.make_async_copy(rows_ref.at[t], rows_ref.at[t], sems.at[1, t]).wait()
        total_ref[...] += jnp.dot(held_ref[t], rows_ref[t], preferred_element_type=jnp.float32)


def tile_scratch(tile, features, columns):
    tiles = sum(f.shape[1] for f in features) // tile
    rows = features[0].shape[0]
    return [
        pltpu.VMEM((tiles, rows, tile), jnp.bfloat16),
        pltpu.VMEM((tiles, tile, columns), jnp.bfloat16),
        pltpu.SemaphoreType.DMA((2, tiles)),
    ]


def products_kernel(tile, count, has_total, starts_ref, weight_ref, *refs):
    features = refs[:count]
    given = refs[count] if has_total else None
    out_ref, held_ref, rows_ref, sems = refs[count + has_total :]
    start_tiles(tile, starts_ref, features, weight_ref, held_ref, rows_ref, sems)
    out_ref[...] = given[...] if has_total else jnp.zeros_like(out_ref)
    add_tiles(held_ref, rows_ref, sems, out_ref)


def products(tile, starts, features, weight, total=None):
    given = [] if total is None else [total]
    return call(
        functools.partial(products_kernel, tile, len(features), len(given)),
        jax.ShapeDtypeStruct((features[0].shape[0], weight.shape[1]), jnp.float32),
        [SCALAR, ANYWHERE] + [ANYWHERE] * len(features) + [VECTOR] * len(given),
        tile_scratch(tile, features, weight.shape[1]),
    )(jnp.stack(starts), weight, *features, *given)


def last_kernel(tile, count, slots, starts_ref, ids_ref, placement_ref, weight_ref, *refs):
    features = refs[:count]
    given, tenant_ref, sum_ref, more_ref = refs[count : count + 4]
    ups = refs[count + 4 : count + 4 + slots]
    out_ref, total_ref, held_ref, rows_ref, sems = refs[count + 4 + slots :]
    start_tiles(tile, starts_ref, features, weight_ref, held_ref, rows_ref, sems)
    shrunk = (sum_ref[...] + more_ref[...]).astype(jnp.bfloat16).astype(jnp.float32)
    stored = slot_of_row(tenant_ref[...], placement_ref, slots)
    spread = jnp.concatenate(
        [jnp.where(stored == (ids_ref[1] ^ offset), shrunk, 0.0) for offset in range(slots)], axis=0
    )
    stacked = jnp.concatenate([up[...] for up in ups], axis=0)
    expanded = jnp.dot(
        spread.T.astype(jnp.bfloat16), stacked, preferred_element_type=jnp.float32
    )
    expanded = expanded.astype(jnp.bfloat16).astype(jnp.float32)
    total_ref[...] = given[...] + LOWRANK_SCALE * expanded
    add_tiles(held_ref, rows_ref, sems, total_ref)
    out_ref[...] = total_ref[...].astype(out_ref.dtype)


def shrink_kernel(tile, slots, owners_ref, placement_ref, tokens_ref, tenant_ref, *refs):
    downs, out_ref, held_ref, down_ref, sums_ref, sems = (
        refs[:slots], refs[slots], *refs[slots + 1 :]
    )
    rank = downs[0].shape[0]
    tiles = tokens_ref.shape[1] // tile
    for k in range(tiles):
        here = pl.ds(k * tile, tile)
        pltpu.make_async_copy(tokens_ref.at[:, here], held_ref.at[k], sems.at[0, k]).start()
        for b, down in enumerate(downs):
            pltpu.make_async_copy(
                down.at[:, here], down_ref.at[k, pl.ds(b * rank, rank)], sems.at[1 + b, k]
            ).start()
    stored = slot_of_row(tenant_ref[...], placement_ref, slots)
    sums_ref[...] = jnp.zeros_like(sums_ref)

    @pl.loop(0, tiles)
    def _(k):
        pltpu.make_async_copy(held_ref.at[k], held_ref.at[k], sems.at[0, k]).wait()
        for b in range(slots):
            block = down_ref.at[k, pl.ds(b * rank, rank)]
            pltpu.make_async_copy(block, block, sems.at[1 + b, k]).wait()
        sums_ref[...] += lax.dot_general(
            held_ref[k], down_ref[k], (((1,), (1,)), ((), ())), preferred_element_type=jnp.float32
        )

    sums = sums_ref[...].T
    total = jnp.zeros(out_ref.shape, jnp.float32)
    for b in range(slots):
        total += jnp.where(stored == owners_ref[b], sums[b * rank : (b + 1) * rank], 0.0)
    out_ref[...] = total


def body(
    tokens, tenant, placement, frozen_projection_weight, lowrank_down_weight, lowrank_up_weight
):
    rows, depth = tokens.shape
    slots = placement.shape[0]
    tensors = lax.axis_size("tensor")
    groups = lax.axis_size("adapter")
    parts = lax.axis_size("parts")
    me = lax.axis_index("tensor")
    group = lax.axis_index("adapter")
    part = lax.axis_index("parts")
    ids = jnp.stack([me, group])
    rank, columns = lowrank_up_weight.shape[1:]
    tenant_row = tenant.reshape(1, rows)
    edges = [0] + [int(depth * cut) // LANES * LANES for cut in CUTS] + [depth]
    tile = math.gcd(*edges)

    down = lowrank_down_weight[0].T
    whole_tiles = down.shape[0] % 16 == 0
    if whole_tiles:
        pieces = call(
            slice_kernel,
            [jax.ShapeDtypeStruct((down.shape[0], depth), down.dtype)] * tensors,
            [SCALAR, ANYWHERE],
            [pltpu.SemaphoreType.DMA((tensors,))],
            [ANYWHERE] * tensors,
            cost=FREE,
            mib=60,
        )(ids, down)
    else:
        pieces = [
            lax.dynamic_slice_in_dim(down, (me ^ flip) * depth, depth, axis=1)
            for flip in range(tensors)
        ]
    neighbour = flipped(tokens, "tensor", 1)
    uncut, pieces = chained(tokens, pieces)
    chunks = call(
        functools.partial(cut_kernel, edges),
        [jax.ShapeDtypeStruct((rows, b - a), tokens.dtype) for a, b in zip(edges, edges[1:])],
        [ANYWHERE],
        [pltpu.SemaphoreType.DMA((len(edges) - 1,))],
        [ANYWHERE] * (len(edges) - 1),
        mib=60,
    )(uncut)
    pieces = [pieces[0]] + [flipped(pieces[f], "tensor", f) for f in range(1, tensors)]
    pieces, chunks = chained(pieces, chunks)
    if whole_tiles:
        own = call(
            functools.partial(order_kernel, down.shape[0]),
            jax.ShapeDtypeStruct((rank, depth), down.dtype),
            [SCALAR] + [ANYWHERE] * tensors,
            [pltpu.SemaphoreType.DMA((tensors,))],
            ANYWHERE,
            cost=FREE,
        )(ids, *pieces)
    else:
        none = jnp.zeros((), down.dtype)
        own = jnp.concatenate(
            [sum(jnp.where((me ^ f) == j, pieces[f], none) for f in range(tensors)) for j in range(tensors)],
            axis=0,
        )

    hops = range(CORES, tensors, CORES)
    far = [[flipped(chunks[0], "tensor", hop) for hop in hops]]

    def spread_out(m):
        starts, features = [], []
        for hop, value in zip(hops, far[m]):
            features += [value, flipped(value, "tensor", 1)]
            starts += [(me ^ hop) * depth + edges[m], (me ^ hop ^ 1) * depth + edges[m]]
        return starts, features

    downs, owners, fetched = [own], [group], []
    flips = list(range(1, groups))
    if parts == 2:
        while len(flips) > 1:
            pair = (flips.pop(-2), flips.pop(-1))
            route = [
                (p * groups + z, p * groups + (z ^ pair[p])) for p in range(parts) for z in range(groups)
            ]
            fetched.append((pair, lax.ppermute(own, ("parts", "adapter"), route)))
    singles = [(flip, flipped(own, "adapter", flip)) for flip in flips]

    own, here = chained(own, tokens)
    total = products(tile, [me * depth], [here], frozen_projection_weight)
    total, last = chained(total, chunks[1])
    far.append([flipped(last, "tensor", hop) for hop in hops])
    for flip, value in singles:
        value, total = chained(value, total)
        downs.append(value)
        owners.append(group ^ flip)
    up = lowrank_up_weight[0]
    for pair, value in fetched:
        value, total = chained(value, total)
        swapped = flipped(value, "parts", 1)
        if pair == fetched[0][0]:
            total, neighbour = chained(total, neighbour)
            total = products(
                tile, [(me ^ 1) * depth], [neighbour], frozen_projection_weight, total
            )
            total, up = chained(total, up)
        swapped, total = chained(swapped, total)
        downs += [value, swapped]
        mine, other = (jnp.where(part == 0, *order) for order in (pair, pair[::-1]))
        owners += [group ^ mine, group ^ other]
    ups = [up] + [flipped(up, "adapter", flip) for flip in range(1, groups)]
    downs, ups = chained(downs, ups)

    tiles = depth // tile
    partial = call(
        functools.partial(shrink_kernel, tile, slots),
        jax.ShapeDtypeStruct((rank, rows), jnp.float32),
        [SCALAR, SCALAR, ANYWHERE, VECTOR] + [ANYWHERE] * slots,
        [
            pltpu.VMEM((tiles, rows, tile), jnp.bfloat16),
            pltpu.VMEM((tiles, slots * rank, tile), jnp.bfloat16),
            pltpu.VMEM((rows, slots * rank), jnp.float32),
            pltpu.SemaphoreType.DMA((1 + slots, tiles)),
        ],
    )(jnp.stack(owners), placement, tokens, tenant_row, *downs)
    far[0], partial = chained(far[0], partial)
    starts, features = spread_out(0)
    total = products(tile, starts[::2], features[::2], frozen_projection_weight, total)
    near, total = chained(features[1::2], total)
    total = products(tile, starts[1::2], near, frozen_projection_weight, total)
    flip = 1
    while flip < tensors // 2:
        received = flipped(partial, "tensor", flip)
        if flip == 1:
            received, total = chained(received, total)
        partial += received
        flip *= 2
    more = flipped(partial, "tensor", flip)
    far[1], total, partial = chained(far[1], total, partial)
    starts, features = spread_out(1)

    return call(
        functools.partial(last_kernel, tile, len(features), slots),
        jax.ShapeDtypeStruct((rows, columns), jnp.bfloat16),
        [SCALAR, SCALAR, SCALAR, ANYWHERE]
        + [ANYWHERE] * len(features)
        + [VECTOR] * (4 + slots),
        [pltpu.VMEM((rows, columns), jnp.float32)] + tile_scratch(tile, features, columns),
    )(
        jnp.stack(starts), ids, placement, frozen_projection_weight, *features, total, tenant_row,
        partial, more, *ups,
    )


def solution(mesh):
    placed = (
        P(("parts", "adapter"), "tensor"),
        P(("parts", "adapter"), None),
        P(),
        P(None, "tensor"),
        P("adapter", None, "tensor"),
        P("adapter", None, "tensor"),
    )
    return jax.shard_map(
        body,
        mesh=mesh,
        in_specs=placed,
        out_specs=P(("parts", "adapter"), "tensor"),
        check_vma=False,
    )
```

```python
import functools
import math

import jax
import jax.numpy as jnp
from jax import lax
from jax.experimental import pallas as pl
from jax.experimental.pallas import tpu as pltpu
from jax.sharding import PartitionSpec as P

LOWRANK_SCALE = 2.0
CORES = 2
LANES = 128
CUTS = (0.25, 0.75)
MIB = 1024 * 1024
FREE = pl.CostEstimate(flops=0, bytes_accessed=0, transcendentals=0)
LONG = pl.CostEstimate(flops=10**11, bytes_accessed=0, transcendentals=0)
ANYWHERE = pl.BlockSpec(memory_space=pl.ANY)
VECTOR = pl.BlockSpec(memory_space=pltpu.VMEM)
SCALAR = pl.BlockSpec(memory_space=pltpu.SMEM)


def flipped(value, axis, flip):
    count = lax.axis_size(axis)
    return lax.ppermute(value, axis, [(i, i ^ flip) for i in range(count)])


def chained(*values):
    return lax.optimization_barrier(values)


def call(kernel, out_shape, in_specs, scratch, out_specs=VECTOR, cost=LONG, mib=48):
    return pl.pallas_call(
        kernel,
        out_shape=out_shape,
        in_specs=in_specs,
        out_specs=out_specs,
        scratch_shapes=scratch,
        cost_estimate=cost,
        compiler_params=pltpu.CompilerParams(vmem_limit_bytes=mib * MIB),
    )


def run_copies(pairs, sems):
    copies = [
        pltpu.make_async_copy(source, target, sems.at[i]) for i, (source, target) in enumerate(pairs)
    ]
    for copy in copies:
        copy.start()
    for copy in copies:
        copy.wait()


def cut_kernel(edges, source_ref, *refs):
    run_copies(
        [(source_ref.at[:, a:b], out) for a, b, out in zip(edges, edges[1:], refs[:-1])], refs[-1]
    )


def slice_kernel(down_ref, *refs):
    outs, sems = refs[:-1], refs[-1]
    me, depth = lax.axis_index("tensor"), outs[0].shape[1]
    run_copies(
        [
            (down_ref.at[:, pl.ds(pl.multiple_of((me ^ flip) * depth, LANES), depth)], out)
            for flip, out in enumerate(outs)
        ],
        sems,
    )


def order_kernel(rank_part, *refs):
    pieces, out_ref, sems = refs[:-2], refs[-2], refs[-1]
    me = lax.axis_index("tensor")
    run_copies(
        [
            (piece, out_ref.at[pl.ds(pl.multiple_of((me ^ f) * rank_part, rank_part), rank_part)])
            for f, piece in enumerate(pieces)
        ],
        sems,
    )


def slot_of_row(tenant, placement_ref, slots):
    stored = jnp.zeros(tenant.shape, jnp.int32)
    for slot in range(slots):
        stored = jnp.where(tenant == slot, placement_ref[slot], stored)
    return stored


def start_tiles(tile, starts_ref, features, weight_ref, held_ref, rows_ref, sems):
    t = 0
    for i, part in enumerate(features):
        for k in range(0, part.shape[1], tile):
            start = pl.multiple_of(starts_ref[i] + k, LANES)
            pltpu.make_async_copy(part.at[:, pl.ds(k, tile)], held_ref.at[t], sems.at[0, t]).start()
            pltpu.make_async_copy(
                weight_ref.at[pl.ds(start, tile)], rows_ref.at[t], sems.at[1, t]
            ).start()
            t += 1


def add_tiles(held_ref, rows_ref, sems, total_ref):
    @pl.loop(0, held_ref.shape[0])
    def _(t):
        pltpu.make_async_copy(held_ref.at[t], held_ref.at[t], sems.at[0, t]).wait()
        pltpu.make_async_copy(rows_ref.at[t], rows_ref.at[t], sems.at[1, t]).wait()
        total_ref[...] += jnp.dot(held_ref[t], rows_ref[t], preferred_element_type=jnp.float32)


def tile_scratch(tile, features, columns):
    tiles = sum(f.shape[1] for f in features) // tile
    rows = features[0].shape[0]
    return [
        pltpu.VMEM((tiles, rows, tile), jnp.bfloat16),
        pltpu.VMEM((tiles, tile, columns), jnp.bfloat16),
        pltpu.SemaphoreType.DMA((2, tiles)),
    ]


def products_kernel(tile, count, has_total, starts_ref, weight_ref, *refs):
    features = refs[:count]
    given = refs[count] if has_total else None
    out_ref, held_ref, rows_ref, sems = refs[count + has_total :]
    start_tiles(tile, starts_ref, features, weight_ref, held_ref, rows_ref, sems)
    out_ref[...] = given[...] if has_total else jnp.zeros_like(out_ref)
    add_tiles(held_ref, rows_ref, sems, out_ref)


def products(tile, starts, features, weight, total=None):
    given = [] if total is None else [total]
    return call(
        functools.partial(products_kernel, tile, len(features), len(given)),
        jax.ShapeDtypeStruct((features[0].shape[0], weight.shape[1]), jnp.float32),
        [SCALAR, ANYWHERE] + [ANYWHERE] * len(features) + [VECTOR] * len(given),
        tile_scratch(tile, features, weight.shape[1]),
    )(jnp.stack(starts), weight, *features, *given)


def last_kernel(tile, count, slots, starts_ref, placement_ref, weight_ref, *refs):
    features = refs[:count]
    given, tenant_ref, sum_ref, more_ref = refs[count : count + 4]
    ups = refs[count + 4 : count + 4 + slots]
    out_ref, total_ref, held_ref, rows_ref, sems = refs[count + 4 + slots :]
    start_tiles(tile, starts_ref, features, weight_ref, held_ref, rows_ref, sems)
    shrunk = (sum_ref[...] + more_ref[...]).astype(jnp.bfloat16).astype(jnp.float32)
    group = lax.axis_index("adapter")
    stored = slot_of_row(tenant_ref[...], placement_ref, slots)
    spread = jnp.concatenate(
        [jnp.where(stored == (group ^ offset), shrunk, 0.0) for offset in range(slots)], axis=0
    )
    stacked = jnp.concatenate([up[...] for up in ups], axis=0)
    expanded = jnp.dot(
        spread.T.astype(jnp.bfloat16), stacked, preferred_element_type=jnp.float32
    )
    expanded = expanded.astype(jnp.bfloat16).astype(jnp.float32)
    total_ref[...] = given[...] + LOWRANK_SCALE * expanded
    add_tiles(held_ref, rows_ref, sems, total_ref)
    out_ref[...] = total_ref[...].astype(out_ref.dtype)


def shrink_kernel(tile, slots, owners_ref, placement_ref, tokens_ref, tenant_ref, *refs):
    downs, out_ref, held_ref, down_ref, sums_ref, sems = (
        refs[:slots], refs[slots], *refs[slots + 1 :]
    )
    rank = downs[0].shape[0]
    tiles = tokens_ref.shape[1] // tile
    for k in range(tiles):
        here = pl.ds(k * tile, tile)
        pltpu.make_async_copy(tokens_ref.at[:, here], held_ref.at[k], sems.at[0, k]).start()
        for b, down in enumerate(downs):
            pltpu.make_async_copy(
                down.at[:, here], down_ref.at[k, pl.ds(b * rank, rank)], sems.at[1 + b, k]
            ).start()
    stored = slot_of_row(tenant_ref[...], placement_ref, slots)
    sums_ref[...] = jnp.zeros_like(sums_ref)

    @pl.loop(0, tiles)
    def _(k):
        pltpu.make_async_copy(held_ref.at[k], held_ref.at[k], sems.at[0, k]).wait()
        for b in range(slots):
            block = down_ref.at[k, pl.ds(b * rank, rank)]
            pltpu.make_async_copy(block, block, sems.at[1 + b, k]).wait()
        sums_ref[...] += lax.dot_general(
            held_ref[k], down_ref[k], (((1,), (1,)), ((), ())), preferred_element_type=jnp.float32
        )

    sums = sums_ref[...].T
    total = jnp.zeros(out_ref.shape, jnp.float32)
    for b in range(slots):
        total += jnp.where(stored == owners_ref[b], sums[b * rank : (b + 1) * rank], 0.0)
    out_ref[...] = total


def body(
    tokens, tenant, placement, frozen_projection_weight, lowrank_down_weight, lowrank_up_weight
):
    rows, depth = tokens.shape
    slots = placement.shape[0]
    tensors = lax.axis_size("tensor")
    groups = lax.axis_size("adapter")
    parts = lax.axis_size("parts")
    me = lax.axis_index("tensor")
    group = lax.axis_index("adapter")
    part = lax.axis_index("parts")
    rank, columns = lowrank_up_weight.shape[1:]
    tenant_row = tenant.reshape(1, rows)
    edges = [0] + [int(depth * cut) // LANES * LANES for cut in CUTS] + [depth]
    tile = math.gcd(*edges)

    down = lowrank_down_weight[0].T
    whole_tiles = down.shape[0] % 16 == 0
    if whole_tiles:
        pieces = call(
            slice_kernel,
            [jax.ShapeDtypeStruct((down.shape[0], depth), down.dtype)] * tensors,
            [ANYWHERE],
            [pltpu.SemaphoreType.DMA((tensors,))],
            [VECTOR] * tensors,
            cost=FREE,
            mib=60,
        )(down)
    else:
        pieces = [
            lax.dynamic_slice_in_dim(down, (me ^ flip) * depth, depth, axis=1)
            for flip in range(tensors)
        ]
    neighbour = flipped(tokens, "tensor", 1)
    uncut, pieces = chained(tokens, pieces)
    chunks = call(
        functools.partial(cut_kernel, edges),
        [jax.ShapeDtypeStruct((rows, b - a), tokens.dtype) for a, b in zip(edges, edges[1:])],
        [ANYWHERE],
        [pltpu.SemaphoreType.DMA((len(edges) - 1,))],
        [VECTOR] * (len(edges) - 1),
        cost=FREE,
        mib=60,
    )(uncut)
    pieces = [pieces[0]] + [flipped(pieces[f], "tensor", f) for f in range(1, tensors)]
    if whole_tiles:
        own = call(
            functools.partial(order_kernel, down.shape[0]),
            jax.ShapeDtypeStruct((rank, depth), down.dtype),
            [ANYWHERE] * tensors,
            [pltpu.SemaphoreType.DMA((tensors,))],
            ANYWHERE,
            cost=FREE,
        )(*pieces)
    else:
        none = jnp.zeros((), down.dtype)
        own = jnp.concatenate(
            [sum(jnp.where((me ^ f) == j, pieces[f], none) for f in range(tensors)) for j in range(tensors)],
            axis=0,
        )

    hops = range(CORES, tensors, CORES)
    far = [[flipped(chunk, "tensor", hop) for hop in hops] for chunk in chunks[:2]]

    def spread_out(m):
        starts, features = [], []
        for hop, value in zip(hops, far[m]):
            features += [value, flipped(value, "tensor", 1)]
            starts += [(me ^ hop) * depth + edges[m], (me ^ hop ^ 1) * depth + edges[m]]
        return starts, features

    downs, owners, fetched = [own], [group], []
    flips = list(range(1, groups))
    if parts == 2:
        while len(flips) > 1:
            pair = (flips.pop(-2), flips.pop(-1))
            route = [
                (p * groups + z, p * groups + (z ^ pair[p])) for p in range(parts) for z in range(groups)
            ]
            fetched.append((pair, lax.ppermute(own, ("parts", "adapter"), route)))
    singles = [(flip, flipped(own, "adapter", flip)) for flip in flips]

    own, here = chained(own, tokens)
    total = products(tile, [me * depth], [here], frozen_projection_weight)
    total, last, up = chained(total, chunks[2], lowrank_up_weight[0])
    far.append([flipped(last, "tensor", hop) for hop in hops])
    for flip, value in singles:
        value, total = chained(value, total)
        downs.append(value)
        owners.append(group ^ flip)
    swaps = []
    for pair, value in fetched:
        value, total = chained(value, total)
        swaps.append((value, flipped(value, "parts", 1)))
        mine, other = (jnp.where(part == 0, *order) for order in (pair, pair[::-1]))
        owners += [group ^ mine, group ^ other]
    ups = [flipped(up, "adapter", flip) for flip in range(1, groups)]
    total = products(tile, [(me ^ 1) * depth], [neighbour], frozen_projection_weight, total)
    starts, features = spread_out(0)
    features, total = chained(features, total)
    total = products(tile, starts, features, frozen_projection_weight, total)
    for value, swapped in swaps:
        swapped, total = chained(swapped, total)
        downs += [value, swapped]
    ups, total = chained(ups, total)
    ups = [up] + ups
    far[1], downs, ups = chained(far[1], downs, ups)

    tiles = depth // tile
    partial = call(
        functools.partial(shrink_kernel, tile, slots),
        jax.ShapeDtypeStruct((rank, rows), jnp.float32),
        [SCALAR, SCALAR, ANYWHERE, VECTOR] + [ANYWHERE] * slots,
        [
            pltpu.VMEM((tiles, rows, tile), jnp.bfloat16),
            pltpu.VMEM((tiles, slots * rank, tile), jnp.bfloat16),
            pltpu.VMEM((rows, slots * rank), jnp.float32),
            pltpu.SemaphoreType.DMA((1 + slots, tiles)),
        ],
    )(jnp.stack(owners), placement, tokens, tenant_row, *downs)
    starts, features = spread_out(1)
    features, partial = chained(features, partial)
    total = products(tile, starts, features, frozen_projection_weight, total)
    flip = 1
    while flip < tensors // 2:
        received = flipped(partial, "tensor", flip)
        if flip == 1:
            received, total = chained(received, total)
        partial += received
        flip *= 2
    more = flipped(partial, "tensor", flip)
    far[2], total, partial = chained(far[2], total, partial)
    starts, features = spread_out(2)

    return call(
        functools.partial(last_kernel, tile, len(features), slots),
        jax.ShapeDtypeStruct((rows, columns), jnp.bfloat16),
        [SCALAR, SCALAR, ANYWHERE]
        + [ANYWHERE] * len(features)
        + [VECTOR] * (4 + slots),
        [pltpu.VMEM((rows, columns), jnp.float32)] + tile_scratch(tile, features, columns),
    )(
        jnp.stack(starts), placement, frozen_projection_weight, *features, total, tenant_row,
        partial, more, *ups,
    )


def solution(mesh):
    placed = (
        P(("parts", "adapter"), "tensor"),
        P(("parts", "adapter"), None),
        P(),
        P(None, "tensor"),
        P("adapter", None, "tensor"),
        P("adapter", None, "tensor"),
    )
    return jax.shard_map(
        body,
        mesh=mesh,
        in_specs=placed,
        out_specs=P(("parts", "adapter"), "tensor"),
        check_vma=False,
    )
```

```python
import functools
import math

import jax
import jax.numpy as jnp
from jax import lax
from jax.experimental import pallas as pl
from jax.experimental.pallas import tpu as pltpu
from jax.sharding import PartitionSpec as P

LOWRANK_SCALE = 2.0
CORES = 2
LANES = 128
CUTS = (0.75,)
MIB = 1024 * 1024
FREE = pl.CostEstimate(flops=0, bytes_accessed=0, transcendentals=0)
LONG = pl.CostEstimate(flops=10**11, bytes_accessed=0, transcendentals=0)
ANYWHERE = pl.BlockSpec(memory_space=pl.ANY)
VECTOR = pl.BlockSpec(memory_space=pltpu.VMEM)
SCALAR = pl.BlockSpec(memory_space=pltpu.SMEM)


def flipped(value, axis, flip):
    count = lax.axis_size(axis)
    return lax.ppermute(value, axis, [(i, i ^ flip) for i in range(count)])


def chained(*values):
    return lax.optimization_barrier(values)


def call(kernel, out_shape, in_specs, scratch, out_specs=VECTOR, cost=LONG, mib=48):
    return pl.pallas_call(
        kernel,
        out_shape=out_shape,
        in_specs=in_specs,
        out_specs=out_specs,
        scratch_shapes=scratch,
        cost_estimate=cost,
        compiler_params=pltpu.CompilerParams(vmem_limit_bytes=mib * MIB),
    )


def run_copies(pairs, sems):
    copies = [
        pltpu.make_async_copy(source, target, sems.at[i]) for i, (source, target) in enumerate(pairs)
    ]
    for copy in copies:
        copy.start()
    for copy in copies:
        copy.wait()


def cut_kernel(edges, source_ref, *refs):
    run_copies(
        [(source_ref.at[:, a:b], out) for a, b, out in zip(edges, edges[1:], refs[:-1])], refs[-1]
    )


def slice_kernel(down_ref, *refs):
    outs, sems = refs[:-1], refs[-1]
    me, depth = lax.axis_index("tensor"), outs[0].shape[1]
    run_copies(
        [
            (down_ref.at[:, pl.ds(pl.multiple_of((me ^ flip) * depth, LANES), depth)], out)
            for flip, out in enumerate(outs)
        ],
        sems,
    )


def order_kernel(rank_part, *refs):
    pieces, out_ref, sems = refs[:-2], refs[-2], refs[-1]
    me = lax.axis_index("tensor")
    run_copies(
        [
            (piece, out_ref.at[pl.ds(pl.multiple_of((me ^ f) * rank_part, rank_part), rank_part)])
            for f, piece in enumerate(pieces)
        ],
        sems,
    )


def slot_of_row(tenant, placement_ref, slots):
    stored = jnp.zeros(tenant.shape, jnp.int32)
    for slot in range(slots):
        stored = jnp.where(tenant == slot, placement_ref[slot], stored)
    return stored


def start_tiles(tile, starts_ref, features, weight_ref, held_ref, rows_ref, sems):
    t = 0
    for i, part in enumerate(features):
        for k in range(0, part.shape[1], tile):
            start = pl.multiple_of(starts_ref[i] + k, LANES)
            pltpu.make_async_copy(part.at[:, pl.ds(k, tile)], held_ref.at[t], sems.at[0, t]).start()
            pltpu.make_async_copy(
                weight_ref.at[pl.ds(start, tile)], rows_ref.at[t], sems.at[1, t]
            ).start()
            t += 1


def add_tiles(held_ref, rows_ref, sems, total_ref):
    @pl.loop(0, held_ref.shape[0])
    def _(t):
        pltpu.make_async_copy(held_ref.at[t], held_ref.at[t], sems.at[0, t]).wait()
        pltpu.make_async_copy(rows_ref.at[t], rows_ref.at[t], sems.at[1, t]).wait()
        total_ref[...] += jnp.dot(held_ref[t], rows_ref[t], preferred_element_type=jnp.float32)


def tile_scratch(tile, features, columns):
    tiles = sum(f.shape[1] for f in features) // tile
    rows = features[0].shape[0]
    return [
        pltpu.VMEM((tiles, rows, tile), jnp.bfloat16),
        pltpu.VMEM((tiles, tile, columns), jnp.bfloat16),
        pltpu.SemaphoreType.DMA((2, tiles)),
    ]


def products_kernel(tile, count, has_total, starts_ref, weight_ref, *refs):
    features = refs[:count]
    given = refs[count] if has_total else None
    out_ref, held_ref, rows_ref, sems = refs[count + has_total :]
    start_tiles(tile, starts_ref, features, weight_ref, held_ref, rows_ref, sems)
    out_ref[...] = given[...] if has_total else jnp.zeros_like(out_ref)
    add_tiles(held_ref, rows_ref, sems, out_ref)


def products(tile, starts, features, weight, total=None):
    given = [] if total is None else [total]
    return call(
        functools.partial(products_kernel, tile, len(features), len(given)),
        jax.ShapeDtypeStruct((features[0].shape[0], weight.shape[1]), jnp.float32),
        [SCALAR, ANYWHERE] + [ANYWHERE] * len(features) + [VECTOR] * len(given),
        tile_scratch(tile, features, weight.shape[1]),
    )(jnp.stack(starts), weight, *features, *given)


def last_kernel(tile, count, slots, starts_ref, owners_ref, placement_ref, weight_ref, *refs):
    features = refs[:count]
    given, tenant_ref, sum_ref, more_ref = refs[count : count + 4]
    ups = refs[count + 4 : count + 4 + slots]
    out_ref, total_ref, held_ref, rows_ref, sems = refs[count + 4 + slots :]
    start_tiles(tile, starts_ref, features, weight_ref, held_ref, rows_ref, sems)
    shrunk = (sum_ref[...] + more_ref[...]).astype(jnp.bfloat16).astype(jnp.float32)
    stored = slot_of_row(tenant_ref[...], placement_ref, slots)
    spread = jnp.concatenate(
        [jnp.where(stored == owners_ref[b], shrunk, 0.0) for b in range(slots)], axis=0
    )
    stacked = jnp.concatenate([up[...] for up in ups], axis=0)
    expanded = jnp.dot(
        spread.T.astype(jnp.bfloat16), stacked, preferred_element_type=jnp.float32
    )
    expanded = expanded.astype(jnp.bfloat16).astype(jnp.float32)
    total_ref[...] = given[...] + LOWRANK_SCALE * expanded
    add_tiles(held_ref, rows_ref, sems, total_ref)
    out_ref[...] = total_ref[...].astype(out_ref.dtype)


def shrink_kernel(tile, slots, owners_ref, placement_ref, tokens_ref, tenant_ref, *refs):
    downs, out_ref, held_ref, down_ref, sums_ref, sems = (
        refs[:slots], refs[slots], *refs[slots + 1 :]
    )
    rank = downs[0].shape[0]
    tiles = tokens_ref.shape[1] // tile
    for k in range(tiles):
        here = pl.ds(k * tile, tile)
        pltpu.make_async_copy(tokens_ref.at[:, here], held_ref.at[k], sems.at[0, k]).start()
        for b, down in enumerate(downs):
            pltpu.make_async_copy(
                down.at[:, here], down_ref.at[k, pl.ds(b * rank, rank)], sems.at[1 + b, k]
            ).start()
    stored = slot_of_row(tenant_ref[...], placement_ref, slots)
    sums_ref[...] = jnp.zeros_like(sums_ref)

    @pl.loop(0, tiles)
    def _(k):
        pltpu.make_async_copy(held_ref.at[k], held_ref.at[k], sems.at[0, k]).wait()
        for b in range(slots):
            block = down_ref.at[k, pl.ds(b * rank, rank)]
            pltpu.make_async_copy(block, block, sems.at[1 + b, k]).wait()
        sums_ref[...] += lax.dot_general(
            held_ref[k], down_ref[k], (((1,), (1,)), ((), ())), preferred_element_type=jnp.float32
        )

    sums = sums_ref[...].T
    total = jnp.zeros(out_ref.shape, jnp.float32)
    for b in range(slots):
        total += jnp.where(stored == owners_ref[b], sums[b * rank : (b + 1) * rank], 0.0)
    out_ref[...] = total


def body(
    tokens, tenant, placement, frozen_projection_weight, lowrank_down_weight, lowrank_up_weight
):
    rows, depth = tokens.shape
    slots = placement.shape[0]
    tensors = lax.axis_size("tensor")
    groups = lax.axis_size("adapter")
    parts = lax.axis_size("parts")
    me = lax.axis_index("tensor")
    group = lax.axis_index("adapter")
    part = lax.axis_index("parts")
    rank, columns = lowrank_up_weight.shape[1:]
    tenant_row = tenant.reshape(1, rows)
    edges = [0] + [int(depth * cut) // LANES * LANES for cut in CUTS] + [depth]
    tile = math.gcd(*edges)

    down = lowrank_down_weight[0].T
    whole_tiles = down.shape[0] % 16 == 0
    if whole_tiles:
        pieces = call(
            slice_kernel,
            [jax.ShapeDtypeStruct((down.shape[0], depth), down.dtype)] * tensors,
            [ANYWHERE],
            [pltpu.SemaphoreType.DMA((tensors,))],
            [VECTOR] * tensors,
            cost=FREE,
            mib=60,
        )(down)
    else:
        pieces = [
            lax.dynamic_slice_in_dim(down, (me ^ flip) * depth, depth, axis=1)
            for flip in range(tensors)
        ]
    neighbour = flipped(tokens, "tensor", 1)
    uncut, pieces = chained(tokens, pieces)
    chunks = call(
        functools.partial(cut_kernel, edges),
        [jax.ShapeDtypeStruct((rows, b - a), tokens.dtype) for a, b in zip(edges, edges[1:])],
        [ANYWHERE],
        [pltpu.SemaphoreType.DMA((len(edges) - 1,))],
        [VECTOR] * (len(edges) - 1),
        cost=FREE,
        mib=60,
    )(uncut)
    pieces = [pieces[0]] + [flipped(pieces[f], "tensor", f) for f in range(1, tensors)]
    if whole_tiles:
        own = call(
            functools.partial(order_kernel, down.shape[0]),
            jax.ShapeDtypeStruct((rank, depth), down.dtype),
            [ANYWHERE] * tensors,
            [pltpu.SemaphoreType.DMA((tensors,))],
            ANYWHERE,
            cost=FREE,
        )(*pieces)
    else:
        none = jnp.zeros((), down.dtype)
        own = jnp.concatenate(
            [sum(jnp.where((me ^ f) == j, pieces[f], none) for f in range(tensors)) for j in range(tensors)],
            axis=0,
        )

    hops = range(CORES, tensors, CORES)
    far = [[flipped(chunk, "tensor", hop) for hop in hops] for chunk in chunks]

    def spread_out(m):
        starts, features = [], []
        for hop, value in zip(hops, far[m]):
            features += [value, flipped(value, "tensor", 1)]
            starts += [(me ^ hop) * depth + edges[m], (me ^ hop ^ 1) * depth + edges[m]]
        return starts, features

    flips = list(range(1, groups))
    pairs = []
    if parts == 2:
        while len(flips) > 1:
            pairs.append((flips.pop(-2), flips.pop(-1)))
    routes = [
        [(p * groups + z, p * groups + (z ^ pair[p])) for p in range(parts) for z in range(groups)]
        for pair in pairs
    ]

    def fetch(value):
        single = [flipped(value, "adapter", flip) for flip in flips]
        return single, [lax.ppermute(value, ("parts", "adapter"), route) for route in routes]

    owners = [group] + [group ^ flip for flip in flips]
    for pair in pairs:
        owners += [
            group ^ jnp.where(part == 0, *pair), group ^ jnp.where(part == 0, pair[1], pair[0])
        ]
    own, neighbour, here = chained(own, neighbour, tokens)
    single, fetched = fetch(own)
    total = products(tile, [me * depth], [here], frozen_projection_weight)
    total, up = chained(total, lowrank_up_weight[0])
    single_up, fetched_up = fetch(up)
    single, fetched, total = chained(single, fetched, total)
    swapped = [flipped(value, "parts", 1) for value in fetched]
    total, neighbour = chained(total, neighbour)
    total = products(tile, [(me ^ 1) * depth], [neighbour], frozen_projection_weight, total)
    single_up, fetched_up, total = chained(single_up, fetched_up, total)
    swapped_up = [flipped(value, "parts", 1) for value in fetched_up]
    downs, ups = [own] + single, [up] + single_up
    for i in range(len(pairs)):
        downs += [fetched[i], swapped[i]]
        ups += [fetched_up[i], swapped_up[i]]
    far[0], downs, ups = chained(far[0], downs, ups)

    owners = jnp.stack(owners)

    tiles = depth // tile
    partial = call(
        functools.partial(shrink_kernel, tile, slots),
        jax.ShapeDtypeStruct((rank, rows), jnp.float32),
        [SCALAR, SCALAR, ANYWHERE, VECTOR] + [ANYWHERE] * slots,
        [
            pltpu.VMEM((tiles, rows, tile), jnp.bfloat16),
            pltpu.VMEM((tiles, slots * rank, tile), jnp.bfloat16),
            pltpu.VMEM((rows, slots * rank), jnp.float32),
            pltpu.SemaphoreType.DMA((1 + slots, tiles)),
        ],
    )(owners, placement, tokens, tenant_row, *downs)
    starts, features = spread_out(0)
    partial, total = chained(partial, total)
    total = products(tile, starts[::2], features[::2], frozen_projection_weight, total)
    flip = 1
    while flip < tensors // 2:
        received = flipped(partial, "tensor", flip)
        if flip == 1:
            received, total = chained(received, total)
        partial += received
        flip *= 2
    more = flipped(partial, "tensor", flip)
    far[1], partial = chained(far[1], partial)
    last_starts, last = spread_out(1)
    total = products(
        tile,
        starts[1::2] + last_starts[::2],
        features[1::2] + last[::2],
        frozen_projection_weight,
        total,
    )
    starts = last_starts[1::2]
    features, more, total = chained(last[1::2], more, total)

    return call(
        functools.partial(last_kernel, tile, len(features), slots),
        jax.ShapeDtypeStruct((rows, columns), jnp.bfloat16),
        [SCALAR, SCALAR, SCALAR, ANYWHERE]
        + [ANYWHERE] * len(features)
        + [VECTOR] * (4 + slots),
        [pltpu.VMEM((rows, columns), jnp.float32)] + tile_scratch(tile, features, columns),
    )(
        jnp.stack(starts), owners, placement, frozen_projection_weight, *features, total, tenant_row,
        partial, more, *ups,
    )


def solution(mesh):
    placed = (
        P(("parts", "adapter"), "tensor"),
        P(("parts", "adapter"), None),
        P(),
        P(None, "tensor"),
        P("adapter", None, "tensor"),
        P("adapter", None, "tensor"),
    )
    return jax.shard_map(
        body,
        mesh=mesh,
        in_specs=placed,
        out_specs=P(("parts", "adapter"), "tensor"),
        check_vma=False,
    )
```

```python
import functools
import math

import jax
import jax.numpy as jnp
from jax import lax
from jax.experimental import pallas as pl
from jax.experimental.pallas import tpu as pltpu
from jax.sharding import PartitionSpec as P

LOWRANK_SCALE = 2.0
CORES = 2
LANES = 128
CUTS = (0.75,)
MIB = 1024 * 1024
FREE = pl.CostEstimate(flops=0, bytes_accessed=0, transcendentals=0)
LONG = pl.CostEstimate(flops=10**11, bytes_accessed=0, transcendentals=0)
ANYWHERE = pl.BlockSpec(memory_space=pl.ANY)
VECTOR = pl.BlockSpec(memory_space=pltpu.VMEM)
SCALAR = pl.BlockSpec(memory_space=pltpu.SMEM)


def flipped(value, axis, flip):
    count = lax.axis_size(axis)
    return lax.ppermute(value, axis, [(i, i ^ flip) for i in range(count)])


def chained(*values):
    return lax.optimization_barrier(values)


def call(kernel, out_shape, in_specs, scratch, out_specs=VECTOR, cost=LONG, mib=48):
    return pl.pallas_call(
        kernel,
        out_shape=out_shape,
        in_specs=in_specs,
        out_specs=out_specs,
        scratch_shapes=scratch,
        cost_estimate=cost,
        compiler_params=pltpu.CompilerParams(vmem_limit_bytes=mib * MIB),
    )


def run_copies(pairs, sems):
    copies = [
        pltpu.make_async_copy(source, target, sems.at[i]) for i, (source, target) in enumerate(pairs)
    ]
    for copy in copies:
        copy.start()
    for copy in copies:
        copy.wait()


def cut_kernel(edges, tokens_ref, down_ref, *refs):
    outs, sems = refs[:-1], refs[-1]
    me, depth = lax.axis_index("tensor"), tokens_ref.shape[1]
    cuts = len(edges) - 1
    pairs = []
    for flip, piece in enumerate(outs[cuts:]):
        start = pl.multiple_of((me ^ flip) * depth, LANES)
        pairs.append((down_ref.at[:, pl.ds(start, depth)], piece))
    for a, b, chunk in zip(edges, edges[1:], outs):
        pairs.append((tokens_ref.at[:, a:b], chunk))
    run_copies(pairs, sems)


def order_kernel(rank_part, *refs):
    pieces, out_ref, sems = refs[:-2], refs[-2], refs[-1]
    me = lax.axis_index("tensor")
    run_copies(
        [
            (piece, out_ref.at[pl.ds(pl.multiple_of((me ^ f) * rank_part, rank_part), rank_part)])
            for f, piece in enumerate(pieces)
        ],
        sems,
    )


def slot_of_row(tenant, placement_ref, slots):
    stored = jnp.zeros(tenant.shape, jnp.int32)
    for slot in range(slots):
        stored = jnp.where(tenant == slot, placement_ref[slot], stored)
    return stored


def start_tiles(tile, starts_ref, features, weight_ref, held_ref, rows_ref, sems):
    t = 0
    for i, part in enumerate(features):
        for k in range(0, part.shape[1], tile):
            start = pl.multiple_of(starts_ref[i] + k, LANES)
            pltpu.make_async_copy(part.at[:, pl.ds(k, tile)], held_ref.at[t], sems.at[0, t]).start()
            pltpu.make_async_copy(
                weight_ref.at[pl.ds(start, tile)], rows_ref.at[t], sems.at[1, t]
            ).start()
            t += 1


def add_tiles(held_ref, rows_ref, sems, total_ref):
    @pl.loop(0, held_ref.shape[0])
    def _(t):
        pltpu.make_async_copy(held_ref.at[t], held_ref.at[t], sems.at[0, t]).wait()
        pltpu.make_async_copy(rows_ref.at[t], rows_ref.at[t], sems.at[1, t]).wait()
        total_ref[...] += jnp.dot(held_ref[t], rows_ref[t], preferred_element_type=jnp.float32)


def tile_scratch(tile, features, columns):
    tiles = sum(f.shape[1] for f in features) // tile
    rows = features[0].shape[0]
    return [
        pltpu.VMEM((tiles, rows, tile), jnp.bfloat16),
        pltpu.VMEM((tiles, tile, columns), jnp.bfloat16),
        pltpu.SemaphoreType.DMA((2, tiles)),
    ]


def products_kernel(tile, count, has_total, starts_ref, weight_ref, *refs):
    features = refs[:count]
    given = refs[count] if has_total else None
    out_ref, held_ref, rows_ref, sems = refs[count + has_total :]
    start_tiles(tile, starts_ref, features, weight_ref, held_ref, rows_ref, sems)
    out_ref[...] = given[...] if has_total else jnp.zeros_like(out_ref)
    add_tiles(held_ref, rows_ref, sems, out_ref)


def products(tile, starts, features, weight, total=None):
    given = [] if total is None else [total]
    return call(
        functools.partial(products_kernel, tile, len(features), len(given)),
        jax.ShapeDtypeStruct((features[0].shape[0], weight.shape[1]), jnp.float32),
        [SCALAR, ANYWHERE] + [ANYWHERE] * len(features) + [VECTOR] * len(given),
        tile_scratch(tile, features, weight.shape[1]),
    )(jnp.stack(starts), weight, *features, *given)


def last_kernel(tile, count, slots, starts_ref, owners_ref, placement_ref, weight_ref, *refs):
    features = refs[:count]
    given, tenant_ref, sum_ref, more_ref = refs[count : count + 4]
    ups = refs[count + 4 : count + 4 + slots]
    out_ref, total_ref, held_ref, rows_ref, sems = refs[count + 4 + slots :]
    start_tiles(tile, starts_ref, features, weight_ref, held_ref, rows_ref, sems)
    shrunk = (sum_ref[...] + more_ref[...]).astype(jnp.bfloat16).astype(jnp.float32)
    stored = slot_of_row(tenant_ref[...], placement_ref, slots)
    spread = jnp.concatenate(
        [jnp.where(stored == owners_ref[b], shrunk, 0.0) for b in range(slots)], axis=0
    )
    stacked = jnp.concatenate([up[...] for up in ups], axis=0)
    expanded = jnp.dot(
        spread.T.astype(jnp.bfloat16), stacked, preferred_element_type=jnp.float32
    )
    expanded = expanded.astype(jnp.bfloat16).astype(jnp.float32)
    total_ref[...] = given[...] + LOWRANK_SCALE * expanded
    add_tiles(held_ref, rows_ref, sems, total_ref)
    out_ref[...] = total_ref[...].astype(out_ref.dtype)


def shrink_kernel(tile, slots, owners_ref, placement_ref, tokens_ref, tenant_ref, *refs):
    downs, out_ref, held_ref, down_ref, sums_ref, sems = (
        refs[:slots], refs[slots], *refs[slots + 1 :]
    )
    rank = downs[0].shape[0]
    tiles = tokens_ref.shape[1] // tile
    for k in range(tiles):
        here = pl.ds(k * tile, tile)
        pltpu.make_async_copy(tokens_ref.at[:, here], held_ref.at[k], sems.at[0, k]).start()
        for b, down in enumerate(downs):
            pltpu.make_async_copy(
                down.at[:, here], down_ref.at[k, pl.ds(b * rank, rank)], sems.at[1 + b, k]
            ).start()
    stored = slot_of_row(tenant_ref[...], placement_ref, slots)
    sums_ref[...] = jnp.zeros_like(sums_ref)

    @pl.loop(0, tiles)
    def _(k):
        pltpu.make_async_copy(held_ref.at[k], held_ref.at[k], sems.at[0, k]).wait()
        for b in range(slots):
            block = down_ref.at[k, pl.ds(b * rank, rank)]
            pltpu.make_async_copy(block, block, sems.at[1 + b, k]).wait()
        sums_ref[...] += lax.dot_general(
            held_ref[k], down_ref[k], (((1,), (1,)), ((), ())), preferred_element_type=jnp.float32
        )

    sums = sums_ref[...].T
    total = jnp.zeros(out_ref.shape, jnp.float32)
    for b in range(slots):
        total += jnp.where(stored == owners_ref[b], sums[b * rank : (b + 1) * rank], 0.0)
    out_ref[...] = total


def body(
    tokens, tenant, placement, frozen_projection_weight, lowrank_down_weight, lowrank_up_weight
):
    rows, depth = tokens.shape
    slots = placement.shape[0]
    tensors = lax.axis_size("tensor")
    groups = lax.axis_size("adapter")
    parts = lax.axis_size("parts")
    me = lax.axis_index("tensor")
    group = lax.axis_index("adapter")
    part = lax.axis_index("parts")
    rank, columns = lowrank_up_weight.shape[1:]
    tenant_row = tenant.reshape(1, rows)
    edges = [0] + [int(depth * cut) // LANES * LANES for cut in CUTS] + [depth]
    tile = math.gcd(*edges)

    down = lowrank_down_weight[0].T
    whole_tiles = down.shape[0] % 16 == 0
    cuts = len(edges) - 1
    if whole_tiles:
        cut = call(
            functools.partial(cut_kernel, edges),
            [jax.ShapeDtypeStruct((rows, b - a), tokens.dtype) for a, b in zip(edges, edges[1:])]
            + [jax.ShapeDtypeStruct((down.shape[0], depth), down.dtype)] * tensors,
            [ANYWHERE, ANYWHERE],
            [pltpu.SemaphoreType.DMA((cuts + tensors,))],
            [VECTOR] * (cuts + tensors),
            cost=FREE,
            mib=60,
        )(tokens, down)
        chunks, pieces = list(cut[:cuts]), list(cut[cuts:])
    else:
        chunks = [tokens[:, a:b] for a, b in zip(edges, edges[1:])]
        pieces = [
            lax.dynamic_slice_in_dim(down, (me ^ flip) * depth, depth, axis=1)
            for flip in range(tensors)
        ]
    neighbour = flipped(tokens, "tensor", 1)
    pieces = [pieces[0]] + [flipped(pieces[f], "tensor", f) for f in range(1, tensors)]
    if whole_tiles:
        own = call(
            functools.partial(order_kernel, down.shape[0]),
            jax.ShapeDtypeStruct((rank, depth), down.dtype),
            [ANYWHERE] * tensors,
            [pltpu.SemaphoreType.DMA((tensors,))],
            ANYWHERE,
            cost=FREE,
        )(*pieces)
    else:
        none = jnp.zeros((), down.dtype)
        own = jnp.concatenate(
            [sum(jnp.where((me ^ f) == j, pieces[f], none) for f in range(tensors)) for j in range(tensors)],
            axis=0,
        )

    hops = range(CORES, tensors, CORES)
    far = [[flipped(chunk, "tensor", hop) for hop in hops] for chunk in chunks]

    def spread_out(m):
        starts, features = [], []
        for hop, value in zip(hops, far[m]):
            features += [value, flipped(value, "tensor", 1)]
            starts += [(me ^ hop) * depth + edges[m], (me ^ hop ^ 1) * depth + edges[m]]
        return starts, features

    flips = list(range(1, groups))
    pairs = []
    if parts == 2:
        while len(flips) > 1:
            pairs.append((flips.pop(-2), flips.pop(-1)))
    routes = [
        [(p * groups + z, p * groups + (z ^ pair[p])) for p in range(parts) for z in range(groups)]
        for pair in pairs
    ]

    def fetch(value):
        single = [flipped(value, "adapter", flip) for flip in flips]
        return single, [lax.ppermute(value, ("parts", "adapter"), route) for route in routes]

    owners = [group] + [group ^ flip for flip in flips]
    for pair in pairs:
        owners += [
            group ^ jnp.where(part == 0, *pair), group ^ jnp.where(part == 0, pair[1], pair[0])
        ]
    own, neighbour, here = chained(own, neighbour, tokens)
    single, fetched = fetch(own)
    total = products(tile, [me * depth], [here], frozen_projection_weight)
    single, fetched, total = chained(single, fetched, total)
    swapped = [flipped(value, "parts", 1) for value in fetched]
    total, neighbour = chained(total, neighbour)
    total = products(tile, [(me ^ 1) * depth], [neighbour], frozen_projection_weight, total)
    total, up = chained(total, lowrank_up_weight[0])
    single_up, fetched_up = fetch(up)
    swapped, total = chained(swapped, total)
    downs = [own] + single
    for i in range(len(pairs)):
        downs += [fetched[i], swapped[i]]
    owners = jnp.stack(owners)

    tiles = depth // tile
    partial = call(
        functools.partial(shrink_kernel, tile, slots),
        jax.ShapeDtypeStruct((rank, rows), jnp.float32),
        [SCALAR, SCALAR, ANYWHERE, VECTOR] + [ANYWHERE] * slots,
        [
            pltpu.VMEM((tiles, rows, tile), jnp.bfloat16),
            pltpu.VMEM((tiles, slots * rank, tile), jnp.bfloat16),
            pltpu.VMEM((rows, slots * rank), jnp.float32),
            pltpu.SemaphoreType.DMA((1 + slots, tiles)),
        ],
    )(owners, placement, tokens, tenant_row, *downs)
    far[0], fetched_up, partial = chained(far[0], fetched_up, partial)
    swapped_up = [flipped(value, "parts", 1) for value in fetched_up]
    ups = [up] + single_up
    for i in range(len(pairs)):
        ups += [fetched_up[i], swapped_up[i]]
    starts, features = spread_out(0)
    total = products(tile, starts[::2], features[::2], frozen_projection_weight, total)
    flip = 1
    while flip < tensors // 2:
        received = flipped(partial, "tensor", flip)
        if flip == 1:
            received, total = chained(received, total)
        partial += received
        flip *= 2
    more = flipped(partial, "tensor", flip)
    total, partial = chained(total, partial)
    total = products(tile, starts[1::2], features[1::2], frozen_projection_weight, total)
    far[1], ups, total = chained(far[1], ups, total)
    starts, features = spread_out(1)
    total = products(tile, starts[::2], features[::2], frozen_projection_weight, total)
    starts = starts[1::2]
    features, more, total = chained(features[1::2], more, total)

    return call(
        functools.partial(last_kernel, tile, len(features), slots),
        jax.ShapeDtypeStruct((rows, columns), jnp.bfloat16),
        [SCALAR, SCALAR, SCALAR, ANYWHERE]
        + [ANYWHERE] * len(features)
        + [VECTOR] * (4 + slots),
        [pltpu.VMEM((rows, columns), jnp.float32)] + tile_scratch(tile, features, columns),
    )(
        jnp.stack(starts), owners, placement, frozen_projection_weight, *features, total, tenant_row,
        partial, more, *ups,
    )


def solution(mesh):
    placed = (
        P(("parts", "adapter"), "tensor"),
        P(("parts", "adapter"), None),
        P(),
        P(None, "tensor"),
        P("adapter", None, "tensor"),
        P("adapter", None, "tensor"),
    )
    return jax.shard_map(
        body,
        mesh=mesh,
        in_specs=placed,
        out_specs=P(("parts", "adapter"), "tensor"),
        check_vma=False,
    )
```

```python
import functools
import math

import jax
import jax.numpy as jnp
from jax import lax
from jax.experimental import pallas as pl
from jax.experimental.pallas import tpu as pltpu
from jax.sharding import PartitionSpec as P

LOWRANK_SCALE = 2.0
CORES = 2
LANES = 128
CUTS = (0.5, 0.75)
MIB = 1024 * 1024
FREE = pl.CostEstimate(flops=0, bytes_accessed=0, transcendentals=0)
LONG = pl.CostEstimate(flops=10**11, bytes_accessed=0, transcendentals=0)
ANYWHERE = pl.BlockSpec(memory_space=pl.ANY)
VECTOR = pl.BlockSpec(memory_space=pltpu.VMEM)
SCALAR = pl.BlockSpec(memory_space=pltpu.SMEM)


def flipped(value, axis, flip):
    count = lax.axis_size(axis)
    return lax.ppermute(value, axis, [(i, i ^ flip) for i in range(count)])


def chained(*values):
    return lax.optimization_barrier(values)


def call(kernel, out_shape, in_specs, scratch, out_specs=VECTOR, cost=LONG, mib=48):
    return pl.pallas_call(
        kernel,
        out_shape=out_shape,
        in_specs=in_specs,
        out_specs=out_specs,
        scratch_shapes=scratch,
        cost_estimate=cost,
        compiler_params=pltpu.CompilerParams(vmem_limit_bytes=mib * MIB),
    )


def run_copies(pairs, sems):
    copies = [
        pltpu.make_async_copy(source, target, sems.at[i]) for i, (source, target) in enumerate(pairs)
    ]
    for copy in copies:
        copy.start()
    for copy in copies:
        copy.wait()


def cut_kernel(edges, tokens_ref, down_ref, *refs):
    outs, sems = refs[:-1], refs[-1]
    me, depth = lax.axis_index("tensor"), tokens_ref.shape[1]
    cuts = len(edges) - 1
    pairs = []
    for flip, piece in enumerate(outs[cuts:]):
        start = pl.multiple_of((me ^ flip) * depth, LANES)
        pairs.append((down_ref.at[:, pl.ds(start, depth)], piece))
    for a, b, chunk in zip(edges, edges[1:], outs):
        pairs.append((tokens_ref.at[:, a:b], chunk))
    run_copies(pairs, sems)


def order_kernel(rank_part, *refs):
    pieces, out_ref, sems = refs[:-2], refs[-2], refs[-1]
    me = lax.axis_index("tensor")
    run_copies(
        [
            (piece, out_ref.at[pl.ds(pl.multiple_of((me ^ f) * rank_part, rank_part), rank_part)])
            for f, piece in enumerate(pieces)
        ],
        sems,
    )


def start_tiles(tile, depth, places, features, weight_ref, held_ref, rows_ref, sems):
    me, t = lax.axis_index("tensor"), 0
    for (flip, first), part in zip(places, features):
        for k in range(0, part.shape[1], tile):
            start = pl.multiple_of((me ^ flip) * depth + first + k, LANES)
            pltpu.make_async_copy(
                weight_ref.at[pl.ds(start, tile)], rows_ref.at[t], sems.at[1, t]
            ).start()
            pltpu.make_async_copy(part.at[:, pl.ds(k, tile)], held_ref.at[t], sems.at[0, t]).start()
            t += 1


def add_tiles(held_ref, rows_ref, sems, total_ref):
    @pl.loop(0, held_ref.shape[0])
    def _(t):
        pltpu.make_async_copy(held_ref.at[t], held_ref.at[t], sems.at[0, t]).wait()
        pltpu.make_async_copy(rows_ref.at[t], rows_ref.at[t], sems.at[1, t]).wait()
        total_ref[...] += jnp.dot(held_ref[t], rows_ref[t], preferred_element_type=jnp.float32)


def tile_scratch(tile, features, columns):
    tiles = sum(f.shape[1] for f in features) // tile
    rows = features[0].shape[0]
    return [
        pltpu.VMEM((tiles, rows, tile), jnp.bfloat16),
        pltpu.VMEM((tiles, tile, columns), jnp.bfloat16),
        pltpu.SemaphoreType.DMA((2, tiles)),
    ]


def first_kernel(tile, depth, places, slots, placement_ref, tenant_ref, weight_ref, *refs):
    count = len(places)
    features = refs[:count]
    out_ref, stored_ref, held_ref, rows_ref, sems = refs[count:]
    start_tiles(tile, depth, places, features, weight_ref, held_ref, rows_ref, sems)
    out_ref[...] = jnp.zeros_like(out_ref)
    stored = jnp.zeros(stored_ref.shape, jnp.int32)
    for slot in range(slots):
        stored = jnp.where(tenant_ref[...] == slot, placement_ref[slot], stored)
    stored_ref[...] = stored
    add_tiles(held_ref, rows_ref, sems, out_ref)


def products_kernel(tile, depth, places, weight_ref, *refs):
    count = len(places)
    features, given = refs[:count], refs[count]
    out_ref, held_ref, rows_ref, sems = refs[count + 1 :]
    start_tiles(tile, depth, places, features, weight_ref, held_ref, rows_ref, sems)
    out_ref[...] = given[...]
    add_tiles(held_ref, rows_ref, sems, out_ref)


def owners_of(flips, pairs):
    group, part = lax.axis_index("adapter"), lax.axis_index("parts")
    owners = [group] + [group ^ flip for flip in flips]
    for near, far in pairs:
        owners += [group ^ (near + part * (far - near)), group ^ (far + part * (near - far))]
    return owners


def last_kernel(tile, depth, places, flips, pairs, slots, weight_ref, *refs):
    count = len(places)
    features = refs[:count]
    given, stored_ref, sum_ref, more_ref = refs[count : count + 4]
    ups = refs[count + 4 : count + 4 + slots]
    (
        out_ref, total_ref, sums_ref, stacked_ref, held_ref, rows_ref, sems, small_sems,
    ) = refs[count + 4 + slots :]
    rank = ups[0].shape[0]
    copies = [(sum_ref, sums_ref.at[0]), (more_ref, sums_ref.at[1])]
    copies += [(up, stacked_ref.at[pl.ds(b * rank, rank)]) for b, up in enumerate(ups)]
    copies = [
        pltpu.make_async_copy(source, target, small_sems.at[i])
        for i, (source, target) in enumerate(copies)
    ]
    for copy in copies:
        copy.start()
    start_tiles(tile, depth, places, features, weight_ref, held_ref, rows_ref, sems)
    for copy in copies:
        copy.wait()
    shrunk = (sums_ref[0] + sums_ref[1]).astype(jnp.bfloat16).astype(jnp.float32)
    spread = jnp.concatenate(
        [jnp.where(stored_ref[...] == owner, shrunk, 0.0) for owner in owners_of(flips, pairs)], axis=0
    )
    expanded = jnp.dot(
        spread.T.astype(jnp.bfloat16), stacked_ref[...], preferred_element_type=jnp.float32
    )
    expanded = expanded.astype(jnp.bfloat16).astype(jnp.float32)
    total_ref[...] = given[...] + LOWRANK_SCALE * expanded
    add_tiles(held_ref, rows_ref, sems, total_ref)
    out_ref[...] = total_ref[...].astype(out_ref.dtype)


def shrink_kernel(tile, flips, pairs, slots, tokens_ref, stored_ref, *refs):
    downs, out_ref, held_ref, down_ref, sums_ref, sems = (
        refs[:slots], refs[slots], *refs[slots + 1 :]
    )
    rank = downs[0].shape[0]
    tiles = tokens_ref.shape[1] // tile
    for k in range(tiles):
        here = pl.ds(k * tile, tile)
        pltpu.make_async_copy(tokens_ref.at[:, here], held_ref.at[k], sems.at[0, k]).start()
        for b, down in enumerate(downs):
            pltpu.make_async_copy(
                down.at[:, here], down_ref.at[k, pl.ds(b * rank, rank)], sems.at[1 + b, k]
            ).start()
    sums_ref[...] = jnp.zeros_like(sums_ref)

    @pl.loop(0, tiles)
    def _(k):
        pltpu.make_async_copy(held_ref.at[k], held_ref.at[k], sems.at[0, k]).wait()
        for b in range(slots):
            block = down_ref.at[k, pl.ds(b * rank, rank)]
            pltpu.make_async_copy(block, block, sems.at[1 + b, k]).wait()
        sums_ref[...] += lax.dot_general(
            held_ref[k], down_ref[k], (((1,), (1,)), ((), ())), preferred_element_type=jnp.float32
        )

    sums = sums_ref[...].T
    total = jnp.zeros(out_ref.shape, jnp.float32)
    for b, owner in enumerate(owners_of(flips, pairs)):
        total += jnp.where(stored_ref[...] == owner, sums[b * rank : (b + 1) * rank], 0.0)
    out_ref[...] = total


def body(
    tokens, tenant, placement, frozen_projection_weight, lowrank_down_weight, lowrank_up_weight
):
    rows, depth = tokens.shape
    slots = placement.shape[0]
    tensors = lax.axis_size("tensor")
    groups = lax.axis_size("adapter")
    parts = lax.axis_size("parts")
    me = lax.axis_index("tensor")
    rank, columns = lowrank_up_weight.shape[1:]
    edges = [0] + [int(depth * cut) // LANES * LANES for cut in CUTS] + [depth]
    tile = math.gcd(*edges)

    down = lowrank_down_weight[0].T
    whole_tiles = down.shape[0] % 16 == 0
    cuts = len(edges) - 1
    if whole_tiles:
        cut = call(
            functools.partial(cut_kernel, edges),
            [jax.ShapeDtypeStruct((rows, b - a), tokens.dtype) for a, b in zip(edges, edges[1:])]
            + [jax.ShapeDtypeStruct((down.shape[0], depth), down.dtype)] * tensors,
            [ANYWHERE, ANYWHERE],
            [pltpu.SemaphoreType.DMA((cuts + tensors,))],
            [VECTOR] * (cuts + tensors),
            cost=FREE,
            mib=60,
        )(tokens, down)
        chunks, pieces = list(cut[:cuts]), list(cut[cuts:])
    else:
        chunks = [tokens[:, a:b] for a, b in zip(edges, edges[1:])]
        pieces = [
            lax.dynamic_slice_in_dim(down, (me ^ flip) * depth, depth, axis=1)
            for flip in range(tensors)
        ]
    neighbour = flipped(tokens, "tensor", 1)
    pieces = [pieces[0]] + [flipped(pieces[f], "tensor", f) for f in range(1, tensors)]
    if whole_tiles:
        own = call(
            functools.partial(order_kernel, down.shape[0]),
            jax.ShapeDtypeStruct((rank, depth), down.dtype),
            [ANYWHERE] * tensors,
            [pltpu.SemaphoreType.DMA((tensors,))],
            ANYWHERE,
            cost=FREE,
        )(*pieces)
    else:
        none = jnp.zeros((), down.dtype)
        own = jnp.concatenate(
            [sum(jnp.where((me ^ f) == j, pieces[f], none) for f in range(tensors)) for j in range(tensors)],
            axis=0,
        )

    hops = range(CORES, tensors, CORES)
    far = [[flipped(chunk, "tensor", hop) for hop in hops] for chunk in chunks]

    def across(m):
        return [flipped(value, "tensor", 1) for value in far[m]]

    def far_places(m):
        return [(hop, edges[m]) for hop in hops]

    def near_places(m):
        return [(hop ^ 1, edges[m]) for hop in hops]

    def products(places, features, total):
        return call(
            functools.partial(products_kernel, tile, depth, places),
            jax.ShapeDtypeStruct((rows, columns), jnp.float32),
            [ANYWHERE] + [ANYWHERE] * len(features) + [VECTOR],
            tile_scratch(tile, features, columns),
        )(frozen_projection_weight, *features, total)

    flips = list(range(1, groups))
    pairs = []
    if parts == 2:
        while len(flips) > 1:
            pairs.append((flips.pop(-2), flips.pop(-1)))
    routes = [
        [(p * groups + z, p * groups + (z ^ pair[p])) for p in range(parts) for z in range(groups)]
        for pair in pairs
    ]

    def fetch_far(value):
        return [lax.ppermute(value, ("parts", "adapter"), route) for route in routes]

    def fetch_near(value):
        return [flipped(value, "adapter", flip) for flip in flips]

    def swap(values):
        return [flipped(value, "parts", 1) for value in values]

    own, neighbour, here = chained(own, neighbour, tokens)
    fetched = fetch_far(own)
    total, stored = call(
        functools.partial(first_kernel, tile, depth, [(0, 0)], slots),
        [
            jax.ShapeDtypeStruct((rows, columns), jnp.float32),
            jax.ShapeDtypeStruct((1, rows), jnp.int32),
        ],
        [SCALAR, VECTOR, ANYWHERE, ANYWHERE],
        tile_scratch(tile, [tokens], columns),
        [VECTOR, VECTOR],
    )(placement, tenant.reshape(1, rows), frozen_projection_weight, here)
    total, own, far[0] = chained(total, own, far[0])
    single = fetch_near(own)
    fetched, total = chained(fetched, total)
    swapped = swap(fetched)
    total, neighbour = chained(total, neighbour)
    total = products([(1, 0)], [neighbour], total)
    near = across(0)
    total = products(far_places(0) + near_places(0), far[0] + near, total)
    total, up = chained(total, lowrank_up_weight[0])
    single_up, fetched_up = fetch_near(up), fetch_far(up)
    single, swapped, total = chained(single, swapped, total)
    downs = [own] + single
    for pair in zip(fetched, swapped):
        downs += pair

    tiles = depth // tile
    partial = call(
        functools.partial(shrink_kernel, tile, flips, pairs, slots),
        jax.ShapeDtypeStruct((rank, rows), jnp.float32),
        [ANYWHERE, VECTOR] + [ANYWHERE] * slots,
        [
            pltpu.VMEM((tiles, rows, tile), jnp.bfloat16),
            pltpu.VMEM((tiles, slots * rank, tile), jnp.bfloat16),
            pltpu.VMEM((rows, slots * rank), jnp.float32),
            pltpu.SemaphoreType.DMA((1 + slots, tiles)),
        ],
    )(tokens, stored, *downs)
    far[1], fetched_up, partial = chained(far[1], fetched_up, partial)
    ups = [up] + single_up
    for pair in zip(fetched_up, swap(fetched_up)):
        ups += pair
    middle = across(1)
    total = products(far_places(1), far[1], total)
    flip = 1
    while flip < tensors // 2:
        received = flipped(partial, "tensor", flip)
        if flip == 1:
            received, total = chained(received, total)
        partial += received
        flip *= 2
    more = flipped(partial, "tensor", flip)
    far[2], ups, total, partial = chained(far[2], ups, total, partial)
    near = across(2)
    total = products(near_places(1) + far_places(2), middle + far[2], total)
    near, more, total = chained(near, more, total)

    return call(
        functools.partial(last_kernel, tile, depth, near_places(2), flips, pairs, slots),
        jax.ShapeDtypeStruct((rows, columns), jnp.bfloat16),
        [ANYWHERE] + [ANYWHERE] * len(near) + [VECTOR] * 2 + [ANYWHERE] * (2 + slots),
        [
            pltpu.VMEM((rows, columns), jnp.float32),
            pltpu.VMEM((2, rank, rows), jnp.float32),
            pltpu.VMEM((slots * rank, columns), jnp.bfloat16),
        ]
        + tile_scratch(tile, near, columns)
        + [pltpu.SemaphoreType.DMA((2 + slots,))],
    )(frozen_projection_weight, *near, total, stored, partial, more, *ups)


def solution(mesh):
    placed = (
        P(("parts", "adapter"), "tensor"),
        P(("parts", "adapter"), None),
        P(),
        P(None, "tensor"),
        P("adapter", None, "tensor"),
        P("adapter", None, "tensor"),
    )
    return jax.shard_map(
        body,
        mesh=mesh,
        in_specs=placed,
        out_specs=P(("parts", "adapter"), "tensor"),
        check_vma=False,
    )
```

```python
import functools
import math

import jax
import jax.numpy as jnp
from jax import lax
from jax.experimental import pallas as pl
from jax.experimental.pallas import tpu as pltpu
from jax.sharding import PartitionSpec as P

LOWRANK_SCALE = 2.0
CORES = 2
LANES = 128
CUTS = (0.5, 0.75)
MIB = 1024 * 1024
FREE = pl.CostEstimate(flops=0, bytes_accessed=0, transcendentals=0)
LONG = pl.CostEstimate(flops=10**11, bytes_accessed=0, transcendentals=0)
ANYWHERE = pl.BlockSpec(memory_space=pl.ANY)
VECTOR = pl.BlockSpec(memory_space=pltpu.VMEM)
SCALAR = pl.BlockSpec(memory_space=pltpu.SMEM)


def flipped(value, axis, flip):
    count = lax.axis_size(axis)
    return lax.ppermute(value, axis, [(i, i ^ flip) for i in range(count)])


def chained(*values):
    return lax.optimization_barrier(values)


def call(kernel, out_shape, in_specs, scratch, out_specs=VECTOR, cost=LONG, mib=48):
    return pl.pallas_call(
        kernel,
        out_shape=out_shape,
        in_specs=in_specs,
        out_specs=out_specs,
        scratch_shapes=scratch,
        cost_estimate=cost,
        compiler_params=pltpu.CompilerParams(vmem_limit_bytes=mib * MIB),
    )


def run_copies(pairs, sems):
    copies = [
        pltpu.make_async_copy(source, target, sems.at[i]) for i, (source, target) in enumerate(pairs)
    ]
    for copy in copies:
        copy.start()
    for copy in copies:
        copy.wait()


def cut_kernel(edges, source_ref, *refs):
    run_copies(
        [(source_ref.at[:, a:b], out) for a, b, out in zip(edges, edges[1:], refs[:-1])], refs[-1]
    )


def order_kernel(rank_part, *refs):
    pieces, out_ref, sems = refs[:-2], refs[-2], refs[-1]
    me = lax.axis_index("tensor")
    run_copies(
        [
            (piece, out_ref.at[pl.ds(pl.multiple_of((me ^ f) * rank_part, rank_part), rank_part)])
            for f, piece in enumerate(pieces)
        ],
        sems,
    )


def start_tiles(tile, depth, places, features, weight_ref, held_ref, rows_ref, sems):
    me, t = lax.axis_index("tensor"), 0
    for (flip, first), part in zip(places, features):
        for k in range(0, part.shape[1], tile):
            start = pl.multiple_of((me ^ flip) * depth + first + k, LANES)
            pltpu.make_async_copy(
                weight_ref.at[pl.ds(start, tile)], rows_ref.at[t], sems.at[1, t]
            ).start()
            pltpu.make_async_copy(part.at[:, pl.ds(k, tile)], held_ref.at[t], sems.at[0, t]).start()
            t += 1


def add_tiles(held_ref, rows_ref, sems, total_ref):
    @pl.loop(0, held_ref.shape[0])
    def _(t):
        pltpu.make_async_copy(held_ref.at[t], held_ref.at[t], sems.at[0, t]).wait()
        pltpu.make_async_copy(rows_ref.at[t], rows_ref.at[t], sems.at[1, t]).wait()
        total_ref[...] += jnp.dot(held_ref[t], rows_ref[t], preferred_element_type=jnp.float32)


def tile_scratch(tile, features, columns):
    tiles = sum(f.shape[1] for f in features) // tile
    rows = features[0].shape[0]
    return [
        pltpu.VMEM((tiles, rows, tile), jnp.bfloat16),
        pltpu.VMEM((tiles, tile, columns), jnp.bfloat16),
        pltpu.SemaphoreType.DMA((2, tiles)),
    ]


def first_kernel(tile, depth, places, slots, placement_ref, tenant_ref, weight_ref, *refs):
    count = len(places)
    features = refs[:count]
    out_ref, stored_ref, held_ref, rows_ref, sems = refs[count:]
    start_tiles(tile, depth, places, features, weight_ref, held_ref, rows_ref, sems)
    out_ref[...] = jnp.zeros_like(out_ref)
    stored = jnp.zeros(stored_ref.shape, jnp.int32)
    for slot in range(slots):
        stored = jnp.where(tenant_ref[...] == slot, placement_ref[slot], stored)
    stored_ref[...] = stored
    add_tiles(held_ref, rows_ref, sems, out_ref)


def products_kernel(tile, depth, places, weight_ref, *refs):
    count = len(places)
    features, given = refs[:count], refs[count]
    out_ref, held_ref, rows_ref, sems = refs[count + 1 :]
    start_tiles(tile, depth, places, features, weight_ref, held_ref, rows_ref, sems)
    out_ref[...] = given[...]
    add_tiles(held_ref, rows_ref, sems, out_ref)


def owners_of(flips, pairs):
    group, part = lax.axis_index("adapter"), lax.axis_index("parts")
    owners = [group] + [group ^ flip for flip in flips]
    for near, far in pairs:
        owners += [group ^ (near + part * (far - near)), group ^ (far + part * (near - far))]
    return owners


def last_kernel(tile, depth, places, flips, pairs, slots, weight_ref, *refs):
    count = len(places)
    features = refs[:count]
    given, stored_ref, sum_ref, more_ref = refs[count : count + 4]
    ups = refs[count + 4 : count + 4 + slots]
    (
        out_ref, total_ref, sums_ref, received_ref, stacked_ref, held_ref, rows_ref, sems, small_sems,
    ) = refs[count + 4 + slots :]
    rank = ups[0].shape[0]
    copies = [(sum_ref, sums_ref), (more_ref, received_ref)]
    copies += [(up, stacked_ref.at[pl.ds(b * rank, rank)]) for b, up in enumerate(ups)]
    copies = [
        pltpu.make_async_copy(source, target, small_sems.at[i])
        for i, (source, target) in enumerate(copies)
    ]
    for copy in copies:
        copy.start()
    start_tiles(tile, depth, places, features, weight_ref, held_ref, rows_ref, sems)
    for copy in copies:
        copy.wait()
    shrunk = (sums_ref[...] + received_ref[...].astype(jnp.float32)).astype(jnp.bfloat16).astype(jnp.float32)
    spread = jnp.concatenate(
        [jnp.where(stored_ref[...] == owner, shrunk, 0.0) for owner in owners_of(flips, pairs)], axis=0
    )
    expanded = jnp.dot(
        spread.T.astype(jnp.bfloat16), stacked_ref[...], preferred_element_type=jnp.float32
    )
    expanded = expanded.astype(jnp.bfloat16).astype(jnp.float32)
    total_ref[...] = given[...] + LOWRANK_SCALE * expanded
    add_tiles(held_ref, rows_ref, sems, total_ref)
    out_ref[...] = total_ref[...].astype(out_ref.dtype)


def shrink_kernel(tile, flips, pairs, slots, tokens_ref, stored_ref, *refs):
    downs, out_ref, held_ref, down_ref, sums_ref, sems = (
        refs[:slots], refs[slots], *refs[slots + 1 :]
    )
    rank = downs[0].shape[0]
    tiles = tokens_ref.shape[1] // tile
    for k in range(tiles):
        here = pl.ds(k * tile, tile)
        pltpu.make_async_copy(tokens_ref.at[:, here], held_ref.at[k], sems.at[0, k]).start()
        for b, down in enumerate(downs):
            pltpu.make_async_copy(
                down.at[:, here], down_ref.at[k, pl.ds(b * rank, rank)], sems.at[1 + b, k]
            ).start()
    sums_ref[...] = jnp.zeros_like(sums_ref)

    @pl.loop(0, tiles)
    def _(k):
        pltpu.make_async_copy(held_ref.at[k], held_ref.at[k], sems.at[0, k]).wait()
        for b in range(slots):
            block = down_ref.at[k, pl.ds(b * rank, rank)]
            pltpu.make_async_copy(block, block, sems.at[1 + b, k]).wait()
        sums_ref[...] += lax.dot_general(
            held_ref[k], down_ref[k], (((1,), (1,)), ((), ())), preferred_element_type=jnp.float32
        )

    sums = sums_ref[...].T
    total = jnp.zeros(out_ref.shape, jnp.float32)
    for b, owner in enumerate(owners_of(flips, pairs)):
        total += jnp.where(stored_ref[...] == owner, sums[b * rank : (b + 1) * rank], 0.0)
    out_ref[...] = total


def body(
    tokens, tenant, placement, frozen_projection_weight, lowrank_down_weight, lowrank_up_weight
):
    rows, depth = tokens.shape
    slots = placement.shape[0]
    tensors = lax.axis_size("tensor")
    groups = lax.axis_size("adapter")
    parts = lax.axis_size("parts")
    me = lax.axis_index("tensor")
    rank, columns = lowrank_up_weight.shape[1:]
    edges = [0] + [int(depth * cut) // LANES * LANES for cut in CUTS] + [depth]
    tile = math.gcd(*edges)

    down = lowrank_down_weight[0].T
    pieces = [
        lax.dynamic_slice_in_dim(down, (me ^ flip) * depth, depth, axis=1)
        for flip in range(tensors)
    ]
    uncut, pieces = chained(tokens, pieces)
    chunks = list(call(
        functools.partial(cut_kernel, edges),
        [jax.ShapeDtypeStruct((rows, b - a), tokens.dtype) for a, b in zip(edges, edges[1:])],
        [ANYWHERE],
        [pltpu.SemaphoreType.DMA((len(edges) - 1,))],
        [VECTOR] * (len(edges) - 1),
        mib=40,
    )(uncut))
    neighbour = flipped(uncut, "tensor", 1)
    pieces = [pieces[0]] + [flipped(pieces[f], "tensor", f) for f in range(1, tensors)]
    pieces, chunks[1] = chained(pieces, chunks[1])
    if down.shape[0] % 16 == 0:
        own = call(
            functools.partial(order_kernel, down.shape[0]),
            jax.ShapeDtypeStruct((rank, depth), down.dtype),
            [ANYWHERE] * tensors,
            [pltpu.SemaphoreType.DMA((tensors,))],
            ANYWHERE,
            cost=FREE,
        )(*pieces)
    else:
        none = jnp.zeros((), down.dtype)
        own = jnp.concatenate(
            [sum(jnp.where((me ^ f) == j, pieces[f], none) for f in range(tensors)) for j in range(tensors)],
            axis=0,
        )

    hops = range(CORES, tensors, CORES)

    def send(m):
        return [flipped(chunks[m], "tensor", hop) for hop in hops]

    far = [send(0), send(1)]

    def across(m):
        return [flipped(value, "tensor", 1) for value in far[m]]

    def far_places(m):
        return [(hop, edges[m]) for hop in hops]

    def near_places(m):
        return [(hop ^ 1, edges[m]) for hop in hops]

    def products(places, features, total):
        return call(
            functools.partial(products_kernel, tile, depth, places),
            jax.ShapeDtypeStruct((rows, columns), jnp.float32),
            [ANYWHERE] + [ANYWHERE] * len(features) + [VECTOR],
            tile_scratch(tile, features, columns),
        )(frozen_projection_weight, *features, total)

    flips = list(range(1, groups))
    pairs = []
    if parts == 2:
        while len(flips) > 1:
            pairs.append((flips.pop(-2), flips.pop(-1)))
    routes = [
        [(p * groups + z, p * groups + (z ^ pair[p])) for p in range(parts) for z in range(groups)]
        for pair in pairs
    ]

    def fetch_far(value):
        return [lax.ppermute(value, ("parts", "adapter"), route) for route in routes]

    def fetch_near(value):
        return [flipped(value, "adapter", flip) for flip in flips]

    def swap(values):
        return [flipped(value, "parts", 1) for value in values]

    own, neighbour, here = chained(own, neighbour, tokens)
    fetched = fetch_far(own)
    total, stored = call(
        functools.partial(first_kernel, tile, depth, [(0, 0)], slots),
        [
            jax.ShapeDtypeStruct((rows, columns), jnp.float32),
            jax.ShapeDtypeStruct((1, rows), jnp.int32),
        ],
        [SCALAR, VECTOR, ANYWHERE, ANYWHERE],
        tile_scratch(tile, [tokens], columns),
        [VECTOR, VECTOR],
    )(placement, tenant.reshape(1, rows), frozen_projection_weight, here)
    total, own, chunks[2] = chained(total, own, chunks[2])
    far.append(send(2))
    single = fetch_near(own)
    fetched, total = chained(fetched, total)
    swapped = swap(fetched)
    far[0], total = chained(far[0], total)
    total, neighbour = chained(total, neighbour)
    total = products([(1, 0)], [neighbour], total)
    near = across(0)
    total = products(far_places(0) + near_places(0), far[0] + near, total)
    total, up = chained(total, lowrank_up_weight[0])
    single_up, fetched_up = fetch_near(up), fetch_far(up)
    single, swapped, total = chained(single, swapped, total)
    downs = [own] + single
    for pair in zip(fetched, swapped):
        downs += pair

    tiles = depth // tile
    partial = call(
        functools.partial(shrink_kernel, tile, flips, pairs, slots),
        jax.ShapeDtypeStruct((rank, rows), jnp.float32),
        [ANYWHERE, VECTOR] + [ANYWHERE] * slots,
        [
            pltpu.VMEM((tiles, rows, tile), jnp.bfloat16),
            pltpu.VMEM((tiles, slots * rank, tile), jnp.bfloat16),
            pltpu.VMEM((rows, slots * rank), jnp.float32),
            pltpu.SemaphoreType.DMA((1 + slots, tiles)),
        ],
    )(tokens, stored, *downs)
    far[1], fetched_up, partial = chained(far[1], fetched_up, partial)
    ups = [up] + single_up
    for pair in zip(fetched_up, swap(fetched_up)):
        ups += pair
    middle = across(1)
    total = products(far_places(1), far[1], total)
    flip = 1
    while flip < tensors // 2:
        received = flipped(partial, "tensor", flip)
        if flip == 1:
            received, total = chained(received, total)
        partial += received
        flip *= 2
    more = flipped(partial.astype(jnp.bfloat16), "tensor", flip)
    far[2], ups, total, partial = chained(far[2], ups, total, partial)
    near = across(2)
    total = products(near_places(1) + far_places(2), middle + far[2], total)
    near, more, total = chained(near, more, total)

    return call(
        functools.partial(last_kernel, tile, depth, near_places(2), flips, pairs, slots),
        jax.ShapeDtypeStruct((rows, columns), jnp.bfloat16),
        [ANYWHERE] + [ANYWHERE] * len(near) + [VECTOR] * 2 + [ANYWHERE] * (2 + slots),
        [
            pltpu.VMEM((rows, columns), jnp.float32),
            pltpu.VMEM((rank, rows), jnp.float32),
            pltpu.VMEM((rank, rows), jnp.bfloat16),
            pltpu.VMEM((slots * rank, columns), jnp.bfloat16),
        ]
        + tile_scratch(tile, near, columns)
        + [pltpu.SemaphoreType.DMA((2 + slots,))],
    )(frozen_projection_weight, *near, total, stored, partial, more, *ups)


def solution(mesh):
    placed = (
        P(("parts", "adapter"), "tensor"),
        P(("parts", "adapter"), None),
        P(),
        P(None, "tensor"),
        P("adapter", None, "tensor"),
        P("adapter", None, "tensor"),
    )
    return jax.shard_map(
        body,
        mesh=mesh,
        in_specs=placed,
        out_specs=P(("parts", "adapter"), "tensor"),
        check_vma=False,
    )
```

```python
import functools
import math

import jax
import jax.numpy as jnp
from jax import lax
from jax.experimental import pallas as pl
from jax.experimental.pallas import tpu as pltpu
from jax.sharding import PartitionSpec as P

LOWRANK_SCALE = 2.0
CORES = 2
LANES = 128
CUTS = (0.75,)
MIB = 1024 * 1024
FREE = pl.CostEstimate(flops=0, bytes_accessed=0, transcendentals=0)
LONG = pl.CostEstimate(flops=10**11, bytes_accessed=0, transcendentals=0)
ANYWHERE = pl.BlockSpec(memory_space=pl.ANY)
VECTOR = pl.BlockSpec(memory_space=pltpu.VMEM)
SCALAR = pl.BlockSpec(memory_space=pltpu.SMEM)


def flipped(value, axis, flip):
    count = lax.axis_size(axis)
    return lax.ppermute(value, axis, [(i, i ^ flip) for i in range(count)])


def chained(*values):
    return lax.optimization_barrier(values)


def call(kernel, out_shape, in_specs, scratch, out_specs=VECTOR, cost=LONG, mib=48):
    return pl.pallas_call(
        kernel,
        out_shape=out_shape,
        in_specs=in_specs,
        out_specs=out_specs,
        scratch_shapes=scratch,
        cost_estimate=cost,
        compiler_params=pltpu.CompilerParams(vmem_limit_bytes=mib * MIB),
    )


def run_copies(pairs, sems):
    copies = [
        pltpu.make_async_copy(source, target, sems.at[i]) for i, (source, target) in enumerate(pairs)
    ]
    for copy in copies:
        copy.start()
    for copy in copies:
        copy.wait()


def cut_kernel(edges, source_ref, *refs):
    run_copies(
        [(source_ref.at[:, a:b], out) for a, b, out in zip(edges, edges[1:], refs[:-1])], refs[-1]
    )


def order_kernel(rank_part, *refs):
    pieces, out_ref, sems = refs[:-2], refs[-2], refs[-1]
    me = lax.axis_index("tensor")
    run_copies(
        [
            (piece, out_ref.at[pl.ds(pl.multiple_of((me ^ f) * rank_part, rank_part), rank_part)])
            for f, piece in enumerate(pieces)
        ],
        sems,
    )


def start_tiles(tile, depth, places, features, weight_ref, held_ref, rows_ref, sems):
    me, t = lax.axis_index("tensor"), 0
    for (flip, first), part in zip(places, features):
        for k in range(0, part.shape[1], tile):
            start = pl.multiple_of((me ^ flip) * depth + first + k, LANES)
            pltpu.make_async_copy(
                weight_ref.at[pl.ds(start, tile)], rows_ref.at[t], sems.at[1, t]
            ).start()
            pltpu.make_async_copy(part.at[:, pl.ds(k, tile)], held_ref.at[t], sems.at[0, t]).start()
            t += 1


def add_tiles(held_ref, rows_ref, sems, total_ref):
    @pl.loop(0, held_ref.shape[0])
    def _(t):
        pltpu.make_async_copy(held_ref.at[t], held_ref.at[t], sems.at[0, t]).wait()
        pltpu.make_async_copy(rows_ref.at[t], rows_ref.at[t], sems.at[1, t]).wait()
        total_ref[...] += jnp.dot(held_ref[t], rows_ref[t], preferred_element_type=jnp.float32)


def tile_scratch(tile, features, columns):
    tiles = sum(f.shape[1] for f in features) // tile
    rows = features[0].shape[0]
    return [
        pltpu.VMEM((tiles, rows, tile), jnp.bfloat16),
        pltpu.VMEM((tiles, tile, columns), jnp.bfloat16),
        pltpu.SemaphoreType.DMA((2, tiles)),
    ]


def first_kernel(tile, depth, places, slots, placement_ref, tenant_ref, weight_ref, *refs):
    count = len(places)
    features = refs[:count]
    out_ref, stored_ref, held_ref, rows_ref, sems = refs[count:]
    start_tiles(tile, depth, places, features, weight_ref, held_ref, rows_ref, sems)
    out_ref[...] = jnp.zeros_like(out_ref)
    stored = jnp.zeros(stored_ref.shape, jnp.int32)
    for slot in range(slots):
        stored = jnp.where(tenant_ref[...] == slot, placement_ref[slot], stored)
    stored_ref[...] = stored
    add_tiles(held_ref, rows_ref, sems, out_ref)


def products_kernel(tile, depth, places, weight_ref, *refs):
    count = len(places)
    features, given = refs[:count], refs[count]
    out_ref, held_ref, rows_ref, sems = refs[count + 1 :]
    start_tiles(tile, depth, places, features, weight_ref, held_ref, rows_ref, sems)
    out_ref[...] = given[...]
    add_tiles(held_ref, rows_ref, sems, out_ref)


def owners_of(flips, pairs):
    group, part = lax.axis_index("adapter"), lax.axis_index("parts")
    owners = [group] + [group ^ flip for flip in flips]
    for near, far in pairs:
        owners += [group ^ (near + part * (far - near)), group ^ (far + part * (near - far))]
    return owners


def last_kernel(tile, depth, places, flips, pairs, slots, weight_ref, *refs):
    count = len(places)
    features = refs[:count]
    given, stored_ref, sum_ref, more_ref = refs[count : count + 4]
    ups = refs[count + 4 : count + 4 + slots]
    (
        out_ref, total_ref, sums_ref, received_ref, stacked_ref, held_ref, rows_ref, sems, small_sems,
    ) = refs[count + 4 + slots :]
    rank = ups[0].shape[0]
    copies = [(sum_ref, sums_ref), (more_ref, received_ref)]
    copies += [(up, stacked_ref.at[pl.ds(b * rank, rank)]) for b, up in enumerate(ups)]
    copies = [
        pltpu.make_async_copy(source, target, small_sems.at[i])
        for i, (source, target) in enumerate(copies)
    ]
    for copy in copies:
        copy.start()
    start_tiles(tile, depth, places, features, weight_ref, held_ref, rows_ref, sems)
    for copy in copies:
        copy.wait()
    shrunk = (sums_ref[...] + received_ref[...].astype(jnp.float32)).astype(jnp.bfloat16).astype(jnp.float32)
    spread = jnp.concatenate(
        [jnp.where(stored_ref[...] == owner, shrunk, 0.0) for owner in owners_of(flips, pairs)], axis=0
    )
    expanded = jnp.dot(
        spread.T.astype(jnp.bfloat16), stacked_ref[...], preferred_element_type=jnp.float32
    )
    expanded = expanded.astype(jnp.bfloat16).astype(jnp.float32)
    total_ref[...] = given[...] + LOWRANK_SCALE * expanded
    add_tiles(held_ref, rows_ref, sems, total_ref)
    out_ref[...] = total_ref[...].astype(out_ref.dtype)


def shrink_kernel(tile, flips, pairs, slots, tokens_ref, stored_ref, *refs):
    downs, out_ref, held_ref, down_ref, sums_ref, sems = (
        refs[:slots], refs[slots], *refs[slots + 1 :]
    )
    rank = downs[0].shape[0]
    tiles = tokens_ref.shape[1] // tile
    for k in range(tiles):
        here = pl.ds(k * tile, tile)
        pltpu.make_async_copy(tokens_ref.at[:, here], held_ref.at[k], sems.at[0, k]).start()
        for b, down in enumerate(downs):
            pltpu.make_async_copy(
                down.at[:, here], down_ref.at[k, pl.ds(b * rank, rank)], sems.at[1 + b, k]
            ).start()
    sums_ref[...] = jnp.zeros_like(sums_ref)

    @pl.loop(0, tiles)
    def _(k):
        pltpu.make_async_copy(held_ref.at[k], held_ref.at[k], sems.at[0, k]).wait()
        for b in range(slots):
            block = down_ref.at[k, pl.ds(b * rank, rank)]
            pltpu.make_async_copy(block, block, sems.at[1 + b, k]).wait()
        sums_ref[...] += lax.dot_general(
            held_ref[k], down_ref[k], (((1,), (1,)), ((), ())), preferred_element_type=jnp.float32
        )

    sums = sums_ref[...].T
    total = jnp.zeros(out_ref.shape, jnp.float32)
    for b, owner in enumerate(owners_of(flips, pairs)):
        total += jnp.where(stored_ref[...] == owner, sums[b * rank : (b + 1) * rank], 0.0)
    out_ref[...] = total


def body(
    tokens, tenant, placement, frozen_projection_weight, lowrank_down_weight, lowrank_up_weight
):
    rows, depth = tokens.shape
    slots = placement.shape[0]
    tensors = lax.axis_size("tensor")
    groups = lax.axis_size("adapter")
    parts = lax.axis_size("parts")
    me = lax.axis_index("tensor")
    rank, columns = lowrank_up_weight.shape[1:]
    edges = [0] + [int(depth * cut) // LANES * LANES for cut in CUTS] + [depth]
    tile = math.gcd(*edges)

    down = lowrank_down_weight[0].T
    pieces = [
        lax.dynamic_slice_in_dim(down, (me ^ flip) * depth, depth, axis=1)
        for flip in range(tensors)
    ]
    uncut, pieces = chained(tokens, pieces)
    chunks = list(call(
        functools.partial(cut_kernel, edges),
        [jax.ShapeDtypeStruct((rows, b - a), tokens.dtype) for a, b in zip(edges, edges[1:])],
        [ANYWHERE],
        [pltpu.SemaphoreType.DMA((len(edges) - 1,))],
        [VECTOR] * (len(edges) - 1),
        mib=40,
    )(uncut))
    neighbour = flipped(uncut, "tensor", 1)
    pieces = [pieces[0]] + [flipped(pieces[f], "tensor", f) for f in range(1, tensors)]
    if down.shape[0] % 16 == 0:
        own = call(
            functools.partial(order_kernel, down.shape[0]),
            jax.ShapeDtypeStruct((rank, depth), down.dtype),
            [ANYWHERE] * tensors,
            [pltpu.SemaphoreType.DMA((tensors,))],
            ANYWHERE,
            cost=FREE,
        )(*pieces)
    else:
        none = jnp.zeros((), down.dtype)
        own = jnp.concatenate(
            [sum(jnp.where((me ^ f) == j, pieces[f], none) for f in range(tensors)) for j in range(tensors)],
            axis=0,
        )

    hops = range(CORES, tensors, CORES)

    far = [[flipped(chunk, "tensor", hop) for hop in hops] for chunk in chunks]

    def across(m):
        return [flipped(value, "tensor", 1) for value in far[m]]

    def far_places(m):
        return [(hop, edges[m]) for hop in hops]

    def near_places(m):
        return [(hop ^ 1, edges[m]) for hop in hops]

    def products(places, features, total):
        return call(
            functools.partial(products_kernel, tile, depth, places),
            jax.ShapeDtypeStruct((rows, columns), jnp.float32),
            [ANYWHERE] + [ANYWHERE] * len(features) + [VECTOR],
            tile_scratch(tile, features, columns),
        )(frozen_projection_weight, *features, total)

    flips = list(range(1, groups))
    pairs = []
    if parts == 2:
        while len(flips) > 1:
            pairs.append((flips.pop(-2), flips.pop(-1)))
    routes = [
        [(p * groups + z, p * groups + (z ^ pair[p])) for p in range(parts) for z in range(groups)]
        for pair in pairs
    ]

    def fetch_far(value):
        return [lax.ppermute(value, ("parts", "adapter"), route) for route in routes]

    def fetch_near(value):
        return [flipped(value, "adapter", flip) for flip in flips]

    def swap(values):
        return [flipped(value, "parts", 1) for value in values]

    own, neighbour, here = chained(own, neighbour, tokens)
    fetched = fetch_far(own)
    total, stored = call(
        functools.partial(first_kernel, tile, depth, [(0, 0)], slots),
        [
            jax.ShapeDtypeStruct((rows, columns), jnp.float32),
            jax.ShapeDtypeStruct((1, rows), jnp.int32),
        ],
        [SCALAR, VECTOR, ANYWHERE, ANYWHERE],
        tile_scratch(tile, [tokens], columns),
        [VECTOR, VECTOR],
    )(placement, tenant.reshape(1, rows), frozen_projection_weight, here)
    total, own, up = chained(total, own, lowrank_up_weight[0])
    single, single_up = fetch_near(own), fetch_near(up)
    fetched, total = chained(fetched, total)
    swapped = swap(fetched)
    fetched_up = fetch_far(up)
    total, neighbour = chained(total, neighbour)
    total = products([(1, 0)], [neighbour], total)
    single, swapped, total = chained(single, swapped, total)
    downs = [own] + single
    for pair in zip(fetched, swapped):
        downs += pair

    tiles = depth // tile
    partial = call(
        functools.partial(shrink_kernel, tile, flips, pairs, slots),
        jax.ShapeDtypeStruct((rank, rows), jnp.float32),
        [ANYWHERE, VECTOR] + [ANYWHERE] * slots,
        [
            pltpu.VMEM((tiles, rows, tile), jnp.bfloat16),
            pltpu.VMEM((tiles, slots * rank, tile), jnp.bfloat16),
            pltpu.VMEM((rows, slots * rank), jnp.float32),
            pltpu.SemaphoreType.DMA((1 + slots, tiles)),
        ],
    )(tokens, stored, *downs)
    far[0], fetched_up, partial = chained(far[0], fetched_up, partial)
    ups = [up] + single_up
    for pair in zip(fetched_up, swap(fetched_up)):
        ups += pair
    near = across(0)
    total = products(far_places(0), far[0], total)
    flip = 1
    while flip < tensors // 2:
        received = flipped(partial, "tensor", flip)
        if flip == 1:
            received, total = chained(received, total)
        partial += received
        flip *= 2
    more = flipped(partial.astype(jnp.bfloat16), "tensor", flip)
    total, partial = chained(total, partial)
    total = products(near_places(0), near, total)
    far[1], ups, total = chained(far[1], ups, total)
    near = across(1)
    total = products(far_places(1), far[1], total)
    near, more, total = chained(near, more, total)

    return call(
        functools.partial(last_kernel, tile, depth, near_places(1), flips, pairs, slots),
        jax.ShapeDtypeStruct((rows, columns), jnp.bfloat16),
        [ANYWHERE] + [ANYWHERE] * len(near) + [VECTOR] * 2 + [ANYWHERE] * (2 + slots),
        [
            pltpu.VMEM((rows, columns), jnp.float32),
            pltpu.VMEM((rank, rows), jnp.float32),
            pltpu.VMEM((rank, rows), jnp.bfloat16),
            pltpu.VMEM((slots * rank, columns), jnp.bfloat16),
        ]
        + tile_scratch(tile, near, columns)
        + [pltpu.SemaphoreType.DMA((2 + slots,))],
    )(frozen_projection_weight, *near, total, stored, partial, more, *ups)


def solution(mesh):
    placed = (
        P(("parts", "adapter"), "tensor"),
        P(("parts", "adapter"), None),
        P(),
        P(None, "tensor"),
        P("adapter", None, "tensor"),
        P("adapter", None, "tensor"),
    )
    return jax.shard_map(
        body,
        mesh=mesh,
        in_specs=placed,
        out_specs=P(("parts", "adapter"), "tensor"),
        check_vma=False,
    )
```

```python
import functools
import math

import jax
import jax.numpy as jnp
from jax import lax
from jax.experimental import pallas as pl
from jax.experimental.pallas import tpu as pltpu
from jax.sharding import PartitionSpec as P

LOWRANK_SCALE = 2.0
CORES = 2
LANES = 128
CUTS = (0.75,)
MIB = 1024 * 1024
FREE = pl.CostEstimate(flops=0, bytes_accessed=0, transcendentals=0)
LONG = pl.CostEstimate(flops=10**11, bytes_accessed=0, transcendentals=0)
ANYWHERE = pl.BlockSpec(memory_space=pl.ANY)
VECTOR = pl.BlockSpec(memory_space=pltpu.VMEM)
SCALAR = pl.BlockSpec(memory_space=pltpu.SMEM)


def flipped(value, axis, flip):
    count = lax.axis_size(axis)
    return lax.ppermute(value, axis, [(i, i ^ flip) for i in range(count)])


def chained(*values):
    return lax.optimization_barrier(values)


def call(kernel, out_shape, in_specs, scratch, out_specs=VECTOR, cost=LONG, mib=48):
    return pl.pallas_call(
        kernel,
        out_shape=out_shape,
        in_specs=in_specs,
        out_specs=out_specs,
        scratch_shapes=scratch,
        cost_estimate=cost,
        compiler_params=pltpu.CompilerParams(vmem_limit_bytes=mib * MIB),
    )


def run_copies(pairs, sems):
    copies = [
        pltpu.make_async_copy(source, target, sems.at[i]) for i, (source, target) in enumerate(pairs)
    ]
    for copy in copies:
        copy.start()
    for copy in copies:
        copy.wait()


def cut_kernel(edges, source_ref, *refs):
    outs, (held_ref, sems) = refs[:-2], refs[-2:]
    steps, rows = held_ref.shape[:2]
    copies = [
        pltpu.make_async_copy(source_ref.at[pl.ds(i * rows, rows)], held_ref.at[i], sems.at[0, i])
        for i in range(steps)
    ]
    for copy in copies:
        copy.start()
    leaving = []
    for i in range(steps):
        copies[i].wait()
        for m, (a, b, out) in enumerate(zip(edges, edges[1:], outs)):
            leaving.append(
                pltpu.make_async_copy(
                    held_ref.at[i, :, pl.ds(a, b - a)],
                    out.at[pl.ds(i * rows, rows)],
                    sems.at[1 + m, i],
                )
            )
            leaving[-1].start()
    for copy in leaving:
        copy.wait()


def order_kernel(rank_part, *refs):
    pieces, out_ref, sems = refs[:-2], refs[-2], refs[-1]
    me = lax.axis_index("tensor")
    run_copies(
        [
            (piece, out_ref.at[pl.ds(pl.multiple_of((me ^ f) * rank_part, rank_part), rank_part)])
            for f, piece in enumerate(pieces)
        ],
        sems,
    )


def start_tiles(tile, depth, places, features, weight_ref, held_ref, rows_ref, sems):
    me, t = lax.axis_index("tensor"), 0
    for (flip, first), part in zip(places, features):
        for k in range(0, part.shape[1], tile):
            start = pl.multiple_of((me ^ flip) * depth + first + k, LANES)
            pltpu.make_async_copy(
                weight_ref.at[pl.ds(start, tile)], rows_ref.at[t], sems.at[1, t]
            ).start()
            pltpu.make_async_copy(part.at[:, pl.ds(k, tile)], held_ref.at[t], sems.at[0, t]).start()
            t += 1


def add_tiles(held_ref, rows_ref, sems, total_ref):
    @pl.loop(0, held_ref.shape[0])
    def _(t):
        pltpu.make_async_copy(held_ref.at[t], held_ref.at[t], sems.at[0, t]).wait()
        pltpu.make_async_copy(rows_ref.at[t], rows_ref.at[t], sems.at[1, t]).wait()
        total_ref[...] += jnp.dot(held_ref[t], rows_ref[t], preferred_element_type=jnp.float32)


def tile_scratch(tile, features, columns):
    tiles = sum(f.shape[1] for f in features) // tile
    rows = features[0].shape[0]
    return [
        pltpu.VMEM((tiles, rows, tile), jnp.bfloat16),
        pltpu.VMEM((tiles, tile, columns), jnp.bfloat16),
        pltpu.SemaphoreType.DMA((2, tiles)),
    ]


def first_kernel(tile, depth, places, slots, placement_ref, tenant_ref, weight_ref, *refs):
    count = len(places)
    features = refs[:count]
    out_ref, stored_ref, held_ref, rows_ref, sems = refs[count:]
    start_tiles(tile, depth, places, features, weight_ref, held_ref, rows_ref, sems)
    out_ref[...] = jnp.zeros_like(out_ref)
    stored = jnp.zeros(stored_ref.shape, jnp.int32)
    for slot in range(slots):
        stored = jnp.where(tenant_ref[...] == slot, placement_ref[slot], stored)
    stored_ref[...] = stored
    add_tiles(held_ref, rows_ref, sems, out_ref)


def products_kernel(tile, depth, places, weight_ref, *refs):
    count = len(places)
    features, given = refs[:count], refs[count]
    out_ref, held_ref, rows_ref, sems = refs[count + 1 :]
    start_tiles(tile, depth, places, features, weight_ref, held_ref, rows_ref, sems)
    out_ref[...] = given[...]
    add_tiles(held_ref, rows_ref, sems, out_ref)


def owners_of(flips, pairs):
    group, part = lax.axis_index("adapter"), lax.axis_index("parts")
    owners = [group] + [group ^ flip for flip in flips]
    for near, far in pairs:
        owners += [group ^ (near + part * (far - near)), group ^ (far + part * (near - far))]
    return owners


def last_kernel(tile, depth, places, flips, pairs, slots, weight_ref, *refs):
    count = len(places)
    features = refs[:count]
    given, stored_ref, sum_ref, more_ref = refs[count : count + 4]
    ups = refs[count + 4 : count + 4 + slots]
    (
        out_ref, total_ref, sums_ref, received_ref, stacked_ref, held_ref, rows_ref, sems, small_sems,
    ) = refs[count + 4 + slots :]
    rank = ups[0].shape[0]
    copies = [(sum_ref, sums_ref), (more_ref, received_ref)]
    copies += [(up, stacked_ref.at[pl.ds(b * rank, rank)]) for b, up in enumerate(ups)]
    copies = [
        pltpu.make_async_copy(source, target, small_sems.at[i])
        for i, (source, target) in enumerate(copies)
    ]
    for copy in copies:
        copy.start()
    start_tiles(tile, depth, places, features, weight_ref, held_ref, rows_ref, sems)
    for copy in copies:
        copy.wait()
    shrunk = (sums_ref[...] + received_ref[...].astype(jnp.float32)).astype(jnp.bfloat16).astype(jnp.float32)
    spread = jnp.concatenate(
        [jnp.where(stored_ref[...] == owner, shrunk, 0.0) for owner in owners_of(flips, pairs)], axis=0
    )
    expanded = jnp.dot(
        spread.T.astype(jnp.bfloat16), stacked_ref[...], preferred_element_type=jnp.float32
    )
    expanded = expanded.astype(jnp.bfloat16).astype(jnp.float32)
    total_ref[...] = given[...] + LOWRANK_SCALE * expanded
    add_tiles(held_ref, rows_ref, sems, total_ref)
    out_ref[...] = total_ref[...].astype(out_ref.dtype)


def shrink_kernel(tile, flips, pairs, slots, tokens_ref, stored_ref, *refs):
    downs, out_ref, held_ref, down_ref, sums_ref, sems = (
        refs[:slots], refs[slots], *refs[slots + 1 :]
    )
    rank = downs[0].shape[0]
    tiles = tokens_ref.shape[1] // tile
    for k in range(tiles):
        here = pl.ds(k * tile, tile)
        pltpu.make_async_copy(tokens_ref.at[:, here], held_ref.at[k], sems.at[0, k]).start()
        for b, down in enumerate(downs):
            pltpu.make_async_copy(
                down.at[:, here], down_ref.at[k, pl.ds(b * rank, rank)], sems.at[1 + b, k]
            ).start()
    sums_ref[...] = jnp.zeros_like(sums_ref)

    @pl.loop(0, tiles)
    def _(k):
        pltpu.make_async_copy(held_ref.at[k], held_ref.at[k], sems.at[0, k]).wait()
        for b in range(slots):
            block = down_ref.at[k, pl.ds(b * rank, rank)]
            pltpu.make_async_copy(block, block, sems.at[1 + b, k]).wait()
        sums_ref[...] += lax.dot_general(
            held_ref[k], down_ref[k], (((1,), (1,)), ((), ())), preferred_element_type=jnp.float32
        )

    sums = sums_ref[...].T
    total = jnp.zeros(out_ref.shape, jnp.float32)
    for b, owner in enumerate(owners_of(flips, pairs)):
        total += jnp.where(stored_ref[...] == owner, sums[b * rank : (b + 1) * rank], 0.0)
    out_ref[...] = total


def body(
    tokens, tenant, placement, frozen_projection_weight, lowrank_down_weight, lowrank_up_weight
):
    rows, depth = tokens.shape
    slots = placement.shape[0]
    tensors = lax.axis_size("tensor")
    groups = lax.axis_size("adapter")
    parts = lax.axis_size("parts")
    me = lax.axis_index("tensor")
    rank, columns = lowrank_up_weight.shape[1:]
    edges = [0] + [int(depth * cut) // LANES * LANES for cut in CUTS] + [depth]
    tile = math.gcd(*edges)

    down = lowrank_down_weight[0].T
    pieces = [
        lax.dynamic_slice_in_dim(down, (me ^ flip) * depth, depth, axis=1)
        for flip in range(tensors)
    ]
    uncut, pieces = chained(tokens, pieces)
    steps = 6
    chunks = list(
        call(
            functools.partial(cut_kernel, edges),
            [jax.ShapeDtypeStruct((rows, b - a), tokens.dtype) for a, b in zip(edges, edges[1:])],
            [ANYWHERE],
            [
                pltpu.VMEM((steps, rows // steps, depth), tokens.dtype),
                pltpu.SemaphoreType.DMA((len(edges), steps)),
            ],
            [ANYWHERE] * (len(edges) - 1),
            mib=56,
        )(uncut)
    )
    pieces = [pieces[0]] + [flipped(pieces[f], "tensor", f) for f in range(1, tensors)]
    pieces[1], here = chained(pieces[1], tokens)
    neighbour = flipped(here, "tensor", 1)
    if down.shape[0] % 16 == 0:
        own = call(
            functools.partial(order_kernel, down.shape[0]),
            jax.ShapeDtypeStruct((rank, depth), down.dtype),
            [ANYWHERE] * tensors,
            [pltpu.SemaphoreType.DMA((tensors,))],
            ANYWHERE,
            cost=FREE,
        )(*pieces)
    else:
        none = jnp.zeros((), down.dtype)
        own = jnp.concatenate(
            [sum(jnp.where((me ^ f) == j, pieces[f], none) for f in range(tensors)) for j in range(tensors)],
            axis=0,
        )

    hops = range(CORES, tensors, CORES)

    def send(m):
        return [flipped(chunks[m], "tensor", hop) for hop in hops]

    far = [send(0)]

    def across(m):
        return [flipped(value, "tensor", 1) for value in far[m]]

    def far_places(m):
        return [(hop, edges[m]) for hop in hops]

    def near_places(m):
        return [(hop ^ 1, edges[m]) for hop in hops]

    def products(places, features, total):
        return call(
            functools.partial(products_kernel, tile, depth, places),
            jax.ShapeDtypeStruct((rows, columns), jnp.float32),
            [ANYWHERE] + [ANYWHERE] * len(features) + [VECTOR],
            tile_scratch(tile, features, columns),
        )(frozen_projection_weight, *features, total)

    flips = list(range(1, groups))
    pairs = []
    if parts == 2:
        while len(flips) > 1:
            pairs.append((flips.pop(-2), flips.pop(-1)))
    routes = [
        [(p * groups + z, p * groups + (z ^ pair[p])) for p in range(parts) for z in range(groups)]
        for pair in pairs
    ]

    def fetch_far(value):
        return [lax.ppermute(value, ("parts", "adapter"), route) for route in routes]

    def fetch_near(value):
        return [flipped(value, "adapter", flip) for flip in flips]

    def swap(values):
        return [flipped(value, "parts", 1) for value in values]

    own, here = chained(own, tokens)
    fetched = fetch_far(own)
    total, stored = call(
        functools.partial(first_kernel, tile, depth, [(0, 0)], slots),
        [
            jax.ShapeDtypeStruct((rows, columns), jnp.float32),
            jax.ShapeDtypeStruct((1, rows), jnp.int32),
        ],
        [SCALAR, VECTOR, ANYWHERE, ANYWHERE],
        tile_scratch(tile, [tokens], columns),
        [VECTOR, VECTOR],
    )(placement, tenant.reshape(1, rows), frozen_projection_weight, here)
    total, own, up, neighbour, chunks[1] = chained(
        total, own, lowrank_up_weight[0], neighbour, chunks[1]
    )
    far.append(send(1))
    single, single_up = fetch_near(own), fetch_near(up)
    fetched, total = chained(fetched, total)
    swapped = swap(fetched)
    fetched_up = fetch_far(up)
    total, neighbour = chained(total, neighbour)
    total = products([(1, 0)], [neighbour], total)
    single, swapped, total = chained(single, swapped, total)
    downs = [own] + single
    for pair in zip(fetched, swapped):
        downs += pair

    tiles = depth // tile
    partial = call(
        functools.partial(shrink_kernel, tile, flips, pairs, slots),
        jax.ShapeDtypeStruct((rank, rows), jnp.float32),
        [ANYWHERE, VECTOR] + [ANYWHERE] * slots,
        [
            pltpu.VMEM((tiles, rows, tile), jnp.bfloat16),
            pltpu.VMEM((tiles, slots * rank, tile), jnp.bfloat16),
            pltpu.VMEM((rows, slots * rank), jnp.float32),
            pltpu.SemaphoreType.DMA((1 + slots, tiles)),
        ],
    )(tokens, stored, *downs)
    far[0], fetched_up, partial = chained(far[0], fetched_up, partial)
    ups = [up] + single_up
    for pair in zip(fetched_up, swap(fetched_up)):
        ups += pair
    near = across(0)
    total = products(far_places(0), far[0], total)
    flip = 1
    while flip < tensors // 2:
        received = flipped(partial, "tensor", flip)
        if flip == 1:
            received, total = chained(received, total)
        partial += received
        flip *= 2
    more = flipped(partial.astype(jnp.bfloat16), "tensor", flip)
    total, partial = chained(total, partial)
    total = products(near_places(0), near, total)
    far[1], ups, total = chained(far[1], ups, total)
    near = across(1)
    total = products(far_places(1), far[1], total)
    near, more, total = chained(near, more, total)

    return call(
        functools.partial(last_kernel, tile, depth, near_places(1), flips, pairs, slots),
        jax.ShapeDtypeStruct((rows, columns), jnp.bfloat16),
        [ANYWHERE] + [ANYWHERE] * len(near) + [VECTOR] * 2 + [ANYWHERE] * (2 + slots),
        [
            pltpu.VMEM((rows, columns), jnp.float32),
            pltpu.VMEM((rank, rows), jnp.float32),
            pltpu.VMEM((rank, rows), jnp.bfloat16),
            pltpu.VMEM((slots * rank, columns), jnp.bfloat16),
        ]
        + tile_scratch(tile, near, columns)
        + [pltpu.SemaphoreType.DMA((2 + slots,))],
    )(frozen_projection_weight, *near, total, stored, partial, more, *ups)


def solution(mesh):
    placed = (
        P(("parts", "adapter"), "tensor"),
        P(("parts", "adapter"), None),
        P(),
        P(None, "tensor"),
        P("adapter", None, "tensor"),
        P("adapter", None, "tensor"),
    )
    return jax.shard_map(
        body,
        mesh=mesh,
        in_specs=placed,
        out_specs=P(("parts", "adapter"), "tensor"),
        check_vma=False,
    )
```

```python
import functools
import math

import jax
import jax.numpy as jnp
from jax import lax
from jax.experimental import pallas as pl
from jax.experimental.pallas import tpu as pltpu
from jax.sharding import PartitionSpec as P

LOWRANK_SCALE = 2.0
CORES = 2
LANES = 128
CUTS = (0.75,)
MIB = 1024 * 1024
FREE = pl.CostEstimate(flops=0, bytes_accessed=0, transcendentals=0)
LONG = pl.CostEstimate(flops=10**11, bytes_accessed=0, transcendentals=0)
ANYWHERE = pl.BlockSpec(memory_space=pl.ANY)
VECTOR = pl.BlockSpec(memory_space=pltpu.VMEM)
SCALAR = pl.BlockSpec(memory_space=pltpu.SMEM)


def flipped(value, axis, flip):
    count = lax.axis_size(axis)
    return lax.ppermute(value, axis, [(i, i ^ flip) for i in range(count)])


def chained(*values):
    return lax.optimization_barrier(values)


def call(kernel, out_shape, in_specs, scratch, out_specs=VECTOR, cost=LONG, mib=48):
    return pl.pallas_call(
        kernel,
        out_shape=out_shape,
        in_specs=in_specs,
        out_specs=out_specs,
        scratch_shapes=scratch,
        cost_estimate=cost,
        compiler_params=pltpu.CompilerParams(vmem_limit_bytes=mib * MIB),
    )


def tile_of(*widths):
    whole = math.gcd(*widths)
    return max(t for t in range(1, whole + 1) if whole % t == 0 and (t == whole or t % LANES == 0) and t <= 768)


def run_copies(pairs, sems):
    copies = [
        pltpu.make_async_copy(source, target, sems.at[i]) for i, (source, target) in enumerate(pairs)
    ]
    for copy in copies:
        copy.start()
    for copy in copies:
        copy.wait()


def cut_kernel(edges, source_ref, *refs):
    outs, (held_ref, sems) = refs[:-2], refs[-2:]
    steps, rows = held_ref.shape[:2]
    copies = [
        pltpu.make_async_copy(source_ref.at[pl.ds(i * rows, rows)], held_ref.at[i], sems.at[0, i])
        for i in range(steps)
    ]
    for copy in copies:
        copy.start()
    leaving = []
    for i in range(steps):
        copies[i].wait()
        for m, (a, b, out) in enumerate(zip(edges, edges[1:], outs)):
            leaving.append(
                pltpu.make_async_copy(
                    held_ref.at[i, :, pl.ds(a, b - a)],
                    out.at[pl.ds(i * rows, rows)],
                    sems.at[1 + m, i],
                )
            )
            leaving[-1].start()
    for copy in leaving:
        copy.wait()


def order_kernel(rank_part, *refs):
    pieces, out_ref, sems = refs[:-2], refs[-2], refs[-1]
    me = lax.axis_index("tensor")
    run_copies(
        [
            (piece, out_ref.at[pl.ds(pl.multiple_of((me ^ f) * rank_part, rank_part), rank_part)])
            for f, piece in enumerate(pieces)
        ],
        sems,
    )


def start_tiles(tile, depth, places, features, weight_ref, held_ref, rows_ref, sems):
    me, t = lax.axis_index("tensor"), 0
    for (flip, first), part in zip(places, features):
        for k in range(0, part.shape[1], tile):
            start = pl.multiple_of((me ^ flip) * depth + first + k, LANES)
            pltpu.make_async_copy(
                weight_ref.at[pl.ds(start, tile)], rows_ref.at[t], sems.at[1, t]
            ).start()
            pltpu.make_async_copy(part.at[:, pl.ds(k, tile)], held_ref.at[t], sems.at[0, t]).start()
            t += 1


def add_tiles(held_ref, rows_ref, sems, total_ref):
    @pl.loop(0, held_ref.shape[0])
    def _(t):
        pltpu.make_async_copy(held_ref.at[t], held_ref.at[t], sems.at[0, t]).wait()
        pltpu.make_async_copy(rows_ref.at[t], rows_ref.at[t], sems.at[1, t]).wait()
        total_ref[...] += jnp.dot(held_ref[t], rows_ref[t], preferred_element_type=jnp.float32)


def tile_scratch(tile, features, columns):
    tiles = sum(f.shape[1] for f in features) // tile
    rows = features[0].shape[0]
    return [
        pltpu.VMEM((tiles, rows, tile), jnp.bfloat16),
        pltpu.VMEM((tiles, tile, columns), jnp.bfloat16),
        pltpu.SemaphoreType.DMA((2, tiles)),
    ]


def first_kernel(tile, depth, places, slots, placement_ref, tenant_ref, weight_ref, *refs):
    count = len(places)
    features = refs[:count]
    out_ref, stored_ref, held_ref, rows_ref, sems = refs[count:]
    start_tiles(tile, depth, places, features, weight_ref, held_ref, rows_ref, sems)
    out_ref[...] = jnp.zeros_like(out_ref)
    stored = jnp.zeros(stored_ref.shape, jnp.int32)
    for slot in range(slots):
        stored = jnp.where(tenant_ref[...] == slot, placement_ref[slot], stored)
    stored_ref[...] = stored
    add_tiles(held_ref, rows_ref, sems, out_ref)


def products_kernel(tile, depth, places, weight_ref, *refs):
    count = len(places)
    features, given = refs[:count], refs[count]
    out_ref, held_ref, rows_ref, sems = refs[count + 1 :]
    start_tiles(tile, depth, places, features, weight_ref, held_ref, rows_ref, sems)
    out_ref[...] = given[...]
    add_tiles(held_ref, rows_ref, sems, out_ref)


def owners_of(flips, pairs):
    group, part = lax.axis_index("adapter"), lax.axis_index("parts")
    owners = [group] + [group ^ flip for flip in flips]
    for near, far in pairs:
        owners += [group ^ (near + part * (far - near)), group ^ (far + part * (near - far))]
    return owners


def last_kernel(tile, depth, places, flips, pairs, slots, weight_ref, *refs):
    count = len(places)
    features = refs[:count]
    given, stored_ref, sum_ref, more_ref = refs[count : count + 4]
    ups = refs[count + 4 : count + 4 + slots]
    (
        out_ref, total_ref, sums_ref, received_ref, stacked_ref, held_ref, rows_ref, sems, small_sems,
    ) = refs[count + 4 + slots :]
    rank = ups[0].shape[0]
    copies = [(sum_ref, sums_ref), (more_ref, received_ref)]
    copies += [(up, stacked_ref.at[pl.ds(b * rank, rank)]) for b, up in enumerate(ups)]
    copies = [
        pltpu.make_async_copy(source, target, small_sems.at[i])
        for i, (source, target) in enumerate(copies)
    ]
    for copy in copies:
        copy.start()
    start_tiles(tile, depth, places, features, weight_ref, held_ref, rows_ref, sems)
    for copy in copies:
        copy.wait()
    shrunk = (sums_ref[...] + received_ref[...].astype(jnp.float32)).astype(jnp.bfloat16).astype(jnp.float32)
    spread = jnp.concatenate(
        [jnp.where(stored_ref[...] == owner, shrunk, 0.0) for owner in owners_of(flips, pairs)], axis=0
    )
    expanded = jnp.dot(
        spread.T.astype(jnp.bfloat16), stacked_ref[...], preferred_element_type=jnp.float32
    )
    expanded = expanded.astype(jnp.bfloat16).astype(jnp.float32)
    total_ref[...] = given[...] + LOWRANK_SCALE * expanded
    add_tiles(held_ref, rows_ref, sems, total_ref)
    out_ref[...] = total_ref[...].astype(out_ref.dtype)


def shrink_kernel(tile, flips, pairs, slots, tokens_ref, stored_ref, *refs):
    downs, out_ref, held_ref, down_ref, sums_ref, sems = (
        refs[:slots], refs[slots], *refs[slots + 1 :]
    )
    rank = downs[0].shape[0]
    tiles = tokens_ref.shape[1] // tile
    for k in range(tiles):
        here = pl.ds(k * tile, tile)
        pltpu.make_async_copy(tokens_ref.at[:, here], held_ref.at[k], sems.at[0, k]).start()
        for b, down in enumerate(downs):
            pltpu.make_async_copy(
                down.at[:, here], down_ref.at[k, pl.ds(b * rank, rank)], sems.at[1 + b, k]
            ).start()
    sums_ref[...] = jnp.zeros_like(sums_ref)

    @pl.loop(0, tiles)
    def _(k):
        pltpu.make_async_copy(held_ref.at[k], held_ref.at[k], sems.at[0, k]).wait()
        for b in range(slots):
            block = down_ref.at[k, pl.ds(b * rank, rank)]
            pltpu.make_async_copy(block, block, sems.at[1 + b, k]).wait()
        sums_ref[...] += lax.dot_general(
            held_ref[k], down_ref[k], (((1,), (1,)), ((), ())), preferred_element_type=jnp.float32
        )

    sums = sums_ref[...].T
    total = jnp.zeros(out_ref.shape, jnp.float32)
    for b, owner in enumerate(owners_of(flips, pairs)):
        total += jnp.where(stored_ref[...] == owner, sums[b * rank : (b + 1) * rank], 0.0)
    out_ref[...] = total


def body(
    tokens, tenant, placement, frozen_projection_weight, lowrank_down_weight, lowrank_up_weight
):
    rows, depth = tokens.shape
    slots = placement.shape[0]
    tensors = lax.axis_size("tensor")
    groups = lax.axis_size("adapter")
    parts = lax.axis_size("parts")
    me = lax.axis_index("tensor")
    rank, columns = lowrank_up_weight.shape[1:]
    edges = [0] + [int(depth * cut) // LANES * LANES for cut in CUTS] + [depth]
    tile = math.gcd(*edges)

    down = lowrank_down_weight[0].T
    pieces = [
        lax.dynamic_slice_in_dim(down, (me ^ flip) * depth, depth, axis=1)
        for flip in range(tensors)
    ]
    uncut, pieces = chained(tokens, pieces)
    steps = 6
    chunks = list(
        call(
            functools.partial(cut_kernel, edges),
            [jax.ShapeDtypeStruct((rows, b - a), tokens.dtype) for a, b in zip(edges, edges[1:])],
            [ANYWHERE],
            [
                pltpu.VMEM((steps, rows // steps, depth), tokens.dtype),
                pltpu.SemaphoreType.DMA((len(edges), steps)),
            ],
            [ANYWHERE] * (len(edges) - 1),
            mib=56,
        )(uncut)
    )
    pieces = [pieces[0]] + [flipped(pieces[f], "tensor", f) for f in range(1, tensors)]
    pieces[1], here = chained(pieces[1], tokens)
    neighbour = flipped(here, "tensor", 1)
    if down.shape[0] % 16 == 0:
        own = call(
            functools.partial(order_kernel, down.shape[0]),
            jax.ShapeDtypeStruct((rank, depth), down.dtype),
            [ANYWHERE] * tensors,
            [pltpu.SemaphoreType.DMA((tensors,))],
            ANYWHERE,
            cost=FREE,
        )(*pieces)
    else:
        none = jnp.zeros((), down.dtype)
        own = jnp.concatenate(
            [sum(jnp.where((me ^ f) == j, pieces[f], none) for f in range(tensors)) for j in range(tensors)],
            axis=0,
        )

    hops = range(CORES, tensors, CORES)

    def send(m):
        return [flipped(chunks[m], "tensor", hop) for hop in hops]

    far = [send(0)]

    def across(m):
        return [flipped(value, "tensor", 1) for value in far[m]]

    def far_places(m):
        return [(hop, edges[m]) for hop in hops]

    def near_places(m):
        return [(hop ^ 1, edges[m]) for hop in hops]

    def products(places, features, total):
        tile = tile_of(*[f.shape[1] for f in features])
        return call(
            functools.partial(products_kernel, tile, depth, places),
            jax.ShapeDtypeStruct((rows, columns), jnp.float32),
            [ANYWHERE] + [ANYWHERE] * len(features) + [VECTOR],
            tile_scratch(tile, features, columns),
        )(frozen_projection_weight, *features, total)

    flips = list(range(1, groups))
    pairs = []
    if parts == 2:
        while len(flips) > 1:
            pairs.append((flips.pop(-2), flips.pop(-1)))
    routes = [
        [(p * groups + z, p * groups + (z ^ pair[p])) for p in range(parts) for z in range(groups)]
        for pair in pairs
    ]

    def fetch_far(value):
        return [lax.ppermute(value, ("parts", "adapter"), route) for route in routes]

    def fetch_near(value):
        return [flipped(value, "adapter", flip) for flip in flips]

    def swap(values):
        return [flipped(value, "parts", 1) for value in values]

    own, here = chained(own, tokens)
    fetched = fetch_far(own)
    total, stored = call(
        functools.partial(first_kernel, tile, depth, [(0, 0)], slots),
        [
            jax.ShapeDtypeStruct((rows, columns), jnp.float32),
            jax.ShapeDtypeStruct((1, rows), jnp.int32),
        ],
        [SCALAR, VECTOR, ANYWHERE, ANYWHERE],
        tile_scratch(tile, [tokens], columns),
        [VECTOR, VECTOR],
    )(placement, tenant.reshape(1, rows), frozen_projection_weight, here)
    total, own, up, neighbour, chunks[1] = chained(
        total, own, lowrank_up_weight[0], neighbour, chunks[1]
    )
    far.append(send(1))
    single, single_up = fetch_near(own), fetch_near(up)
    fetched, total = chained(fetched, total)
    swapped = swap(fetched)
    fetched_up = fetch_far(up)
    total, neighbour = chained(total, neighbour)
    total = products([(1, 0)], [neighbour], total)
    single, swapped, single_up, fetched_up, total = chained(
        single, swapped, single_up, fetched_up, total
    )
    downs = [own] + single
    for pair in zip(fetched, swapped):
        downs += pair

    tiles = depth // tile
    partial = call(
        functools.partial(shrink_kernel, tile, flips, pairs, slots),
        jax.ShapeDtypeStruct((rank, rows), jnp.float32),
        [ANYWHERE, VECTOR] + [ANYWHERE] * slots,
        [
            pltpu.VMEM((tiles, rows, tile), jnp.bfloat16),
            pltpu.VMEM((tiles, slots * rank, tile), jnp.bfloat16),
            pltpu.VMEM((rows, slots * rank), jnp.float32),
            pltpu.SemaphoreType.DMA((1 + slots, tiles)),
        ],
    )(tokens, stored, *downs)
    swapped_up = swap(fetched_up)
    far[0], swapped_up, partial = chained(far[0], swapped_up, partial)
    ups = [up] + single_up
    for pair in zip(fetched_up, swapped_up):
        ups += pair
    near = across(0)
    total = products(far_places(0), far[0], total)
    flip = 1
    while flip < tensors // 2:
        received = flipped(partial, "tensor", flip)
        if flip == 1:
            received, total = chained(received, total)
        partial += received
        flip *= 2
    more = flipped(partial.astype(jnp.bfloat16), "tensor", flip)
    total, partial = chained(total, partial)
    total = products(near_places(0), near, total)
    far[1], ups, total = chained(far[1], ups, total)
    near = across(1)
    total = products(far_places(1), far[1], total)
    near, more, total = chained(near, more, total)

    return call(
        functools.partial(last_kernel, tile, depth, near_places(1), flips, pairs, slots),
        jax.ShapeDtypeStruct((rows, columns), jnp.bfloat16),
        [ANYWHERE] + [ANYWHERE] * len(near) + [VECTOR] * 2 + [ANYWHERE] * (2 + slots),
        [
            pltpu.VMEM((rows, columns), jnp.float32),
            pltpu.VMEM((rank, rows), jnp.float32),
            pltpu.VMEM((rank, rows), jnp.bfloat16),
            pltpu.VMEM((slots * rank, columns), jnp.bfloat16),
        ]
        + tile_scratch(tile, near, columns)
        + [pltpu.SemaphoreType.DMA((2 + slots,))],
    )(frozen_projection_weight, *near, total, stored, partial, more, *ups)


def solution(mesh):
    placed = (
        P(("parts", "adapter"), "tensor"),
        P(("parts", "adapter"), None),
        P(),
        P(None, "tensor"),
        P("adapter", None, "tensor"),
        P("adapter", None, "tensor"),
    )
    return jax.shard_map(
        body,
        mesh=mesh,
        in_specs=placed,
        out_specs=P(("parts", "adapter"), "tensor"),
        check_vma=False,
    )
```

```python
import functools
import math

import jax
import jax.numpy as jnp
from jax import lax
from jax.experimental import pallas as pl
from jax.experimental.pallas import tpu as pltpu
from jax.sharding import PartitionSpec as P

LOWRANK_SCALE = 2.0
CORES = 2
LANES = 128
CUTS = (0.75,)
MIB = 1024 * 1024
FREE = pl.CostEstimate(flops=0, bytes_accessed=0, transcendentals=0)
LONG = pl.CostEstimate(flops=10**11, bytes_accessed=0, transcendentals=0)
ANYWHERE = pl.BlockSpec(memory_space=pl.ANY)
VECTOR = pl.BlockSpec(memory_space=pltpu.VMEM)
SCALAR = pl.BlockSpec(memory_space=pltpu.SMEM)


def flipped(value, axis, flip):
    count = lax.axis_size(axis)
    return lax.ppermute(value, axis, [(i, i ^ flip) for i in range(count)])


def chained(*values):
    return lax.optimization_barrier(values)


def call(kernel, out_shape, in_specs, scratch, out_specs=VECTOR, cost=LONG, mib=48):
    return pl.pallas_call(
        kernel,
        out_shape=out_shape,
        in_specs=in_specs,
        out_specs=out_specs,
        scratch_shapes=scratch,
        cost_estimate=cost,
        compiler_params=pltpu.CompilerParams(vmem_limit_bytes=mib * MIB),
    )


def run_copies(pairs, sems):
    copies = [
        pltpu.make_async_copy(source, target, sems.at[i]) for i, (source, target) in enumerate(pairs)
    ]
    for copy in copies:
        copy.start()
    for copy in copies:
        copy.wait()


def cut_kernel(edges, source_ref, *refs):
    outs, (held_ref, sems) = refs[:-2], refs[-2:]
    steps, rows = held_ref.shape[:2]
    copies = [
        pltpu.make_async_copy(source_ref.at[pl.ds(i * rows, rows)], held_ref.at[i], sems.at[0, i])
        for i in range(steps)
    ]
    for copy in copies:
        copy.start()
    leaving = []
    for i in range(steps):
        copies[i].wait()
        for m, (a, b, out) in enumerate(zip(edges, edges[1:], outs)):
            leaving.append(
                pltpu.make_async_copy(
                    held_ref.at[i, :, pl.ds(a, b - a)],
                    out.at[pl.ds(i * rows, rows)],
                    sems.at[1 + m, i],
                )
            )
            leaving[-1].start()
    for copy in leaving:
        copy.wait()


def order_kernel(rank_part, *refs):
    pieces, out_ref, sems = refs[:-2], refs[-2], refs[-1]
    me = lax.axis_index("tensor")
    run_copies(
        [
            (piece, out_ref.at[pl.ds(pl.multiple_of((me ^ f) * rank_part, rank_part), rank_part)])
            for f, piece in enumerate(pieces)
        ],
        sems,
    )


def start_tiles(tile, depth, places, features, weight_ref, held_ref, rows_ref, sems):
    me, t = lax.axis_index("tensor"), 0
    for (flip, first, skip, width), part in zip(places, features):
        for k in range(0, width, tile):
            start = pl.multiple_of((me ^ flip) * depth + first + k, LANES)
            pltpu.make_async_copy(
                weight_ref.at[pl.ds(start, tile)], rows_ref.at[t], sems.at[1, t]
            ).start()
            pltpu.make_async_copy(part.at[:, pl.ds(skip + k, tile)], held_ref.at[t], sems.at[0, t]).start()
            t += 1


def add_tiles(held_ref, rows_ref, sems, total_ref):
    @pl.loop(0, held_ref.shape[0])
    def _(t):
        pltpu.make_async_copy(held_ref.at[t], held_ref.at[t], sems.at[0, t]).wait()
        pltpu.make_async_copy(rows_ref.at[t], rows_ref.at[t], sems.at[1, t]).wait()
        total_ref[...] += jnp.dot(held_ref[t], rows_ref[t], preferred_element_type=jnp.float32)


def tile_scratch(tile, rows, places, columns):
    tiles = sum(place[3] for place in places) // tile
    return [
        pltpu.VMEM((tiles, rows, tile), jnp.bfloat16),
        pltpu.VMEM((tiles, tile, columns), jnp.bfloat16),
        pltpu.SemaphoreType.DMA((2, tiles)),
    ]


def first_kernel(tile, depth, places, slots, placement_ref, tenant_ref, weight_ref, *refs):
    count = len(places)
    features = refs[:count]
    out_ref, stored_ref, held_ref, rows_ref, sems = refs[count:]
    start_tiles(tile, depth, places, features, weight_ref, held_ref, rows_ref, sems)
    out_ref[...] = jnp.zeros_like(out_ref)
    stored = jnp.zeros(stored_ref.shape, jnp.int32)
    for slot in range(slots):
        stored = jnp.where(tenant_ref[...] == slot, placement_ref[slot], stored)
    stored_ref[...] = stored
    add_tiles(held_ref, rows_ref, sems, out_ref)


def products_kernel(tile, depth, places, weight_ref, *refs):
    count = len(places)
    features, given = refs[:count], refs[count]
    out_ref, held_ref, rows_ref, sems = refs[count + 1 :]
    start_tiles(tile, depth, places, features, weight_ref, held_ref, rows_ref, sems)
    out_ref[...] = given[...]
    add_tiles(held_ref, rows_ref, sems, out_ref)


def owners_of(flips, pairs):
    group, part = lax.axis_index("adapter"), lax.axis_index("parts")
    owners = [group] + [group ^ flip for flip in flips]
    for near, far in pairs:
        owners += [group ^ (near + part * (far - near)), group ^ (far + part * (near - far))]
    return owners


def last_kernel(tile, depth, places, flips, pairs, slots, weight_ref, *refs):
    count = len(places)
    features = refs[:count]
    given, stored_ref, sum_ref, more_ref = refs[count : count + 4]
    ups = refs[count + 4 : count + 4 + slots]
    (
        out_ref, total_ref, sums_ref, received_ref, stacked_ref, held_ref, rows_ref, sems, small_sems,
    ) = refs[count + 4 + slots :]
    rank = ups[0].shape[0]
    copies = [(sum_ref, sums_ref), (more_ref, received_ref)]
    copies += [(up, stacked_ref.at[pl.ds(b * rank, rank)]) for b, up in enumerate(ups)]
    copies = [
        pltpu.make_async_copy(source, target, small_sems.at[i])
        for i, (source, target) in enumerate(copies)
    ]
    for copy in copies:
        copy.start()
    start_tiles(tile, depth, places, features, weight_ref, held_ref, rows_ref, sems)
    for copy in copies:
        copy.wait()
    shrunk = (sums_ref[...] + received_ref[...].astype(jnp.float32)).astype(jnp.bfloat16).astype(jnp.float32)
    spread = jnp.concatenate(
        [jnp.where(stored_ref[...] == owner, shrunk, 0.0) for owner in owners_of(flips, pairs)], axis=0
    )
    expanded = jnp.dot(
        spread.T.astype(jnp.bfloat16), stacked_ref[...], preferred_element_type=jnp.float32
    )
    expanded = expanded.astype(jnp.bfloat16).astype(jnp.float32)
    total_ref[...] = given[...] + LOWRANK_SCALE * expanded
    add_tiles(held_ref, rows_ref, sems, total_ref)
    out_ref[...] = total_ref[...].astype(out_ref.dtype)


def shrink_kernel(tile, flips, pairs, slots, tokens_ref, stored_ref, *refs):
    downs, out_ref, held_ref, down_ref, sums_ref, sems = (
        refs[:slots], refs[slots], *refs[slots + 1 :]
    )
    rank = downs[0].shape[0]
    tiles = tokens_ref.shape[1] // tile
    for k in range(tiles):
        here = pl.ds(k * tile, tile)
        pltpu.make_async_copy(tokens_ref.at[:, here], held_ref.at[k], sems.at[0, k]).start()
        for b, down in enumerate(downs):
            pltpu.make_async_copy(
                down.at[:, here], down_ref.at[k, pl.ds(b * rank, rank)], sems.at[1 + b, k]
            ).start()
    sums_ref[...] = jnp.zeros_like(sums_ref)

    @pl.loop(0, tiles)
    def _(k):
        pltpu.make_async_copy(held_ref.at[k], held_ref.at[k], sems.at[0, k]).wait()
        for b in range(slots):
            block = down_ref.at[k, pl.ds(b * rank, rank)]
            pltpu.make_async_copy(block, block, sems.at[1 + b, k]).wait()
        sums_ref[...] += lax.dot_general(
            held_ref[k], down_ref[k], (((1,), (1,)), ((), ())), preferred_element_type=jnp.float32
        )

    sums = sums_ref[...].T
    total = jnp.zeros(out_ref.shape, jnp.float32)
    for b, owner in enumerate(owners_of(flips, pairs)):
        total += jnp.where(stored_ref[...] == owner, sums[b * rank : (b + 1) * rank], 0.0)
    out_ref[...] = total


def body(
    tokens, tenant, placement, frozen_projection_weight, lowrank_down_weight, lowrank_up_weight
):
    rows, depth = tokens.shape
    slots = placement.shape[0]
    tensors = lax.axis_size("tensor")
    groups = lax.axis_size("adapter")
    parts = lax.axis_size("parts")
    me = lax.axis_index("tensor")
    rank, columns = lowrank_up_weight.shape[1:]
    edges = [0] + [int(depth * cut) // LANES * LANES for cut in CUTS] + [depth]
    tile = math.gcd(*edges)

    down = lowrank_down_weight[0].T
    pieces = [
        lax.dynamic_slice_in_dim(down, (me ^ flip) * depth, depth, axis=1)
        for flip in range(tensors)
    ]
    uncut, pieces = chained(tokens, pieces)
    steps = 6
    chunks = list(
        call(
            functools.partial(cut_kernel, edges),
            [jax.ShapeDtypeStruct((rows, b - a), tokens.dtype) for a, b in zip(edges, edges[1:])],
            [ANYWHERE],
            [
                pltpu.VMEM((steps, rows // steps, depth), tokens.dtype),
                pltpu.SemaphoreType.DMA((len(edges), steps)),
            ],
            [ANYWHERE] * (len(edges) - 1),
            cost=FREE,
            mib=56,
        )(uncut)
    )
    pieces = [pieces[0]] + [flipped(pieces[f], "tensor", f) for f in range(1, tensors)]
    pieces[1], here = chained(pieces[1], tokens)
    neighbour = flipped(here, "tensor", 1)
    if down.shape[0] % 16 == 0:
        own = call(
            functools.partial(order_kernel, down.shape[0]),
            jax.ShapeDtypeStruct((rank, depth), down.dtype),
            [ANYWHERE] * tensors,
            [pltpu.SemaphoreType.DMA((tensors,))],
            ANYWHERE,
            cost=FREE,
        )(*pieces)
    else:
        none = jnp.zeros((), down.dtype)
        own = jnp.concatenate(
            [sum(jnp.where((me ^ f) == j, pieces[f], none) for f in range(tensors)) for j in range(tensors)],
            axis=0,
        )

    hops = range(CORES, tensors, CORES)

    def send(m):
        return [flipped(chunks[m], "tensor", hop) for hop in hops]

    far = [send(0)]

    def across(m):
        return [flipped(value, "tensor", 1) for value in far[m]]

    def far_places(m):
        return [(hop, edges[m], 0, edges[m + 1] - edges[m]) for hop in hops]

    def near_places(m):
        return [(hop ^ 1, edges[m], 0, edges[m + 1] - edges[m]) for hop in hops]

    def products(places, features, total):
        return call(
            functools.partial(products_kernel, tile, depth, places),
            jax.ShapeDtypeStruct((rows, columns), jnp.float32),
            [ANYWHERE] + [ANYWHERE] * len(features) + [VECTOR],
            tile_scratch(tile, rows, places, columns),
        )(frozen_projection_weight, *features, total)

    flips = list(range(1, groups))
    pairs = []
    if parts == 2:
        while len(flips) > 1:
            pairs.append((flips.pop(-2), flips.pop(-1)))
    routes = [
        [(p * groups + z, p * groups + (z ^ pair[p])) for p in range(parts) for z in range(groups)]
        for pair in pairs
    ]

    def fetch_far(value):
        return [lax.ppermute(value, ("parts", "adapter"), route) for route in routes]

    def fetch_near(value):
        return [flipped(value, "adapter", flip) for flip in flips]

    def swap(values):
        return [flipped(value, "parts", 1) for value in values]

    own, here = chained(own, tokens)
    fetched = fetch_far(own)
    places = [(0, 0, 0, depth // 2)]
    total, stored = call(
        functools.partial(first_kernel, tile, depth, places, slots),
        [
            jax.ShapeDtypeStruct((rows, columns), jnp.float32),
            jax.ShapeDtypeStruct((1, rows), jnp.int32),
        ],
        [SCALAR, VECTOR, ANYWHERE, ANYWHERE],
        tile_scratch(tile, rows, places, columns),
        [VECTOR, VECTOR],
    )(placement, tenant.reshape(1, rows), frozen_projection_weight, here)
    total, own, up, neighbour, chunks[1] = chained(
        total, own, lowrank_up_weight[0], neighbour, chunks[1]
    )
    far.append(send(1))
    single, single_up = fetch_near(own), fetch_near(up)
    total = products([(0, depth // 2, depth // 2, depth // 2)], [here], total)
    fetched, single_up, total, up = chained(fetched, single_up, total, up)
    swapped = swap(fetched)
    fetched_up = fetch_far(up)
    total, neighbour = chained(total, neighbour)
    total = products([(1, 0, 0, depth)], [neighbour], total)
    fetched_up, total = chained(fetched_up, total)
    swapped_up = swap(fetched_up)
    single, swapped, total = chained(single, swapped, total)
    downs = [own] + single
    for pair in zip(fetched, swapped):
        downs += pair

    tiles = depth // tile
    partial = call(
        functools.partial(shrink_kernel, tile, flips, pairs, slots),
        jax.ShapeDtypeStruct((rank, rows), jnp.float32),
        [ANYWHERE, VECTOR] + [ANYWHERE] * slots,
        [
            pltpu.VMEM((tiles, rows, tile), jnp.bfloat16),
            pltpu.VMEM((tiles, slots * rank, tile), jnp.bfloat16),
            pltpu.VMEM((rows, slots * rank), jnp.float32),
            pltpu.SemaphoreType.DMA((1 + slots, tiles)),
        ],
    )(tokens, stored, *downs)
    far[0], partial = chained(far[0], partial)
    ups = [up] + single_up
    for pair in zip(fetched_up, swapped_up):
        ups += pair
    near = across(0)
    total = products(far_places(0), far[0], total)
    flip = 1
    while flip < tensors // 2:
        received = flipped(partial, "tensor", flip)
        if flip == 1:
            received, total = chained(received, total)
        partial += received
        flip *= 2
    more = flipped(partial.astype(jnp.bfloat16), "tensor", flip)
    total, partial = chained(total, partial)
    total = products(near_places(0), near, total)
    far[1], ups, total = chained(far[1], ups, total)
    near = across(1)
    total = products(far_places(1), far[1], total)
    near, more, total = chained(near, more, total)

    places = near_places(1)
    return call(
        functools.partial(last_kernel, tile, depth, places, flips, pairs, slots),
        jax.ShapeDtypeStruct((rows, columns), jnp.bfloat16),
        [ANYWHERE] + [ANYWHERE] * len(near) + [VECTOR] * 2 + [ANYWHERE] * (2 + slots),
        [
            pltpu.VMEM((rows, columns), jnp.float32),
            pltpu.VMEM((rank, rows), jnp.float32),
            pltpu.VMEM((rank, rows), jnp.bfloat16),
            pltpu.VMEM((slots * rank, columns), jnp.bfloat16),
        ]
        + tile_scratch(tile, rows, places, columns)
        + [pltpu.SemaphoreType.DMA((2 + slots,))],
    )(frozen_projection_weight, *near, total, stored, partial, more, *ups)


def solution(mesh):
    placed = (
        P(("parts", "adapter"), "tensor"),
        P(("parts", "adapter"), None),
        P(),
        P(None, "tensor"),
        P("adapter", None, "tensor"),
        P("adapter", None, "tensor"),
    )
    return jax.shard_map(
        body,
        mesh=mesh,
        in_specs=placed,
        out_specs=P(("parts", "adapter"), "tensor"),
        check_vma=False,
    )
```

```python
import functools
import math

import jax
import jax.numpy as jnp
from jax import lax
from jax.experimental import pallas as pl
from jax.experimental.pallas import tpu as pltpu
from jax.sharding import PartitionSpec as P

LOWRANK_SCALE = 2.0
CORES = 2
LANES = 128
CUTS = (0.75,)
MIB = 1024 * 1024
FREE = pl.CostEstimate(flops=0, bytes_accessed=0, transcendentals=0)
LONG = pl.CostEstimate(flops=10**11, bytes_accessed=0, transcendentals=0)
ANYWHERE = pl.BlockSpec(memory_space=pl.ANY)
VECTOR = pl.BlockSpec(memory_space=pltpu.VMEM)
SCALAR = pl.BlockSpec(memory_space=pltpu.SMEM)


def flipped(value, axis, flip):
    count = lax.axis_size(axis)
    return lax.ppermute(value, axis, [(i, i ^ flip) for i in range(count)])


def chained(*values):
    return lax.optimization_barrier(values)


def call(kernel, out_shape, in_specs, scratch, out_specs=VECTOR, cost=LONG, mib=24):
    return pl.pallas_call(
        kernel,
        out_shape=out_shape,
        in_specs=in_specs,
        out_specs=out_specs,
        scratch_shapes=scratch,
        cost_estimate=cost,
        compiler_params=pltpu.CompilerParams(vmem_limit_bytes=mib * MIB),
    )


def run_copies(pairs, sems):
    copies = [
        pltpu.make_async_copy(source, target, sems.at[i]) for i, (source, target) in enumerate(pairs)
    ]
    for copy in copies:
        copy.start()
    for copy in copies:
        copy.wait()


def cut_kernel(edges, source_ref, *refs):
    outs, (held_ref, sems) = refs[:-2], refs[-2:]
    steps, rows = held_ref.shape[:2]
    copies = [
        pltpu.make_async_copy(source_ref.at[pl.ds(i * rows, rows)], held_ref.at[i], sems.at[0, i])
        for i in range(steps)
    ]
    for copy in copies:
        copy.start()
    leaving = []
    for i in range(steps):
        copies[i].wait()
        for m, (a, b, out) in enumerate(zip(edges, edges[1:], outs)):
            leaving.append(
                pltpu.make_async_copy(
                    held_ref.at[i, :, pl.ds(a, b - a)],
                    out.at[pl.ds(i * rows, rows)],
                    sems.at[1 + m, i],
                )
            )
            leaving[-1].start()
    for copy in leaving:
        copy.wait()


def order_kernel(rank_part, *refs):
    pieces, out_ref, sems = refs[:-2], refs[-2], refs[-1]
    me = lax.axis_index("tensor")
    run_copies(
        [
            (piece, out_ref.at[pl.ds(pl.multiple_of((me ^ f) * rank_part, rank_part), rank_part)])
            for f, piece in enumerate(pieces)
        ],
        sems,
    )


def start_tiles(tile, depth, places, features, weight_ref, held_ref, rows_ref, sems):
    me, t = lax.axis_index("tensor"), 0
    for (flip, first, skip, width), part in zip(places, features):
        for k in range(0, width, tile):
            start = pl.multiple_of((me ^ flip) * depth + first + k, LANES)
            pltpu.make_async_copy(
                weight_ref.at[pl.ds(start, tile)], rows_ref.at[t], sems.at[1, t]
            ).start()
            pltpu.make_async_copy(part.at[:, pl.ds(skip + k, tile)], held_ref.at[t], sems.at[0, t]).start()
            t += 1


def add_tiles(held_ref, rows_ref, sems, total_ref):
    @pl.loop(0, held_ref.shape[0])
    def _(t):
        pltpu.make_async_copy(held_ref.at[t], held_ref.at[t], sems.at[0, t]).wait()
        pltpu.make_async_copy(rows_ref.at[t], rows_ref.at[t], sems.at[1, t]).wait()
        total_ref[...] += jnp.dot(held_ref[t], rows_ref[t], preferred_element_type=jnp.float32)


def tile_scratch(tile, rows, places, columns):
    tiles = sum(place[3] for place in places) // tile
    return [
        pltpu.VMEM((tiles, rows, tile), jnp.bfloat16),
        pltpu.VMEM((tiles, tile, columns), jnp.bfloat16),
        pltpu.SemaphoreType.DMA((2, tiles)),
    ]


def first_kernel(tile, depth, places, slots, placement_ref, tenant_ref, weight_ref, *refs):
    count = len(places)
    features = refs[:count]
    out_ref, stored_ref, held_ref, rows_ref, sems = refs[count:]
    start_tiles(tile, depth, places, features, weight_ref, held_ref, rows_ref, sems)
    out_ref[...] = jnp.zeros_like(out_ref)
    stored = jnp.zeros(stored_ref.shape, jnp.int32)
    for slot in range(slots):
        stored = jnp.where(tenant_ref[...] == slot, placement_ref[slot], stored)
    stored_ref[...] = stored
    add_tiles(held_ref, rows_ref, sems, out_ref)


def products_kernel(tile, depth, places, weight_ref, *refs):
    count = len(places)
    features, given = refs[:count], refs[count]
    out_ref, held_ref, rows_ref, sems = refs[count + 1 :]
    start_tiles(tile, depth, places, features, weight_ref, held_ref, rows_ref, sems)
    out_ref[...] = given[...]
    add_tiles(held_ref, rows_ref, sems, out_ref)


def owners_of(flips, pairs):
    group, part = lax.axis_index("adapter"), lax.axis_index("parts")
    owners = [group] + [group ^ flip for flip in flips]
    for near, far in pairs:
        owners += [group ^ (near + part * (far - near)), group ^ (far + part * (near - far))]
    return owners


def last_kernel(tile, depth, places, flips, pairs, slots, weight_ref, *refs):
    count = len(places)
    features = refs[:count]
    given, stored_ref, sum_ref, more_ref = refs[count : count + 4]
    ups = refs[count + 4 : count + 4 + slots]
    (
        out_ref, total_ref, sums_ref, received_ref, stacked_ref, held_ref, rows_ref, sems, small_sems,
    ) = refs[count + 4 + slots :]
    rank = ups[0].shape[0]
    copies = [(sum_ref, sums_ref), (more_ref, received_ref)]
    copies += [(up, stacked_ref.at[pl.ds(b * rank, rank)]) for b, up in enumerate(ups)]
    copies = [
        pltpu.make_async_copy(source, target, small_sems.at[i])
        for i, (source, target) in enumerate(copies)
    ]
    for copy in copies:
        copy.start()
    start_tiles(tile, depth, places, features, weight_ref, held_ref, rows_ref, sems)
    total_ref[...] = given[...]
    add_tiles(held_ref, rows_ref, sems, total_ref)
    for copy in copies:
        copy.wait()
    shrunk = (sums_ref[...] + received_ref[...].astype(jnp.float32)).astype(jnp.bfloat16).astype(jnp.float32)
    spread = jnp.concatenate(
        [jnp.where(stored_ref[...] == owner, shrunk, 0.0) for owner in owners_of(flips, pairs)], axis=0
    )
    expanded = jnp.dot(
        spread.T.astype(jnp.bfloat16), stacked_ref[...], preferred_element_type=jnp.float32
    )
    expanded = expanded.astype(jnp.bfloat16).astype(jnp.float32)
    out_ref[...] = (total_ref[...] + LOWRANK_SCALE * expanded).astype(out_ref.dtype)


def shrink_kernel(tile, flips, pairs, slots, tokens_ref, stored_ref, *refs):
    downs, out_ref, held_ref, down_ref, sums_ref, sems = (
        refs[:slots], refs[slots], *refs[slots + 1 :]
    )
    rank = downs[0].shape[0]
    tiles = tokens_ref.shape[1] // tile
    for k in range(tiles):
        here = pl.ds(k * tile, tile)
        pltpu.make_async_copy(tokens_ref.at[:, here], held_ref.at[k], sems.at[0, k]).start()
        for b, down in enumerate(downs):
            pltpu.make_async_copy(
                down.at[:, here], down_ref.at[k, pl.ds(b * rank, rank)], sems.at[1 + b, k]
            ).start()
    sums_ref[...] = jnp.zeros_like(sums_ref)

    @pl.loop(0, tiles)
    def _(k):
        pltpu.make_async_copy(held_ref.at[k], held_ref.at[k], sems.at[0, k]).wait()
        for b in range(slots):
            block = down_ref.at[k, pl.ds(b * rank, rank)]
            pltpu.make_async_copy(block, block, sems.at[1 + b, k]).wait()
        sums_ref[...] += lax.dot_general(
            held_ref[k], down_ref[k], (((1,), (1,)), ((), ())), preferred_element_type=jnp.float32
        )

    sums = sums_ref[...].T
    total = jnp.zeros(out_ref.shape, jnp.float32)
    for b, owner in enumerate(owners_of(flips, pairs)):
        total += jnp.where(stored_ref[...] == owner, sums[b * rank : (b + 1) * rank], 0.0)
    out_ref[...] = total


def body(
    tokens, tenant, placement, frozen_projection_weight, lowrank_down_weight, lowrank_up_weight
):
    rows, depth = tokens.shape
    slots = placement.shape[0]
    tensors = lax.axis_size("tensor")
    groups = lax.axis_size("adapter")
    parts = lax.axis_size("parts")
    me = lax.axis_index("tensor")
    rank, columns = lowrank_up_weight.shape[1:]
    edges = [0] + [int(depth * cut) // LANES * LANES for cut in CUTS] + [depth]
    tile = math.gcd(*edges)

    down = lowrank_down_weight[0].T
    pieces = [
        lax.dynamic_slice_in_dim(down, (me ^ flip) * depth, depth, axis=1)
        for flip in range(tensors)
    ]
    uncut, pieces = chained(tokens, pieces)
    steps = 6
    chunks = list(
        call(
            functools.partial(cut_kernel, edges),
            [jax.ShapeDtypeStruct((rows, b - a), tokens.dtype) for a, b in zip(edges, edges[1:])],
            [ANYWHERE],
            [
                pltpu.VMEM((steps, rows // steps, depth), tokens.dtype),
                pltpu.SemaphoreType.DMA((len(edges), steps)),
            ],
            [ANYWHERE] * (len(edges) - 1),
            cost=FREE,
            mib=56,
        )(uncut)
    )
    pieces = [pieces[0]] + [flipped(pieces[f], "tensor", f) for f in range(1, tensors)]
    pieces[1], here = chained(pieces[1], tokens)
    neighbour = flipped(here, "tensor", 1)
    if down.shape[0] % 16 == 0:
        own = call(
            functools.partial(order_kernel, down.shape[0]),
            jax.ShapeDtypeStruct((rank, depth), down.dtype),
            [ANYWHERE] * tensors,
            [pltpu.SemaphoreType.DMA((tensors,))],
            ANYWHERE,
            cost=FREE,
        )(*pieces)
    else:
        none = jnp.zeros((), down.dtype)
        own = jnp.concatenate(
            [sum(jnp.where((me ^ f) == j, pieces[f], none) for f in range(tensors)) for j in range(tensors)],
            axis=0,
        )

    hops = range(CORES, tensors, CORES)

    def send(m):
        return [flipped(chunks[m], "tensor", hop) for hop in hops]

    far = [send(0)]

    def across(m):
        return [flipped(value, "tensor", 1) for value in far[m]]

    def far_places(m):
        return [(hop, edges[m], 0, edges[m + 1] - edges[m]) for hop in hops]

    def near_places(m):
        return [(hop ^ 1, edges[m], 0, edges[m + 1] - edges[m]) for hop in hops]

    def products(places, features, total):
        return call(
            functools.partial(products_kernel, tile, depth, places),
            jax.ShapeDtypeStruct((rows, columns), jnp.float32),
            [ANYWHERE] + [ANYWHERE] * len(features) + [VECTOR],
            tile_scratch(tile, rows, places, columns),
        )(frozen_projection_weight, *features, total)

    flips = list(range(1, groups))
    pairs = []
    if parts == 2:
        while len(flips) > 1:
            pairs.append((flips.pop(-2), flips.pop(-1)))
    routes = [
        [(p * groups + z, p * groups + (z ^ pair[p])) for p in range(parts) for z in range(groups)]
        for pair in pairs
    ]

    def fetch_far(value):
        return [lax.ppermute(value, ("parts", "adapter"), route) for route in routes]

    def fetch_near(value):
        return [flipped(value, "adapter", flip) for flip in flips]

    def swap(values):
        return [flipped(value, "parts", 1) for value in values]

    own, here = chained(own, tokens)
    fetched = fetch_far(own)
    places = [(0, 0, 0, depth // 2)]
    total, stored = call(
        functools.partial(first_kernel, tile, depth, places, slots),
        [
            jax.ShapeDtypeStruct((rows, columns), jnp.float32),
            jax.ShapeDtypeStruct((1, rows), jnp.int32),
        ],
        [SCALAR, VECTOR, ANYWHERE, ANYWHERE],
        tile_scratch(tile, rows, places, columns),
        [VECTOR, VECTOR],
    )(placement, tenant.reshape(1, rows), frozen_projection_weight, here)
    total, own, up, neighbour, chunks[1] = chained(
        total, own, lowrank_up_weight[0], neighbour, chunks[1]
    )
    far.append(send(1))
    single, single_up = fetch_near(own), fetch_near(up)
    total = products([(0, depth // 2, depth // 2, depth // 2)], [here], total)
    fetched, single_up, total, up = chained(fetched, single_up, total, up)
    swapped = swap(fetched)
    fetched_up = fetch_far(up)
    total, neighbour = chained(total, neighbour)
    total = products([(1, 0, 0, depth)], [neighbour], total)
    fetched_up, total = chained(fetched_up, total)
    swapped_up = swap(fetched_up)
    single, swapped, total = chained(single, swapped, total)
    downs = [own] + single
    for pair in zip(fetched, swapped):
        downs += pair

    tiles = depth // tile
    partial = call(
        functools.partial(shrink_kernel, tile, flips, pairs, slots),
        jax.ShapeDtypeStruct((rank, rows), jnp.float32),
        [ANYWHERE, VECTOR] + [ANYWHERE] * slots,
        [
            pltpu.VMEM((tiles, rows, tile), jnp.bfloat16),
            pltpu.VMEM((tiles, slots * rank, tile), jnp.bfloat16),
            pltpu.VMEM((rows, slots * rank), jnp.float32),
            pltpu.SemaphoreType.DMA((1 + slots, tiles)),
        ],
    )(tokens, stored, *downs)
    far[0], partial = chained(far[0], partial)
    ups = [up] + single_up
    for pair in zip(fetched_up, swapped_up):
        ups += pair
    near = across(0)
    total = products(far_places(0), far[0], total)
    flip = 1
    while flip < tensors // 2:
        received = flipped(partial, "tensor", flip)
        if flip == 1:
            received, total = chained(received, total)
        partial += received
        flip *= 2
    more = flipped(partial.astype(jnp.bfloat16), "tensor", flip)
    total, partial = chained(total, partial)
    total = products(near_places(0), near, total)
    far[1], ups, total = chained(far[1], ups, total)
    near = across(1)
    total = products(far_places(1), far[1], total)
    near, more, total = chained(near, more, total)

    places = near_places(1)
    return call(
        functools.partial(last_kernel, tile, depth, places, flips, pairs, slots),
        jax.ShapeDtypeStruct((rows, columns), jnp.bfloat16),
        [ANYWHERE] + [ANYWHERE] * len(near) + [VECTOR] * 2 + [ANYWHERE] * (2 + slots),
        [
            pltpu.VMEM((rows, columns), jnp.float32),
            pltpu.VMEM((rank, rows), jnp.float32),
            pltpu.VMEM((rank, rows), jnp.bfloat16),
            pltpu.VMEM((slots * rank, columns), jnp.bfloat16),
        ]
        + tile_scratch(tile, rows, places, columns)
        + [pltpu.SemaphoreType.DMA((2 + slots,))],
    )(frozen_projection_weight, *near, total, stored, partial, more, *ups)


def solution(mesh):
    placed = (
        P(("parts", "adapter"), "tensor"),
        P(("parts", "adapter"), None),
        P(),
        P(None, "tensor"),
        P("adapter", None, "tensor"),
        P("adapter", None, "tensor"),
    )
    return jax.shard_map(
        body,
        mesh=mesh,
        in_specs=placed,
        out_specs=P(("parts", "adapter"), "tensor"),
        check_vma=False,
    )
```

```python
import functools
import math

import jax
import jax.numpy as jnp
from jax import lax
from jax.experimental import pallas as pl
from jax.experimental.pallas import tpu as pltpu
from jax.sharding import PartitionSpec as P

LOWRANK_SCALE = 2.0
CORES = 2
LANES = 128
CUTS = (0.75,)
MIB = 1024 * 1024
FREE = pl.CostEstimate(flops=0, bytes_accessed=0, transcendentals=0)
LONG = pl.CostEstimate(flops=10**11, bytes_accessed=0, transcendentals=0)
ANYWHERE = pl.BlockSpec(memory_space=pl.ANY)
VECTOR = pl.BlockSpec(memory_space=pltpu.VMEM)
SCALAR = pl.BlockSpec(memory_space=pltpu.SMEM)


def flipped(value, axis, flip):
    count = lax.axis_size(axis)
    return lax.ppermute(value, axis, [(i, i ^ flip) for i in range(count)])


def chained(*values):
    return lax.optimization_barrier(values)


def call(kernel, out_shape, in_specs, scratch, out_specs=VECTOR, cost=LONG, mib=24):
    return pl.pallas_call(
        kernel,
        out_shape=out_shape,
        in_specs=in_specs,
        out_specs=out_specs,
        scratch_shapes=scratch,
        cost_estimate=cost,
        compiler_params=pltpu.CompilerParams(vmem_limit_bytes=mib * MIB),
    )


def run_copies(pairs, sems):
    copies = [
        pltpu.make_async_copy(source, target, sems.at[i]) for i, (source, target) in enumerate(pairs)
    ]
    for copy in copies:
        copy.start()
    for copy in copies:
        copy.wait()


def cut_kernel(edges, tokens_ref, down_ref, *refs):
    cuts = len(edges) - 1
    outs, pieces = refs[:cuts], refs[cuts:-4]
    held_ref, slices_ref, sems, slice_sems = refs[-4:]
    me, depth = lax.axis_index("tensor"), tokens_ref.shape[1]
    steps, rows = held_ref.shape[:2]
    arriving = []
    for i in range(len(pieces)):
        start = pl.multiple_of((me ^ (i + 1)) * depth, LANES)
        arriving.append(
            pltpu.make_async_copy(
                down_ref.at[:, pl.ds(start, depth)], slices_ref.at[i], slice_sems.at[0, i]
            )
        )
    copies = [
        pltpu.make_async_copy(tokens_ref.at[pl.ds(i * rows, rows)], held_ref.at[i], sems.at[0, i])
        for i in range(steps)
    ]
    for copy in arriving + copies:
        copy.start()
    leaving = []
    for i, piece in enumerate(pieces):
        arriving[i].wait()
        leaving.append(pltpu.make_async_copy(slices_ref.at[i], piece, slice_sems.at[1, i]))
        leaving[-1].start()
    for i in range(steps):
        copies[i].wait()
        for m, (a, b, out) in enumerate(zip(edges, edges[1:], outs)):
            leaving.append(
                pltpu.make_async_copy(
                    held_ref.at[i, :, pl.ds(a, b - a)],
                    out.at[pl.ds(i * rows, rows)],
                    sems.at[1 + m, i],
                )
            )
            leaving[-1].start()
    for copy in leaving:
        copy.wait()


def order_kernel(down_ref, *refs):
    pieces, out_ref, sems = refs[:-2], refs[-2], refs[-1]
    me = lax.axis_index("tensor")
    part, depth = pieces[0].shape
    mine = down_ref.at[:, pl.ds(pl.multiple_of(me * depth, LANES), depth)]
    run_copies(
        [
            (piece, out_ref.at[pl.ds(pl.multiple_of((me ^ f) * part, part), part)])
            for f, piece in enumerate((mine, *pieces))
        ],
        sems,
    )


def start_tiles(tile, depth, places, features, weight_ref, held_ref, rows_ref, sems):
    me, t = lax.axis_index("tensor"), 0
    for (flip, first, skip, width), part in zip(places, features):
        for k in range(0, width, tile):
            start = pl.multiple_of((me ^ flip) * depth + first + k, LANES)
            pltpu.make_async_copy(
                weight_ref.at[pl.ds(start, tile)], rows_ref.at[t], sems.at[1, t]
            ).start()
            pltpu.make_async_copy(part.at[:, pl.ds(skip + k, tile)], held_ref.at[t], sems.at[0, t]).start()
            t += 1


def add_tiles(held_ref, rows_ref, sems, total_ref):
    @pl.loop(0, held_ref.shape[0])
    def _(t):
        pltpu.make_async_copy(held_ref.at[t], held_ref.at[t], sems.at[0, t]).wait()
        pltpu.make_async_copy(rows_ref.at[t], rows_ref.at[t], sems.at[1, t]).wait()
        total_ref[...] += jnp.dot(held_ref[t], rows_ref[t], preferred_element_type=jnp.float32)


def tile_scratch(tile, rows, places, columns):
    tiles = sum(place[3] for place in places) // tile
    return [
        pltpu.VMEM((tiles, rows, tile), jnp.bfloat16),
        pltpu.VMEM((tiles, tile, columns), jnp.bfloat16),
        pltpu.SemaphoreType.DMA((2, tiles)),
    ]


def first_kernel(tile, depth, places, slots, placement_ref, tenant_ref, weight_ref, *refs):
    count = len(places)
    features = refs[:count]
    out_ref, stored_ref, held_ref, rows_ref, sems = refs[count:]
    start_tiles(tile, depth, places, features, weight_ref, held_ref, rows_ref, sems)
    out_ref[...] = jnp.zeros_like(out_ref)
    stored = jnp.zeros(stored_ref.shape, jnp.int32)
    for slot in range(slots):
        stored = jnp.where(tenant_ref[...] == slot, placement_ref[slot], stored)
    stored_ref[...] = stored
    add_tiles(held_ref, rows_ref, sems, out_ref)


def products_kernel(tile, depth, places, weight_ref, *refs):
    count = len(places)
    features, given = refs[:count], refs[count]
    out_ref, held_ref, rows_ref, sems = refs[count + 1 :]
    start_tiles(tile, depth, places, features, weight_ref, held_ref, rows_ref, sems)
    out_ref[...] = given[...]
    add_tiles(held_ref, rows_ref, sems, out_ref)


def owners_of(flips, pairs):
    group, part = lax.axis_index("adapter"), lax.axis_index("parts")
    owners = [group] + [group ^ flip for flip in flips]
    for near, far in pairs:
        owners += [group ^ (near + part * (far - near)), group ^ (far + part * (near - far))]
    return owners


def last_kernel(tile, depth, places, flips, pairs, slots, weight_ref, *refs):
    count = len(places)
    features = refs[:count]
    given, stored_ref, sum_ref, more_ref = refs[count : count + 4]
    ups = refs[count + 4 : count + 4 + slots]
    (
        out_ref, total_ref, sums_ref, received_ref, stacked_ref, held_ref, rows_ref, sems, small_sems,
    ) = refs[count + 4 + slots :]
    rank = ups[0].shape[0]
    copies = [(sum_ref, sums_ref), (more_ref, received_ref)]
    copies += [(up, stacked_ref.at[pl.ds(b * rank, rank)]) for b, up in enumerate(ups)]
    copies = [
        pltpu.make_async_copy(source, target, small_sems.at[i])
        for i, (source, target) in enumerate(copies)
    ]
    for copy in copies:
        copy.start()
    start_tiles(tile, depth, places, features, weight_ref, held_ref, rows_ref, sems)
    total_ref[...] = given[...]
    add_tiles(held_ref, rows_ref, sems, total_ref)
    for copy in copies:
        copy.wait()
    shrunk = (sums_ref[...] + received_ref[...].astype(jnp.float32)).astype(jnp.bfloat16).astype(jnp.float32)
    spread = jnp.concatenate(
        [jnp.where(stored_ref[...] == owner, shrunk, 0.0) for owner in owners_of(flips, pairs)], axis=0
    )
    expanded = jnp.dot(
        spread.T.astype(jnp.bfloat16), stacked_ref[...], preferred_element_type=jnp.float32
    )
    expanded = expanded.astype(jnp.bfloat16).astype(jnp.float32)
    out_ref[...] = (total_ref[...] + LOWRANK_SCALE * expanded).astype(out_ref.dtype)


def shrink_kernel(tile, flips, pairs, slots, tokens_ref, stored_ref, *refs):
    downs, out_ref, held_ref, down_ref, sums_ref, sems = (
        refs[:slots], refs[slots], *refs[slots + 1 :]
    )
    rank = downs[0].shape[0]
    tiles = tokens_ref.shape[1] // tile
    for k in range(tiles):
        here = pl.ds(k * tile, tile)
        pltpu.make_async_copy(tokens_ref.at[:, here], held_ref.at[k], sems.at[0, k]).start()
        for b, down in enumerate(downs):
            pltpu.make_async_copy(
                down.at[:, here], down_ref.at[k, pl.ds(b * rank, rank)], sems.at[1 + b, k]
            ).start()
    sums_ref[...] = jnp.zeros_like(sums_ref)

    @pl.loop(0, tiles)
    def _(k):
        pltpu.make_async_copy(held_ref.at[k], held_ref.at[k], sems.at[0, k]).wait()
        for b in range(slots):
            block = down_ref.at[k, pl.ds(b * rank, rank)]
            pltpu.make_async_copy(block, block, sems.at[1 + b, k]).wait()
        sums_ref[...] += lax.dot_general(
            held_ref[k], down_ref[k], (((1,), (1,)), ((), ())), preferred_element_type=jnp.float32
        )

    sums = sums_ref[...].T
    total = jnp.zeros(out_ref.shape, jnp.float32)
    for b, owner in enumerate(owners_of(flips, pairs)):
        total += jnp.where(stored_ref[...] == owner, sums[b * rank : (b + 1) * rank], 0.0)
    out_ref[...] = total


def body(
    tokens, tenant, placement, frozen_projection_weight, lowrank_down_weight, lowrank_up_weight
):
    rows, depth = tokens.shape
    slots = placement.shape[0]
    tensors = lax.axis_size("tensor")
    groups = lax.axis_size("adapter")
    parts = lax.axis_size("parts")
    me = lax.axis_index("tensor")
    rank, columns = lowrank_up_weight.shape[1:]
    edges = [0] + [int(depth * cut) // LANES * LANES for cut in CUTS] + [depth]
    tile = math.gcd(*edges)

    down = lowrank_down_weight[0].T
    by_copies = down.shape[0] % 16 == 0
    cuts, steps = len(edges) - 1, 6
    if by_copies:
        made = call(
            functools.partial(cut_kernel, edges),
            [jax.ShapeDtypeStruct((rows, b - a), tokens.dtype) for a, b in zip(edges, edges[1:])]
            + [jax.ShapeDtypeStruct((down.shape[0], depth), down.dtype)] * (tensors - 1),
            [ANYWHERE] * 2,
            [
                pltpu.VMEM((steps, rows // steps, depth), tokens.dtype),
                pltpu.VMEM((tensors - 1, down.shape[0], depth), down.dtype),
                pltpu.SemaphoreType.DMA((1 + cuts, steps)),
                pltpu.SemaphoreType.DMA((2, tensors - 1)),
            ],
            [ANYWHERE] * (cuts + tensors - 1),
            cost=FREE,
            mib=56,
        )(tokens, down)
        chunks, pieces = list(made[:cuts]), list(made[cuts:])
    else:
        chunks = [tokens[:, a:b] for a, b in zip(edges, edges[1:])]
        pieces = [
            lax.dynamic_slice_in_dim(down, (me ^ flip) * depth, depth, axis=1)
            for flip in range(1, tensors)
        ]
    pieces = [flipped(piece, "tensor", i + 1) for i, piece in enumerate(pieces)]
    pieces[0], here = chained(pieces[0], tokens)
    neighbour = flipped(here, "tensor", 1)
    if by_copies:
        own = call(
            order_kernel,
            jax.ShapeDtypeStruct((rank, depth), down.dtype),
            [ANYWHERE] * tensors,
            [pltpu.SemaphoreType.DMA((tensors,))],
            VECTOR,
            cost=FREE,
        )(down, *pieces)
    else:
        pieces = [lax.dynamic_slice_in_dim(down, me * depth, depth, axis=1)] + pieces
        none = jnp.zeros((), down.dtype)
        own = jnp.concatenate(
            [sum(jnp.where((me ^ f) == j, pieces[f], none) for f in range(tensors)) for j in range(tensors)],
            axis=0,
        )

    hops = range(CORES, tensors, CORES)

    def send(m):
        return [flipped(chunks[m], "tensor", hop) for hop in hops]

    far = [send(0)]

    def across(m):
        return [flipped(value, "tensor", 1) for value in far[m]]

    def far_places(m):
        return [(hop, edges[m], 0, edges[m + 1] - edges[m]) for hop in hops]

    def near_places(m):
        return [(hop ^ 1, edges[m], 0, edges[m + 1] - edges[m]) for hop in hops]

    def products(places, features, total):
        return call(
            functools.partial(products_kernel, tile, depth, places),
            jax.ShapeDtypeStruct((rows, columns), jnp.float32),
            [ANYWHERE] + [ANYWHERE] * len(features) + [VECTOR],
            tile_scratch(tile, rows, places, columns),
        )(frozen_projection_weight, *features, total)

    flips = list(range(1, groups))
    pairs = []
    if parts == 2:
        while len(flips) > 1:
            pairs.append((flips.pop(-2), flips.pop(-1)))
    routes = [
        [(p * groups + z, p * groups + (z ^ pair[p])) for p in range(parts) for z in range(groups)]
        for pair in pairs
    ]

    def fetch_far(value):
        return [lax.ppermute(value, ("parts", "adapter"), route) for route in routes]

    def fetch_near(value):
        return [flipped(value, "adapter", flip) for flip in flips]

    def swap(values):
        return [flipped(value, "parts", 1) for value in values]

    own, here = chained(own, tokens)
    fetched = fetch_far(own)
    places = [(0, 0, 0, depth // 2)]
    total, stored = call(
        functools.partial(first_kernel, tile, depth, places, slots),
        [
            jax.ShapeDtypeStruct((rows, columns), jnp.float32),
            jax.ShapeDtypeStruct((1, rows), jnp.int32),
        ],
        [SCALAR, VECTOR, ANYWHERE, ANYWHERE],
        tile_scratch(tile, rows, places, columns),
        [VECTOR, VECTOR],
    )(placement, tenant.reshape(1, rows), frozen_projection_weight, here)
    total, own, up, neighbour, chunks[1] = chained(
        total, own, lowrank_up_weight[0], neighbour, chunks[1]
    )
    far.append(send(1))
    single, single_up = fetch_near(own), fetch_near(up)
    total = products([(0, depth // 2, depth // 2, depth // 2)], [here], total)
    fetched, single_up, total = chained(fetched, single_up, total)
    swapped = swap(fetched)
    total, neighbour = chained(total, neighbour)
    total = products([(1, 0, 0, depth)], [neighbour], total)
    total, up = chained(total, up)
    fetched_up = fetch_far(up)
    single, swapped, total = chained(single, swapped, total)
    downs = [own] + single
    for pair in zip(fetched, swapped):
        downs += pair

    tiles = depth // tile
    partial = call(
        functools.partial(shrink_kernel, tile, flips, pairs, slots),
        jax.ShapeDtypeStruct((rank, rows), jnp.float32),
        [ANYWHERE, VECTOR] + [ANYWHERE] * slots,
        [
            pltpu.VMEM((tiles, rows, tile), jnp.bfloat16),
            pltpu.VMEM((tiles, slots * rank, tile), jnp.bfloat16),
            pltpu.VMEM((rows, slots * rank), jnp.float32),
            pltpu.SemaphoreType.DMA((1 + slots, tiles)),
        ],
    )(tokens, stored, *downs)
    far[0], fetched_up, partial = chained(far[0], fetched_up, partial)
    swapped_up = swap(fetched_up)
    ups = [up] + single_up
    for pair in zip(fetched_up, swapped_up):
        ups += pair
    near = across(0)
    total = products(far_places(0), far[0], total)
    flip = 1
    while flip < tensors // 2:
        received = flipped(partial, "tensor", flip)
        if flip == 1:
            received, total = chained(received, total)
        partial += received
        flip *= 2
    more = flipped(partial.astype(jnp.bfloat16), "tensor", flip)
    total, partial = chained(total, partial)
    total = products(near_places(0), near, total)
    far[1], ups, total = chained(far[1], ups, total)
    near = across(1)
    total = products(far_places(1), far[1], total)
    near, more, total = chained(near, more, total)

    places = near_places(1)
    return call(
        functools.partial(last_kernel, tile, depth, places, flips, pairs, slots),
        jax.ShapeDtypeStruct((rows, columns), jnp.bfloat16),
        [ANYWHERE] + [ANYWHERE] * len(near) + [VECTOR] * 2 + [ANYWHERE] * (2 + slots),
        [
            pltpu.VMEM((rows, columns), jnp.float32),
            pltpu.VMEM((rank, rows), jnp.float32),
            pltpu.VMEM((rank, rows), jnp.bfloat16),
            pltpu.VMEM((slots * rank, columns), jnp.bfloat16),
        ]
        + tile_scratch(tile, rows, places, columns)
        + [pltpu.SemaphoreType.DMA((2 + slots,))],
    )(frozen_projection_weight, *near, total, stored, partial, more, *ups)


def solution(mesh):
    placed = (
        P(("parts", "adapter"), "tensor"),
        P(("parts", "adapter"), None),
        P(),
        P(None, "tensor"),
        P("adapter", None, "tensor"),
        P("adapter", None, "tensor"),
    )
    return jax.shard_map(
        body,
        mesh=mesh,
        in_specs=placed,
        out_specs=P(("parts", "adapter"), "tensor"),
        check_vma=False,
    )
```

```python
import functools
import math

import jax
import jax.numpy as jnp
from jax import lax
from jax.experimental import pallas as pl
from jax.experimental.pallas import tpu as pltpu
from jax.sharding import PartitionSpec as P

LOWRANK_SCALE = 2.0
CORES = 2
LANES = 128
CUTS = (0.75,)
MIB = 1024 * 1024
FREE = pl.CostEstimate(flops=0, bytes_accessed=0, transcendentals=0)
LONG = pl.CostEstimate(flops=10**11, bytes_accessed=0, transcendentals=0)
ANYWHERE = pl.BlockSpec(memory_space=pl.ANY)
VECTOR = pl.BlockSpec(memory_space=pltpu.VMEM)
SCALAR = pl.BlockSpec(memory_space=pltpu.SMEM)


def flipped(value, axis, flip):
    count = lax.axis_size(axis)
    return lax.ppermute(value, axis, [(i, i ^ flip) for i in range(count)])


def chained(*values):
    return lax.optimization_barrier(values)


def call(kernel, out_shape, in_specs, scratch, out_specs=VECTOR, cost=LONG, mib=24):
    return pl.pallas_call(
        kernel,
        out_shape=out_shape,
        in_specs=in_specs,
        out_specs=out_specs,
        scratch_shapes=scratch,
        cost_estimate=cost,
        compiler_params=pltpu.CompilerParams(vmem_limit_bytes=mib * MIB),
    )


def run_copies(pairs, sems):
    copies = [
        pltpu.make_async_copy(source, target, sems.at[i]) for i, (source, target) in enumerate(pairs)
    ]
    for copy in copies:
        copy.start()
    for copy in copies:
        copy.wait()


def cut_kernel(edges, source_ref, *refs):
    outs, (held_ref, sems) = refs[:-2], refs[-2:]
    steps, rows = held_ref.shape[:2]
    copies = [
        pltpu.make_async_copy(source_ref.at[pl.ds(i * rows, rows)], held_ref.at[i], sems.at[0, i])
        for i in range(steps)
    ]
    for copy in copies:
        copy.start()
    leaving = []
    for i in range(steps):
        copies[i].wait()
        for m, (a, b, out) in enumerate(zip(edges, edges[1:], outs)):
            leaving.append(
                pltpu.make_async_copy(
                    held_ref.at[i, :, pl.ds(a, b - a)],
                    out.at[pl.ds(i * rows, rows)],
                    sems.at[1 + m, i],
                )
            )
            leaving[-1].start()
    for copy in leaving:
        copy.wait()


def order_kernel(rank_part, *refs):
    pieces, out_ref, sems = refs[:-2], refs[-2], refs[-1]
    me = lax.axis_index("tensor")
    run_copies(
        [
            (piece, out_ref.at[pl.ds(pl.multiple_of((me ^ f) * rank_part, rank_part), rank_part)])
            for f, piece in enumerate(pieces)
        ],
        sems,
    )


def start_tiles(tile, depth, places, features, weight_ref, held_ref, rows_ref, sems):
    me, t = lax.axis_index("tensor"), 0
    for (flip, first, skip, width), part in zip(places, features):
        for k in range(0, width, tile):
            start = pl.multiple_of((me ^ flip) * depth + first + k, LANES)
            pltpu.make_async_copy(
                weight_ref.at[pl.ds(start, tile)], rows_ref.at[t], sems.at[1, t]
            ).start()
            pltpu.make_async_copy(part.at[:, pl.ds(skip + k, tile)], held_ref.at[t], sems.at[0, t]).start()
            t += 1


def add_tiles(held_ref, rows_ref, sems, total_ref):
    @pl.loop(0, held_ref.shape[0])
    def _(t):
        pltpu.make_async_copy(held_ref.at[t], held_ref.at[t], sems.at[0, t]).wait()
        pltpu.make_async_copy(rows_ref.at[t], rows_ref.at[t], sems.at[1, t]).wait()
        total_ref[...] += jnp.dot(held_ref[t], rows_ref[t], preferred_element_type=jnp.float32)


def tile_scratch(tile, rows, places, columns):
    tiles = sum(place[3] for place in places) // tile
    return [
        pltpu.VMEM((tiles, rows, tile), jnp.bfloat16),
        pltpu.VMEM((tiles, tile, columns), jnp.bfloat16),
        pltpu.SemaphoreType.DMA((2, tiles)),
    ]


def first_kernel(tile, depth, places, slots, placement_ref, tenant_ref, weight_ref, *refs):
    count = len(places)
    features = refs[:count]
    out_ref, stored_ref, held_ref, rows_ref, sems = refs[count:]
    start_tiles(tile, depth, places, features, weight_ref, held_ref, rows_ref, sems)
    out_ref[...] = jnp.zeros_like(out_ref)
    stored = jnp.zeros(stored_ref.shape, jnp.int32)
    for slot in range(slots):
        stored = jnp.where(tenant_ref[...] == slot, placement_ref[slot], stored)
    stored_ref[...] = stored
    add_tiles(held_ref, rows_ref, sems, out_ref)


def products_kernel(tile, depth, places, weight_ref, *refs):
    count = len(places)
    features, given = refs[:count], refs[count]
    out_ref, held_ref, rows_ref, sems = refs[count + 1 :]
    start_tiles(tile, depth, places, features, weight_ref, held_ref, rows_ref, sems)
    out_ref[...] = given[...]
    add_tiles(held_ref, rows_ref, sems, out_ref)


def owners_of(flips, pairs):
    group, part = lax.axis_index("adapter"), lax.axis_index("parts")
    owners = [group] + [group ^ flip for flip in flips]
    for near, far in pairs:
        owners += [group ^ (near + part * (far - near)), group ^ (far + part * (near - far))]
    return owners


def last_kernel(tile, depth, places, flips, pairs, slots, weight_ref, *refs):
    count = len(places)
    features = refs[:count]
    given, stored_ref, sum_ref, more_ref = refs[count : count + 4]
    ups = refs[count + 4 : count + 4 + slots]
    (
        out_ref, total_ref, sums_ref, received_ref, stacked_ref, held_ref, rows_ref, sems, small_sems,
    ) = refs[count + 4 + slots :]
    rank = ups[0].shape[0]
    copies = [(sum_ref, sums_ref), (more_ref, received_ref)]
    copies += [(up, stacked_ref.at[pl.ds(b * rank, rank)]) for b, up in enumerate(ups)]
    copies = [
        pltpu.make_async_copy(source, target, small_sems.at[i])
        for i, (source, target) in enumerate(copies)
    ]
    for copy in copies:
        copy.start()
    start_tiles(tile, depth, places, features, weight_ref, held_ref, rows_ref, sems)
    total_ref[...] = given[...]
    add_tiles(held_ref, rows_ref, sems, total_ref)
    for copy in copies:
        copy.wait()
    shrunk = (sums_ref[...] + received_ref[...].astype(jnp.float32)).astype(jnp.bfloat16).astype(jnp.float32)
    spread = jnp.concatenate(
        [jnp.where(stored_ref[...] == owner, shrunk, 0.0) for owner in owners_of(flips, pairs)], axis=0
    )
    expanded = jnp.dot(
        spread.T.astype(jnp.bfloat16), stacked_ref[...], preferred_element_type=jnp.float32
    )
    expanded = expanded.astype(jnp.bfloat16).astype(jnp.float32)
    out_ref[...] = (total_ref[...] + LOWRANK_SCALE * expanded).astype(out_ref.dtype)


def shrink_kernel(tile, flips, pairs, slots, tokens_ref, stored_ref, *refs):
    downs, out_ref, held_ref, down_ref, sums_ref, sems = (
        refs[:slots], refs[slots], *refs[slots + 1 :]
    )
    rank = downs[0].shape[0]
    tiles = tokens_ref.shape[1] // tile
    for k in range(tiles):
        here = pl.ds(k * tile, tile)
        pltpu.make_async_copy(tokens_ref.at[:, here], held_ref.at[k], sems.at[0, k]).start()
        for b, down in enumerate(downs):
            pltpu.make_async_copy(
                down.at[:, here], down_ref.at[k, pl.ds(b * rank, rank)], sems.at[1 + b, k]
            ).start()
    sums_ref[...] = jnp.zeros_like(sums_ref)

    @pl.loop(0, tiles)
    def _(k):
        pltpu.make_async_copy(held_ref.at[k], held_ref.at[k], sems.at[0, k]).wait()
        for b in range(slots):
            block = down_ref.at[k, pl.ds(b * rank, rank)]
            pltpu.make_async_copy(block, block, sems.at[1 + b, k]).wait()
        sums_ref[...] += lax.dot_general(
            held_ref[k], down_ref[k], (((1,), (1,)), ((), ())), preferred_element_type=jnp.float32
        )

    sums = sums_ref[...].T
    total = jnp.zeros(out_ref.shape, jnp.float32)
    for b, owner in enumerate(owners_of(flips, pairs)):
        total += jnp.where(stored_ref[...] == owner, sums[b * rank : (b + 1) * rank], 0.0)
    out_ref[...] = total


def body(
    tokens, tenant, placement, frozen_projection_weight, lowrank_down_weight, lowrank_up_weight
):
    rows, depth = tokens.shape
    slots = placement.shape[0]
    tensors = lax.axis_size("tensor")
    groups = lax.axis_size("adapter")
    parts = lax.axis_size("parts")
    me = lax.axis_index("tensor")
    rank, columns = lowrank_up_weight.shape[1:]
    edges = [0] + [int(depth * cut) // LANES * LANES for cut in CUTS] + [depth]
    tile = math.gcd(*edges)

    down = lowrank_down_weight[0].T
    pieces = [
        lax.dynamic_slice_in_dim(down, (me ^ flip) * depth, depth, axis=1)
        for flip in range(tensors)
    ]
    uncut, pieces = chained(tokens, pieces)
    steps = 6
    chunks = list(
        call(
            functools.partial(cut_kernel, edges),
            [jax.ShapeDtypeStruct((rows, b - a), tokens.dtype) for a, b in zip(edges, edges[1:])],
            [ANYWHERE],
            [
                pltpu.VMEM((steps, rows // steps, depth), tokens.dtype),
                pltpu.SemaphoreType.DMA((len(edges), steps)),
            ],
            [ANYWHERE] * (len(edges) - 1),
            cost=FREE,
            mib=56,
        )(uncut)
    )
    pieces = [pieces[0]] + [flipped(pieces[f], "tensor", f) for f in range(1, tensors)]
    pieces[1], here = chained(pieces[1], tokens)
    neighbour = flipped(here, "tensor", 1)
    if down.shape[0] % 16 == 0:
        own = call(
            functools.partial(order_kernel, down.shape[0]),
            jax.ShapeDtypeStruct((rank, depth), down.dtype),
            [ANYWHERE] * tensors,
            [pltpu.SemaphoreType.DMA((tensors,))],
            ANYWHERE,
            cost=FREE,
        )(*pieces)
    else:
        none = jnp.zeros((), down.dtype)
        own = jnp.concatenate(
            [sum(jnp.where((me ^ f) == j, pieces[f], none) for f in range(tensors)) for j in range(tensors)],
            axis=0,
        )

    hops = range(CORES, tensors, CORES)

    def send(m):
        return [flipped(chunks[m], "tensor", hop) for hop in hops]

    far = [send(0)]

    def across(m):
        return [flipped(value, "tensor", 1) for value in far[m]]

    def far_places(m):
        return [(hop, edges[m], 0, edges[m + 1] - edges[m]) for hop in hops]

    def near_places(m):
        return [(hop ^ 1, edges[m], 0, edges[m + 1] - edges[m]) for hop in hops]

    def products(places, features, total):
        return call(
            functools.partial(products_kernel, tile, depth, places),
            jax.ShapeDtypeStruct((rows, columns), jnp.float32),
            [ANYWHERE] + [ANYWHERE] * len(features) + [VECTOR],
            tile_scratch(tile, rows, places, columns),
        )(frozen_projection_weight, *features, total)

    flips = list(range(1, groups))
    pairs = []
    if parts == 2:
        while len(flips) > 1:
            pairs.append((flips.pop(-2), flips.pop(-1)))
    routes = [
        [(p * groups + z, p * groups + (z ^ pair[p])) for p in range(parts) for z in range(groups)]
        for pair in pairs
    ]

    def fetch_far(value):
        return [lax.ppermute(value, ("parts", "adapter"), route) for route in routes]

    def fetch_near(value):
        return [flipped(value, "adapter", flip) for flip in flips]

    def swap(values):
        return [flipped(value, "parts", 1) for value in values]

    own, here = chained(own, tokens)
    fetched = fetch_far(own)
    places = [(0, 0, 0, depth // 2)]
    total, stored = call(
        functools.partial(first_kernel, tile, depth, places, slots),
        [
            jax.ShapeDtypeStruct((rows, columns), jnp.float32),
            jax.ShapeDtypeStruct((1, rows), jnp.int32),
        ],
        [SCALAR, VECTOR, ANYWHERE, ANYWHERE],
        tile_scratch(tile, rows, places, columns),
        [VECTOR, VECTOR],
    )(placement, tenant.reshape(1, rows), frozen_projection_weight, here)
    total, own, up, neighbour, chunks[1] = chained(
        total, own, lowrank_up_weight[0], neighbour, chunks[1]
    )
    far.append(send(1))
    single, single_up = fetch_near(own), fetch_near(up)
    total = products([(0, depth // 2, depth // 2, depth // 2)], [here], total)
    fetched, single_up, total = chained(fetched, single_up, total)
    swapped = swap(fetched)
    total, neighbour = chained(total, neighbour)
    total = products([(1, 0, 0, depth)], [neighbour], total)
    total, up = chained(total, up)
    fetched_up = fetch_far(up)
    single, swapped, total = chained(single, swapped, total)
    downs = [own] + single
    for pair in zip(fetched, swapped):
        downs += pair

    tiles = depth // tile
    partial = call(
        functools.partial(shrink_kernel, tile, flips, pairs, slots),
        jax.ShapeDtypeStruct((rank, rows), jnp.float32),
        [ANYWHERE, VECTOR] + [ANYWHERE] * slots,
        [
            pltpu.VMEM((tiles, rows, tile), jnp.bfloat16),
            pltpu.VMEM((tiles, slots * rank, tile), jnp.bfloat16),
            pltpu.VMEM((rows, slots * rank), jnp.float32),
            pltpu.SemaphoreType.DMA((1 + slots, tiles)),
        ],
    )(tokens, stored, *downs)
    far[0], fetched_up, partial = chained(far[0], fetched_up, partial)
    swapped_up = swap(fetched_up)
    ups = [up] + single_up
    for pair in zip(fetched_up, swapped_up):
        ups += pair
    near = across(0)
    total = products(far_places(0), far[0], total)
    flip = 1
    while flip < tensors // 2:
        received = flipped(partial, "tensor", flip)
        if flip == 1:
            received, total = chained(received, total)
        partial += received
        flip *= 2
    more = flipped(partial.astype(jnp.bfloat16), "tensor", flip)
    total, partial = chained(total, partial)
    total = products(near_places(0), near, total)
    far[1], ups, total = chained(far[1], ups, total)
    near = across(1)
    total = products(far_places(1), far[1], total)
    near, more, total = chained(near, more, total)

    places = near_places(1)
    return call(
        functools.partial(last_kernel, tile, depth, places, flips, pairs, slots),
        jax.ShapeDtypeStruct((rows, columns), jnp.bfloat16),
        [ANYWHERE] + [ANYWHERE] * len(near) + [VECTOR] * 2 + [ANYWHERE] * (2 + slots),
        [
            pltpu.VMEM((rows, columns), jnp.float32),
            pltpu.VMEM((rank, rows), jnp.float32),
            pltpu.VMEM((rank, rows), jnp.bfloat16),
            pltpu.VMEM((slots * rank, columns), jnp.bfloat16),
        ]
        + tile_scratch(tile, rows, places, columns)
        + [pltpu.SemaphoreType.DMA((2 + slots,))],
    )(frozen_projection_weight, *near, total, stored, partial, more, *ups)


def solution(mesh):
    placed = (
        P(("parts", "adapter"), "tensor"),
        P(("parts", "adapter"), None),
        P(),
        P(None, "tensor"),
        P("adapter", None, "tensor"),
        P("adapter", None, "tensor"),
    )
    return jax.shard_map(
        body,
        mesh=mesh,
        in_specs=placed,
        out_specs=P(("parts", "adapter"), "tensor"),
        check_vma=False,
    )
```

```python
import functools
import math

import jax
import jax.numpy as jnp
from jax import lax
from jax.experimental import pallas as pl
from jax.experimental.pallas import tpu as pltpu
from jax.sharding import PartitionSpec as P

LOWRANK_SCALE = 2.0
CORES = 2
LANES = 128
FIRST = ((1, 3, 0, 2), (1, 2, 3, 0))
SECOND = ((2, 0, 3, 1), (3, 0, 1, 2))
CUTS = (0.75,)
MIB = 1024 * 1024
FREE = pl.CostEstimate(flops=0, bytes_accessed=0, transcendentals=0)
LONG = pl.CostEstimate(flops=10**11, bytes_accessed=0, transcendentals=0)
ANYWHERE = pl.BlockSpec(memory_space=pl.ANY)
VECTOR = pl.BlockSpec(memory_space=pltpu.VMEM)
SCALAR = pl.BlockSpec(memory_space=pltpu.SMEM)


def flipped(value, axis, flip):
    count = lax.axis_size(axis)
    return lax.ppermute(value, axis, [(i, i ^ flip) for i in range(count)])


def chained(*values):
    return lax.optimization_barrier(values)


def call(kernel, out_shape, in_specs, scratch, out_specs=VECTOR, cost=LONG, mib=24):
    return pl.pallas_call(
        kernel,
        out_shape=out_shape,
        in_specs=in_specs,
        out_specs=out_specs,
        scratch_shapes=scratch,
        cost_estimate=cost,
        compiler_params=pltpu.CompilerParams(vmem_limit_bytes=mib * MIB),
    )


def run_copies(pairs, sems):
    copies = [
        pltpu.make_async_copy(source, target, sems.at[i]) for i, (source, target) in enumerate(pairs)
    ]
    for copy in copies:
        copy.start()
    for copy in copies:
        copy.wait()


def cut_kernel(edges, source_ref, *refs):
    outs, (held_ref, sems) = refs[:-2], refs[-2:]
    steps, rows = held_ref.shape[:2]
    copies = [
        pltpu.make_async_copy(source_ref.at[pl.ds(i * rows, rows)], held_ref.at[i], sems.at[0, i])
        for i in range(steps)
    ]
    for copy in copies:
        copy.start()
    leaving = []
    for i in range(steps):
        copies[i].wait()
        for m, (a, b, out) in enumerate(zip(edges, edges[1:], outs)):
            leaving.append(
                pltpu.make_async_copy(
                    held_ref.at[i, :, pl.ds(a, b - a)],
                    out.at[pl.ds(i * rows, rows)],
                    sems.at[1 + m, i],
                )
            )
            leaving[-1].start()
    for copy in leaving:
        copy.wait()


def order_kernel(rank_part, *refs):
    pieces, out_ref, sems = refs[:-2], refs[-2], refs[-1]
    me = lax.axis_index("tensor")
    run_copies(
        [
            (piece, out_ref.at[pl.ds(pl.multiple_of((me ^ f) * rank_part, rank_part), rank_part)])
            for f, piece in enumerate(pieces)
        ],
        sems,
    )


def start_tiles(tile, depth, places, features, weight_ref, held_ref, rows_ref, sems):
    me, t = lax.axis_index("tensor"), 0
    for (flip, first, skip, width), part in zip(places, features):
        for k in range(0, width, tile):
            start = pl.multiple_of((me ^ flip) * depth + first + k, LANES)
            pltpu.make_async_copy(
                weight_ref.at[pl.ds(start, tile)], rows_ref.at[t], sems.at[1, t]
            ).start()
            pltpu.make_async_copy(part.at[:, pl.ds(skip + k, tile)], held_ref.at[t], sems.at[0, t]).start()
            t += 1


def add_tiles(held_ref, rows_ref, sems, total_ref):
    @pl.loop(0, held_ref.shape[0])
    def _(t):
        pltpu.make_async_copy(held_ref.at[t], held_ref.at[t], sems.at[0, t]).wait()
        pltpu.make_async_copy(rows_ref.at[t], rows_ref.at[t], sems.at[1, t]).wait()
        total_ref[...] += jnp.dot(held_ref[t], rows_ref[t], preferred_element_type=jnp.float32)


def tile_scratch(tile, rows, places, columns):
    tiles = sum(place[3] for place in places) // tile
    return [
        pltpu.VMEM((tiles, rows, tile), jnp.bfloat16),
        pltpu.VMEM((tiles, tile, columns), jnp.bfloat16),
        pltpu.SemaphoreType.DMA((2, tiles)),
    ]


def first_kernel(tile, depth, places, slots, placement_ref, tenant_ref, weight_ref, *refs):
    count = len(places)
    features = refs[:count]
    out_ref, stored_ref, held_ref, rows_ref, sems = refs[count:]
    start_tiles(tile, depth, places, features, weight_ref, held_ref, rows_ref, sems)
    out_ref[...] = jnp.zeros_like(out_ref)
    stored = jnp.zeros(stored_ref.shape, jnp.int32)
    for slot in range(slots):
        stored = jnp.where(tenant_ref[...] == slot, placement_ref[slot], stored)
    stored_ref[...] = stored
    add_tiles(held_ref, rows_ref, sems, out_ref)


def products_kernel(tile, depth, places, weight_ref, *refs):
    count = len(places)
    features, given = refs[:count], refs[count]
    out_ref, held_ref, rows_ref, sems = refs[count + 1 :]
    start_tiles(tile, depth, places, features, weight_ref, held_ref, rows_ref, sems)
    out_ref[...] = given[...]
    add_tiles(held_ref, rows_ref, sems, out_ref)


def is_mixed(groups, parts):
    return groups == 4 and parts == 2


def source(group, part, table):
    found = 0
    for p, targets in enumerate(table):
        for z, target in enumerate(targets):
            found = found + jnp.where((part == p) & (group == target), z, 0)
    return found


def owners_of(groups, mixed):
    group = lax.axis_index("adapter")
    if not mixed:
        return [group ^ flip for flip in range(groups)]
    part = lax.axis_index("parts")
    return [group, source(group, part, FIRST), source(group, part, SECOND), group ^ (3 - part)]


def last_kernel(tile, depth, places, slots, weight_ref, *refs):
    count = len(places)
    features = refs[:count]
    given, stored_ref, sum_ref, more_ref = refs[count : count + 4]
    ups = refs[count + 4 : count + 4 + slots]
    (
        out_ref, total_ref, sums_ref, received_ref, stacked_ref, held_ref, rows_ref, sems, small_sems,
    ) = refs[count + 4 + slots :]
    rank = ups[0].shape[0]
    copies = [(sum_ref, sums_ref), (more_ref, received_ref)]
    copies += [(up, stacked_ref.at[pl.ds(b * rank, rank)]) for b, up in enumerate(ups)]
    copies = [
        pltpu.make_async_copy(source, target, small_sems.at[i])
        for i, (source, target) in enumerate(copies)
    ]
    for copy in copies:
        copy.start()
    start_tiles(tile, depth, places, features, weight_ref, held_ref, rows_ref, sems)
    total_ref[...] = given[...]
    add_tiles(held_ref, rows_ref, sems, total_ref)
    for copy in copies:
        copy.wait()
    shrunk = (sums_ref[...] + received_ref[...].astype(jnp.float32)).astype(jnp.bfloat16).astype(jnp.float32)
    spread = jnp.concatenate(
        [jnp.where(stored_ref[...] == owner, shrunk, 0.0) for owner in owners_of(slots, False)], axis=0
    )
    expanded = jnp.dot(
        spread.T.astype(jnp.bfloat16), stacked_ref[...], preferred_element_type=jnp.float32
    )
    expanded = expanded.astype(jnp.bfloat16).astype(jnp.float32)
    out_ref[...] = (total_ref[...] + LOWRANK_SCALE * expanded).astype(out_ref.dtype)


def shrink_kernel(tile, mixed, slots, tokens_ref, stored_ref, *refs):
    downs, out_ref, held_ref, down_ref, sums_ref, sems = (
        refs[:slots], refs[slots], *refs[slots + 1 :]
    )
    rank = downs[0].shape[0]
    tiles = tokens_ref.shape[1] // tile
    for k in range(tiles):
        here = pl.ds(k * tile, tile)
        pltpu.make_async_copy(tokens_ref.at[:, here], held_ref.at[k], sems.at[0, k]).start()
        for b, down in enumerate(downs):
            pltpu.make_async_copy(
                down.at[:, here], down_ref.at[k, pl.ds(b * rank, rank)], sems.at[1 + b, k]
            ).start()
    sums_ref[...] = jnp.zeros_like(sums_ref)

    @pl.loop(0, tiles)
    def _(k):
        pltpu.make_async_copy(held_ref.at[k], held_ref.at[k], sems.at[0, k]).wait()
        for b in range(slots):
            block = down_ref.at[k, pl.ds(b * rank, rank)]
            pltpu.make_async_copy(block, block, sems.at[1 + b, k]).wait()
        sums_ref[...] += lax.dot_general(
            held_ref[k], down_ref[k], (((1,), (1,)), ((), ())), preferred_element_type=jnp.float32
        )

    sums = sums_ref[...].T
    total = jnp.zeros(out_ref.shape, jnp.float32)
    for b, owner in enumerate(owners_of(slots, mixed)):
        total += jnp.where(stored_ref[...] == owner, sums[b * rank : (b + 1) * rank], 0.0)
    out_ref[...] = total


def body(
    tokens, tenant, placement, frozen_projection_weight, lowrank_down_weight, lowrank_up_weight
):
    rows, depth = tokens.shape
    slots = placement.shape[0]
    tensors = lax.axis_size("tensor")
    groups = lax.axis_size("adapter")
    parts = lax.axis_size("parts")
    me = lax.axis_index("tensor")
    rank, columns = lowrank_up_weight.shape[1:]
    edges = [0] + [int(depth * cut) // LANES * LANES for cut in CUTS] + [depth]
    tile = math.gcd(*edges)

    down = lowrank_down_weight[0].T
    pieces = [
        lax.dynamic_slice_in_dim(down, (me ^ flip) * depth, depth, axis=1)
        for flip in range(tensors)
    ]
    uncut, pieces = chained(tokens, pieces)
    steps = 6
    chunks = list(
        call(
            functools.partial(cut_kernel, edges),
            [jax.ShapeDtypeStruct((rows, b - a), tokens.dtype) for a, b in zip(edges, edges[1:])],
            [ANYWHERE],
            [
                pltpu.VMEM((steps, rows // steps, depth), tokens.dtype),
                pltpu.SemaphoreType.DMA((len(edges), steps)),
            ],
            [ANYWHERE] * (len(edges) - 1),
            cost=FREE,
            mib=56,
        )(uncut)
    )
    pieces = [pieces[0]] + [flipped(pieces[f], "tensor", f) for f in range(1, tensors)]
    pieces[1], here = chained(pieces[1], tokens)
    neighbour = flipped(here, "tensor", 1)
    if down.shape[0] % 16 == 0:
        own = call(
            functools.partial(order_kernel, down.shape[0]),
            jax.ShapeDtypeStruct((rank, depth), down.dtype),
            [ANYWHERE] * tensors,
            [pltpu.SemaphoreType.DMA((tensors,))],
            ANYWHERE,
            cost=FREE,
        )(*pieces)
    else:
        none = jnp.zeros((), down.dtype)
        own = jnp.concatenate(
            [sum(jnp.where((me ^ f) == j, pieces[f], none) for f in range(tensors)) for j in range(tensors)],
            axis=0,
        )

    hops = range(CORES, tensors, CORES)

    def send(m):
        return [flipped(chunks[m], "tensor", hop) for hop in hops]

    far = [send(0)]

    def across(m):
        return [flipped(value, "tensor", 1) for value in far[m]]

    def far_places(m):
        return [(hop, edges[m], 0, edges[m + 1] - edges[m]) for hop in hops]

    def near_places(m):
        return [(hop ^ 1, edges[m], 0, edges[m + 1] - edges[m]) for hop in hops]

    def products(places, features, total):
        return call(
            functools.partial(products_kernel, tile, depth, places),
            jax.ShapeDtypeStruct((rows, columns), jnp.float32),
            [ANYWHERE] + [ANYWHERE] * len(features) + [VECTOR],
            tile_scratch(tile, rows, places, columns),
        )(frozen_projection_weight, *features, total)

    mixed = is_mixed(groups, parts)
    own, here = chained(own, tokens)
    if mixed:
        held = [
            lax.ppermute(
                own,
                ("parts", "adapter"),
                [(p * groups + z, p * groups + table[p][z]) for p in range(parts) for z in range(groups)],
            )
            for table in (FIRST, SECOND)
        ]
    else:
        held = [flipped(own, "adapter", flip) for flip in range(1, groups)]
    places = [(0, 0, 0, depth // 2)]
    total, stored = call(
        functools.partial(first_kernel, tile, depth, places, slots),
        [
            jax.ShapeDtypeStruct((rows, columns), jnp.float32),
            jax.ShapeDtypeStruct((1, rows), jnp.int32),
        ],
        [SCALAR, VECTOR, ANYWHERE, ANYWHERE],
        tile_scratch(tile, rows, places, columns),
        [VECTOR, VECTOR],
    )(placement, tenant.reshape(1, rows), frozen_projection_weight, here)
    total, up, neighbour, chunks[1] = chained(total, lowrank_up_weight[0], neighbour, chunks[1])
    far.append(send(1))
    ups = [up, flipped(up, "adapter", 1)]
    total = products([(0, depth // 2, depth // 2, depth // 2)], [here], total)
    held, total = chained(held, total)
    if mixed:
        group, part = lax.axis_index("adapter"), lax.axis_index("parts")
        far_one = jnp.where(source(group, part, FIRST) == (group ^ 1), held[1], held[0])
        held.append(flipped(far_one, "parts", 1))
    ups[1], total = chained(ups[1], total)
    total, neighbour = chained(total, neighbour)
    total = products([(1, 0, 0, depth)], [neighbour], total)
    total, up = chained(total, up)
    later = [flipped(up, "adapter", flip) for flip in range(2, groups)]
    held, total = chained(held, total)
    downs = [own] + held

    tiles = depth // tile
    partial = call(
        functools.partial(shrink_kernel, tile, mixed, slots),
        jax.ShapeDtypeStruct((rank, rows), jnp.float32),
        [ANYWHERE, VECTOR] + [ANYWHERE] * slots,
        [
            pltpu.VMEM((tiles, rows, tile), jnp.bfloat16),
            pltpu.VMEM((tiles, slots * rank, tile), jnp.bfloat16),
            pltpu.VMEM((rows, slots * rank), jnp.float32),
            pltpu.SemaphoreType.DMA((1 + slots, tiles)),
        ],
    )(tokens, stored, *downs)
    far[0], later, partial = chained(far[0], later, partial)
    ups += later
    near = across(0)
    total = products(far_places(0), far[0], total)
    flip = 1
    while flip < tensors // 2:
        received = flipped(partial, "tensor", flip)
        if flip == 1:
            received, total = chained(received, total)
        partial += received
        flip *= 2
    more = flipped(partial.astype(jnp.bfloat16), "tensor", flip)
    total, partial = chained(total, partial)
    total = products(near_places(0), near, total)
    far[1], ups, total = chained(far[1], ups, total)
    near = across(1)
    total = products(far_places(1), far[1], total)
    near, more, total = chained(near, more, total)

    places = near_places(1)
    return call(
        functools.partial(last_kernel, tile, depth, places, slots),
        jax.ShapeDtypeStruct((rows, columns), jnp.bfloat16),
        [ANYWHERE] + [ANYWHERE] * len(near) + [VECTOR] * 2 + [ANYWHERE] * (2 + slots),
        [
            pltpu.VMEM((rows, columns), jnp.float32),
            pltpu.VMEM((rank, rows), jnp.float32),
            pltpu.VMEM((rank, rows), jnp.bfloat16),
            pltpu.VMEM((slots * rank, columns), jnp.bfloat16),
        ]
        + tile_scratch(tile, rows, places, columns)
        + [pltpu.SemaphoreType.DMA((2 + slots,))],
    )(frozen_projection_weight, *near, total, stored, partial, more, *ups)


def solution(mesh):
    placed = (
        P(("parts", "adapter"), "tensor"),
        P(("parts", "adapter"), None),
        P(),
        P(None, "tensor"),
        P("adapter", None, "tensor"),
        P("adapter", None, "tensor"),
    )
    return jax.shard_map(
        body,
        mesh=mesh,
        in_specs=placed,
        out_specs=P(("parts", "adapter"), "tensor"),
        check_vma=False,
    )
```

```python
import functools
import math

import jax
import jax.numpy as jnp
from jax import lax
from jax.experimental import pallas as pl
from jax.experimental.pallas import tpu as pltpu
from jax.sharding import PartitionSpec as P

LOWRANK_SCALE = 2.0
CORES = 2
LANES = 128
CUTS = (0.75,)
MIB = 1024 * 1024
FREE = pl.CostEstimate(flops=0, bytes_accessed=0, transcendentals=0)
LONG = pl.CostEstimate(flops=10**11, bytes_accessed=0, transcendentals=0)
ANYWHERE = pl.BlockSpec(memory_space=pl.ANY)
VECTOR = pl.BlockSpec(memory_space=pltpu.VMEM)
SCALAR = pl.BlockSpec(memory_space=pltpu.SMEM)


def flipped(value, axis, flip):
    count = lax.axis_size(axis)
    return lax.ppermute(value, axis, [(i, i ^ flip) for i in range(count)])


def chained(*values):
    return lax.optimization_barrier(values)


def call(kernel, out_shape, in_specs, scratch, out_specs=VECTOR, cost=LONG, mib=24):
    return pl.pallas_call(
        kernel,
        out_shape=out_shape,
        in_specs=in_specs,
        out_specs=out_specs,
        scratch_shapes=scratch,
        cost_estimate=cost,
        compiler_params=pltpu.CompilerParams(vmem_limit_bytes=mib * MIB),
    )


def run_copies(pairs, sems):
    copies = [
        pltpu.make_async_copy(source, target, sems.at[i]) for i, (source, target) in enumerate(pairs)
    ]
    for copy in copies:
        copy.start()
    for copy in copies:
        copy.wait()


def cut_kernel(edges, source_ref, *refs):
    outs, (held_ref, sems) = refs[:-2], refs[-2:]
    steps, rows = held_ref.shape[:2]
    copies = [
        pltpu.make_async_copy(source_ref.at[pl.ds(i * rows, rows)], held_ref.at[i], sems.at[0, i])
        for i in range(steps)
    ]
    for copy in copies:
        copy.start()
    leaving = []
    for i in range(steps):
        copies[i].wait()
        for m, (a, b, out) in enumerate(zip(edges, edges[1:], outs)):
            leaving.append(
                pltpu.make_async_copy(
                    held_ref.at[i, :, pl.ds(a, b - a)],
                    out.at[pl.ds(i * rows, rows)],
                    sems.at[1 + m, i],
                )
            )
            leaving[-1].start()
    for copy in leaving:
        copy.wait()


def order_kernel(rank_part, *refs):
    pieces, out_ref, sems = refs[:-2], refs[-2], refs[-1]
    me = lax.axis_index("tensor")
    run_copies(
        [
            (piece, out_ref.at[pl.ds(pl.multiple_of((me ^ f) * rank_part, rank_part), rank_part)])
            for f, piece in enumerate(pieces)
        ],
        sems,
    )


def start_tiles(tile, depth, places, features, weight_ref, held_ref, rows_ref, sems):
    me, t = lax.axis_index("tensor"), 0
    for (flip, first, skip, width), part in zip(places, features):
        for k in range(0, width, tile):
            start = pl.multiple_of((me ^ flip) * depth + first + k, LANES)
            pltpu.make_async_copy(
                weight_ref.at[pl.ds(start, tile)], rows_ref.at[t], sems.at[1, t]
            ).start()
            pltpu.make_async_copy(part.at[:, pl.ds(skip + k, tile)], held_ref.at[t], sems.at[0, t]).start()
            t += 1


def add_tiles(held_ref, rows_ref, sems, total_ref):
    @pl.loop(0, held_ref.shape[0])
    def _(t):
        pltpu.make_async_copy(held_ref.at[t], held_ref.at[t], sems.at[0, t]).wait()
        pltpu.make_async_copy(rows_ref.at[t], rows_ref.at[t], sems.at[1, t]).wait()
        total_ref[...] += jnp.dot(held_ref[t], rows_ref[t], preferred_element_type=jnp.float32)


def tile_scratch(tile, rows, places, columns):
    tiles = sum(place[3] for place in places) // tile
    return [
        pltpu.VMEM((tiles, rows, tile), jnp.bfloat16),
        pltpu.VMEM((tiles, tile, columns), jnp.bfloat16),
        pltpu.SemaphoreType.DMA((2, tiles)),
    ]


def first_kernel(tile, depth, places, slots, placement_ref, tenant_ref, weight_ref, *refs):
    count = len(places)
    features = refs[:count]
    out_ref, stored_ref, held_ref, rows_ref, sems = refs[count:]
    start_tiles(tile, depth, places, features, weight_ref, held_ref, rows_ref, sems)
    out_ref[...] = jnp.zeros_like(out_ref)
    stored = jnp.zeros(stored_ref.shape, jnp.int32)
    for slot in range(slots):
        stored = jnp.where(tenant_ref[...] == slot, placement_ref[slot], stored)
    stored_ref[...] = stored
    add_tiles(held_ref, rows_ref, sems, out_ref)


def products_kernel(tile, depth, places, weight_ref, *refs):
    count = len(places)
    features, given = refs[:count], refs[count]
    out_ref, held_ref, rows_ref, sems = refs[count + 1 :]
    start_tiles(tile, depth, places, features, weight_ref, held_ref, rows_ref, sems)
    out_ref[...] = given[...]
    add_tiles(held_ref, rows_ref, sems, out_ref)


def owners_of(flips, pairs):
    group, part = lax.axis_index("adapter"), lax.axis_index("parts")
    owners = [group] + [group ^ flip for flip in flips]
    for near, far in pairs:
        owners += [group ^ (near + part * (far - near)), group ^ (far + part * (near - far))]
    return owners


def last_kernel(tile, depth, places, flips, pairs, slots, weight_ref, *refs):
    count = len(places)
    features = refs[:count]
    given, stored_ref, sum_ref, more_ref = refs[count : count + 4]
    ups = refs[count + 4 : count + 4 + slots]
    (
        out_ref, total_ref, sums_ref, received_ref, stacked_ref, held_ref, rows_ref, sems, small_sems,
    ) = refs[count + 4 + slots :]
    rank = ups[0].shape[0]
    copies = [(sum_ref, sums_ref), (more_ref, received_ref)]
    copies += [(up, stacked_ref.at[pl.ds(b * rank, rank)]) for b, up in enumerate(ups)]
    copies = [
        pltpu.make_async_copy(source, target, small_sems.at[i])
        for i, (source, target) in enumerate(copies)
    ]
    for copy in copies:
        copy.start()
    start_tiles(tile, depth, places, features, weight_ref, held_ref, rows_ref, sems)
    total_ref[...] = given[...]
    add_tiles(held_ref, rows_ref, sems, total_ref)
    for copy in copies:
        copy.wait()
    shrunk = (sums_ref[...] + received_ref[...].astype(jnp.float32)).astype(jnp.bfloat16).astype(jnp.float32)
    spread = jnp.concatenate(
        [jnp.where(stored_ref[...] == owner, shrunk, 0.0) for owner in owners_of(flips, pairs)], axis=0
    )
    expanded = jnp.dot(
        spread.T.astype(jnp.bfloat16), stacked_ref[...], preferred_element_type=jnp.float32
    )
    expanded = expanded.astype(jnp.bfloat16).astype(jnp.float32)
    out_ref[...] = (total_ref[...] + LOWRANK_SCALE * expanded).astype(out_ref.dtype)


def shrink_kernel(tile, flips, pairs, slots, tokens_ref, stored_ref, *refs):
    downs, out_ref, held_ref, down_ref, sums_ref, sems = (
        refs[:slots], refs[slots], *refs[slots + 1 :]
    )
    rank = downs[0].shape[0]
    tiles = tokens_ref.shape[1] // tile
    for k in range(tiles):
        here = pl.ds(k * tile, tile)
        pltpu.make_async_copy(tokens_ref.at[:, here], held_ref.at[k], sems.at[0, k]).start()
        for b, down in enumerate(downs):
            pltpu.make_async_copy(
                down.at[:, here], down_ref.at[k, pl.ds(b * rank, rank)], sems.at[1 + b, k]
            ).start()
    sums_ref[...] = jnp.zeros_like(sums_ref)

    @pl.loop(0, tiles)
    def _(k):
        pltpu.make_async_copy(held_ref.at[k], held_ref.at[k], sems.at[0, k]).wait()
        for b in range(slots):
            block = down_ref.at[k, pl.ds(b * rank, rank)]
            pltpu.make_async_copy(block, block, sems.at[1 + b, k]).wait()
        sums_ref[...] += lax.dot_general(
            held_ref[k], down_ref[k], (((1,), (1,)), ((), ())), preferred_element_type=jnp.float32
        )

    sums = sums_ref[...].T
    total = jnp.zeros(out_ref.shape, jnp.float32)
    for b, owner in enumerate(owners_of(flips, pairs)):
        total += jnp.where(stored_ref[...] == owner, sums[b * rank : (b + 1) * rank], 0.0)
    out_ref[...] = total


def body(
    tokens, tenant, placement, frozen_projection_weight, lowrank_down_weight, lowrank_up_weight
):
    rows, depth = tokens.shape
    slots = placement.shape[0]
    tensors = lax.axis_size("tensor")
    groups = lax.axis_size("adapter")
    parts = lax.axis_size("parts")
    me = lax.axis_index("tensor")
    rank, columns = lowrank_up_weight.shape[1:]
    edges = [0] + [int(depth * cut) // LANES * LANES for cut in CUTS] + [depth]
    tile = math.gcd(*edges)

    down = lowrank_down_weight[0].T
    pieces = [
        lax.dynamic_slice_in_dim(down, (me ^ flip) * depth, depth, axis=1)
        for flip in range(tensors)
    ]
    uncut, pieces = chained(tokens, pieces)
    steps = 6
    chunks = list(
        call(
            functools.partial(cut_kernel, edges),
            [jax.ShapeDtypeStruct((rows, b - a), tokens.dtype) for a, b in zip(edges, edges[1:])],
            [ANYWHERE],
            [
                pltpu.VMEM((steps, rows // steps, depth), tokens.dtype),
                pltpu.SemaphoreType.DMA((len(edges), steps)),
            ],
            [ANYWHERE] * (len(edges) - 1),
            cost=FREE,
            mib=56,
        )(uncut)
    )
    pieces = [pieces[0]] + [flipped(pieces[f], "tensor", f) for f in range(1, tensors)]
    if down.shape[0] % 16 == 0:
        own = call(
            functools.partial(order_kernel, down.shape[0]),
            jax.ShapeDtypeStruct((rank, depth), down.dtype),
            [ANYWHERE] * tensors,
            [pltpu.SemaphoreType.DMA((tensors,))],
            ANYWHERE,
            cost=FREE,
        )(*pieces)
    else:
        none = jnp.zeros((), down.dtype)
        own = jnp.concatenate(
            [sum(jnp.where((me ^ f) == j, pieces[f], none) for f in range(tensors)) for j in range(tensors)],
            axis=0,
        )

    hops = range(CORES, tensors, CORES)

    def send(m):
        return [flipped(chunks[m], "tensor", hop) for hop in hops]

    far = [send(0)]

    def across(m):
        return [flipped(value, "tensor", 1) for value in far[m]]

    def far_places(m):
        return [(hop, edges[m], 0, edges[m + 1] - edges[m]) for hop in hops]

    def near_places(m):
        return [(hop ^ 1, edges[m], 0, edges[m + 1] - edges[m]) for hop in hops]

    def products(places, features, total):
        return call(
            functools.partial(products_kernel, tile, depth, places),
            jax.ShapeDtypeStruct((rows, columns), jnp.float32),
            [ANYWHERE] + [ANYWHERE] * len(features) + [VECTOR],
            tile_scratch(tile, rows, places, columns),
        )(frozen_projection_weight, *features, total)

    flips = list(range(1, groups))
    pairs = []
    if parts == 2:
        while len(flips) > 1:
            pairs.append((flips.pop(-2), flips.pop(-1)))
    routes = [
        [(p * groups + z, p * groups + (z ^ pair[p])) for p in range(parts) for z in range(groups)]
        for pair in pairs
    ]

    def fetch_far(value):
        return [lax.ppermute(value, ("parts", "adapter"), route) for route in routes]

    def fetch_near(value):
        return [flipped(value, "adapter", flip) for flip in flips]

    def swap(values):
        return [flipped(value, "parts", 1) for value in values]

    own, here = chained(own, tokens)
    fetched = fetch_far(own)
    places = [(0, 0, 0, depth // 2)]
    total, stored = call(
        functools.partial(first_kernel, tile, depth, places, slots),
        [
            jax.ShapeDtypeStruct((rows, columns), jnp.float32),
            jax.ShapeDtypeStruct((1, rows), jnp.int32),
        ],
        [SCALAR, VECTOR, ANYWHERE, ANYWHERE],
        tile_scratch(tile, rows, places, columns),
        [VECTOR, VECTOR],
    )(placement, tenant.reshape(1, rows), frozen_projection_weight, here)
    total, own, there, chunks[1] = chained(total, own, tokens, chunks[1])
    neighbour = flipped(there, "tensor", 1)
    far.append(send(1))
    single = fetch_near(own)
    total = products([(0, depth // 2, depth // 2, depth // 2)], [here], total)
    fetched, neighbour, total = chained(fetched, neighbour, total)
    swapped = swap(fetched)
    total = products([(1, 0, 0, depth)], [neighbour], total)
    total, up = chained(total, lowrank_up_weight[0])
    fetched_up, single_up = fetch_far(up), fetch_near(up)
    single, swapped, total = chained(single, swapped, total)
    downs = [own] + single
    for pair in zip(fetched, swapped):
        downs += pair

    tiles = depth // tile
    partial = call(
        functools.partial(shrink_kernel, tile, flips, pairs, slots),
        jax.ShapeDtypeStruct((rank, rows), jnp.float32),
        [ANYWHERE, VECTOR] + [ANYWHERE] * slots,
        [
            pltpu.VMEM((tiles, rows, tile), jnp.bfloat16),
            pltpu.VMEM((tiles, slots * rank, tile), jnp.bfloat16),
            pltpu.VMEM((rows, slots * rank), jnp.float32),
            pltpu.SemaphoreType.DMA((1 + slots, tiles)),
        ],
    )(tokens, stored, *downs)
    far[0], fetched_up, partial = chained(far[0], fetched_up, partial)
    swapped_up = swap(fetched_up)
    ups = [up] + single_up
    for pair in zip(fetched_up, swapped_up):
        ups += pair
    near = across(0)
    total = products(far_places(0), far[0], total)
    flip = 1
    while flip < tensors // 2:
        received = flipped(partial, "tensor", flip)
        if flip == 1:
            received, total = chained(received, total)
        partial += received
        flip *= 2
    more = flipped(partial.astype(jnp.bfloat16), "tensor", flip)
    total, partial = chained(total, partial)
    total = products(near_places(0), near, total)
    far[1], ups, total = chained(far[1], ups, total)
    near = across(1)
    total = products(far_places(1), far[1], total)
    near, more, total = chained(near, more, total)

    places = near_places(1)
    return call(
        functools.partial(last_kernel, tile, depth, places, flips, pairs, slots),
        jax.ShapeDtypeStruct((rows, columns), jnp.bfloat16),
        [ANYWHERE] + [ANYWHERE] * len(near) + [VECTOR] * 2 + [ANYWHERE] * (2 + slots),
        [
            pltpu.VMEM((rows, columns), jnp.float32),
            pltpu.VMEM((rank, rows), jnp.float32),
            pltpu.VMEM((rank, rows), jnp.bfloat16),
            pltpu.VMEM((slots * rank, columns), jnp.bfloat16),
        ]
        + tile_scratch(tile, rows, places, columns)
        + [pltpu.SemaphoreType.DMA((2 + slots,))],
    )(frozen_projection_weight, *near, total, stored, partial, more, *ups)


def solution(mesh):
    placed = (
        P(("parts", "adapter"), "tensor"),
        P(("parts", "adapter"), None),
        P(),
        P(None, "tensor"),
        P("adapter", None, "tensor"),
        P("adapter", None, "tensor"),
    )
    return jax.shard_map(
        body,
        mesh=mesh,
        in_specs=placed,
        out_specs=P(("parts", "adapter"), "tensor"),
        check_vma=False,
    )
```

```python
import functools
import math

import jax
import jax.numpy as jnp
from jax import lax
from jax.experimental import pallas as pl
from jax.experimental.pallas import tpu as pltpu
from jax.sharding import PartitionSpec as P

LOWRANK_SCALE = 2.0
CORES = 2
LANES = 128
CUTS = (0.75,)
MIB = 1024 * 1024
FREE = pl.CostEstimate(flops=0, bytes_accessed=0, transcendentals=0)
LONG = pl.CostEstimate(flops=10**11, bytes_accessed=0, transcendentals=0)
ANYWHERE = pl.BlockSpec(memory_space=pl.ANY)
VECTOR = pl.BlockSpec(memory_space=pltpu.VMEM)
SCALAR = pl.BlockSpec(memory_space=pltpu.SMEM)


def flipped(value, axis, flip):
    count = lax.axis_size(axis)
    return lax.ppermute(value, axis, [(i, i ^ flip) for i in range(count)])


def chained(*values):
    return lax.optimization_barrier(values)


def call(kernel, out_shape, in_specs, scratch, out_specs=VECTOR, cost=LONG, mib=24):
    return pl.pallas_call(
        kernel,
        out_shape=out_shape,
        in_specs=in_specs,
        out_specs=out_specs,
        scratch_shapes=scratch,
        cost_estimate=cost,
        compiler_params=pltpu.CompilerParams(vmem_limit_bytes=mib * MIB),
    )


def run_copies(pairs, sems):
    copies = [
        pltpu.make_async_copy(source, target, sems.at[i]) for i, (source, target) in enumerate(pairs)
    ]
    for copy in copies:
        copy.start()
    for copy in copies:
        copy.wait()


def cut_kernel(edges, source_ref, *refs):
    outs, (held_ref, sems) = refs[:-2], refs[-2:]
    steps, rows = held_ref.shape[:2]
    copies = [
        pltpu.make_async_copy(source_ref.at[pl.ds(i * rows, rows)], held_ref.at[i], sems.at[0, i])
        for i in range(steps)
    ]
    for copy in copies:
        copy.start()
    leaving = []
    for i in range(steps):
        copies[i].wait()
        for m, (a, b, out) in enumerate(zip(edges, edges[1:], outs)):
            leaving.append(
                pltpu.make_async_copy(
                    held_ref.at[i, :, pl.ds(a, b - a)],
                    out.at[pl.ds(i * rows, rows)],
                    sems.at[1 + m, i],
                )
            )
            leaving[-1].start()
    for copy in leaving:
        copy.wait()


def order_kernel(rank_part, *refs):
    pieces, out_ref, sems = refs[:-2], refs[-2], refs[-1]
    me = lax.axis_index("tensor")
    run_copies(
        [
            (piece, out_ref.at[pl.ds(pl.multiple_of((me ^ f) * rank_part, rank_part), rank_part)])
            for f, piece in enumerate(pieces)
        ],
        sems,
    )


def start_tiles(tile, depth, places, features, weight_ref, held_ref, rows_ref, sems):
    me, t = lax.axis_index("tensor"), 0
    for (flip, first, skip, width), part in zip(places, features):
        for k in range(0, width, tile):
            start = pl.multiple_of((me ^ flip) * depth + first + k, LANES)
            pltpu.make_async_copy(
                weight_ref.at[pl.ds(start, tile)], rows_ref.at[t], sems.at[1, t]
            ).start()
            pltpu.make_async_copy(part.at[:, pl.ds(skip + k, tile)], held_ref.at[t], sems.at[0, t]).start()
            t += 1


def add_tiles(held_ref, rows_ref, sems, total_ref):
    @pl.loop(0, held_ref.shape[0])
    def _(t):
        pltpu.make_async_copy(held_ref.at[t], held_ref.at[t], sems.at[0, t]).wait()
        pltpu.make_async_copy(rows_ref.at[t], rows_ref.at[t], sems.at[1, t]).wait()
        total_ref[...] += jnp.dot(held_ref[t], rows_ref[t], preferred_element_type=jnp.float32)


def tile_scratch(tile, rows, places, columns):
    tiles = sum(place[3] for place in places) // tile
    return [
        pltpu.VMEM((tiles, rows, tile), jnp.bfloat16),
        pltpu.VMEM((tiles, tile, columns), jnp.bfloat16),
        pltpu.SemaphoreType.DMA((2, tiles)),
    ]


def first_kernel(tile, depth, places, slots, placement_ref, tenant_ref, weight_ref, *refs):
    count = len(places)
    features = refs[:count]
    out_ref, stored_ref, held_ref, rows_ref, sems = refs[count:]
    start_tiles(tile, depth, places, features, weight_ref, held_ref, rows_ref, sems)
    out_ref[...] = jnp.zeros_like(out_ref)
    stored = jnp.zeros(stored_ref.shape, jnp.int32)
    for slot in range(slots):
        stored = jnp.where(tenant_ref[...] == slot, placement_ref[slot], stored)
    stored_ref[...] = stored
    add_tiles(held_ref, rows_ref, sems, out_ref)


def products_kernel(tile, depth, places, weight_ref, *refs):
    count = len(places)
    features, given = refs[:count], refs[count]
    out_ref, held_ref, rows_ref, sems = refs[count + 1 :]
    start_tiles(tile, depth, places, features, weight_ref, held_ref, rows_ref, sems)
    out_ref[...] = given[...]
    add_tiles(held_ref, rows_ref, sems, out_ref)


def products_and_sum_kernel(tile, depth, places, weight_ref, *refs):
    count = len(places)
    features, (given, one, other) = refs[:count], refs[count : count + 3]
    out_ref, sum_ref, rounded_ref, held_ref, rows_ref, sems = refs[count + 3 :]
    start_tiles(tile, depth, places, features, weight_ref, held_ref, rows_ref, sems)
    out_ref[...] = given[...]
    sum_ref[...] = one[...] + other[...]
    rounded_ref[...] = sum_ref[...].astype(rounded_ref.dtype)
    add_tiles(held_ref, rows_ref, sems, out_ref)


def owners_of(flips, pairs):
    group, part = lax.axis_index("adapter"), lax.axis_index("parts")
    owners = [group] + [group ^ flip for flip in flips]
    for near, far in pairs:
        owners += [group ^ (near + part * (far - near)), group ^ (far + part * (near - far))]
    return owners


def last_kernel(tile, depth, places, flips, pairs, slots, weight_ref, *refs):
    count = len(places)
    features = refs[:count]
    given, stored_ref, sum_ref, more_ref = refs[count : count + 4]
    ups = refs[count + 4 : count + 4 + slots]
    (
        out_ref, total_ref, sums_ref, received_ref, stacked_ref, held_ref, rows_ref, sems, small_sems,
    ) = refs[count + 4 + slots :]
    rank = ups[0].shape[0]
    copies = [(sum_ref, sums_ref), (more_ref, received_ref)]
    copies += [(up, stacked_ref.at[pl.ds(b * rank, rank)]) for b, up in enumerate(ups)]
    copies = [
        pltpu.make_async_copy(source, target, small_sems.at[i])
        for i, (source, target) in enumerate(copies)
    ]
    for copy in copies:
        copy.start()
    start_tiles(tile, depth, places, features, weight_ref, held_ref, rows_ref, sems)
    total_ref[...] = given[...]
    add_tiles(held_ref, rows_ref, sems, total_ref)
    for copy in copies:
        copy.wait()
    shrunk = (sums_ref[...] + received_ref[...].astype(jnp.float32)).astype(jnp.bfloat16).astype(jnp.float32)
    spread = jnp.concatenate(
        [jnp.where(stored_ref[...] == owner, shrunk, 0.0) for owner in owners_of(flips, pairs)], axis=0
    )
    expanded = jnp.dot(
        spread.T.astype(jnp.bfloat16), stacked_ref[...], preferred_element_type=jnp.float32
    )
    expanded = expanded.astype(jnp.bfloat16).astype(jnp.float32)
    out_ref[...] = (total_ref[...] + LOWRANK_SCALE * expanded).astype(out_ref.dtype)


def shrink_kernel(tile, flips, pairs, slots, tokens_ref, stored_ref, *refs):
    downs, out_ref, held_ref, down_ref, sums_ref, sems = (
        refs[:slots], refs[slots], *refs[slots + 1 :]
    )
    rank = downs[0].shape[0]
    tiles = tokens_ref.shape[1] // tile
    for k in range(tiles):
        here = pl.ds(k * tile, tile)
        pltpu.make_async_copy(tokens_ref.at[:, here], held_ref.at[k], sems.at[0, k]).start()
        for b, down in enumerate(downs):
            pltpu.make_async_copy(
                down.at[:, here], down_ref.at[k, pl.ds(b * rank, rank)], sems.at[1 + b, k]
            ).start()
    sums_ref[...] = jnp.zeros_like(sums_ref)

    @pl.loop(0, tiles)
    def _(k):
        pltpu.make_async_copy(held_ref.at[k], held_ref.at[k], sems.at[0, k]).wait()
        for b in range(slots):
            block = down_ref.at[k, pl.ds(b * rank, rank)]
            pltpu.make_async_copy(block, block, sems.at[1 + b, k]).wait()
        sums_ref[...] += lax.dot_general(
            held_ref[k], down_ref[k], (((1,), (1,)), ((), ())), preferred_element_type=jnp.float32
        )

    sums = sums_ref[...].T
    total = jnp.zeros(out_ref.shape, jnp.float32)
    for b, owner in enumerate(owners_of(flips, pairs)):
        total += jnp.where(stored_ref[...] == owner, sums[b * rank : (b + 1) * rank], 0.0)
    out_ref[...] = total


def body(
    tokens, tenant, placement, frozen_projection_weight, lowrank_down_weight, lowrank_up_weight
):
    rows, depth = tokens.shape
    slots = placement.shape[0]
    tensors = lax.axis_size("tensor")
    groups = lax.axis_size("adapter")
    parts = lax.axis_size("parts")
    me = lax.axis_index("tensor")
    rank, columns = lowrank_up_weight.shape[1:]
    edges = [0] + [int(depth * cut) // LANES * LANES for cut in CUTS] + [depth]
    tile = math.gcd(*edges)

    down = lowrank_down_weight[0].T
    pieces = [
        lax.dynamic_slice_in_dim(down, (me ^ flip) * depth, depth, axis=1)
        for flip in range(tensors)
    ]
    uncut, pieces = chained(tokens, pieces)
    steps = 6
    chunks = list(
        call(
            functools.partial(cut_kernel, edges),
            [jax.ShapeDtypeStruct((rows, b - a), tokens.dtype) for a, b in zip(edges, edges[1:])],
            [ANYWHERE],
            [
                pltpu.VMEM((steps, rows // steps, depth), tokens.dtype),
                pltpu.SemaphoreType.DMA((len(edges), steps)),
            ],
            [ANYWHERE] * (len(edges) - 1),
            cost=FREE,
            mib=56,
        )(uncut)
    )
    pieces = [pieces[0]] + [flipped(pieces[f], "tensor", f) for f in range(1, tensors)]
    if down.shape[0] % 16 == 0:
        own = call(
            functools.partial(order_kernel, down.shape[0]),
            jax.ShapeDtypeStruct((rank, depth), down.dtype),
            [ANYWHERE] * tensors,
            [pltpu.SemaphoreType.DMA((tensors,))],
            ANYWHERE,
            cost=FREE,
        )(*pieces)
    else:
        none = jnp.zeros((), down.dtype)
        own = jnp.concatenate(
            [sum(jnp.where((me ^ f) == j, pieces[f], none) for f in range(tensors)) for j in range(tensors)],
            axis=0,
        )

    hops = range(CORES, tensors, CORES)

    def send(m):
        return [flipped(chunks[m], "tensor", hop) for hop in hops]

    far = [send(0)]

    def across(m):
        return [flipped(value, "tensor", 1) for value in far[m]]

    def far_places(m):
        return [(hop, edges[m], 0, edges[m + 1] - edges[m]) for hop in hops]

    def near_places(m):
        return [(hop ^ 1, edges[m], 0, edges[m + 1] - edges[m]) for hop in hops]

    def products(places, features, total):
        return call(
            functools.partial(products_kernel, tile, depth, places),
            jax.ShapeDtypeStruct((rows, columns), jnp.float32),
            [ANYWHERE] + [ANYWHERE] * len(features) + [VECTOR],
            tile_scratch(tile, rows, places, columns),
        )(frozen_projection_weight, *features, total)

    flips = list(range(1, groups))
    pairs = []
    if parts == 2:
        while len(flips) > 1:
            pairs.append((flips.pop(-2), flips.pop(-1)))
    routes = [
        [(p * groups + z, p * groups + (z ^ pair[p])) for p in range(parts) for z in range(groups)]
        for pair in pairs
    ]

    def fetch_far(value):
        return [lax.ppermute(value, ("parts", "adapter"), route) for route in routes]

    def fetch_near(value):
        return [flipped(value, "adapter", flip) for flip in flips]

    def swap(values):
        return [flipped(value, "parts", 1) for value in values]

    own, here = chained(own, tokens)
    fetched = fetch_far(own)
    places = [(0, 0, 0, depth // 2)]
    total, stored = call(
        functools.partial(first_kernel, tile, depth, places, slots),
        [
            jax.ShapeDtypeStruct((rows, columns), jnp.float32),
            jax.ShapeDtypeStruct((1, rows), jnp.int32),
        ],
        [SCALAR, VECTOR, ANYWHERE, ANYWHERE],
        tile_scratch(tile, rows, places, columns),
        [VECTOR, VECTOR],
    )(placement, tenant.reshape(1, rows), frozen_projection_weight, here)
    total, own, there, chunks[1] = chained(total, own, tokens, chunks[1])
    neighbour = flipped(there, "tensor", 1)
    far.append(send(1))
    single = fetch_near(own)
    total = products([(0, depth // 2, depth // 2, depth // 2)], [here], total)
    fetched, neighbour, total = chained(fetched, neighbour, total)
    swapped = swap(fetched)
    total = products([(1, 0, 0, depth // 2)], [neighbour], total)
    total, up = chained(total, lowrank_up_weight[0])
    fetched_up, single_up = fetch_far(up), fetch_near(up)
    single, swapped, total = chained(single, swapped, total)
    downs = [own] + single
    for pair in zip(fetched, swapped):
        downs += pair

    tiles = depth // tile
    partial = call(
        functools.partial(shrink_kernel, tile, flips, pairs, slots),
        jax.ShapeDtypeStruct((rank, rows), jnp.float32),
        [ANYWHERE, VECTOR] + [ANYWHERE] * slots,
        [
            pltpu.VMEM((tiles, rows, tile), jnp.bfloat16),
            pltpu.VMEM((tiles, slots * rank, tile), jnp.bfloat16),
            pltpu.VMEM((rows, slots * rank), jnp.float32),
            pltpu.SemaphoreType.DMA((1 + slots, tiles)),
        ],
    )(tokens, stored, *downs)
    received = flipped(partial, "tensor", 1)
    total, partial = chained(total, partial)
    total = products([(1, depth // 2, depth // 2, depth // 2)], [neighbour], total)
    far[0], fetched_up, received, total = chained(far[0], fetched_up, received, total)
    ups = [up] + single_up
    for pair in zip(fetched_up, swap(fetched_up)):
        ups += pair
    near = across(0)
    places = far_places(0)
    total, partial, rounded = call(
        functools.partial(products_and_sum_kernel, tile, depth, places),
        [
            jax.ShapeDtypeStruct((rows, columns), jnp.float32),
            jax.ShapeDtypeStruct((rank, rows), jnp.float32),
            jax.ShapeDtypeStruct((rank, rows), jnp.bfloat16),
        ],
        [ANYWHERE] + [ANYWHERE] * len(places) + [VECTOR] * 3,
        tile_scratch(tile, rows, places, columns),
        [VECTOR] * 3,
    )(frozen_projection_weight, *far[0], total, partial, received)
    flip = CORES
    while flip < tensors // 2:
        partial += flipped(partial, "tensor", flip)
        rounded = partial.astype(jnp.bfloat16)
        flip *= 2
    more = flipped(rounded, "tensor", flip)
    total, partial = chained(total, partial)
    total = products(near_places(0), near, total)
    far[1], ups, total = chained(far[1], ups, total)
    near = across(1)
    total = products(far_places(1), far[1], total)
    near, more, total = chained(near, more, total)

    places = near_places(1)
    return call(
        functools.partial(last_kernel, tile, depth, places, flips, pairs, slots),
        jax.ShapeDtypeStruct((rows, columns), jnp.bfloat16),
        [ANYWHERE] + [ANYWHERE] * len(near) + [VECTOR] * 2 + [ANYWHERE] * (2 + slots),
        [
            pltpu.VMEM((rows, columns), jnp.float32),
            pltpu.VMEM((rank, rows), jnp.float32),
            pltpu.VMEM((rank, rows), jnp.bfloat16),
            pltpu.VMEM((slots * rank, columns), jnp.bfloat16),
        ]
        + tile_scratch(tile, rows, places, columns)
        + [pltpu.SemaphoreType.DMA((2 + slots,))],
    )(frozen_projection_weight, *near, total, stored, partial, more, *ups)


def solution(mesh):
    placed = (
        P(("parts", "adapter"), "tensor"),
        P(("parts", "adapter"), None),
        P(),
        P(None, "tensor"),
        P("adapter", None, "tensor"),
        P("adapter", None, "tensor"),
    )
    return jax.shard_map(
        body,
        mesh=mesh,
        in_specs=placed,
        out_specs=P(("parts", "adapter"), "tensor"),
        check_vma=False,
    )
```

```python
import functools
import math

import jax
import jax.numpy as jnp
from jax import lax
from jax.experimental import pallas as pl
from jax.experimental.pallas import tpu as pltpu
from jax.sharding import PartitionSpec as P

LOWRANK_SCALE = 2.0
CORES = 2
LANES = 128
CUTS = (0.0625, 0.8125)
MIB = 1024 * 1024
FREE = pl.CostEstimate(flops=0, bytes_accessed=0, transcendentals=0)
LONG = pl.CostEstimate(flops=10**11, bytes_accessed=0, transcendentals=0)
ANYWHERE = pl.BlockSpec(memory_space=pl.ANY)
VECTOR = pl.BlockSpec(memory_space=pltpu.VMEM)
SCALAR = pl.BlockSpec(memory_space=pltpu.SMEM)


def flipped(value, axis, flip):
    count = lax.axis_size(axis)
    return lax.ppermute(value, axis, [(i, i ^ flip) for i in range(count)])


def chained(*values):
    return lax.optimization_barrier(values)


def call(kernel, out_shape, in_specs, scratch, out_specs=VECTOR, cost=LONG, mib=24):
    return pl.pallas_call(
        kernel,
        out_shape=out_shape,
        in_specs=in_specs,
        out_specs=out_specs,
        scratch_shapes=scratch,
        cost_estimate=cost,
        compiler_params=pltpu.CompilerParams(vmem_limit_bytes=mib * MIB),
    )


def tile_of(*widths):
    whole = math.gcd(*widths)
    return max(t for t in range(1, whole + 1) if whole % t == 0 and (t == whole or t % LANES == 0) and t <= 640)


def run_copies(pairs, sems):
    copies = [
        pltpu.make_async_copy(source, target, sems.at[i]) for i, (source, target) in enumerate(pairs)
    ]
    for copy in copies:
        copy.start()
    for copy in copies:
        copy.wait()


def first_cut_kernel(width, source_ref, out_ref, sems):
    run_copies([(source_ref.at[:, pl.ds(0, width)], out_ref)], sems)


def cut_kernel(edges, source_ref, *refs):
    outs, (held_ref, sems) = refs[:-2], refs[-2:]
    steps, rows = held_ref.shape[:2]
    copies = [
        pltpu.make_async_copy(
            source_ref.at[pl.ds(i * rows, rows), pl.ds(edges[0], edges[-1] - edges[0])],
            held_ref.at[i],
            sems.at[0, i],
        )
        for i in range(steps)
    ]
    for copy in copies:
        copy.start()
    leaving = []
    for i in range(steps):
        copies[i].wait()
        for m, (a, b, out) in enumerate(zip(edges, edges[1:], outs)):
            leaving.append(
                pltpu.make_async_copy(
                    held_ref.at[i, :, pl.ds(a - edges[0], b - a)],
                    out.at[pl.ds(i * rows, rows)],
                    sems.at[1 + m, i],
                )
            )
            leaving[-1].start()
    for copy in leaving:
        copy.wait()


def order_kernel(down_ref, other_ref, *refs):
    pieces, out_ref, sems = refs[:-2], refs[-2], refs[-1]
    me = lax.axis_index("tensor")
    part, depth = down_ref.shape[0], out_ref.shape[1]
    mine = pl.ds(pl.multiple_of(me * depth, LANES), depth)
    run_copies(
        [
            (piece, out_ref.at[pl.ds(pl.multiple_of((me ^ f) * part, part), part)])
            for f, piece in enumerate((down_ref.at[:, mine], other_ref.at[:, mine], *pieces))
        ],
        sems,
    )


def start_tiles(tile, depth, places, features, weight_ref, held_ref, rows_ref, sems):
    me, t = lax.axis_index("tensor"), 0
    for (flip, first, skip, width), part in zip(places, features):
        for k in range(0, width, tile):
            start = pl.multiple_of((me ^ flip) * depth + first + k, LANES)
            pltpu.make_async_copy(
                weight_ref.at[pl.ds(start, tile)], rows_ref.at[t], sems.at[1, t]
            ).start()
            pltpu.make_async_copy(part.at[:, pl.ds(skip + k, tile)], held_ref.at[t], sems.at[0, t]).start()
            t += 1


def add_tiles(held_ref, rows_ref, sems, total_ref):
    @pl.loop(0, held_ref.shape[0])
    def _(t):
        pltpu.make_async_copy(held_ref.at[t], held_ref.at[t], sems.at[0, t]).wait()
        pltpu.make_async_copy(rows_ref.at[t], rows_ref.at[t], sems.at[1, t]).wait()
        total_ref[...] += jnp.dot(held_ref[t], rows_ref[t], preferred_element_type=jnp.float32)


def tile_scratch(tile, rows, places, columns):
    tiles = sum(place[3] for place in places) // tile
    return [
        pltpu.VMEM((tiles, rows, tile), jnp.bfloat16),
        pltpu.VMEM((tiles, tile, columns), jnp.bfloat16),
        pltpu.SemaphoreType.DMA((2, tiles)),
    ]


def first_kernel(tile, depth, places, slots, placement_ref, tenant_ref, weight_ref, *refs):
    count = len(places)
    features = refs[:count]
    out_ref, stored_ref, held_ref, rows_ref, sems = refs[count:]
    start_tiles(tile, depth, places, features, weight_ref, held_ref, rows_ref, sems)
    out_ref[...] = jnp.zeros_like(out_ref)
    stored = jnp.zeros(stored_ref.shape, jnp.int32)
    for slot in range(slots):
        stored = jnp.where(tenant_ref[...] == slot, placement_ref[slot], stored)
    stored_ref[...] = stored
    add_tiles(held_ref, rows_ref, sems, out_ref)


def products_kernel(tile, depth, places, weight_ref, *refs):
    count = len(places)
    features, given = refs[:count], refs[count]
    out_ref, held_ref, rows_ref, sems = refs[count + 1 :]
    start_tiles(tile, depth, places, features, weight_ref, held_ref, rows_ref, sems)
    out_ref[...] = given[...]
    add_tiles(held_ref, rows_ref, sems, out_ref)


def products_and_sum_kernel(tile, depth, places, weight_ref, *refs):
    count = len(places)
    features, (given, one, other) = refs[:count], refs[count : count + 3]
    out_ref, sum_ref, rounded_ref, held_ref, rows_ref, sems = refs[count + 3 :]
    start_tiles(tile, depth, places, features, weight_ref, held_ref, rows_ref, sems)
    out_ref[...] = given[...]
    sum_ref[...] = one[...] + other[...]
    rounded_ref[...] = sum_ref[...].astype(rounded_ref.dtype)
    add_tiles(held_ref, rows_ref, sems, out_ref)


def owners_of(flips, pairs):
    group, part = lax.axis_index("adapter"), lax.axis_index("parts")
    owners = [group] + [group ^ flip for flip in flips]
    for near, far in pairs:
        owners += [group ^ (near + part * (far - near)), group ^ (far + part * (near - far))]
    return owners


def last_kernel(tile, depth, places, flips, pairs, slots, weight_ref, *refs):
    count = len(places)
    features = refs[:count]
    given, stored_ref, sum_ref, more_ref = refs[count : count + 4]
    ups = refs[count + 4 : count + 4 + slots]
    (
        out_ref, total_ref, sums_ref, received_ref, stacked_ref, held_ref, rows_ref, sems, small_sems,
    ) = refs[count + 4 + slots :]
    rank = ups[0].shape[0]
    copies = [(sum_ref, sums_ref), (more_ref, received_ref)]
    copies += [(up, stacked_ref.at[pl.ds(b * rank, rank)]) for b, up in enumerate(ups)]
    copies = [
        pltpu.make_async_copy(source, target, small_sems.at[i])
        for i, (source, target) in enumerate(copies)
    ]
    for copy in copies:
        copy.start()
    start_tiles(tile, depth, places, features, weight_ref, held_ref, rows_ref, sems)
    total_ref[...] = given[...]
    add_tiles(held_ref, rows_ref, sems, total_ref)
    for copy in copies:
        copy.wait()
    shrunk = (sums_ref[...] + received_ref[...].astype(jnp.float32)).astype(jnp.bfloat16).astype(jnp.float32)
    spread = jnp.concatenate(
        [jnp.where(stored_ref[...] == owner, shrunk, 0.0) for owner in owners_of(flips, pairs)], axis=0
    )
    expanded = jnp.dot(
        spread.T.astype(jnp.bfloat16), stacked_ref[...], preferred_element_type=jnp.float32
    )
    expanded = expanded.astype(jnp.bfloat16).astype(jnp.float32)
    out_ref[...] = (total_ref[...] + LOWRANK_SCALE * expanded).astype(out_ref.dtype)


def shrink_kernel(tile, flips, pairs, slots, tokens_ref, stored_ref, *refs):
    downs, out_ref, held_ref, down_ref, sums_ref, sems = (
        refs[:slots], refs[slots], *refs[slots + 1 :]
    )
    rank = downs[0].shape[0]
    tiles = tokens_ref.shape[1] // tile
    for k in range(tiles):
        here = pl.ds(k * tile, tile)
        pltpu.make_async_copy(tokens_ref.at[:, here], held_ref.at[k], sems.at[0, k]).start()
        for b, down in enumerate(downs):
            pltpu.make_async_copy(
                down.at[:, here], down_ref.at[k, pl.ds(b * rank, rank)], sems.at[1 + b, k]
            ).start()
    sums_ref[...] = jnp.zeros_like(sums_ref)

    @pl.loop(0, tiles)
    def _(k):
        pltpu.make_async_copy(held_ref.at[k], held_ref.at[k], sems.at[0, k]).wait()
        for b in range(slots):
            block = down_ref.at[k, pl.ds(b * rank, rank)]
            pltpu.make_async_copy(block, block, sems.at[1 + b, k]).wait()
        sums_ref[...] += lax.dot_general(
            held_ref[k], down_ref[k], (((1,), (1,)), ((), ())), preferred_element_type=jnp.float32
        )

    sums = sums_ref[...].T
    total = jnp.zeros(out_ref.shape, jnp.float32)
    for b, owner in enumerate(owners_of(flips, pairs)):
        total += jnp.where(stored_ref[...] == owner, sums[b * rank : (b + 1) * rank], 0.0)
    out_ref[...] = total


def body(
    tokens, tenant, placement, frozen_projection_weight, lowrank_down_weight, lowrank_up_weight
):
    rows, depth = tokens.shape
    slots = placement.shape[0]
    tensors = lax.axis_size("tensor")
    groups = lax.axis_size("adapter")
    parts = lax.axis_size("parts")
    me = lax.axis_index("tensor")
    rank, columns = lowrank_up_weight.shape[1:]
    edges = [0] + [max(LANES, int(depth * cut) // LANES * LANES) for cut in CUTS] + [depth]
    tile = tile_of(depth)

    down = lowrank_down_weight[0].T

    def cut(array, first):
        ranges, steps = edges[first:], 6
        return list(
            call(
                functools.partial(cut_kernel, ranges),
                [jax.ShapeDtypeStruct((rows, b - a), array.dtype) for a, b in zip(ranges, ranges[1:])],
                [ANYWHERE],
                [
                    pltpu.VMEM((steps, rows // steps, ranges[-1] - ranges[0]), array.dtype),
                    pltpu.SemaphoreType.DMA((len(ranges), steps)),
                ],
                [ANYWHERE] * (len(ranges) - 1),
                mib=56,
            )(array)
        )

    def slice_for(array, flip):
        return lax.dynamic_slice_in_dim(array, (me ^ flip) * depth, depth, axis=1)

    other = flipped(down, "tensor", 1)
    small = call(
        functools.partial(first_cut_kernel, edges[1]),
        jax.ShapeDtypeStruct((rows, edges[1]), tokens.dtype),
        [ANYWHERE],
        [pltpu.SemaphoreType.DMA((1,))],
        mib=56,
    )(tokens)
    hops = range(CORES, tensors, CORES)
    far = [[flipped(small, "tensor", hop) for hop in hops]]
    other, rest, uncut = chained(other, down, tokens)
    pieces = [slice_for(rest, flip) for flip in range(CORES, tensors)]
    uncut, pieces = chained(uncut, pieces)
    chunks = [small] + cut(uncut, 1)
    pieces = [flipped(piece, "tensor", CORES + i) for i, piece in enumerate(pieces)]
    if down.shape[0] % 16 == 0:
        own = call(
            order_kernel,
            jax.ShapeDtypeStruct((rank, depth), down.dtype),
            [ANYWHERE] * tensors,
            [pltpu.SemaphoreType.DMA((tensors,))],
            ANYWHERE,
            cost=FREE,
        )(down, other, *pieces)
    else:
        pieces = [slice_for(down, 0), slice_for(other, 0)] + pieces
        none = jnp.zeros((), down.dtype)
        own = jnp.concatenate(
            [sum(jnp.where((me ^ f) == j, pieces[f], none) for f in range(tensors)) for j in range(tensors)],
            axis=0,
        )

    def send(m):
        return [flipped(chunks[m], "tensor", hop) for hop in hops]

    far.append(send(1))

    def across(m):
        return [flipped(value, "tensor", 1) for value in far[m]]

    def far_places(m):
        return [(hop, edges[m], 0, edges[m + 1] - edges[m]) for hop in hops]

    def near_places(m):
        return [(hop ^ 1, edges[m], 0, edges[m + 1] - edges[m]) for hop in hops]

    def products(places, features, total):
        tile = tile_of(*[place[3] for place in places])
        return call(
            functools.partial(products_kernel, tile, depth, places),
            jax.ShapeDtypeStruct((rows, columns), jnp.float32),
            [ANYWHERE] + [ANYWHERE] * len(features) + [VECTOR],
            tile_scratch(tile, rows, places, columns),
        )(frozen_projection_weight, *features, total)

    flips = list(range(1, groups))
    pairs = []
    if parts == 2:
        while len(flips) > 1:
            pairs.append((flips.pop(-2), flips.pop(-1)))
    routes = [
        [(p * groups + z, p * groups + (z ^ pair[p])) for p in range(parts) for z in range(groups)]
        for pair in pairs
    ]

    def fetch_far(value):
        return [lax.ppermute(value, ("parts", "adapter"), route) for route in routes]

    def fetch_near(value):
        return [flipped(value, "adapter", flip) for flip in flips]

    def swap(values):
        return [flipped(value, "parts", 1) for value in values]

    own, here, far[0] = chained(own, tokens, far[0])
    fetched = fetch_far(own)
    near = across(0)
    places = [(0, 0, 0, depth // 2)]
    total, stored = call(
        functools.partial(first_kernel, tile, depth, places, slots),
        [
            jax.ShapeDtypeStruct((rows, columns), jnp.float32),
            jax.ShapeDtypeStruct((1, rows), jnp.int32),
        ],
        [SCALAR, VECTOR, ANYWHERE, ANYWHERE],
        tile_scratch(tile, rows, places, columns),
        [VECTOR, VECTOR],
    )(placement, tenant.reshape(1, rows), frozen_projection_weight, here)
    total, own, there, chunks[2] = chained(total, own, tokens, chunks[2])
    neighbour = flipped(there, "tensor", 1)
    far.append(send(2))
    single = fetch_near(own)
    total = products([(0, depth // 2, depth // 2, depth // 2)], [here], total)
    near, total = chained(near, total)
    total = products(far_places(0) + near_places(0), far[0] + near, total)
    fetched, neighbour, total = chained(fetched, neighbour, total)
    swapped = swap(fetched)
    total = products([(1, 0, 0, depth // 2)], [neighbour], total)
    total, up = chained(total, lowrank_up_weight[0])
    fetched_up, single_up = fetch_far(up), fetch_near(up)
    single, swapped, total = chained(single, swapped, total)
    downs = [own] + single
    for pair in zip(fetched, swapped):
        downs += pair

    tiles = depth // tile
    partial = call(
        functools.partial(shrink_kernel, tile, flips, pairs, slots),
        jax.ShapeDtypeStruct((rank, rows), jnp.float32),
        [ANYWHERE, VECTOR] + [ANYWHERE] * slots,
        [
            pltpu.VMEM((tiles, rows, tile), jnp.bfloat16),
            pltpu.VMEM((tiles, slots * rank, tile), jnp.bfloat16),
            pltpu.VMEM((rows, slots * rank), jnp.float32),
            pltpu.SemaphoreType.DMA((1 + slots, tiles)),
        ],
    )(tokens, stored, *downs)
    received = flipped(partial, "tensor", 1)
    total, partial = chained(total, partial)
    total = products([(1, depth // 2, depth // 2, depth // 2)], [neighbour], total)
    far[1], fetched_up, received, total = chained(far[1], fetched_up, received, total)
    ups = [up] + single_up
    for pair in zip(fetched_up, swap(fetched_up)):
        ups += pair
    near = across(1)
    places = far_places(1)
    tile = tile_of(*[place[3] for place in places])
    total, partial, rounded = call(
        functools.partial(products_and_sum_kernel, tile, depth, places),
        [
            jax.ShapeDtypeStruct((rows, columns), jnp.float32),
            jax.ShapeDtypeStruct((rank, rows), jnp.float32),
            jax.ShapeDtypeStruct((rank, rows), jnp.bfloat16),
        ],
        [ANYWHERE] + [ANYWHERE] * len(places) + [VECTOR] * 3,
        tile_scratch(tile, rows, places, columns),
        [VECTOR] * 3,
    )(frozen_projection_weight, *far[1], total, partial, received)
    flip = CORES
    while flip < tensors // 2:
        partial += flipped(partial, "tensor", flip)
        rounded = partial.astype(jnp.bfloat16)
        flip *= 2
    more = flipped(rounded, "tensor", flip)
    total, partial = chained(total, partial)
    total = products(near_places(1), near, total)
    far[2], ups, total = chained(far[2], ups, total)
    near = across(2)
    total = products(far_places(2), far[2], total)
    near, more, total = chained(near, more, total)

    places = near_places(2)
    tile = tile_of(*[place[3] for place in places])
    return call(
        functools.partial(last_kernel, tile, depth, places, flips, pairs, slots),
        jax.ShapeDtypeStruct((rows, columns), jnp.bfloat16),
        [ANYWHERE] + [ANYWHERE] * len(near) + [VECTOR] * 2 + [ANYWHERE] * (2 + slots),
        [
            pltpu.VMEM((rows, columns), jnp.float32),
            pltpu.VMEM((rank, rows), jnp.float32),
            pltpu.VMEM((rank, rows), jnp.bfloat16),
            pltpu.VMEM((slots * rank, columns), jnp.bfloat16),
        ]
        + tile_scratch(tile, rows, places, columns)
        + [pltpu.SemaphoreType.DMA((2 + slots,))],
    )(frozen_projection_weight, *near, total, stored, partial, more, *ups)


def solution(mesh):
    placed = (
        P(("parts", "adapter"), "tensor"),
        P(("parts", "adapter"), None),
        P(),
        P(None, "tensor"),
        P("adapter", None, "tensor"),
        P("adapter", None, "tensor"),
    )
    return jax.shard_map(
        body,
        mesh=mesh,
        in_specs=placed,
        out_specs=P(("parts", "adapter"), "tensor"),
        check_vma=False,
    )
```

```python
import functools
import math

import jax
import jax.numpy as jnp
from jax import lax
from jax.experimental import pallas as pl
from jax.experimental.pallas import tpu as pltpu
from jax.sharding import PartitionSpec as P

LOWRANK_SCALE = 2.0
CORES = 2
LANES = 128
CUTS = (0.75,)
MIB = 1024 * 1024
FREE = pl.CostEstimate(flops=0, bytes_accessed=0, transcendentals=0)
LONG = pl.CostEstimate(flops=10**11, bytes_accessed=0, transcendentals=0)
ANYWHERE = pl.BlockSpec(memory_space=pl.ANY)
VECTOR = pl.BlockSpec(memory_space=pltpu.VMEM)
SCALAR = pl.BlockSpec(memory_space=pltpu.SMEM)


def flipped(value, axis, flip):
    count = lax.axis_size(axis)
    return lax.ppermute(value, axis, [(i, i ^ flip) for i in range(count)])


def chained(*values):
    return lax.optimization_barrier(values)


def call(kernel, out_shape, in_specs, scratch, out_specs=VECTOR, cost=LONG, mib=24):
    return pl.pallas_call(
        kernel,
        out_shape=out_shape,
        in_specs=in_specs,
        out_specs=out_specs,
        scratch_shapes=scratch,
        cost_estimate=cost,
        compiler_params=pltpu.CompilerParams(vmem_limit_bytes=mib * MIB),
    )


def run_copies(pairs, sems):
    copies = [
        pltpu.make_async_copy(source, target, sems.at[i]) for i, (source, target) in enumerate(pairs)
    ]
    for copy in copies:
        copy.start()
    for copy in copies:
        copy.wait()


def cut_kernel(edges, source_ref, *refs):
    outs, (held_ref, sems) = refs[:-2], refs[-2:]
    steps, rows = held_ref.shape[:2]
    copies = [
        pltpu.make_async_copy(source_ref.at[pl.ds(i * rows, rows)], held_ref.at[i], sems.at[0, i])
        for i in range(steps)
    ]
    for copy in copies:
        copy.start()
    leaving = []
    for i in range(steps):
        copies[i].wait()
        for m, (a, b, out) in enumerate(zip(edges, edges[1:], outs)):
            leaving.append(
                pltpu.make_async_copy(
                    held_ref.at[i, :, pl.ds(a, b - a)],
                    out.at[pl.ds(i * rows, rows)],
                    sems.at[1 + m, i],
                )
            )
            leaving[-1].start()
    for copy in leaving:
        copy.wait()


def order_kernel(down_ref, other_ref, *refs):
    pieces, out_ref, sems = refs[:-2], refs[-2], refs[-1]
    me = lax.axis_index("tensor")
    part, depth = down_ref.shape[0], out_ref.shape[1]
    mine = pl.ds(pl.multiple_of(me * depth, LANES), depth)
    run_copies(
        [
            (piece, out_ref.at[pl.ds(pl.multiple_of((me ^ f) * part, part), part)])
            for f, piece in enumerate((down_ref.at[:, mine], other_ref.at[:, mine], *pieces))
        ],
        sems,
    )


def start_tiles(tile, depth, places, features, weight_ref, held_ref, rows_ref, sems):
    me, t = lax.axis_index("tensor"), 0
    for (flip, first, skip, width), part in zip(places, features):
        for k in range(0, width, tile):
            start = pl.multiple_of((me ^ flip) * depth + first + k, LANES)
            pltpu.make_async_copy(
                weight_ref.at[pl.ds(start, tile)], rows_ref.at[t], sems.at[1, t]
            ).start()
            pltpu.make_async_copy(part.at[:, pl.ds(skip + k, tile)], held_ref.at[t], sems.at[0, t]).start()
            t += 1


def add_tiles(held_ref, rows_ref, sems, total_ref):
    @pl.loop(0, held_ref.shape[0])
    def _(t):
        pltpu.make_async_copy(held_ref.at[t], held_ref.at[t], sems.at[0, t]).wait()
        pltpu.make_async_copy(rows_ref.at[t], rows_ref.at[t], sems.at[1, t]).wait()
        total_ref[...] += jnp.dot(held_ref[t], rows_ref[t], preferred_element_type=jnp.float32)


def tile_scratch(tile, rows, places, columns):
    tiles = sum(place[3] for place in places) // tile
    return [
        pltpu.VMEM((tiles, rows, tile), jnp.bfloat16),
        pltpu.VMEM((tiles, tile, columns), jnp.bfloat16),
        pltpu.SemaphoreType.DMA((2, tiles)),
    ]


def first_kernel(tile, depth, places, slots, placement_ref, tenant_ref, weight_ref, *refs):
    count = len(places)
    features = refs[:count]
    out_ref, stored_ref, held_ref, rows_ref, sems = refs[count:]
    start_tiles(tile, depth, places, features, weight_ref, held_ref, rows_ref, sems)
    out_ref[...] = jnp.zeros_like(out_ref)
    stored = jnp.zeros(stored_ref.shape, jnp.int32)
    for slot in range(slots):
        stored = jnp.where(tenant_ref[...] == slot, placement_ref[slot], stored)
    stored_ref[...] = stored
    add_tiles(held_ref, rows_ref, sems, out_ref)


def products_kernel(tile, depth, places, weight_ref, *refs):
    count = len(places)
    features, given = refs[:count], refs[count]
    out_ref, held_ref, rows_ref, sems = refs[count + 1 :]
    start_tiles(tile, depth, places, features, weight_ref, held_ref, rows_ref, sems)
    out_ref[...] = given[...]
    add_tiles(held_ref, rows_ref, sems, out_ref)


def products_and_sum_kernel(tile, depth, places, weight_ref, *refs):
    count = len(places)
    features, (given, one, other) = refs[:count], refs[count : count + 3]
    out_ref, sum_ref, rounded_ref, held_ref, rows_ref, sems = refs[count + 3 :]
    start_tiles(tile, depth, places, features, weight_ref, held_ref, rows_ref, sems)
    out_ref[...] = given[...]
    sum_ref[...] = one[...] + other[...]
    rounded_ref[...] = sum_ref[...].astype(rounded_ref.dtype)
    add_tiles(held_ref, rows_ref, sems, out_ref)


def owners_of(flips, pairs):
    group, part = lax.axis_index("adapter"), lax.axis_index("parts")
    owners = [group] + [group ^ flip for flip in flips]
    for near, far in pairs:
        owners += [group ^ (near + part * (far - near)), group ^ (far + part * (near - far))]
    return owners


def last_kernel(tile, depth, places, flips, pairs, slots, weight_ref, *refs):
    count = len(places)
    features = refs[:count]
    given, stored_ref, sum_ref, more_ref = refs[count : count + 4]
    ups = refs[count + 4 : count + 4 + slots]
    (
        out_ref, total_ref, sums_ref, received_ref, stacked_ref, held_ref, rows_ref, sems, small_sems,
    ) = refs[count + 4 + slots :]
    rank = ups[0].shape[0]
    copies = [(sum_ref, sums_ref), (more_ref, received_ref)]
    copies += [(up, stacked_ref.at[pl.ds(b * rank, rank)]) for b, up in enumerate(ups)]
    copies = [
        pltpu.make_async_copy(source, target, small_sems.at[i])
        for i, (source, target) in enumerate(copies)
    ]
    for copy in copies:
        copy.start()
    start_tiles(tile, depth, places, features, weight_ref, held_ref, rows_ref, sems)
    total_ref[...] = given[...]
    add_tiles(held_ref, rows_ref, sems, total_ref)
    for copy in copies:
        copy.wait()
    shrunk = (sums_ref[...] + received_ref[...].astype(jnp.float32)).astype(jnp.bfloat16).astype(jnp.float32)
    spread = jnp.concatenate(
        [jnp.where(stored_ref[...] == owner, shrunk, 0.0) for owner in owners_of(flips, pairs)], axis=0
    )
    expanded = jnp.dot(
        spread.T.astype(jnp.bfloat16), stacked_ref[...], preferred_element_type=jnp.float32
    )
    expanded = expanded.astype(jnp.bfloat16).astype(jnp.float32)
    out_ref[...] = (total_ref[...] + LOWRANK_SCALE * expanded).astype(out_ref.dtype)


def shrink_kernel(tile, flips, pairs, slots, tokens_ref, stored_ref, *refs):
    downs, out_ref, held_ref, down_ref, sums_ref, sems = (
        refs[:slots], refs[slots], *refs[slots + 1 :]
    )
    rank = downs[0].shape[0]
    tiles = tokens_ref.shape[1] // tile
    for k in range(tiles):
        here = pl.ds(k * tile, tile)
        pltpu.make_async_copy(tokens_ref.at[:, here], held_ref.at[k], sems.at[0, k]).start()
        for b, down in enumerate(downs):
            pltpu.make_async_copy(
                down.at[:, here], down_ref.at[k, pl.ds(b * rank, rank)], sems.at[1 + b, k]
            ).start()
    sums_ref[...] = jnp.zeros_like(sums_ref)

    @pl.loop(0, tiles)
    def _(k):
        pltpu.make_async_copy(held_ref.at[k], held_ref.at[k], sems.at[0, k]).wait()
        for b in range(slots):
            block = down_ref.at[k, pl.ds(b * rank, rank)]
            pltpu.make_async_copy(block, block, sems.at[1 + b, k]).wait()
        sums_ref[...] += lax.dot_general(
            held_ref[k], down_ref[k], (((1,), (1,)), ((), ())), preferred_element_type=jnp.float32
        )

    sums = sums_ref[...].T
    total = jnp.zeros(out_ref.shape, jnp.float32)
    for b, owner in enumerate(owners_of(flips, pairs)):
        total += jnp.where(stored_ref[...] == owner, sums[b * rank : (b + 1) * rank], 0.0)
    out_ref[...] = total


def body(
    tokens, tenant, placement, frozen_projection_weight, lowrank_down_weight, lowrank_up_weight
):
    rows, depth = tokens.shape
    slots = placement.shape[0]
    tensors = lax.axis_size("tensor")
    groups = lax.axis_size("adapter")
    parts = lax.axis_size("parts")
    me = lax.axis_index("tensor")
    rank, columns = lowrank_up_weight.shape[1:]
    edges = [0] + [int(depth * cut) // LANES * LANES for cut in CUTS] + [depth]
    tile = math.gcd(*edges)

    down = lowrank_down_weight[0].T

    def slice_for(array, flip):
        return lax.dynamic_slice_in_dim(array, (me ^ flip) * depth, depth, axis=1)

    other = flipped(down, "tensor", 1)
    pieces = [slice_for(down, flip) for flip in range(CORES, tensors)]
    uncut, pieces = chained(tokens, pieces)
    steps = 6
    chunks = list(
        call(
            functools.partial(cut_kernel, edges),
            [jax.ShapeDtypeStruct((rows, b - a), tokens.dtype) for a, b in zip(edges, edges[1:])],
            [ANYWHERE],
            [
                pltpu.VMEM((steps, rows // steps, depth), tokens.dtype),
                pltpu.SemaphoreType.DMA((len(edges), steps)),
            ],
            [ANYWHERE] * (len(edges) - 1),
            cost=FREE,
            mib=56,
        )(uncut)
    )
    pieces = [flipped(piece, "tensor", CORES + i) for i, piece in enumerate(pieces)]
    if down.shape[0] % 16 == 0:
        own = call(
            order_kernel,
            jax.ShapeDtypeStruct((rank, depth), down.dtype),
            [ANYWHERE] * tensors,
            [pltpu.SemaphoreType.DMA((tensors,))],
            VECTOR,
            cost=FREE,
        )(down, other, *pieces)
    else:
        pieces = [slice_for(down, 0), slice_for(other, 0)] + pieces
        none = jnp.zeros((), down.dtype)
        own = jnp.concatenate(
            [sum(jnp.where((me ^ f) == j, pieces[f], none) for f in range(tensors)) for j in range(tensors)],
            axis=0,
        )

    hops = range(CORES, tensors, CORES)

    def send(m):
        return [flipped(chunks[m], "tensor", hop) for hop in hops]

    far = [send(0)]

    def across(m):
        return [flipped(value, "tensor", 1) for value in far[m]]

    def far_places(m):
        return [(hop, edges[m], 0, edges[m + 1] - edges[m]) for hop in hops]

    def near_places(m):
        return [(hop ^ 1, edges[m], 0, edges[m + 1] - edges[m]) for hop in hops]

    def products(places, features, total):
        return call(
            functools.partial(products_kernel, tile, depth, places),
            jax.ShapeDtypeStruct((rows, columns), jnp.float32),
            [ANYWHERE] + [ANYWHERE] * len(features) + [VECTOR],
            tile_scratch(tile, rows, places, columns),
        )(frozen_projection_weight, *features, total)

    flips = list(range(1, groups))
    pairs = []
    if parts == 2:
        while len(flips) > 1:
            pairs.append((flips.pop(-2), flips.pop(-1)))
    routes = [
        [(p * groups + z, p * groups + (z ^ pair[p])) for p in range(parts) for z in range(groups)]
        for pair in pairs
    ]

    def fetch_far(value):
        return [lax.ppermute(value, ("parts", "adapter"), route) for route in routes]

    def fetch_near(value):
        return [flipped(value, "adapter", flip) for flip in flips]

    def swap(values):
        return [flipped(value, "parts", 1) for value in values]

    own, here = chained(own, tokens)
    fetched = fetch_far(own)
    places = [(0, 0, 0, depth // 2)]
    total, stored = call(
        functools.partial(first_kernel, tile, depth, places, slots),
        [
            jax.ShapeDtypeStruct((rows, columns), jnp.float32),
            jax.ShapeDtypeStruct((1, rows), jnp.int32),
        ],
        [SCALAR, VECTOR, ANYWHERE, ANYWHERE],
        tile_scratch(tile, rows, places, columns),
        [VECTOR, VECTOR],
    )(placement, tenant.reshape(1, rows), frozen_projection_weight, here)
    total, own, there, chunks[1] = chained(total, own, tokens, chunks[1])
    neighbour = flipped(there, "tensor", 1)
    far.append(send(1))
    single = fetch_near(own)
    total = products([(0, depth // 2, depth // 2, depth // 2)], [here], total)
    fetched, neighbour, total = chained(fetched, neighbour, total)
    swapped = swap(fetched)
    total = products([(1, 0, 0, depth // 2)], [neighbour], total)
    total, up = chained(total, lowrank_up_weight[0])
    fetched_up, single_up = fetch_far(up), fetch_near(up)
    single, swapped, total = chained(single, swapped, total)
    downs = [own] + single
    for pair in zip(fetched, swapped):
        downs += pair

    tiles = depth // tile
    partial = call(
        functools.partial(shrink_kernel, tile, flips, pairs, slots),
        jax.ShapeDtypeStruct((rank, rows), jnp.float32),
        [ANYWHERE, VECTOR] + [ANYWHERE] * slots,
        [
            pltpu.VMEM((tiles, rows, tile), jnp.bfloat16),
            pltpu.VMEM((tiles, slots * rank, tile), jnp.bfloat16),
            pltpu.VMEM((rows, slots * rank), jnp.float32),
            pltpu.SemaphoreType.DMA((1 + slots, tiles)),
        ],
    )(tokens, stored, *downs)
    received = flipped(partial, "tensor", 1)
    total, partial = chained(total, partial)
    total = products([(1, depth // 2, depth // 2, depth // 2)], [neighbour], total)
    far[0], fetched_up, received, total = chained(far[0], fetched_up, received, total)
    ups = [up] + single_up
    for pair in zip(fetched_up, swap(fetched_up)):
        ups += pair
    near = across(0)
    places = far_places(0)
    total, partial, rounded = call(
        functools.partial(products_and_sum_kernel, tile, depth, places),
        [
            jax.ShapeDtypeStruct((rows, columns), jnp.float32),
            jax.ShapeDtypeStruct((rank, rows), jnp.float32),
            jax.ShapeDtypeStruct((rank, rows), jnp.bfloat16),
        ],
        [ANYWHERE] + [ANYWHERE] * len(places) + [VECTOR] * 3,
        tile_scratch(tile, rows, places, columns),
        [VECTOR] * 3,
    )(frozen_projection_weight, *far[0], total, partial, received)
    flip = CORES
    while flip < tensors // 2:
        partial += flipped(partial, "tensor", flip)
        rounded = partial.astype(jnp.bfloat16)
        flip *= 2
    more = flipped(rounded, "tensor", flip)
    total, partial = chained(total, partial)
    total = products(near_places(0), near, total)
    far[1], ups, total = chained(far[1], ups, total)
    near = across(1)
    total = products(far_places(1), far[1], total)
    near, more, total = chained(near, more, total)

    places = near_places(1)
    return call(
        functools.partial(last_kernel, tile, depth, places, flips, pairs, slots),
        jax.ShapeDtypeStruct((rows, columns), jnp.bfloat16),
        [ANYWHERE] + [ANYWHERE] * len(near) + [VECTOR] * 2 + [ANYWHERE] * (2 + slots),
        [
            pltpu.VMEM((rows, columns), jnp.float32),
            pltpu.VMEM((rank, rows), jnp.float32),
            pltpu.VMEM((rank, rows), jnp.bfloat16),
            pltpu.VMEM((slots * rank, columns), jnp.bfloat16),
        ]
        + tile_scratch(tile, rows, places, columns)
        + [pltpu.SemaphoreType.DMA((2 + slots,))],
    )(frozen_projection_weight, *near, total, stored, partial, more, *ups)


def solution(mesh):
    placed = (
        P(("parts", "adapter"), "tensor"),
        P(("parts", "adapter"), None),
        P(),
        P(None, "tensor"),
        P("adapter", None, "tensor"),
        P("adapter", None, "tensor"),
    )
    return jax.shard_map(
        body,
        mesh=mesh,
        in_specs=placed,
        out_specs=P(("parts", "adapter"), "tensor"),
        check_vma=False,
    )
```

```python
import functools
import math

import jax
import jax.numpy as jnp
from jax import lax
from jax.experimental import pallas as pl
from jax.experimental.pallas import tpu as pltpu
from jax.sharding import PartitionSpec as P

LOWRANK_SCALE = 2.0
CORES = 2
LANES = 128
CUTS = (0.75,)
MIB = 1024 * 1024
FREE = pl.CostEstimate(flops=0, bytes_accessed=0, transcendentals=0)
LONG = pl.CostEstimate(flops=10**11, bytes_accessed=0, transcendentals=0)
ANYWHERE = pl.BlockSpec(memory_space=pl.ANY)
VECTOR = pl.BlockSpec(memory_space=pltpu.VMEM)
SCALAR = pl.BlockSpec(memory_space=pltpu.SMEM)


def flipped(value, axis, flip):
    count = lax.axis_size(axis)
    return lax.ppermute(value, axis, [(i, i ^ flip) for i in range(count)])


def chained(*values):
    return lax.optimization_barrier(values)


def call(kernel, out_shape, in_specs, scratch, out_specs=VECTOR, cost=LONG, mib=24):
    return pl.pallas_call(
        kernel,
        out_shape=out_shape,
        in_specs=in_specs,
        out_specs=out_specs,
        scratch_shapes=scratch,
        cost_estimate=cost,
        compiler_params=pltpu.CompilerParams(vmem_limit_bytes=mib * MIB),
    )


def run_copies(pairs, sems):
    copies = [
        pltpu.make_async_copy(source, target, sems.at[i]) for i, (source, target) in enumerate(pairs)
    ]
    for copy in copies:
        copy.start()
    for copy in copies:
        copy.wait()


def cut_kernel(edges, source_ref, *refs):
    outs, (held_ref, sems) = refs[:-2], refs[-2:]
    steps, rows = held_ref.shape[:2]
    copies = [
        pltpu.make_async_copy(source_ref.at[pl.ds(i * rows, rows)], held_ref.at[i], sems.at[0, i])
        for i in range(steps)
    ]
    for copy in copies:
        copy.start()
    leaving = []
    for i in range(steps):
        copies[i].wait()
        for m, (a, b, out) in enumerate(zip(edges, edges[1:], outs)):
            leaving.append(
                pltpu.make_async_copy(
                    held_ref.at[i, :, pl.ds(a, b - a)],
                    out.at[pl.ds(i * rows, rows)],
                    sems.at[1 + m, i],
                )
            )
            leaving[-1].start()
    for copy in leaving:
        copy.wait()


def order_kernel(rank_part, *refs):
    pieces, out_ref, sems = refs[:-2], refs[-2], refs[-1]
    me = lax.axis_index("tensor")
    run_copies(
        [
            (piece, out_ref.at[pl.ds(pl.multiple_of((me ^ f) * rank_part, rank_part), rank_part)])
            for f, piece in enumerate(pieces)
        ],
        sems,
    )


def start_tiles(tile, depth, places, features, weight_ref, held_ref, rows_ref, sems):
    me, t = lax.axis_index("tensor"), 0
    for (flip, first, skip, width), part in zip(places, features):
        for k in range(0, width, tile):
            start = pl.multiple_of((me ^ flip) * depth + first + k, LANES)
            pltpu.make_async_copy(
                weight_ref.at[pl.ds(start, tile)], rows_ref.at[t], sems.at[1, t]
            ).start()
            pltpu.make_async_copy(part.at[:, pl.ds(skip + k, tile)], held_ref.at[t], sems.at[0, t]).start()
            t += 1


def add_tiles(held_ref, rows_ref, sems, total_ref, given_ref):
    pltpu.make_async_copy(held_ref.at[0], held_ref.at[0], sems.at[0, 0]).wait()
    pltpu.make_async_copy(rows_ref.at[0], rows_ref.at[0], sems.at[1, 0]).wait()
    total_ref[...] = given_ref[...] + jnp.dot(
        held_ref[0], rows_ref[0], preferred_element_type=jnp.float32
    )
    if held_ref.shape[0] == 1:
        return

    @pl.loop(1, held_ref.shape[0])
    def _(t):
        pltpu.make_async_copy(held_ref.at[t], held_ref.at[t], sems.at[0, t]).wait()
        pltpu.make_async_copy(rows_ref.at[t], rows_ref.at[t], sems.at[1, t]).wait()
        total_ref[...] += jnp.dot(held_ref[t], rows_ref[t], preferred_element_type=jnp.float32)


def tile_scratch(tile, rows, places, columns):
    tiles = sum(place[3] for place in places) // tile
    return [
        pltpu.VMEM((tiles, rows, tile), jnp.bfloat16),
        pltpu.VMEM((tiles, tile, columns), jnp.bfloat16),
        pltpu.SemaphoreType.DMA((2, tiles)),
    ]


def first_kernel(tile, depth, places, slots, placement_ref, tenant_ref, weight_ref, *refs):
    count = len(places)
    features = refs[:count]
    out_ref, stored_ref, held_ref, rows_ref, sems = refs[count:]
    start_tiles(tile, depth, places, features, weight_ref, held_ref, rows_ref, sems)
    out_ref[...] = jnp.zeros_like(out_ref)
    stored = jnp.zeros(stored_ref.shape, jnp.int32)
    for slot in range(slots):
        stored = jnp.where(tenant_ref[...] == slot, placement_ref[slot], stored)
    stored_ref[...] = stored
    add_tiles(held_ref, rows_ref, sems, out_ref, out_ref)


def products_kernel(tile, depth, places, weight_ref, *refs):
    count = len(places)
    features, given = refs[:count], refs[count]
    out_ref, held_ref, rows_ref, sems = refs[count + 1 :]
    start_tiles(tile, depth, places, features, weight_ref, held_ref, rows_ref, sems)
    add_tiles(held_ref, rows_ref, sems, out_ref, given)


def owners_of(flips, pairs):
    group, part = lax.axis_index("adapter"), lax.axis_index("parts")
    owners = [group] + [group ^ flip for flip in flips]
    for near, far in pairs:
        owners += [group ^ (near + part * (far - near)), group ^ (far + part * (near - far))]
    return owners


def last_kernel(tile, depth, places, flips, pairs, slots, weight_ref, *refs):
    count = len(places)
    features = refs[:count]
    given, stored_ref, sum_ref, more_ref = refs[count : count + 4]
    ups = refs[count + 4 : count + 4 + slots]
    (
        out_ref, total_ref, sums_ref, received_ref, stacked_ref, held_ref, rows_ref, sems, small_sems,
    ) = refs[count + 4 + slots :]
    rank = ups[0].shape[0]
    copies = [(sum_ref, sums_ref), (more_ref, received_ref)]
    copies += [(up, stacked_ref.at[pl.ds(b * rank, rank)]) for b, up in enumerate(ups)]
    copies = [
        pltpu.make_async_copy(source, target, small_sems.at[i])
        for i, (source, target) in enumerate(copies)
    ]
    for copy in copies:
        copy.start()
    start_tiles(tile, depth, places, features, weight_ref, held_ref, rows_ref, sems)
    add_tiles(held_ref, rows_ref, sems, total_ref, given)
    for copy in copies:
        copy.wait()
    shrunk = (sums_ref[...] + received_ref[...].astype(jnp.float32)).astype(jnp.bfloat16).astype(jnp.float32)
    spread = jnp.concatenate(
        [jnp.where(stored_ref[...] == owner, shrunk, 0.0) for owner in owners_of(flips, pairs)], axis=0
    )
    expanded = lax.dot_general(
        spread.astype(jnp.bfloat16),
        stacked_ref[...],
        (((0,), (0,)), ((), ())),
        preferred_element_type=jnp.float32,
    )
    expanded = expanded.astype(jnp.bfloat16).astype(jnp.float32)
    out_ref[...] = (total_ref[...] + LOWRANK_SCALE * expanded).astype(out_ref.dtype)


def shrink_kernel(tile, flips, pairs, slots, tokens_ref, stored_ref, *refs):
    downs, out_ref, held_ref, down_ref, sums_ref, sems = (
        refs[:slots], refs[slots], *refs[slots + 1 :]
    )
    rank = downs[0].shape[0]
    tiles = tokens_ref.shape[1] // tile
    for k in range(tiles):
        here = pl.ds(k * tile, tile)
        pltpu.make_async_copy(tokens_ref.at[:, here], held_ref.at[k], sems.at[0, k]).start()
        for b, down in enumerate(downs):
            pltpu.make_async_copy(
                down.at[:, here], down_ref.at[k, pl.ds(b * rank, rank)], sems.at[1 + b, k]
            ).start()
    sums_ref[...] = jnp.zeros_like(sums_ref)

    @pl.loop(0, tiles)
    def _(k):
        pltpu.make_async_copy(held_ref.at[k], held_ref.at[k], sems.at[0, k]).wait()
        for b in range(slots):
            block = down_ref.at[k, pl.ds(b * rank, rank)]
            pltpu.make_async_copy(block, block, sems.at[1 + b, k]).wait()
        sums_ref[...] += lax.dot_general(
            held_ref[k], down_ref[k], (((1,), (1,)), ((), ())), preferred_element_type=jnp.float32
        )

    sums = sums_ref[...].T
    total = jnp.zeros(out_ref.shape, jnp.float32)
    for b, owner in enumerate(owners_of(flips, pairs)):
        total += jnp.where(stored_ref[...] == owner, sums[b * rank : (b + 1) * rank], 0.0)
    out_ref[...] = total


def body(
    tokens, tenant, placement, frozen_projection_weight, lowrank_down_weight, lowrank_up_weight
):
    rows, depth = tokens.shape
    slots = placement.shape[0]
    tensors = lax.axis_size("tensor")
    groups = lax.axis_size("adapter")
    parts = lax.axis_size("parts")
    me = lax.axis_index("tensor")
    rank, columns = lowrank_up_weight.shape[1:]
    edges = [0] + [int(depth * cut) // LANES * LANES for cut in CUTS] + [depth]
    tile = math.gcd(*edges)

    down = lowrank_down_weight[0].T
    pieces = [
        lax.dynamic_slice_in_dim(down, (me ^ flip) * depth, depth, axis=1)
        for flip in range(tensors)
    ]
    uncut, pieces = chained(tokens, pieces)
    steps = 6
    chunks = list(
        call(
            functools.partial(cut_kernel, edges),
            [jax.ShapeDtypeStruct((rows, b - a), tokens.dtype) for a, b in zip(edges, edges[1:])],
            [ANYWHERE],
            [
                pltpu.VMEM((steps, rows // steps, depth), tokens.dtype),
                pltpu.SemaphoreType.DMA((len(edges), steps)),
            ],
            [ANYWHERE] * (len(edges) - 1),
            cost=FREE,
            mib=56,
        )(uncut)
    )
    pieces = [pieces[0]] + [flipped(pieces[f], "tensor", f) for f in range(1, tensors)]
    pieces[1], here = chained(pieces[1], tokens)
    neighbour = flipped(here, "tensor", 1)
    if down.shape[0] % 16 == 0:
        own = call(
            functools.partial(order_kernel, down.shape[0]),
            jax.ShapeDtypeStruct((rank, depth), down.dtype),
            [ANYWHERE] * tensors,
            [pltpu.SemaphoreType.DMA((tensors,))],
            ANYWHERE,
            cost=FREE,
        )(*pieces)
    else:
        none = jnp.zeros((), down.dtype)
        own = jnp.concatenate(
            [sum(jnp.where((me ^ f) == j, pieces[f], none) for f in range(tensors)) for j in range(tensors)],
            axis=0,
        )

    hops = range(CORES, tensors, CORES)

    def send(m):
        return [flipped(chunks[m], "tensor", hop) for hop in hops]

    far = [send(0)]

    def across(m):
        return [flipped(value, "tensor", 1) for value in far[m]]

    def far_places(m):
        return [(hop, edges[m], 0, edges[m + 1] - edges[m]) for hop in hops]

    def near_places(m):
        return [(hop ^ 1, edges[m], 0, edges[m + 1] - edges[m]) for hop in hops]

    def products(places, features, total):
        return call(
            functools.partial(products_kernel, tile, depth, places),
            jax.ShapeDtypeStruct((rows, columns), jnp.float32),
            [ANYWHERE] + [ANYWHERE] * len(features) + [VECTOR],
            tile_scratch(tile, rows, places, columns),
        )(frozen_projection_weight, *features, total)

    flips = list(range(1, groups))
    pairs = []
    if parts == 2:
        while len(flips) > 1:
            pairs.append((flips.pop(-2), flips.pop(-1)))
    routes = [
        [(p * groups + z, p * groups + (z ^ pair[p])) for p in range(parts) for z in range(groups)]
        for pair in pairs
    ]

    def fetch_far(value):
        return [lax.ppermute(value, ("parts", "adapter"), route) for route in routes]

    def fetch_near(value):
        return [flipped(value, "adapter", flip) for flip in flips]

    def swap(values):
        return [flipped(value, "parts", 1) for value in values]

    own, here = chained(own, tokens)
    fetched = fetch_far(own)
    places = [(0, 0, 0, depth // 2)]
    total, stored = call(
        functools.partial(first_kernel, tile, depth, places, slots),
        [
            jax.ShapeDtypeStruct((rows, columns), jnp.float32),
            jax.ShapeDtypeStruct((1, rows), jnp.int32),
        ],
        [SCALAR, VECTOR, ANYWHERE, ANYWHERE],
        tile_scratch(tile, rows, places, columns),
        [VECTOR, VECTOR],
    )(placement, tenant.reshape(1, rows), frozen_projection_weight, here)
    total, own, up, neighbour, chunks[1] = chained(
        total, own, lowrank_up_weight[0], neighbour, chunks[1]
    )
    far.append(send(1))
    single, single_up = fetch_near(own), fetch_near(up)
    total = products([(0, depth // 2, depth // 2, depth // 2)], [here], total)
    fetched, single_up, total = chained(fetched, single_up, total)
    swapped = swap(fetched)
    total, neighbour = chained(total, neighbour)
    total = products([(1, 0, 0, depth)], [neighbour], total)
    total, up = chained(total, up)
    fetched_up = fetch_far(up)
    single, swapped, total = chained(single, swapped, total)
    downs = [own] + single
    for pair in zip(fetched, swapped):
        downs += pair

    tiles = depth // tile
    partial = call(
        functools.partial(shrink_kernel, tile, flips, pairs, slots),
        jax.ShapeDtypeStruct((rank, rows), jnp.float32),
        [ANYWHERE, VECTOR] + [ANYWHERE] * slots,
        [
            pltpu.VMEM((tiles, rows, tile), jnp.bfloat16),
            pltpu.VMEM((tiles, slots * rank, tile), jnp.bfloat16),
            pltpu.VMEM((rows, slots * rank), jnp.float32),
            pltpu.SemaphoreType.DMA((1 + slots, tiles)),
        ],
    )(tokens, stored, *downs)
    far[0], fetched_up, partial = chained(far[0], fetched_up, partial)
    swapped_up = swap(fetched_up)
    ups = [up] + single_up
    for pair in zip(fetched_up, swapped_up):
        ups += pair
    near = across(0)
    total = products(far_places(0), far[0], total)
    flip = 1
    while flip < tensors // 2:
        received = flipped(partial, "tensor", flip)
        if flip == 1:
            received, total = chained(received, total)
        partial += received
        flip *= 2
    more = flipped(partial.astype(jnp.bfloat16), "tensor", flip)
    total, partial = chained(total, partial)
    total = products(near_places(0), near, total)
    far[1], ups, total = chained(far[1], ups, total)
    near = across(1)
    total = products(far_places(1), far[1], total)
    near, more, total = chained(near, more, total)

    places = near_places(1)
    return call(
        functools.partial(last_kernel, tile, depth, places, flips, pairs, slots),
        jax.ShapeDtypeStruct((rows, columns), jnp.bfloat16),
        [ANYWHERE] + [ANYWHERE] * len(near) + [VECTOR] * 2 + [ANYWHERE] * (2 + slots),
        [
            pltpu.VMEM((rows, columns), jnp.float32),
            pltpu.VMEM((rank, rows), jnp.float32),
            pltpu.VMEM((rank, rows), jnp.bfloat16),
            pltpu.VMEM((slots * rank, columns), jnp.bfloat16),
        ]
        + tile_scratch(tile, rows, places, columns)
        + [pltpu.SemaphoreType.DMA((2 + slots,))],
    )(frozen_projection_weight, *near, total, stored, partial, more, *ups)


def solution(mesh):
    placed = (
        P(("parts", "adapter"), "tensor"),
        P(("parts", "adapter"), None),
        P(),
        P(None, "tensor"),
        P("adapter", None, "tensor"),
        P("adapter", None, "tensor"),
    )
    return jax.shard_map(
        body,
        mesh=mesh,
        in_specs=placed,
        out_specs=P(("parts", "adapter"), "tensor"),
        check_vma=False,
    )
```

```python
import functools
import math

import jax
import jax.numpy as jnp
from jax import lax
from jax.experimental import pallas as pl
from jax.experimental.pallas import tpu as pltpu
from jax.sharding import PartitionSpec as P

LOWRANK_SCALE = 2.0
CORES = 2
LANES = 128
CUTS = (0.75,)
MIB = 1024 * 1024
FREE = pl.CostEstimate(flops=0, bytes_accessed=0, transcendentals=0)
LONG = pl.CostEstimate(flops=10**11, bytes_accessed=0, transcendentals=0)
ANYWHERE = pl.BlockSpec(memory_space=pl.ANY)
VECTOR = pl.BlockSpec(memory_space=pltpu.VMEM)
SCALAR = pl.BlockSpec(memory_space=pltpu.SMEM)


def flipped(value, axis, flip):
    count = lax.axis_size(axis)
    return lax.ppermute(value, axis, [(i, i ^ flip) for i in range(count)])


def chained(*values):
    return lax.optimization_barrier(values)


def call(kernel, out_shape, in_specs, scratch, out_specs=VECTOR, cost=LONG, mib=24):
    return pl.pallas_call(
        kernel,
        out_shape=out_shape,
        in_specs=in_specs,
        out_specs=out_specs,
        scratch_shapes=scratch,
        cost_estimate=cost,
        compiler_params=pltpu.CompilerParams(vmem_limit_bytes=mib * MIB),
    )


def run_copies(pairs, sems):
    copies = [
        pltpu.make_async_copy(source, target, sems.at[i]) for i, (source, target) in enumerate(pairs)
    ]
    for copy in copies:
        copy.start()
    for copy in copies:
        copy.wait()


def cut_kernel(edges, source_ref, *refs):
    outs, (held_ref, sems) = refs[:-2], refs[-2:]
    steps, rows = held_ref.shape[:2]
    copies = [
        pltpu.make_async_copy(source_ref.at[pl.ds(i * rows, rows)], held_ref.at[i], sems.at[0, i])
        for i in range(steps)
    ]
    for copy in copies:
        copy.start()
    leaving = []
    for i in range(steps):
        copies[i].wait()
        for m, (a, b, out) in enumerate(zip(edges, edges[1:], outs)):
            leaving.append(
                pltpu.make_async_copy(
                    held_ref.at[i, :, pl.ds(a, b - a)],
                    out.at[pl.ds(i * rows, rows)],
                    sems.at[1 + m, i],
                )
            )
            leaving[-1].start()
    for copy in leaving:
        copy.wait()


def order_kernel(rank_part, *refs):
    pieces, out_ref, sems = refs[:-2], refs[-2], refs[-1]
    me = lax.axis_index("tensor")
    run_copies(
        [
            (piece, out_ref.at[pl.ds(pl.multiple_of((me ^ f) * rank_part, rank_part), rank_part)])
            for f, piece in enumerate(pieces)
        ],
        sems,
    )


def start_tiles(tile, depth, places, features, weight_ref, held_ref, rows_ref, sems):
    me, t = lax.axis_index("tensor"), 0
    for (flip, first, skip, width), part in zip(places, features):
        for k in range(0, width, tile):
            start = pl.multiple_of((me ^ flip) * depth + first + k, LANES)
            pltpu.make_async_copy(
                weight_ref.at[pl.ds(start, tile)], rows_ref.at[t], sems.at[1, t]
            ).start()
            pltpu.make_async_copy(part.at[:, pl.ds(skip + k, tile)], held_ref.at[t], sems.at[0, t]).start()
            t += 1


def add_tiles(held_ref, rows_ref, sems, total_ref, given_ref):
    pltpu.make_async_copy(held_ref.at[0], held_ref.at[0], sems.at[0, 0]).wait()
    pltpu.make_async_copy(rows_ref.at[0], rows_ref.at[0], sems.at[1, 0]).wait()
    total_ref[...] = given_ref[...] + jnp.dot(
        held_ref[0], rows_ref[0], preferred_element_type=jnp.float32
    )
    if held_ref.shape[0] == 1:
        return

    @pl.loop(1, held_ref.shape[0])
    def _(t):
        pltpu.make_async_copy(held_ref.at[t], held_ref.at[t], sems.at[0, t]).wait()
        pltpu.make_async_copy(rows_ref.at[t], rows_ref.at[t], sems.at[1, t]).wait()
        total_ref[...] += jnp.dot(held_ref[t], rows_ref[t], preferred_element_type=jnp.float32)


def tile_scratch(tile, rows, places, columns):
    tiles = sum(place[3] for place in places) // tile
    return [
        pltpu.VMEM((tiles, rows, tile), jnp.bfloat16),
        pltpu.VMEM((tiles, tile, columns), jnp.bfloat16),
        pltpu.SemaphoreType.DMA((2, tiles)),
    ]


def first_kernel(tile, depth, places, slots, placement_ref, tenant_ref, weight_ref, *refs):
    count = len(places)
    features = refs[:count]
    out_ref, stored_ref, held_ref, rows_ref, sems = refs[count:]
    start_tiles(tile, depth, places, features, weight_ref, held_ref, rows_ref, sems)
    out_ref[...] = jnp.zeros_like(out_ref)
    stored = jnp.zeros(stored_ref.shape, jnp.int32)
    for slot in range(slots):
        stored = jnp.where(tenant_ref[...] == slot, placement_ref[slot], stored)
    stored_ref[...] = stored
    add_tiles(held_ref, rows_ref, sems, out_ref, out_ref)


def products_kernel(tile, depth, places, weight_ref, *refs):
    count = len(places)
    features, given = refs[:count], refs[count]
    out_ref, held_ref, rows_ref, sems = refs[count + 1 :]
    start_tiles(tile, depth, places, features, weight_ref, held_ref, rows_ref, sems)
    add_tiles(held_ref, rows_ref, sems, out_ref, given)


def owners_of(flips, pairs):
    group, part = lax.axis_index("adapter"), lax.axis_index("parts")
    owners = [group] + [group ^ flip for flip in flips]
    for near, far in pairs:
        owners += [group ^ (near + part * (far - near)), group ^ (far + part * (near - far))]
    return owners


def last_kernel(depth, places, flips, pairs, slots, weight_ref, *refs):
    count = len(places)
    features = refs[:count]
    given, stored_ref, sum_ref, more_ref = refs[count : count + 4]
    ups = refs[count + 4 : count + 4 + slots]
    out_ref, total_ref, sums_ref, received_ref, stacked_ref, small_sems = refs[count + 4 + slots :]
    rank = ups[0].shape[0]
    copies = [(sum_ref, sums_ref), (more_ref, received_ref)]
    copies += [(up, stacked_ref.at[pl.ds(b * rank, rank)]) for b, up in enumerate(ups)]
    copies = [
        pltpu.make_async_copy(source, target, small_sems.at[i])
        for i, (source, target) in enumerate(copies)
    ]
    for copy in copies:
        copy.start()
    me, sum_so_far = lax.axis_index("tensor"), given
    for (flip, first, skip, width), part in zip(places, features):
        start = pl.multiple_of((me ^ flip) * depth + first, LANES)
        total_ref[...] = sum_so_far[...] + jnp.dot(
            part[:, skip : skip + width],
            weight_ref[pl.ds(start, width)],
            preferred_element_type=jnp.float32,
        )
        sum_so_far = total_ref
    for copy in copies:
        copy.wait()
    shrunk = (sums_ref[...] + received_ref[...].astype(jnp.float32)).astype(jnp.bfloat16).astype(jnp.float32)
    spread = jnp.concatenate(
        [jnp.where(stored_ref[...] == owner, shrunk, 0.0) for owner in owners_of(flips, pairs)], axis=0
    )
    expanded = lax.dot_general(
        spread.astype(jnp.bfloat16),
        stacked_ref[...],
        (((0,), (0,)), ((), ())),
        preferred_element_type=jnp.float32,
    )
    expanded = expanded.astype(jnp.bfloat16).astype(jnp.float32)
    out_ref[...] = (total_ref[...] + LOWRANK_SCALE * expanded).astype(out_ref.dtype)


def shrink_kernel(tile, flips, pairs, slots, tokens_ref, stored_ref, *refs):
    downs, out_ref, held_ref, down_ref, sums_ref, sems = (
        refs[:slots], refs[slots], *refs[slots + 1 :]
    )
    rank = downs[0].shape[0]
    tiles = tokens_ref.shape[1] // tile
    for k in range(tiles):
        here = pl.ds(k * tile, tile)
        pltpu.make_async_copy(tokens_ref.at[:, here], held_ref.at[k], sems.at[0, k]).start()
        for b, down in enumerate(downs):
            pltpu.make_async_copy(
                down.at[:, here], down_ref.at[k, pl.ds(b * rank, rank)], sems.at[1 + b, k]
            ).start()
    sums_ref[...] = jnp.zeros_like(sums_ref)

    @pl.loop(0, tiles)
    def _(k):
        pltpu.make_async_copy(held_ref.at[k], held_ref.at[k], sems.at[0, k]).wait()
        for b in range(slots):
            block = down_ref.at[k, pl.ds(b * rank, rank)]
            pltpu.make_async_copy(block, block, sems.at[1 + b, k]).wait()
        sums_ref[...] += lax.dot_general(
            held_ref[k], down_ref[k], (((1,), (1,)), ((), ())), preferred_element_type=jnp.float32
        )

    sums = sums_ref[...].T
    total = jnp.zeros(out_ref.shape, jnp.float32)
    for b, owner in enumerate(owners_of(flips, pairs)):
        total += jnp.where(stored_ref[...] == owner, sums[b * rank : (b + 1) * rank], 0.0)
    out_ref[...] = total


def body(
    tokens, tenant, placement, frozen_projection_weight, lowrank_down_weight, lowrank_up_weight
):
    rows, depth = tokens.shape
    slots = placement.shape[0]
    tensors = lax.axis_size("tensor")
    groups = lax.axis_size("adapter")
    parts = lax.axis_size("parts")
    me = lax.axis_index("tensor")
    rank, columns = lowrank_up_weight.shape[1:]
    edges = [0] + [int(depth * cut) // LANES * LANES for cut in CUTS] + [depth]
    tile = math.gcd(*edges)

    down = lowrank_down_weight[0].T
    pieces = [
        lax.dynamic_slice_in_dim(down, (me ^ flip) * depth, depth, axis=1)
        for flip in range(tensors)
    ]
    uncut, pieces = chained(tokens, pieces)
    steps = 6
    chunks = list(
        call(
            functools.partial(cut_kernel, edges),
            [jax.ShapeDtypeStruct((rows, b - a), tokens.dtype) for a, b in zip(edges, edges[1:])],
            [ANYWHERE],
            [
                pltpu.VMEM((steps, rows // steps, depth), tokens.dtype),
                pltpu.SemaphoreType.DMA((len(edges), steps)),
            ],
            [ANYWHERE] * (len(edges) - 1),
            cost=FREE,
            mib=56,
        )(uncut)
    )
    pieces = [pieces[0]] + [flipped(pieces[f], "tensor", f) for f in range(1, tensors)]
    pieces[1], here = chained(pieces[1], tokens)
    neighbour = flipped(here, "tensor", 1)
    if down.shape[0] % 16 == 0:
        own = call(
            functools.partial(order_kernel, down.shape[0]),
            jax.ShapeDtypeStruct((rank, depth), down.dtype),
            [ANYWHERE] * tensors,
            [pltpu.SemaphoreType.DMA((tensors,))],
            ANYWHERE,
            cost=FREE,
        )(*pieces)
    else:
        none = jnp.zeros((), down.dtype)
        own = jnp.concatenate(
            [sum(jnp.where((me ^ f) == j, pieces[f], none) for f in range(tensors)) for j in range(tensors)],
            axis=0,
        )

    hops = range(CORES, tensors, CORES)

    def send(m):
        return [flipped(chunks[m], "tensor", hop) for hop in hops]

    far = [send(0)]

    def across(m):
        return [flipped(value, "tensor", 1) for value in far[m]]

    def far_places(m):
        return [(hop, edges[m], 0, edges[m + 1] - edges[m]) for hop in hops]

    def near_places(m):
        return [(hop ^ 1, edges[m], 0, edges[m + 1] - edges[m]) for hop in hops]

    def products(places, features, total):
        return call(
            functools.partial(products_kernel, tile, depth, places),
            jax.ShapeDtypeStruct((rows, columns), jnp.float32),
            [ANYWHERE] + [ANYWHERE] * len(features) + [VECTOR],
            tile_scratch(tile, rows, places, columns),
        )(frozen_projection_weight, *features, total)

    flips = list(range(1, groups))
    pairs = []
    if parts == 2:
        while len(flips) > 1:
            pairs.append((flips.pop(-2), flips.pop(-1)))
    routes = [
        [(p * groups + z, p * groups + (z ^ pair[p])) for p in range(parts) for z in range(groups)]
        for pair in pairs
    ]

    def fetch_far(value):
        return [lax.ppermute(value, ("parts", "adapter"), route) for route in routes]

    def fetch_near(value):
        return [flipped(value, "adapter", flip) for flip in flips]

    def swap(values):
        return [flipped(value, "parts", 1) for value in values]

    own, here = chained(own, tokens)
    fetched = fetch_far(own)
    places = [(0, 0, 0, depth // 2)]
    total, stored = call(
        functools.partial(first_kernel, tile, depth, places, slots),
        [
            jax.ShapeDtypeStruct((rows, columns), jnp.float32),
            jax.ShapeDtypeStruct((1, rows), jnp.int32),
        ],
        [SCALAR, VECTOR, ANYWHERE, ANYWHERE],
        tile_scratch(tile, rows, places, columns),
        [VECTOR, VECTOR],
    )(placement, tenant.reshape(1, rows), frozen_projection_weight, here)
    total, own, up, neighbour, chunks[1] = chained(
        total, own, lowrank_up_weight[0], neighbour, chunks[1]
    )
    far.append(send(1))
    single, single_up = fetch_near(own), fetch_near(up)
    total = products([(0, depth // 2, depth // 2, depth // 2)], [here], total)
    fetched, single_up, total = chained(fetched, single_up, total)
    swapped = swap(fetched)
    total, neighbour = chained(total, neighbour)
    total = products([(1, 0, 0, depth)], [neighbour], total)
    total, up = chained(total, up)
    fetched_up = fetch_far(up)
    single, swapped, total = chained(single, swapped, total)
    downs = [own] + single
    for pair in zip(fetched, swapped):
        downs += pair

    tiles = depth // tile
    partial = call(
        functools.partial(shrink_kernel, tile, flips, pairs, slots),
        jax.ShapeDtypeStruct((rank, rows), jnp.float32),
        [ANYWHERE, VECTOR] + [ANYWHERE] * slots,
        [
            pltpu.VMEM((tiles, rows, tile), jnp.bfloat16),
            pltpu.VMEM((tiles, slots * rank, tile), jnp.bfloat16),
            pltpu.VMEM((rows, slots * rank), jnp.float32),
            pltpu.SemaphoreType.DMA((1 + slots, tiles)),
        ],
    )(tokens, stored, *downs)
    far[0], fetched_up, partial = chained(far[0], fetched_up, partial)
    swapped_up = swap(fetched_up)
    ups = [up] + single_up
    for pair in zip(fetched_up, swapped_up):
        ups += pair
    near = across(0)
    total = products(far_places(0), far[0], total)
    flip = 1
    while flip < tensors // 2:
        received = flipped(partial, "tensor", flip)
        if flip == 1:
            received, total = chained(received, total)
        partial += received
        flip *= 2
    more = flipped(partial.astype(jnp.bfloat16), "tensor", flip)
    total, partial = chained(total, partial)
    total = products(near_places(0), near, total)
    far[1], ups, total = chained(far[1], ups, total)
    near = across(1)
    total = products(far_places(1), far[1], total)
    near, more, total = chained(near, more, total)

    places = near_places(1)
    return call(
        functools.partial(last_kernel, depth, places, flips, pairs, slots),
        jax.ShapeDtypeStruct((rows, columns), jnp.bfloat16),
        [VECTOR] * (len(near) + 3) + [ANYWHERE] * (2 + slots),
        [
            pltpu.VMEM((rows, columns), jnp.float32),
            pltpu.VMEM((rank, rows), jnp.float32),
            pltpu.VMEM((rank, rows), jnp.bfloat16),
            pltpu.VMEM((slots * rank, columns), jnp.bfloat16),
        ]
        + [pltpu.SemaphoreType.DMA((2 + slots,))],
    )(frozen_projection_weight, *near, total, stored, partial, more, *ups)


def solution(mesh):
    placed = (
        P(("parts", "adapter"), "tensor"),
        P(("parts", "adapter"), None),
        P(),
        P(None, "tensor"),
        P("adapter", None, "tensor"),
        P("adapter", None, "tensor"),
    )
    return jax.shard_map(
        body,
        mesh=mesh,
        in_specs=placed,
        out_specs=P(("parts", "adapter"), "tensor"),
        check_vma=False,
    )
```

```python
import functools
import math

import jax
import jax.numpy as jnp
from jax import lax
from jax.experimental import pallas as pl
from jax.experimental.pallas import tpu as pltpu
from jax.sharding import PartitionSpec as P

LOWRANK_SCALE = 2.0
CORES = 2
LANES = 128
CUTS = (0.75,)
MIB = 1024 * 1024
FREE = pl.CostEstimate(flops=0, bytes_accessed=0, transcendentals=0)
LONG = pl.CostEstimate(flops=10**11, bytes_accessed=0, transcendentals=0)
ANYWHERE = pl.BlockSpec(memory_space=pl.ANY)
VECTOR = pl.BlockSpec(memory_space=pltpu.VMEM)
SCALAR = pl.BlockSpec(memory_space=pltpu.SMEM)


def flipped(value, axis, flip):
    count = lax.axis_size(axis)
    return lax.ppermute(value, axis, [(i, i ^ flip) for i in range(count)])


def chained(*values):
    return lax.optimization_barrier(values)


def call(kernel, out_shape, in_specs, scratch, out_specs=VECTOR, cost=LONG, mib=24):
    return pl.pallas_call(
        kernel,
        out_shape=out_shape,
        in_specs=in_specs,
        out_specs=out_specs,
        scratch_shapes=scratch,
        cost_estimate=cost,
        compiler_params=pltpu.CompilerParams(vmem_limit_bytes=mib * MIB),
    )


def run_copies(pairs, sems):
    copies = [
        pltpu.make_async_copy(source, target, sems.at[i]) for i, (source, target) in enumerate(pairs)
    ]
    for copy in copies:
        copy.start()
    for copy in copies:
        copy.wait()


def cut_kernel(edges, source_ref, *refs):
    outs, (held_ref, sems) = refs[:-2], refs[-2:]
    steps, rows = held_ref.shape[:2]
    copies = [
        pltpu.make_async_copy(
            source_ref.at[pl.ds(i * rows, rows), pl.ds(edges[0], edges[-1] - edges[0])],
            held_ref.at[i],
            sems.at[0, i],
        )
        for i in range(steps)
    ]
    for copy in copies:
        copy.start()
    leaving = []
    for i in range(steps):
        copies[i].wait()
        for m, (a, b, out) in enumerate(zip(edges, edges[1:], outs)):
            leaving.append(
                pltpu.make_async_copy(
                    held_ref.at[i, :, pl.ds(a - edges[0], b - a)],
                    out.at[pl.ds(i * rows, rows)],
                    sems.at[1 + m, i],
                )
            )
            leaving[-1].start()
    for copy in leaving:
        copy.wait()


def order_kernel(rank_part, *refs):
    pieces, out_ref, sems = refs[:-2], refs[-2], refs[-1]
    me = lax.axis_index("tensor")
    run_copies(
        [
            (piece, out_ref.at[pl.ds(pl.multiple_of((me ^ f) * rank_part, rank_part), rank_part)])
            for f, piece in enumerate(pieces)
        ],
        sems,
    )


def start_tiles(tile, depth, places, features, weight_ref, held_ref, rows_ref, sems):
    me, t = lax.axis_index("tensor"), 0
    for (flip, first, skip, width), part in zip(places, features):
        for k in range(0, width, tile):
            start = pl.multiple_of((me ^ flip) * depth + first + k, LANES)
            pltpu.make_async_copy(
                weight_ref.at[pl.ds(start, tile)], rows_ref.at[t], sems.at[1, t]
            ).start()
            pltpu.make_async_copy(part.at[:, pl.ds(skip + k, tile)], held_ref.at[t], sems.at[0, t]).start()
            t += 1


def add_tiles(held_ref, rows_ref, sems, total_ref, given_ref):
    pltpu.make_async_copy(held_ref.at[0], held_ref.at[0], sems.at[0, 0]).wait()
    pltpu.make_async_copy(rows_ref.at[0], rows_ref.at[0], sems.at[1, 0]).wait()
    total_ref[...] = given_ref[...] + jnp.dot(
        held_ref[0], rows_ref[0], preferred_element_type=jnp.float32
    )
    if held_ref.shape[0] == 1:
        return

    @pl.loop(1, held_ref.shape[0])
    def _(t):
        pltpu.make_async_copy(held_ref.at[t], held_ref.at[t], sems.at[0, t]).wait()
        pltpu.make_async_copy(rows_ref.at[t], rows_ref.at[t], sems.at[1, t]).wait()
        total_ref[...] += jnp.dot(held_ref[t], rows_ref[t], preferred_element_type=jnp.float32)


def tile_scratch(tile, rows, places, columns):
    tiles = sum(place[3] for place in places) // tile
    return [
        pltpu.VMEM((tiles, rows, tile), jnp.bfloat16),
        pltpu.VMEM((tiles, tile, columns), jnp.bfloat16),
        pltpu.SemaphoreType.DMA((2, tiles)),
    ]


def first_kernel(tile, depth, places, slots, placement_ref, tenant_ref, weight_ref, *refs):
    count = len(places)
    features = refs[:count]
    out_ref, stored_ref, held_ref, rows_ref, sems = refs[count:]
    start_tiles(tile, depth, places, features, weight_ref, held_ref, rows_ref, sems)
    out_ref[...] = jnp.zeros_like(out_ref)
    stored = jnp.zeros(stored_ref.shape, jnp.int32)
    for slot in range(slots):
        stored = jnp.where(tenant_ref[...] == slot, placement_ref[slot], stored)
    stored_ref[...] = stored
    add_tiles(held_ref, rows_ref, sems, out_ref, out_ref)


def products_kernel(tile, depth, places, weight_ref, *refs):
    count = len(places)
    features, given = refs[:count], refs[count]
    out_ref, held_ref, rows_ref, sems = refs[count + 1 :]
    start_tiles(tile, depth, places, features, weight_ref, held_ref, rows_ref, sems)
    add_tiles(held_ref, rows_ref, sems, out_ref, given)


def owners_of(flips, pairs):
    group, part = lax.axis_index("adapter"), lax.axis_index("parts")
    owners = [group] + [group ^ flip for flip in flips]
    for near, far in pairs:
        owners += [group ^ (near + part * (far - near)), group ^ (far + part * (near - far))]
    return owners


def last_kernel(depth, places, flips, pairs, slots, weight_ref, *refs):
    count = len(places)
    features = refs[:count]
    given, stored_ref, sum_ref, more_ref = refs[count : count + 4]
    ups = refs[count + 4 : count + 4 + slots]
    out_ref, total_ref, sums_ref, received_ref, stacked_ref, small_sems = refs[count + 4 + slots :]
    rank = ups[0].shape[0]
    copies = [(sum_ref, sums_ref), (more_ref, received_ref)]
    copies += [(up, stacked_ref.at[pl.ds(b * rank, rank)]) for b, up in enumerate(ups)]
    copies = [
        pltpu.make_async_copy(source, target, small_sems.at[i])
        for i, (source, target) in enumerate(copies)
    ]
    for copy in copies:
        copy.start()
    me, sum_so_far = lax.axis_index("tensor"), given
    for (flip, first, skip, width), part in zip(places, features):
        start = pl.multiple_of((me ^ flip) * depth + first, LANES)
        total_ref[...] = sum_so_far[...] + jnp.dot(
            part[:, skip : skip + width],
            weight_ref[pl.ds(start, width)],
            preferred_element_type=jnp.float32,
        )
        sum_so_far = total_ref
    for copy in copies:
        copy.wait()
    shrunk = (sums_ref[...] + received_ref[...].astype(jnp.float32)).astype(jnp.bfloat16).astype(jnp.float32)
    spread = jnp.concatenate(
        [jnp.where(stored_ref[...] == owner, shrunk, 0.0) for owner in owners_of(flips, pairs)], axis=0
    )
    expanded = lax.dot_general(
        spread.astype(jnp.bfloat16),
        stacked_ref[...],
        (((0,), (0,)), ((), ())),
        preferred_element_type=jnp.float32,
    )
    expanded = expanded.astype(jnp.bfloat16).astype(jnp.float32)
    out_ref[...] = (total_ref[...] + LOWRANK_SCALE * expanded).astype(out_ref.dtype)


def shrink_kernel(tile, flips, pairs, slots, tokens_ref, stored_ref, *refs):
    downs, out_ref, held_ref, down_ref, sums_ref, sems = (
        refs[:slots], refs[slots], *refs[slots + 1 :]
    )
    rank = downs[0].shape[0]
    tiles = tokens_ref.shape[1] // tile
    for k in range(tiles):
        here = pl.ds(k * tile, tile)
        pltpu.make_async_copy(tokens_ref.at[:, here], held_ref.at[k], sems.at[0, k]).start()
        for b, down in enumerate(downs):
            pltpu.make_async_copy(
                down.at[:, here], down_ref.at[k, pl.ds(b * rank, rank)], sems.at[1 + b, k]
            ).start()
    sums_ref[...] = jnp.zeros_like(sums_ref)

    @pl.loop(0, tiles)
    def _(k):
        pltpu.make_async_copy(held_ref.at[k], held_ref.at[k], sems.at[0, k]).wait()
        for b in range(slots):
            block = down_ref.at[k, pl.ds(b * rank, rank)]
            pltpu.make_async_copy(block, block, sems.at[1 + b, k]).wait()
        sums_ref[...] += lax.dot_general(
            held_ref[k], down_ref[k], (((1,), (1,)), ((), ())), preferred_element_type=jnp.float32
        )

    sums = sums_ref[...].T
    total = jnp.zeros(out_ref.shape, jnp.float32)
    for b, owner in enumerate(owners_of(flips, pairs)):
        total += jnp.where(stored_ref[...] == owner, sums[b * rank : (b + 1) * rank], 0.0)
    out_ref[...] = total


def body(
    tokens, tenant, placement, frozen_projection_weight, lowrank_down_weight, lowrank_up_weight
):
    rows, depth = tokens.shape
    slots = placement.shape[0]
    tensors = lax.axis_size("tensor")
    groups = lax.axis_size("adapter")
    parts = lax.axis_size("parts")
    me = lax.axis_index("tensor")
    rank, columns = lowrank_up_weight.shape[1:]
    edges = [0] + [int(depth * cut) // LANES * LANES for cut in CUTS] + [depth]
    tile = math.gcd(*edges)

    down = lowrank_down_weight[0].T
    pieces = [
        lax.dynamic_slice_in_dim(down, (me ^ flip) * depth, depth, axis=1)
        for flip in range(tensors)
    ]
    uncut, pieces = chained(tokens, pieces)

    def cut(array, m, mib, steps=3):
        ends = edges[m : m + 2]
        return call(
            functools.partial(cut_kernel, ends),
            [jax.ShapeDtypeStruct((rows, ends[1] - ends[0]), array.dtype)],
            [ANYWHERE],
            [
                pltpu.VMEM((steps, rows // steps, ends[1] - ends[0]), array.dtype),
                pltpu.SemaphoreType.DMA((2, steps)),
            ],
            [ANYWHERE],
            mib=mib,
        )(array)[0]

    chunks = [cut(uncut, 0, 56)]
    pieces = [pieces[0]] + [flipped(pieces[f], "tensor", f) for f in range(1, tensors)]
    pieces[1], here = chained(pieces[1], tokens)
    neighbour = flipped(here, "tensor", 1)
    if down.shape[0] % 16 == 0:
        own = call(
            functools.partial(order_kernel, down.shape[0]),
            jax.ShapeDtypeStruct((rank, depth), down.dtype),
            [ANYWHERE] * tensors,
            [pltpu.SemaphoreType.DMA((tensors,))],
            ANYWHERE,
            cost=FREE,
        )(*pieces)
    else:
        none = jnp.zeros((), down.dtype)
        own = jnp.concatenate(
            [sum(jnp.where((me ^ f) == j, pieces[f], none) for f in range(tensors)) for j in range(tensors)],
            axis=0,
        )

    hops = range(CORES, tensors, CORES)

    def send(m):
        return [flipped(chunks[m], "tensor", hop) for hop in hops]

    far = [send(0)]

    def across(m):
        return [flipped(value, "tensor", 1) for value in far[m]]

    def far_places(m):
        return [(hop, edges[m], 0, edges[m + 1] - edges[m]) for hop in hops]

    def near_places(m):
        return [(hop ^ 1, edges[m], 0, edges[m + 1] - edges[m]) for hop in hops]

    def products(places, features, total):
        return call(
            functools.partial(products_kernel, tile, depth, places),
            jax.ShapeDtypeStruct((rows, columns), jnp.float32),
            [ANYWHERE] + [ANYWHERE] * len(features) + [VECTOR],
            tile_scratch(tile, rows, places, columns),
        )(frozen_projection_weight, *features, total)

    flips = list(range(1, groups))
    pairs = []
    if parts == 2:
        while len(flips) > 1:
            pairs.append((flips.pop(-2), flips.pop(-1)))
    routes = [
        [(p * groups + z, p * groups + (z ^ pair[p])) for p in range(parts) for z in range(groups)]
        for pair in pairs
    ]

    def fetch_far(value):
        return [lax.ppermute(value, ("parts", "adapter"), route) for route in routes]

    def fetch_near(value):
        return [flipped(value, "adapter", flip) for flip in flips]

    def swap(values):
        return [flipped(value, "parts", 1) for value in values]

    own, here = chained(own, tokens)
    fetched = fetch_far(own)
    places = [(0, 0, 0, depth // 2)]
    total, stored = call(
        functools.partial(first_kernel, tile, depth, places, slots),
        [
            jax.ShapeDtypeStruct((rows, columns), jnp.float32),
            jax.ShapeDtypeStruct((1, rows), jnp.int32),
        ],
        [SCALAR, VECTOR, ANYWHERE, ANYWHERE],
        tile_scratch(tile, rows, places, columns),
        [VECTOR, VECTOR],
    )(placement, tenant.reshape(1, rows), frozen_projection_weight, here)
    total, own, up, neighbour, uncut = chained(total, own, lowrank_up_weight[0], neighbour, tokens)
    chunks.append(cut(uncut, 1, 24))
    far.append(send(1))
    single, single_up = fetch_near(own), fetch_near(up)
    total = products([(0, depth // 2, depth // 2, depth // 2)], [here], total)
    fetched, single_up, total = chained(fetched, single_up, total)
    swapped = swap(fetched)
    total, neighbour = chained(total, neighbour)
    total = products([(1, 0, 0, depth)], [neighbour], total)
    total, up = chained(total, up)
    fetched_up = fetch_far(up)
    single, swapped, total = chained(single, swapped, total)
    downs = [own] + single
    for pair in zip(fetched, swapped):
        downs += pair

    tiles = depth // tile
    partial = call(
        functools.partial(shrink_kernel, tile, flips, pairs, slots),
        jax.ShapeDtypeStruct((rank, rows), jnp.float32),
        [ANYWHERE, VECTOR] + [ANYWHERE] * slots,
        [
            pltpu.VMEM((tiles, rows, tile), jnp.bfloat16),
            pltpu.VMEM((tiles, slots * rank, tile), jnp.bfloat16),
            pltpu.VMEM((rows, slots * rank), jnp.float32),
            pltpu.SemaphoreType.DMA((1 + slots, tiles)),
        ],
    )(tokens, stored, *downs)
    far[0], fetched_up, partial = chained(far[0], fetched_up, partial)
    swapped_up = swap(fetched_up)
    ups = [up] + single_up
    for pair in zip(fetched_up, swapped_up):
        ups += pair
    near = across(0)
    total = products(far_places(0), far[0], total)
    flip = 1
    while flip < tensors // 2:
        received = flipped(partial, "tensor", flip)
        if flip == 1:
            received, total = chained(received, total)
        partial += received
        flip *= 2
    more = flipped(partial.astype(jnp.bfloat16), "tensor", flip)
    total, partial = chained(total, partial)
    total = products(near_places(0), near, total)
    far[1], ups, total = chained(far[1], ups, total)
    near = across(1)
    total = products(far_places(1), far[1], total)
    near, more, total = chained(near, more, total)

    places = near_places(1)
    return call(
        functools.partial(last_kernel, depth, places, flips, pairs, slots),
        jax.ShapeDtypeStruct((rows, columns), jnp.bfloat16),
        [VECTOR] * (len(near) + 3) + [ANYWHERE] * (2 + slots),
        [
            pltpu.VMEM((rows, columns), jnp.float32),
            pltpu.VMEM((rank, rows), jnp.float32),
            pltpu.VMEM((rank, rows), jnp.bfloat16),
            pltpu.VMEM((slots * rank, columns), jnp.bfloat16),
        ]
        + [pltpu.SemaphoreType.DMA((2 + slots,))],
    )(frozen_projection_weight, *near, total, stored, partial, more, *ups)


def solution(mesh):
    placed = (
        P(("parts", "adapter"), "tensor"),
        P(("parts", "adapter"), None),
        P(),
        P(None, "tensor"),
        P("adapter", None, "tensor"),
        P("adapter", None, "tensor"),
    )
    return jax.shard_map(
        body,
        mesh=mesh,
        in_specs=placed,
        out_specs=P(("parts", "adapter"), "tensor"),
        check_vma=False,
    )
```

```python
import functools
import math

import jax
import jax.numpy as jnp
from jax import lax
from jax.experimental import pallas as pl
from jax.experimental.pallas import tpu as pltpu
from jax.sharding import PartitionSpec as P

LOWRANK_SCALE = 2.0
CORES = 2
LANES = 128
CUTS = (0.75,)
MIB = 1024 * 1024
FREE = pl.CostEstimate(flops=0, bytes_accessed=0, transcendentals=0)
LONG = pl.CostEstimate(flops=10**11, bytes_accessed=0, transcendentals=0)
ANYWHERE = pl.BlockSpec(memory_space=pl.ANY)
VECTOR = pl.BlockSpec(memory_space=pltpu.VMEM)
SCALAR = pl.BlockSpec(memory_space=pltpu.SMEM)


def flipped(value, axis, flip):
    count = lax.axis_size(axis)
    return lax.ppermute(value, axis, [(i, i ^ flip) for i in range(count)])


def chained(*values):
    return lax.optimization_barrier(values)


def call(kernel, out_shape, in_specs, scratch, out_specs=VECTOR, cost=LONG, mib=24):
    return pl.pallas_call(
        kernel,
        out_shape=out_shape,
        in_specs=in_specs,
        out_specs=out_specs,
        scratch_shapes=scratch,
        cost_estimate=cost,
        compiler_params=pltpu.CompilerParams(vmem_limit_bytes=mib * MIB),
    )


def run_copies(pairs, sems):
    copies = [
        pltpu.make_async_copy(source, target, sems.at[i]) for i, (source, target) in enumerate(pairs)
    ]
    for copy in copies:
        copy.start()
    for copy in copies:
        copy.wait()


def cut_kernel(edges, source_ref, *refs):
    outs, (held_ref, sems) = refs[:-2], refs[-2:]
    steps, rows = held_ref.shape[:2]
    copies = [
        pltpu.make_async_copy(source_ref.at[pl.ds(i * rows, rows)], held_ref.at[i], sems.at[0, i])
        for i in range(steps)
    ]
    for copy in copies:
        copy.start()
    leaving = []
    for i in range(steps):
        copies[i].wait()
        for m, (a, b, out) in enumerate(zip(edges, edges[1:], outs)):
            leaving.append(
                pltpu.make_async_copy(
                    held_ref.at[i, :, pl.ds(a, b - a)],
                    out.at[pl.ds(i * rows, rows)],
                    sems.at[1 + m, i],
                )
            )
            leaving[-1].start()
    for copy in leaving:
        copy.wait()


def order_kernel(rank_part, *refs):
    pieces, out_ref, sems = refs[:-2], refs[-2], refs[-1]
    me = lax.axis_index("tensor")
    run_copies(
        [
            (piece, out_ref.at[pl.ds(pl.multiple_of((me ^ f) * rank_part, rank_part), rank_part)])
            for f, piece in enumerate(pieces)
        ],
        sems,
    )


def start_tiles(tile, depth, places, features, weight_ref, held_ref, rows_ref, sems):
    me, t = lax.axis_index("tensor"), 0
    for (flip, first, skip, width), part in zip(places, features):
        for k in range(0, width, tile):
            start = pl.multiple_of((me ^ flip) * depth + first + k, LANES)
            pltpu.make_async_copy(
                weight_ref.at[pl.ds(start, tile)], rows_ref.at[t], sems.at[1, t]
            ).start()
            pltpu.make_async_copy(part.at[:, pl.ds(skip + k, tile)], held_ref.at[t], sems.at[0, t]).start()
            t += 1


def add_tiles(held_ref, rows_ref, sems, total_ref, given_ref):
    pltpu.make_async_copy(held_ref.at[0], held_ref.at[0], sems.at[0, 0]).wait()
    pltpu.make_async_copy(rows_ref.at[0], rows_ref.at[0], sems.at[1, 0]).wait()
    total_ref[...] = given_ref[...] + jnp.dot(
        held_ref[0], rows_ref[0], preferred_element_type=jnp.float32
    )
    if held_ref.shape[0] == 1:
        return

    @pl.loop(1, held_ref.shape[0])
    def _(t):
        pltpu.make_async_copy(held_ref.at[t], held_ref.at[t], sems.at[0, t]).wait()
        pltpu.make_async_copy(rows_ref.at[t], rows_ref.at[t], sems.at[1, t]).wait()
        total_ref[...] += jnp.dot(held_ref[t], rows_ref[t], preferred_element_type=jnp.float32)


def tile_scratch(tile, rows, places, columns):
    tiles = sum(place[3] for place in places) // tile
    return [
        pltpu.VMEM((tiles, rows, tile), jnp.bfloat16),
        pltpu.VMEM((tiles, tile, columns), jnp.bfloat16),
        pltpu.SemaphoreType.DMA((2, tiles)),
    ]


def first_kernel(tile, depth, places, slots, placement_ref, tenant_ref, weight_ref, *refs):
    count = len(places)
    features = refs[:count]
    out_ref, stored_ref, held_ref, rows_ref, sems = refs[count:]
    start_tiles(tile, depth, places, features, weight_ref, held_ref, rows_ref, sems)
    out_ref[...] = jnp.zeros_like(out_ref)
    stored = jnp.zeros(stored_ref.shape, jnp.int32)
    for slot in range(slots):
        stored = jnp.where(tenant_ref[...] == slot, placement_ref[slot], stored)
    stored_ref[...] = stored
    add_tiles(held_ref, rows_ref, sems, out_ref, out_ref)


def products_kernel(tile, depth, places, weight_ref, *refs):
    count = len(places)
    features, given = refs[:count], refs[count]
    out_ref, held_ref, rows_ref, sems = refs[count + 1 :]
    start_tiles(tile, depth, places, features, weight_ref, held_ref, rows_ref, sems)
    add_tiles(held_ref, rows_ref, sems, out_ref, given)


def owners_of(flips, pairs):
    group, part = lax.axis_index("adapter"), lax.axis_index("parts")
    owners = [group] + [group ^ flip for flip in flips]
    for near, far in pairs:
        owners += [group ^ (near + part * (far - near)), group ^ (far + part * (near - far))]
    return owners


def last_kernel(depth, places, flips, pairs, slots, weight_ref, *refs):
    count = len(places)
    features = refs[:count]
    given, stored_ref, sum_ref, more_ref = refs[count : count + 4]
    ups = refs[count + 4 : count + 4 + slots]
    out_ref, total_ref, sums_ref, received_ref, stacked_ref, small_sems = refs[count + 4 + slots :]
    rank = ups[0].shape[0]
    copies = [(sum_ref, sums_ref), (more_ref, received_ref)]
    copies += [(up, stacked_ref.at[pl.ds(b * rank, rank)]) for b, up in enumerate(ups)]
    copies = [
        pltpu.make_async_copy(source, target, small_sems.at[i])
        for i, (source, target) in enumerate(copies)
    ]
    for copy in copies:
        copy.start()
    me, sum_so_far = lax.axis_index("tensor"), given
    for (flip, first, skip, width), part in zip(places, features):
        start = pl.multiple_of((me ^ flip) * depth + first, LANES)
        total_ref[...] = sum_so_far[...] + jnp.dot(
            part[:, skip : skip + width],
            weight_ref[pl.ds(start, width)],
            preferred_element_type=jnp.float32,
        )
        sum_so_far = total_ref
    for copy in copies:
        copy.wait()
    shrunk = (sums_ref[...] + received_ref[...].astype(jnp.float32)).astype(jnp.bfloat16).astype(jnp.float32)
    spread = jnp.concatenate(
        [jnp.where(stored_ref[...] == owner, shrunk, 0.0) for owner in owners_of(flips, pairs)], axis=0
    )
    expanded = lax.dot_general(
        spread.astype(jnp.bfloat16),
        stacked_ref[...],
        (((0,), (0,)), ((), ())),
        preferred_element_type=jnp.float32,
    )
    expanded = expanded.astype(jnp.bfloat16).astype(jnp.float32)
    out_ref[...] = (total_ref[...] + LOWRANK_SCALE * expanded).astype(out_ref.dtype)


def shrink_kernel(tile, flips, pairs, slots, tokens_ref, stored_ref, *refs):
    downs, out_ref, held_ref, down_ref, sums_ref, sems = (
        refs[:slots], refs[slots], *refs[slots + 1 :]
    )
    rank = downs[0].shape[0]
    tiles = tokens_ref.shape[1] // tile
    for k in range(tiles):
        here = pl.ds(k * tile, tile)
        pltpu.make_async_copy(tokens_ref.at[:, here], held_ref.at[k], sems.at[0, k]).start()
        for b, down in enumerate(downs):
            pltpu.make_async_copy(
                down.at[:, here], down_ref.at[k, pl.ds(b * rank, rank)], sems.at[1 + b, k]
            ).start()
    sums_ref[...] = jnp.zeros_like(sums_ref)

    @pl.loop(0, tiles)
    def _(k):
        pltpu.make_async_copy(held_ref.at[k], held_ref.at[k], sems.at[0, k]).wait()
        for b in range(slots):
            block = down_ref.at[k, pl.ds(b * rank, rank)]
            pltpu.make_async_copy(block, block, sems.at[1 + b, k]).wait()
        sums_ref[...] += lax.dot_general(
            held_ref[k], down_ref[k], (((1,), (1,)), ((), ())), preferred_element_type=jnp.float32
        )

    sums = sums_ref[...].T
    total = jnp.zeros(out_ref.shape, jnp.float32)
    for b, owner in enumerate(owners_of(flips, pairs)):
        total += jnp.where(stored_ref[...] == owner, sums[b * rank : (b + 1) * rank], 0.0)
    out_ref[...] = total


def body(
    tokens, tenant, placement, frozen_projection_weight, lowrank_down_weight, lowrank_up_weight
):
    rows, depth = tokens.shape
    slots = placement.shape[0]
    tensors = lax.axis_size("tensor")
    groups = lax.axis_size("adapter")
    parts = lax.axis_size("parts")
    me = lax.axis_index("tensor")
    rank, columns = lowrank_up_weight.shape[1:]
    edges = [0] + [int(depth * cut) // LANES * LANES for cut in CUTS] + [depth]
    tile = math.gcd(*edges)

    down = lowrank_down_weight[0].T
    pieces = [
        lax.dynamic_slice_in_dim(down, (me ^ flip) * depth, depth, axis=1)
        for flip in range(tensors)
    ]
    uncut, pieces = chained(tokens, pieces)
    steps = 3
    chunks = list(
        call(
            functools.partial(cut_kernel, edges),
            [jax.ShapeDtypeStruct((rows, b - a), tokens.dtype) for a, b in zip(edges, edges[1:])],
            [ANYWHERE],
            [
                pltpu.VMEM((steps, rows // steps, depth), tokens.dtype),
                pltpu.SemaphoreType.DMA((len(edges), steps)),
            ],
            [ANYWHERE] * (len(edges) - 1),
            cost=FREE,
            mib=56,
        )(uncut)
    )
    pieces = [pieces[0]] + [flipped(pieces[f], "tensor", f) for f in range(1, tensors)]
    pieces[1], here = chained(pieces[1], tokens)
    neighbour = flipped(here, "tensor", 1)
    if down.shape[0] % 16 == 0:
        own = call(
            functools.partial(order_kernel, down.shape[0]),
            jax.ShapeDtypeStruct((rank, depth), down.dtype),
            [ANYWHERE] * tensors,
            [pltpu.SemaphoreType.DMA((tensors,))],
            ANYWHERE,
            cost=FREE,
        )(*pieces)
    else:
        none = jnp.zeros((), down.dtype)
        own = jnp.concatenate(
            [sum(jnp.where((me ^ f) == j, pieces[f], none) for f in range(tensors)) for j in range(tensors)],
            axis=0,
        )

    hops = range(CORES, tensors, CORES)

    def send(m):
        return [flipped(chunks[m], "tensor", hop) for hop in hops]

    far = [send(0)]

    def across(m):
        return [flipped(value, "tensor", 1) for value in far[m]]

    def far_places(m):
        return [(hop, edges[m], 0, edges[m + 1] - edges[m]) for hop in hops]

    def near_places(m):
        return [(hop ^ 1, edges[m], 0, edges[m + 1] - edges[m]) for hop in hops]

    def products(places, features, total):
        return call(
            functools.partial(products_kernel, tile, depth, places),
            jax.ShapeDtypeStruct((rows, columns), jnp.float32),
            [ANYWHERE] + [ANYWHERE] * len(features) + [VECTOR],
            tile_scratch(tile, rows, places, columns),
        )(frozen_projection_weight, *features, total)

    flips = list(range(1, groups))
    pairs = []
    if parts == 2:
        while len(flips) > 1:
            pairs.append((flips.pop(-2), flips.pop(-1)))
    routes = [
        [(p * groups + z, p * groups + (z ^ pair[p])) for p in range(parts) for z in range(groups)]
        for pair in pairs
    ]

    def fetch_far(value):
        return [lax.ppermute(value, ("parts", "adapter"), route) for route in routes]

    def fetch_near(value):
        return [flipped(value, "adapter", flip) for flip in flips]

    def swap(values):
        return [flipped(value, "parts", 1) for value in values]

    own, here = chained(own, tokens)
    fetched = fetch_far(own)
    places = [(0, 0, 0, depth // 2)]
    total, stored = call(
        functools.partial(first_kernel, tile, depth, places, slots),
        [
            jax.ShapeDtypeStruct((rows, columns), jnp.float32),
            jax.ShapeDtypeStruct((1, rows), jnp.int32),
        ],
        [SCALAR, VECTOR, ANYWHERE, ANYWHERE],
        tile_scratch(tile, rows, places, columns),
        [VECTOR, VECTOR],
    )(placement, tenant.reshape(1, rows), frozen_projection_weight, here)
    total, own, up, neighbour, chunks[1] = chained(
        total, own, lowrank_up_weight[0], neighbour, chunks[1]
    )
    far.append(send(1))
    single, single_up = fetch_near(own), fetch_near(up)
    total = products([(0, depth // 2, depth // 2, depth // 2)], [here], total)
    fetched, single_up, total = chained(fetched, single_up, total)
    swapped = swap(fetched)
    total, neighbour = chained(total, neighbour)
    total = products([(1, 0, 0, depth)], [neighbour], total)
    total, up = chained(total, up)
    fetched_up = fetch_far(up)
    single, swapped, total = chained(single, swapped, total)
    downs = [own] + single
    for pair in zip(fetched, swapped):
        downs += pair

    tiles = depth // tile
    partial = call(
        functools.partial(shrink_kernel, tile, flips, pairs, slots),
        jax.ShapeDtypeStruct((rank, rows), jnp.float32),
        [ANYWHERE, VECTOR] + [ANYWHERE] * slots,
        [
            pltpu.VMEM((tiles, rows, tile), jnp.bfloat16),
            pltpu.VMEM((tiles, slots * rank, tile), jnp.bfloat16),
            pltpu.VMEM((rows, slots * rank), jnp.float32),
            pltpu.SemaphoreType.DMA((1 + slots, tiles)),
        ],
    )(tokens, stored, *downs)
    far[0], fetched_up, partial = chained(far[0], fetched_up, partial)
    swapped_up = swap(fetched_up)
    ups = [up] + single_up
    for pair in zip(fetched_up, swapped_up):
        ups += pair
    near = across(0)
    total = products(far_places(0), far[0], total)
    flip = 1
    while flip < tensors // 2:
        received = flipped(partial, "tensor", flip)
        if flip == 1:
            received, total = chained(received, total)
        partial += received
        flip *= 2
    more = flipped(partial.astype(jnp.bfloat16), "tensor", flip)
    total, partial = chained(total, partial)
    total = products(near_places(0), near, total)
    far[1], ups, total = chained(far[1], ups, total)
    near = across(1)
    total = products(far_places(1), far[1], total)
    near, more, total = chained(near, more, total)

    places = near_places(1)
    return call(
        functools.partial(last_kernel, depth, places, flips, pairs, slots),
        jax.ShapeDtypeStruct((rows, columns), jnp.bfloat16),
        [VECTOR] * (len(near) + 3) + [ANYWHERE] * (2 + slots),
        [
            pltpu.VMEM((rows, columns), jnp.float32),
            pltpu.VMEM((rank, rows), jnp.float32),
            pltpu.VMEM((rank, rows), jnp.bfloat16),
            pltpu.VMEM((slots * rank, columns), jnp.bfloat16),
        ]
        + [pltpu.SemaphoreType.DMA((2 + slots,))],
    )(frozen_projection_weight, *near, total, stored, partial, more, *ups)


def solution(mesh):
    placed = (
        P(("parts", "adapter"), "tensor"),
        P(("parts", "adapter"), None),
        P(),
        P(None, "tensor"),
        P("adapter", None, "tensor"),
        P("adapter", None, "tensor"),
    )
    return jax.shard_map(
        body,
        mesh=mesh,
        in_specs=placed,
        out_specs=P(("parts", "adapter"), "tensor"),
        check_vma=False,
    )
```

```python
import functools
import math

import jax
import jax.numpy as jnp
from jax import lax
from jax.experimental import pallas as pl
from jax.experimental.pallas import tpu as pltpu
from jax.sharding import PartitionSpec as P

LOWRANK_SCALE = 2.0
CORES = 2
LANES = 128
CUTS = (0.75,)
MIB = 1024 * 1024
FREE = pl.CostEstimate(flops=0, bytes_accessed=0, transcendentals=0)
LONG = pl.CostEstimate(flops=10**11, bytes_accessed=0, transcendentals=0)
ANYWHERE = pl.BlockSpec(memory_space=pl.ANY)
VECTOR = pl.BlockSpec(memory_space=pltpu.VMEM)
SCALAR = pl.BlockSpec(memory_space=pltpu.SMEM)


def flipped(value, axis, flip):
    count = lax.axis_size(axis)
    return lax.ppermute(value, axis, [(i, i ^ flip) for i in range(count)])


def chained(*values):
    return lax.optimization_barrier(values)


def call(kernel, out_shape, in_specs, scratch, out_specs=VECTOR, cost=LONG, mib=24):
    return pl.pallas_call(
        kernel,
        out_shape=out_shape,
        in_specs=in_specs,
        out_specs=out_specs,
        scratch_shapes=scratch,
        cost_estimate=cost,
        compiler_params=pltpu.CompilerParams(vmem_limit_bytes=mib * MIB),
    )


def run_copies(pairs, sems):
    copies = [
        pltpu.make_async_copy(source, target, sems.at[i]) for i, (source, target) in enumerate(pairs)
    ]
    for copy in copies:
        copy.start()
    for copy in copies:
        copy.wait()


def cut_kernel(edges, source_ref, *refs):
    outs, (held_ref, sems) = refs[:-2], refs[-2:]
    steps, rows = held_ref.shape[:2]
    copies = [
        pltpu.make_async_copy(source_ref.at[pl.ds(i * rows, rows)], held_ref.at[i], sems.at[0, i])
        for i in range(steps)
    ]
    for copy in copies:
        copy.start()
    leaving = []
    for i in range(steps):
        copies[i].wait()
        for m, (a, b, out) in enumerate(zip(edges, edges[1:], outs)):
            leaving.append(
                pltpu.make_async_copy(
                    held_ref.at[i, :, pl.ds(a, b - a)],
                    out.at[pl.ds(i * rows, rows)],
                    sems.at[1 + m, i],
                )
            )
            leaving[-1].start()
    for copy in leaving:
        copy.wait()


def order_kernel(rank_part, *refs):
    pieces, out_ref, sems = refs[:-2], refs[-2], refs[-1]
    me = lax.axis_index("tensor")
    run_copies(
        [
            (piece, out_ref.at[pl.ds(pl.multiple_of((me ^ f) * rank_part, rank_part), rank_part)])
            for f, piece in enumerate(pieces)
        ],
        sems,
    )


def start_tiles(tile, depth, places, features, weight_ref, held_ref, rows_ref, sems):
    me, t = lax.axis_index("tensor"), 0
    for (flip, first, skip, width), part in zip(places, features):
        for k in range(0, width, tile):
            start = pl.multiple_of((me ^ flip) * depth + first + k, LANES)
            pltpu.make_async_copy(
                weight_ref.at[pl.ds(start, tile)], rows_ref.at[t], sems.at[1, t]
            ).start()
            pltpu.make_async_copy(part.at[:, pl.ds(skip + k, tile)], held_ref.at[t], sems.at[0, t]).start()
            t += 1


def add_tiles(held_ref, rows_ref, sems, total_ref, given_ref):
    pltpu.make_async_copy(held_ref.at[0], held_ref.at[0], sems.at[0, 0]).wait()
    pltpu.make_async_copy(rows_ref.at[0], rows_ref.at[0], sems.at[1, 0]).wait()
    total_ref[...] = given_ref[...] + jnp.dot(
        held_ref[0], rows_ref[0], preferred_element_type=jnp.float32
    )
    if held_ref.shape[0] == 1:
        return

    @pl.loop(1, held_ref.shape[0])
    def _(t):
        pltpu.make_async_copy(held_ref.at[t], held_ref.at[t], sems.at[0, t]).wait()
        pltpu.make_async_copy(rows_ref.at[t], rows_ref.at[t], sems.at[1, t]).wait()
        total_ref[...] += jnp.dot(held_ref[t], rows_ref[t], preferred_element_type=jnp.float32)


def tile_scratch(tile, rows, places, columns):
    tiles = sum(place[3] for place in places) // tile
    return [
        pltpu.VMEM((tiles, rows, tile), jnp.bfloat16),
        pltpu.VMEM((tiles, tile, columns), jnp.bfloat16),
        pltpu.SemaphoreType.DMA((2, tiles)),
    ]


def first_kernel(tile, depth, places, slots, placement_ref, tenant_ref, weight_ref, *refs):
    count = len(places)
    features = refs[:count]
    out_ref, stored_ref, held_ref, rows_ref, sems = refs[count:]
    start_tiles(tile, depth, places, features, weight_ref, held_ref, rows_ref, sems)
    out_ref[...] = jnp.zeros_like(out_ref)
    stored = jnp.zeros(stored_ref.shape, jnp.int32)
    for slot in range(slots):
        stored = jnp.where(tenant_ref[...] == slot, placement_ref[slot], stored)
    stored_ref[...] = stored
    add_tiles(held_ref, rows_ref, sems, out_ref, out_ref)


def products_kernel(tile, depth, places, weight_ref, *refs):
    count = len(places)
    features, given = refs[:count], refs[count]
    out_ref, held_ref, rows_ref, sems = refs[count + 1 :]
    start_tiles(tile, depth, places, features, weight_ref, held_ref, rows_ref, sems)
    add_tiles(held_ref, rows_ref, sems, out_ref, given)


def owners_of(flips, pairs):
    group, part = lax.axis_index("adapter"), lax.axis_index("parts")
    owners = [group] + [group ^ flip for flip in flips]
    for near, far in pairs:
        owners += [group ^ (near + part * (far - near)), group ^ (far + part * (near - far))]
    return owners


def spread_kernel(tile, depth, places, flips, pairs, slots, weight_ref, *refs):
    count = len(places)
    features = refs[:count]
    given, stored_ref, sum_ref, more_ref = refs[count : count + 4]
    ups = refs[count + 4 : count + 4 + slots]
    (
        out_ref, spread_ref, stacked_ref, sums_ref, received_ref, held_ref, rows_ref, sems, small_sems,
    ) = refs[count + 4 + slots :]
    rank = ups[0].shape[0]
    copies = [(sum_ref, sums_ref), (more_ref, received_ref)]
    copies += [(up, stacked_ref.at[pl.ds(b * rank, rank)]) for b, up in enumerate(ups)]
    copies = [
        pltpu.make_async_copy(source, target, small_sems.at[i])
        for i, (source, target) in enumerate(copies)
    ]
    for copy in copies:
        copy.start()
    start_tiles(tile, depth, places, features, weight_ref, held_ref, rows_ref, sems)
    add_tiles(held_ref, rows_ref, sems, out_ref, given)
    for copy in copies:
        copy.wait()
    shrunk = (sums_ref[...] + received_ref[...].astype(jnp.float32)).astype(jnp.bfloat16).astype(jnp.float32)
    for b, owner in enumerate(owners_of(flips, pairs)):
        block = jnp.where(stored_ref[...] == owner, shrunk, 0.0)
        spread_ref[b * rank : (b + 1) * rank] = block.astype(spread_ref.dtype)


def last_kernel(depth, places, weight_ref, *refs):
    count = len(places)
    features = refs[:count]
    given, spread_ref, stacked_ref, out_ref, total_ref = refs[count:]
    expanded = lax.dot_general(
        spread_ref[...], stacked_ref[...], (((0,), (0,)), ((), ())), preferred_element_type=jnp.float32
    )
    expanded = expanded.astype(jnp.bfloat16).astype(jnp.float32)
    total_ref[...] = given[...] + LOWRANK_SCALE * expanded
    me = lax.axis_index("tensor")
    for (flip, first, skip, width), part in zip(places, features):
        start = pl.multiple_of((me ^ flip) * depth + first, LANES)
        total_ref[...] += jnp.dot(
            part[:, skip : skip + width],
            weight_ref[pl.ds(start, width)],
            preferred_element_type=jnp.float32,
        )
    out_ref[...] = total_ref[...].astype(out_ref.dtype)


def shrink_kernel(tile, flips, pairs, slots, tokens_ref, stored_ref, *refs):
    downs, out_ref, held_ref, down_ref, sums_ref, sems = (
        refs[:slots], refs[slots], *refs[slots + 1 :]
    )
    rank = downs[0].shape[0]
    tiles = tokens_ref.shape[1] // tile
    for k in range(tiles):
        here = pl.ds(k * tile, tile)
        pltpu.make_async_copy(tokens_ref.at[:, here], held_ref.at[k], sems.at[0, k]).start()
        for b, down in enumerate(downs):
            pltpu.make_async_copy(
                down.at[:, here], down_ref.at[k, pl.ds(b * rank, rank)], sems.at[1 + b, k]
            ).start()
    sums_ref[...] = jnp.zeros_like(sums_ref)

    @pl.loop(0, tiles)
    def _(k):
        pltpu.make_async_copy(held_ref.at[k], held_ref.at[k], sems.at[0, k]).wait()
        for b in range(slots):
            block = down_ref.at[k, pl.ds(b * rank, rank)]
            pltpu.make_async_copy(block, block, sems.at[1 + b, k]).wait()
        sums_ref[...] += lax.dot_general(
            held_ref[k], down_ref[k], (((1,), (1,)), ((), ())), preferred_element_type=jnp.float32
        )

    sums = sums_ref[...].T
    total = jnp.zeros(out_ref.shape, jnp.float32)
    for b, owner in enumerate(owners_of(flips, pairs)):
        total += jnp.where(stored_ref[...] == owner, sums[b * rank : (b + 1) * rank], 0.0)
    out_ref[...] = total


def body(
    tokens, tenant, placement, frozen_projection_weight, lowrank_down_weight, lowrank_up_weight
):
    rows, depth = tokens.shape
    slots = placement.shape[0]
    tensors = lax.axis_size("tensor")
    groups = lax.axis_size("adapter")
    parts = lax.axis_size("parts")
    me = lax.axis_index("tensor")
    rank, columns = lowrank_up_weight.shape[1:]
    edges = [0] + [int(depth * cut) // LANES * LANES for cut in CUTS] + [depth]
    tile = math.gcd(*edges)

    down = lowrank_down_weight[0].T
    pieces = [
        lax.dynamic_slice_in_dim(down, (me ^ flip) * depth, depth, axis=1)
        for flip in range(tensors)
    ]
    uncut, pieces = chained(tokens, pieces)
    steps = 6
    chunks = list(
        call(
            functools.partial(cut_kernel, edges),
            [jax.ShapeDtypeStruct((rows, b - a), tokens.dtype) for a, b in zip(edges, edges[1:])],
            [ANYWHERE],
            [
                pltpu.VMEM((steps, rows // steps, depth), tokens.dtype),
                pltpu.SemaphoreType.DMA((len(edges), steps)),
            ],
            [ANYWHERE] * (len(edges) - 1),
            cost=FREE,
            mib=56,
        )(uncut)
    )
    pieces = [pieces[0]] + [flipped(pieces[f], "tensor", f) for f in range(1, tensors)]
    pieces[1], here = chained(pieces[1], tokens)
    neighbour = flipped(here, "tensor", 1)
    if down.shape[0] % 16 == 0:
        own = call(
            functools.partial(order_kernel, down.shape[0]),
            jax.ShapeDtypeStruct((rank, depth), down.dtype),
            [ANYWHERE] * tensors,
            [pltpu.SemaphoreType.DMA((tensors,))],
            ANYWHERE,
            cost=FREE,
        )(*pieces)
    else:
        none = jnp.zeros((), down.dtype)
        own = jnp.concatenate(
            [sum(jnp.where((me ^ f) == j, pieces[f], none) for f in range(tensors)) for j in range(tensors)],
            axis=0,
        )

    hops = range(CORES, tensors, CORES)

    def send(m):
        return [flipped(chunks[m], "tensor", hop) for hop in hops]

    far = [send(0)]

    def across(m):
        return [flipped(value, "tensor", 1) for value in far[m]]

    def far_places(m):
        return [(hop, edges[m], 0, edges[m + 1] - edges[m]) for hop in hops]

    def near_places(m):
        return [(hop ^ 1, edges[m], 0, edges[m + 1] - edges[m]) for hop in hops]

    def products(places, features, total):
        return call(
            functools.partial(products_kernel, tile, depth, places),
            jax.ShapeDtypeStruct((rows, columns), jnp.float32),
            [ANYWHERE] + [ANYWHERE] * len(features) + [VECTOR],
            tile_scratch(tile, rows, places, columns),
        )(frozen_projection_weight, *features, total)

    flips = list(range(1, groups))
    pairs = []
    if parts == 2:
        while len(flips) > 1:
            pairs.append((flips.pop(-2), flips.pop(-1)))
    routes = [
        [(p * groups + z, p * groups + (z ^ pair[p])) for p in range(parts) for z in range(groups)]
        for pair in pairs
    ]

    def fetch_far(value):
        return [lax.ppermute(value, ("parts", "adapter"), route) for route in routes]

    def fetch_near(value):
        return [flipped(value, "adapter", flip) for flip in flips]

    def swap(values):
        return [flipped(value, "parts", 1) for value in values]

    own, here = chained(own, tokens)
    fetched = fetch_far(own)
    places = [(0, 0, 0, depth // 2)]
    total, stored = call(
        functools.partial(first_kernel, tile, depth, places, slots),
        [
            jax.ShapeDtypeStruct((rows, columns), jnp.float32),
            jax.ShapeDtypeStruct((1, rows), jnp.int32),
        ],
        [SCALAR, VECTOR, ANYWHERE, ANYWHERE],
        tile_scratch(tile, rows, places, columns),
        [VECTOR, VECTOR],
    )(placement, tenant.reshape(1, rows), frozen_projection_weight, here)
    total, own, up, neighbour, chunks[1] = chained(
        total, own, lowrank_up_weight[0], neighbour, chunks[1]
    )
    far.append(send(1))
    single, single_up = fetch_near(own), fetch_near(up)
    total = products([(0, depth // 2, depth // 2, depth // 2)], [here], total)
    fetched, single_up, total = chained(fetched, single_up, total)
    swapped = swap(fetched)
    total, neighbour = chained(total, neighbour)
    total = products([(1, 0, 0, depth)], [neighbour], total)
    total, up = chained(total, up)
    fetched_up = fetch_far(up)
    single, swapped, total = chained(single, swapped, total)
    downs = [own] + single
    for pair in zip(fetched, swapped):
        downs += pair

    tiles = depth // tile
    partial = call(
        functools.partial(shrink_kernel, tile, flips, pairs, slots),
        jax.ShapeDtypeStruct((rank, rows), jnp.float32),
        [ANYWHERE, VECTOR] + [ANYWHERE] * slots,
        [
            pltpu.VMEM((tiles, rows, tile), jnp.bfloat16),
            pltpu.VMEM((tiles, slots * rank, tile), jnp.bfloat16),
            pltpu.VMEM((rows, slots * rank), jnp.float32),
            pltpu.SemaphoreType.DMA((1 + slots, tiles)),
        ],
    )(tokens, stored, *downs)
    far[0], fetched_up, partial = chained(far[0], fetched_up, partial)
    swapped_up = swap(fetched_up)
    ups = [up] + single_up
    for pair in zip(fetched_up, swapped_up):
        ups += pair
    near = across(0)
    total = products(far_places(0), far[0], total)
    flip = 1
    while flip < tensors // 2:
        received = flipped(partial, "tensor", flip)
        if flip == 1:
            received, total = chained(received, total)
        partial += received
        flip *= 2
    more = flipped(partial.astype(jnp.bfloat16), "tensor", flip)
    total, partial = chained(total, partial)
    total = products(near_places(0), near, total)
    far[1], ups, total = chained(far[1], ups, total)
    near = across(1)
    places = far_places(1)
    total, spread, stacked = call(
        functools.partial(spread_kernel, tile, depth, places, flips, pairs, slots),
        [
            jax.ShapeDtypeStruct((rows, columns), jnp.float32),
            jax.ShapeDtypeStruct((slots * rank, rows), jnp.bfloat16),
            jax.ShapeDtypeStruct((slots * rank, columns), jnp.bfloat16),
        ],
        [ANYWHERE] * (1 + len(places)) + [VECTOR] * 2 + [ANYWHERE] * (2 + slots),
        [pltpu.VMEM((rank, rows), jnp.float32), pltpu.VMEM((rank, rows), jnp.bfloat16)]
        + tile_scratch(tile, rows, places, columns)
        + [pltpu.SemaphoreType.DMA((2 + slots,))],
        [VECTOR] * 3,
    )(frozen_projection_weight, *far[1], total, stored, partial, more, *ups)
    near, total = chained(near, total)
    return call(
        functools.partial(last_kernel, depth, near_places(1)),
        jax.ShapeDtypeStruct((rows, columns), jnp.bfloat16),
        [VECTOR] * (len(near) + 4),
        [pltpu.VMEM((rows, columns), jnp.float32)],
    )(frozen_projection_weight, *near, total, spread, stacked)


def solution(mesh):
    placed = (
        P(("parts", "adapter"), "tensor"),
        P(("parts", "adapter"), None),
        P(),
        P(None, "tensor"),
        P("adapter", None, "tensor"),
        P("adapter", None, "tensor"),
    )
    return jax.shard_map(
        body,
        mesh=mesh,
        in_specs=placed,
        out_specs=P(("parts", "adapter"), "tensor"),
        check_vma=False,
    )
```

```python
import functools
import math

import jax
import jax.numpy as jnp
from jax import lax
from jax.experimental import pallas as pl
from jax.experimental.pallas import tpu as pltpu
from jax.sharding import PartitionSpec as P

LOWRANK_SCALE = 2.0
CORES = 2
LANES = 128
CUTS = (0.75,)
MIB = 1024 * 1024
FREE = pl.CostEstimate(flops=0, bytes_accessed=0, transcendentals=0)
LONG = pl.CostEstimate(flops=10**11, bytes_accessed=0, transcendentals=0)
ANYWHERE = pl.BlockSpec(memory_space=pl.ANY)
VECTOR = pl.BlockSpec(memory_space=pltpu.VMEM)
SCALAR = pl.BlockSpec(memory_space=pltpu.SMEM)


def flipped(value, axis, flip):
    count = lax.axis_size(axis)
    return lax.ppermute(value, axis, [(i, i ^ flip) for i in range(count)])


def chained(*values):
    return lax.optimization_barrier(values)


def call(kernel, out_shape, in_specs, scratch, out_specs=VECTOR, cost=LONG, mib=24):
    return pl.pallas_call(
        kernel,
        out_shape=out_shape,
        in_specs=in_specs,
        out_specs=out_specs,
        scratch_shapes=scratch,
        cost_estimate=cost,
        compiler_params=pltpu.CompilerParams(vmem_limit_bytes=mib * MIB),
    )


def run_copies(pairs, sems):
    copies = [
        pltpu.make_async_copy(source, target, sems.at[i]) for i, (source, target) in enumerate(pairs)
    ]
    for copy in copies:
        copy.start()
    for copy in copies:
        copy.wait()


def cut_kernel(edges, source_ref, *refs):
    outs, (held_ref, sems) = refs[:-2], refs[-2:]
    steps, rows = held_ref.shape[:2]
    copies = [
        pltpu.make_async_copy(source_ref.at[pl.ds(i * rows, rows)], held_ref.at[i], sems.at[0, i])
        for i in range(steps)
    ]
    for copy in copies:
        copy.start()
    leaving = []
    for i in range(steps):
        copies[i].wait()
        for m, (a, b, out) in enumerate(zip(edges, edges[1:], outs)):
            leaving.append(
                pltpu.make_async_copy(
                    held_ref.at[i, :, pl.ds(a, b - a)],
                    out.at[pl.ds(i * rows, rows)],
                    sems.at[1 + m, i],
                )
            )
            leaving[-1].start()
    for copy in leaving:
        copy.wait()


def order_kernel(rank_part, *refs):
    pieces, out_ref, sems = refs[:-2], refs[-2], refs[-1]
    me = lax.axis_index("tensor")
    run_copies(
        [
            (piece, out_ref.at[pl.ds(pl.multiple_of((me ^ f) * rank_part, rank_part), rank_part)])
            for f, piece in enumerate(pieces)
        ],
        sems,
    )


def start_tiles(tile, depth, places, features, weight_ref, held_ref, rows_ref, sems):
    me, t = lax.axis_index("tensor"), 0
    for (flip, first, skip, width), part in zip(places, features):
        for k in range(0, width, tile):
            start = pl.multiple_of((me ^ flip) * depth + first + k, LANES)
            pltpu.make_async_copy(
                weight_ref.at[pl.ds(start, tile)], rows_ref.at[t], sems.at[1, t]
            ).start()
            pltpu.make_async_copy(part.at[:, pl.ds(skip + k, tile)], held_ref.at[t], sems.at[0, t]).start()
            t += 1


def add_tiles(held_ref, rows_ref, sems, total_ref, given_ref):
    pltpu.make_async_copy(held_ref.at[0], held_ref.at[0], sems.at[0, 0]).wait()
    pltpu.make_async_copy(rows_ref.at[0], rows_ref.at[0], sems.at[1, 0]).wait()
    total_ref[...] = given_ref[...] + jnp.dot(
        held_ref[0], rows_ref[0], preferred_element_type=jnp.float32
    )
    if held_ref.shape[0] == 1:
        return

    @pl.loop(1, held_ref.shape[0])
    def _(t):
        pltpu.make_async_copy(held_ref.at[t], held_ref.at[t], sems.at[0, t]).wait()
        pltpu.make_async_copy(rows_ref.at[t], rows_ref.at[t], sems.at[1, t]).wait()
        total_ref[...] += jnp.dot(held_ref[t], rows_ref[t], preferred_element_type=jnp.float32)


def tile_scratch(tile, rows, places, columns):
    tiles = sum(place[3] for place in places) // tile
    return [
        pltpu.VMEM((tiles, rows, tile), jnp.bfloat16),
        pltpu.VMEM((tiles, tile, columns), jnp.bfloat16),
        pltpu.SemaphoreType.DMA((2, tiles)),
    ]


def first_kernel(tile, depth, places, slots, placement_ref, tenant_ref, weight_ref, *refs):
    count = len(places)
    features = refs[:count]
    out_ref, stored_ref, held_ref, rows_ref, sems = refs[count:]
    start_tiles(tile, depth, places, features, weight_ref, held_ref, rows_ref, sems)
    out_ref[...] = jnp.zeros_like(out_ref)
    stored = jnp.zeros(stored_ref.shape, jnp.int32)
    for slot in range(slots):
        stored = jnp.where(tenant_ref[...] == slot, placement_ref[slot], stored)
    stored_ref[...] = stored
    add_tiles(held_ref, rows_ref, sems, out_ref, out_ref)


def products_kernel(tile, depth, places, weight_ref, *refs):
    count = len(places)
    features, given = refs[:count], refs[count]
    out_ref, held_ref, rows_ref, sems = refs[count + 1 :]
    start_tiles(tile, depth, places, features, weight_ref, held_ref, rows_ref, sems)
    add_tiles(held_ref, rows_ref, sems, out_ref, given)


def owners_of(flips, pairs):
    group, part = lax.axis_index("adapter"), lax.axis_index("parts")
    owners = [group] + [group ^ flip for flip in flips]
    for near, far in pairs:
        owners += [group ^ (near + part * (far - near)), group ^ (far + part * (near - far))]
    return owners


def spread_kernel(tile, depth, places, flips, pairs, slots, weight_ref, *refs):
    count = len(places)
    features = refs[:count]
    given, stored_ref, sum_ref, more_ref = refs[count : count + 4]
    ups = refs[count + 4 : count + 4 + slots]
    (
        out_ref, spread_ref, stacked_ref, sums_ref, received_ref, held_ref, rows_ref, sems, small_sems,
    ) = refs[count + 4 + slots :]
    rank = ups[0].shape[0]
    copies = [(sum_ref, sums_ref), (more_ref, received_ref)]
    copies += [(up, stacked_ref.at[pl.ds(b * rank, rank)]) for b, up in enumerate(ups)]
    copies = [
        pltpu.make_async_copy(source, target, small_sems.at[i])
        for i, (source, target) in enumerate(copies)
    ]
    start_tiles(tile, depth, places, features, weight_ref, held_ref, rows_ref, sems)
    for copy in copies:
        copy.start()
    add_tiles(held_ref, rows_ref, sems, out_ref, given)
    for copy in copies[:2]:
        copy.wait()
    shrunk = (sums_ref[...] + received_ref[...].astype(jnp.float32)).astype(jnp.bfloat16).astype(jnp.float32)
    for b, owner in enumerate(owners_of(flips, pairs)):
        block = jnp.where(stored_ref[...] == owner, shrunk, 0.0)
        spread_ref[b * rank : (b + 1) * rank] = block.astype(spread_ref.dtype)
    for copy in copies[2:]:
        copy.wait()


def last_kernel(depth, places, weight_ref, *refs):
    count = len(places)
    features = refs[:count]
    given, spread_ref, stacked_ref, out_ref, total_ref = refs[count:]
    expanded = lax.dot_general(
        spread_ref[...], stacked_ref[...], (((0,), (0,)), ((), ())), preferred_element_type=jnp.float32
    )
    expanded = expanded.astype(jnp.bfloat16).astype(jnp.float32)
    total_ref[...] = given[...] + LOWRANK_SCALE * expanded
    me = lax.axis_index("tensor")
    for (flip, first, skip, width), part in zip(places, features):
        start = pl.multiple_of((me ^ flip) * depth + first, LANES)
        total_ref[...] += jnp.dot(
            part[:, skip : skip + width],
            weight_ref[pl.ds(start, width)],
            preferred_element_type=jnp.float32,
        )
    out_ref[...] = total_ref[...].astype(out_ref.dtype)


def shrink_kernel(tile, flips, pairs, slots, tokens_ref, stored_ref, *refs):
    downs, out_ref, held_ref, down_ref, sums_ref, sems = (
        refs[:slots], refs[slots], *refs[slots + 1 :]
    )
    rank = downs[0].shape[0]
    tiles = tokens_ref.shape[1] // tile
    for k in range(tiles):
        here = pl.ds(k * tile, tile)
        pltpu.make_async_copy(tokens_ref.at[:, here], held_ref.at[k], sems.at[0, k]).start()
        for b, down in enumerate(downs):
            pltpu.make_async_copy(
                down.at[:, here], down_ref.at[k, pl.ds(b * rank, rank)], sems.at[1 + b, k]
            ).start()
    sums_ref[...] = jnp.zeros_like(sums_ref)

    @pl.loop(0, tiles)
    def _(k):
        pltpu.make_async_copy(held_ref.at[k], held_ref.at[k], sems.at[0, k]).wait()
        for b in range(slots):
            block = down_ref.at[k, pl.ds(b * rank, rank)]
            pltpu.make_async_copy(block, block, sems.at[1 + b, k]).wait()
        sums_ref[...] += lax.dot_general(
            held_ref[k], down_ref[k], (((1,), (1,)), ((), ())), preferred_element_type=jnp.float32
        )

    sums = sums_ref[...].T
    total = jnp.zeros(out_ref.shape, jnp.float32)
    for b, owner in enumerate(owners_of(flips, pairs)):
        total += jnp.where(stored_ref[...] == owner, sums[b * rank : (b + 1) * rank], 0.0)
    out_ref[...] = total


def body(
    tokens, tenant, placement, frozen_projection_weight, lowrank_down_weight, lowrank_up_weight
):
    rows, depth = tokens.shape
    slots = placement.shape[0]
    tensors = lax.axis_size("tensor")
    groups = lax.axis_size("adapter")
    parts = lax.axis_size("parts")
    me = lax.axis_index("tensor")
    rank, columns = lowrank_up_weight.shape[1:]
    edges = [0] + [int(depth * cut) // LANES * LANES for cut in CUTS] + [depth]
    tile = math.gcd(*edges)

    down = lowrank_down_weight[0].T
    pieces = [
        lax.dynamic_slice_in_dim(down, (me ^ flip) * depth, depth, axis=1)
        for flip in range(tensors)
    ]
    uncut, pieces = chained(tokens, pieces)
    steps = 6
    chunks = list(
        call(
            functools.partial(cut_kernel, edges),
            [jax.ShapeDtypeStruct((rows, b - a), tokens.dtype) for a, b in zip(edges, edges[1:])],
            [ANYWHERE],
            [
                pltpu.VMEM((steps, rows // steps, depth), tokens.dtype),
                pltpu.SemaphoreType.DMA((len(edges), steps)),
            ],
            [ANYWHERE] * (len(edges) - 1),
            cost=FREE,
            mib=56,
        )(uncut)
    )
    pieces = [pieces[0]] + [flipped(pieces[f], "tensor", f) for f in range(1, tensors)]
    pieces[1], here = chained(pieces[1], tokens)
    neighbour = flipped(here, "tensor", 1)
    if down.shape[0] % 16 == 0:
        own = call(
            functools.partial(order_kernel, down.shape[0]),
            jax.ShapeDtypeStruct((rank, depth), down.dtype),
            [ANYWHERE] * tensors,
            [pltpu.SemaphoreType.DMA((tensors,))],
            ANYWHERE,
            cost=FREE,
        )(*pieces)
    else:
        none = jnp.zeros((), down.dtype)
        own = jnp.concatenate(
            [sum(jnp.where((me ^ f) == j, pieces[f], none) for f in range(tensors)) for j in range(tensors)],
            axis=0,
        )

    hops = range(CORES, tensors, CORES)

    def send(m):
        return [flipped(chunks[m], "tensor", hop) for hop in hops]

    far = [send(0)]

    def across(m):
        return [flipped(value, "tensor", 1) for value in far[m]]

    def far_places(m):
        return [(hop, edges[m], 0, edges[m + 1] - edges[m]) for hop in hops]

    def near_places(m):
        return [(hop ^ 1, edges[m], 0, edges[m + 1] - edges[m]) for hop in hops]

    def products(places, features, total):
        return call(
            functools.partial(products_kernel, tile, depth, places),
            jax.ShapeDtypeStruct((rows, columns), jnp.float32),
            [ANYWHERE] + [ANYWHERE] * len(features) + [VECTOR],
            tile_scratch(tile, rows, places, columns),
        )(frozen_projection_weight, *features, total)

    flips = list(range(1, groups))
    pairs = []
    if parts == 2:
        while len(flips) > 1:
            pairs.append((flips.pop(-2), flips.pop(-1)))
    routes = [
        [(p * groups + z, p * groups + (z ^ pair[p])) for p in range(parts) for z in range(groups)]
        for pair in pairs
    ]

    def fetch_far(value):
        return [lax.ppermute(value, ("parts", "adapter"), route) for route in routes]

    def fetch_near(value):
        return [flipped(value, "adapter", flip) for flip in flips]

    def swap(values):
        return [flipped(value, "parts", 1) for value in values]

    own, here = chained(own, tokens)
    fetched = fetch_far(own)
    places = [(0, 0, 0, depth // 2)]
    total, stored = call(
        functools.partial(first_kernel, tile, depth, places, slots),
        [
            jax.ShapeDtypeStruct((rows, columns), jnp.float32),
            jax.ShapeDtypeStruct((1, rows), jnp.int32),
        ],
        [SCALAR, VECTOR, ANYWHERE, ANYWHERE],
        tile_scratch(tile, rows, places, columns),
        [VECTOR, VECTOR],
    )(placement, tenant.reshape(1, rows), frozen_projection_weight, here)
    total, own, up, neighbour, chunks[1] = chained(
        total, own, lowrank_up_weight[0], neighbour, chunks[1]
    )
    far.append(send(1))
    single, single_up = fetch_near(own), fetch_near(up)
    total = products([(0, depth // 2, depth // 2, depth // 2)], [here], total)
    fetched, single_up, total = chained(fetched, single_up, total)
    swapped = swap(fetched)
    total, neighbour = chained(total, neighbour)
    total = products([(1, 0, 0, depth)], [neighbour], total)
    total, up = chained(total, up)
    fetched_up = fetch_far(up)
    single, swapped, total = chained(single, swapped, total)
    downs = [own] + single
    for pair in zip(fetched, swapped):
        downs += pair

    tiles = depth // tile
    partial = call(
        functools.partial(shrink_kernel, tile, flips, pairs, slots),
        jax.ShapeDtypeStruct((rank, rows), jnp.float32),
        [ANYWHERE, VECTOR] + [ANYWHERE] * slots,
        [
            pltpu.VMEM((tiles, rows, tile), jnp.bfloat16),
            pltpu.VMEM((tiles, slots * rank, tile), jnp.bfloat16),
            pltpu.VMEM((rows, slots * rank), jnp.float32),
            pltpu.SemaphoreType.DMA((1 + slots, tiles)),
        ],
    )(tokens, stored, *downs)
    far[0], fetched_up, partial = chained(far[0], fetched_up, partial)
    swapped_up = swap(fetched_up)
    ups = [up] + single_up
    for pair in zip(fetched_up, swapped_up):
        ups += pair
    near = across(0)
    total = products(far_places(0), far[0], total)
    flip = 1
    while flip < tensors // 2:
        received = flipped(partial, "tensor", flip)
        if flip == 1:
            received, total = chained(received, total)
        partial += received
        flip *= 2
    more = flipped(partial.astype(jnp.bfloat16), "tensor", flip)
    total, partial = chained(total, partial)
    total = products(near_places(0), near, total)
    far[1], ups, total = chained(far[1], ups, total)
    near = across(1)
    places = far_places(1)
    total, spread, stacked = call(
        functools.partial(spread_kernel, tile, depth, places, flips, pairs, slots),
        [
            jax.ShapeDtypeStruct((rows, columns), jnp.float32),
            jax.ShapeDtypeStruct((slots * rank, rows), jnp.bfloat16),
            jax.ShapeDtypeStruct((slots * rank, columns), jnp.bfloat16),
        ],
        [ANYWHERE] * (1 + len(places)) + [VECTOR] * 2 + [ANYWHERE] * (2 + slots),
        [pltpu.VMEM((rank, rows), jnp.float32), pltpu.VMEM((rank, rows), jnp.bfloat16)]
        + tile_scratch(tile, rows, places, columns)
        + [pltpu.SemaphoreType.DMA((2 + slots,))],
        [VECTOR] * 3,
    )(frozen_projection_weight, *far[1], total, stored, partial, more, *ups)
    near, total = chained(near, total)
    return call(
        functools.partial(last_kernel, depth, near_places(1)),
        jax.ShapeDtypeStruct((rows, columns), jnp.bfloat16),
        [VECTOR] * (len(near) + 4),
        [pltpu.VMEM((rows, columns), jnp.float32)],
    )(frozen_projection_weight, *near, total, spread, stacked)


def solution(mesh):
    placed = (
        P(("parts", "adapter"), "tensor"),
        P(("parts", "adapter"), None),
        P(),
        P(None, "tensor"),
        P("adapter", None, "tensor"),
        P("adapter", None, "tensor"),
    )
    return jax.shard_map(
        body,
        mesh=mesh,
        in_specs=placed,
        out_specs=P(("parts", "adapter"), "tensor"),
        check_vma=False,
    )
```

```python
import functools
import math

import jax
import jax.numpy as jnp
from jax import lax
from jax.experimental import pallas as pl
from jax.experimental.pallas import tpu as pltpu
from jax.sharding import PartitionSpec as P

LOWRANK_SCALE = 2.0
CORES = 2
LANES = 128
CUTS = (0.75,)
MIB = 1024 * 1024
FREE = pl.CostEstimate(flops=0, bytes_accessed=0, transcendentals=0)
LONG = pl.CostEstimate(flops=10**11, bytes_accessed=0, transcendentals=0)
ANYWHERE = pl.BlockSpec(memory_space=pl.ANY)
VECTOR = pl.BlockSpec(memory_space=pltpu.VMEM)
SCALAR = pl.BlockSpec(memory_space=pltpu.SMEM)


def flipped(value, axis, flip):
    count = lax.axis_size(axis)
    return lax.ppermute(value, axis, [(i, i ^ flip) for i in range(count)])


def chained(*values):
    return lax.optimization_barrier(values)


def call(kernel, out_shape, in_specs, scratch, out_specs=VECTOR, cost=LONG, mib=24):
    return pl.pallas_call(
        kernel,
        out_shape=out_shape,
        in_specs=in_specs,
        out_specs=out_specs,
        scratch_shapes=scratch,
        cost_estimate=cost,
        compiler_params=pltpu.CompilerParams(vmem_limit_bytes=mib * MIB),
    )


def run_copies(pairs, sems):
    copies = [
        pltpu.make_async_copy(source, target, sems.at[i]) for i, (source, target) in enumerate(pairs)
    ]
    for copy in copies:
        copy.start()
    for copy in copies:
        copy.wait()


def cut_kernel(edges, source_ref, *refs):
    outs, (held_ref, sems) = refs[:-2], refs[-2:]
    steps, rows = held_ref.shape[:2]
    copies = [
        pltpu.make_async_copy(source_ref.at[pl.ds(i * rows, rows)], held_ref.at[i], sems.at[0, i])
        for i in range(steps)
    ]
    for copy in copies:
        copy.start()
    leaving = []
    for i in range(steps):
        copies[i].wait()
        for m, (a, b, out) in enumerate(zip(edges, edges[1:], outs)):
            leaving.append(
                pltpu.make_async_copy(
                    held_ref.at[i, :, pl.ds(a, b - a)],
                    out.at[pl.ds(i * rows, rows)],
                    sems.at[1 + m, i],
                )
            )
            leaving[-1].start()
    for copy in leaving:
        copy.wait()


def order_kernel(rank_part, *refs):
    pieces, out_ref, sems = refs[:-2], refs[-2], refs[-1]
    me = lax.axis_index("tensor")
    run_copies(
        [
            (piece, out_ref.at[pl.ds(pl.multiple_of((me ^ f) * rank_part, rank_part), rank_part)])
            for f, piece in enumerate(pieces)
        ],
        sems,
    )


def start_tiles(tile, depth, places, features, weight_ref, held_ref, rows_ref, sems):
    me, t = lax.axis_index("tensor"), 0
    for (flip, first, skip, width), part in zip(places, features):
        for k in range(0, width, tile):
            start = pl.multiple_of((me ^ flip) * depth + first + k, LANES)
            pltpu.make_async_copy(part.at[:, pl.ds(skip + k, tile)], held_ref.at[t], sems.at[0, t]).start()
            pltpu.make_async_copy(
                weight_ref.at[pl.ds(start, tile)], rows_ref.at[t], sems.at[1, t]
            ).start()
            t += 1


def add_tiles(held_ref, rows_ref, sems, total_ref, given_ref):
    pltpu.make_async_copy(held_ref.at[0], held_ref.at[0], sems.at[0, 0]).wait()
    pltpu.make_async_copy(rows_ref.at[0], rows_ref.at[0], sems.at[1, 0]).wait()
    total_ref[...] = given_ref[...] + jnp.dot(
        held_ref[0], rows_ref[0], preferred_element_type=jnp.float32
    )
    if held_ref.shape[0] == 1:
        return

    @pl.loop(1, held_ref.shape[0])
    def _(t):
        pltpu.make_async_copy(held_ref.at[t], held_ref.at[t], sems.at[0, t]).wait()
        pltpu.make_async_copy(rows_ref.at[t], rows_ref.at[t], sems.at[1, t]).wait()
        total_ref[...] += jnp.dot(held_ref[t], rows_ref[t], preferred_element_type=jnp.float32)


def tile_scratch(tile, rows, places, columns):
    tiles = sum(place[3] for place in places) // tile
    return [
        pltpu.VMEM((tiles, rows, tile), jnp.bfloat16),
        pltpu.VMEM((tiles, tile, columns), jnp.bfloat16),
        pltpu.SemaphoreType.DMA((2, tiles)),
    ]


def first_kernel(tile, depth, places, slots, placement_ref, tenant_ref, weight_ref, *refs):
    count = len(places)
    features = refs[:count]
    out_ref, stored_ref, held_ref, rows_ref, sems = refs[count:]
    start_tiles(tile, depth, places, features, weight_ref, held_ref, rows_ref, sems)
    out_ref[...] = jnp.zeros_like(out_ref)
    stored = jnp.zeros(stored_ref.shape, jnp.int32)
    for slot in range(slots):
        stored = jnp.where(tenant_ref[...] == slot, placement_ref[slot], stored)
    stored_ref[...] = stored
    add_tiles(held_ref, rows_ref, sems, out_ref, out_ref)


def products_kernel(tile, depth, places, weight_ref, *refs):
    count = len(places)
    features, given = refs[:count], refs[count]
    out_ref, held_ref, rows_ref, sems = refs[count + 1 :]
    start_tiles(tile, depth, places, features, weight_ref, held_ref, rows_ref, sems)
    add_tiles(held_ref, rows_ref, sems, out_ref, given)


def owners_of(flips, pairs):
    group, part = lax.axis_index("adapter"), lax.axis_index("parts")
    owners = [group] + [group ^ flip for flip in flips]
    for near, far in pairs:
        owners += [group ^ (near + part * (far - near)), group ^ (far + part * (near - far))]
    return owners


def spread_kernel(tile, depth, places, flips, pairs, slots, weight_ref, *refs):
    count = len(places)
    features = refs[:count]
    given, stored_ref, sum_ref, more_ref = refs[count : count + 4]
    ups = refs[count + 4 : count + 4 + slots]
    (
        out_ref, spread_ref, stacked_ref, sums_ref, received_ref, held_ref, rows_ref, sems, small_sems,
    ) = refs[count + 4 + slots :]
    rank = ups[0].shape[0]
    copies = [(sum_ref, sums_ref), (more_ref, received_ref)]
    copies += [(up, stacked_ref.at[pl.ds(b * rank, rank)]) for b, up in enumerate(ups)]
    copies = [
        pltpu.make_async_copy(source, target, small_sems.at[i])
        for i, (source, target) in enumerate(copies)
    ]
    start_tiles(tile, depth, places, features, weight_ref, held_ref, rows_ref, sems)
    for copy in copies:
        copy.start()
    add_tiles(held_ref, rows_ref, sems, out_ref, given)
    for copy in copies[:2]:
        copy.wait()
    shrunk = (sums_ref[...] + received_ref[...].astype(jnp.float32)).astype(jnp.bfloat16).astype(jnp.float32)
    for b, owner in enumerate(owners_of(flips, pairs)):
        block = jnp.where(stored_ref[...] == owner, shrunk, 0.0)
        spread_ref[b * rank : (b + 1) * rank] = block.astype(spread_ref.dtype)
    for copy in copies[2:]:
        copy.wait()


def last_kernel(depth, places, weight_ref, *refs):
    count = len(places)
    features = refs[:count]
    given, spread_ref, stacked_ref, out_ref, total_ref = refs[count:]
    expanded = lax.dot_general(
        spread_ref[...], stacked_ref[...], (((0,), (0,)), ((), ())), preferred_element_type=jnp.float32
    )
    expanded = expanded.astype(jnp.bfloat16).astype(jnp.float32)
    total_ref[...] = given[...] + LOWRANK_SCALE * expanded
    me = lax.axis_index("tensor")
    for (flip, first, skip, width), part in zip(places, features):
        start = pl.multiple_of((me ^ flip) * depth + first, LANES)
        total_ref[...] += jnp.dot(
            part[:, skip : skip + width],
            weight_ref[pl.ds(start, width)],
            preferred_element_type=jnp.float32,
        )
    out_ref[...] = total_ref[...].astype(out_ref.dtype)


def shrink_kernel(tile, flips, pairs, slots, tokens_ref, stored_ref, *refs):
    downs, out_ref, held_ref, down_ref, sums_ref, sems = (
        refs[:slots], refs[slots], *refs[slots + 1 :]
    )
    rank = downs[0].shape[0]
    tiles = tokens_ref.shape[1] // tile
    for k in range(tiles):
        here = pl.ds(k * tile, tile)
        pltpu.make_async_copy(tokens_ref.at[:, here], held_ref.at[k], sems.at[0, k]).start()
        for b, down in enumerate(downs):
            pltpu.make_async_copy(
                down.at[:, here], down_ref.at[k, pl.ds(b * rank, rank)], sems.at[1 + b, k]
            ).start()
    sums_ref[...] = jnp.zeros_like(sums_ref)

    @pl.loop(0, tiles)
    def _(k):
        pltpu.make_async_copy(held_ref.at[k], held_ref.at[k], sems.at[0, k]).wait()
        for b in range(slots):
            block = down_ref.at[k, pl.ds(b * rank, rank)]
            pltpu.make_async_copy(block, block, sems.at[1 + b, k]).wait()
        sums_ref[...] += lax.dot_general(
            held_ref[k], down_ref[k], (((1,), (1,)), ((), ())), preferred_element_type=jnp.float32
        )

    sums = sums_ref[...].T
    total = jnp.zeros(out_ref.shape, jnp.float32)
    for b, owner in enumerate(owners_of(flips, pairs)):
        total += jnp.where(stored_ref[...] == owner, sums[b * rank : (b + 1) * rank], 0.0)
    out_ref[...] = total


def body(
    tokens, tenant, placement, frozen_projection_weight, lowrank_down_weight, lowrank_up_weight
):
    rows, depth = tokens.shape
    slots = placement.shape[0]
    tensors = lax.axis_size("tensor")
    groups = lax.axis_size("adapter")
    parts = lax.axis_size("parts")
    me = lax.axis_index("tensor")
    rank, columns = lowrank_up_weight.shape[1:]
    edges = [0] + [int(depth * cut) // LANES * LANES for cut in CUTS] + [depth]
    tile = math.gcd(*edges)

    down = lowrank_down_weight[0].T
    pieces = [
        lax.dynamic_slice_in_dim(down, (me ^ flip) * depth, depth, axis=1)
        for flip in range(tensors)
    ]
    uncut, pieces = chained(tokens, pieces)
    steps = 6
    chunks = list(
        call(
            functools.partial(cut_kernel, edges),
            [jax.ShapeDtypeStruct((rows, b - a), tokens.dtype) for a, b in zip(edges, edges[1:])],
            [ANYWHERE],
            [
                pltpu.VMEM((steps, rows // steps, depth), tokens.dtype),
                pltpu.SemaphoreType.DMA((len(edges), steps)),
            ],
            [ANYWHERE] * (len(edges) - 1),
            cost=FREE,
            mib=56,
        )(uncut)
    )
    pieces = [pieces[0]] + [flipped(pieces[f], "tensor", f) for f in range(1, tensors)]
    pieces[1], here = chained(pieces[1], tokens)
    neighbour = flipped(here, "tensor", 1)
    if down.shape[0] % 16 == 0:
        own = call(
            functools.partial(order_kernel, down.shape[0]),
            jax.ShapeDtypeStruct((rank, depth), down.dtype),
            [ANYWHERE] * tensors,
            [pltpu.SemaphoreType.DMA((tensors,))],
            ANYWHERE,
            cost=FREE,
        )(*pieces)
    else:
        none = jnp.zeros((), down.dtype)
        own = jnp.concatenate(
            [sum(jnp.where((me ^ f) == j, pieces[f], none) for f in range(tensors)) for j in range(tensors)],
            axis=0,
        )

    hops = range(CORES, tensors, CORES)

    def send(m):
        return [flipped(chunks[m], "tensor", hop) for hop in hops]

    far = [send(0)]

    def across(m):
        return [flipped(value, "tensor", 1) for value in far[m]]

    def far_places(m):
        return [(hop, edges[m], 0, edges[m + 1] - edges[m]) for hop in hops]

    def near_places(m):
        return [(hop ^ 1, edges[m], 0, edges[m + 1] - edges[m]) for hop in hops]

    def products(places, features, total):
        return call(
            functools.partial(products_kernel, tile, depth, places),
            jax.ShapeDtypeStruct((rows, columns), jnp.float32),
            [ANYWHERE] + [ANYWHERE] * len(features) + [VECTOR],
            tile_scratch(tile, rows, places, columns),
        )(frozen_projection_weight, *features, total)

    flips = list(range(1, groups))
    pairs = []
    if parts == 2:
        while len(flips) > 1:
            pairs.append((flips.pop(-2), flips.pop(-1)))
    routes = [
        [(p * groups + z, p * groups + (z ^ pair[p])) for p in range(parts) for z in range(groups)]
        for pair in pairs
    ]

    def fetch_far(value):
        return [lax.ppermute(value, ("parts", "adapter"), route) for route in routes]

    def fetch_near(value):
        return [flipped(value, "adapter", flip) for flip in flips]

    def swap(values):
        return [flipped(value, "parts", 1) for value in values]

    own, here = chained(own, tokens)
    fetched = fetch_far(own)
    places = [(0, 0, 0, depth // 2)]
    total, stored = call(
        functools.partial(first_kernel, tile, depth, places, slots),
        [
            jax.ShapeDtypeStruct((rows, columns), jnp.float32),
            jax.ShapeDtypeStruct((1, rows), jnp.int32),
        ],
        [SCALAR, VECTOR, ANYWHERE, ANYWHERE],
        tile_scratch(tile, rows, places, columns),
        [VECTOR, VECTOR],
    )(placement, tenant.reshape(1, rows), frozen_projection_weight, here)
    total, own, up, neighbour, chunks[1] = chained(
        total, own, lowrank_up_weight[0], neighbour, chunks[1]
    )
    far.append(send(1))
    single, single_up = fetch_near(own), fetch_near(up)
    total = products([(0, depth // 2, depth // 2, depth // 2)], [here], total)
    fetched, single_up, total = chained(fetched, single_up, total)
    swapped = swap(fetched)
    total, neighbour = chained(total, neighbour)
    total = products([(1, 0, 0, depth)], [neighbour], total)
    total, up = chained(total, up)
    fetched_up = fetch_far(up)
    single, swapped, total = chained(single, swapped, total)
    downs = [own] + single
    for pair in zip(fetched, swapped):
        downs += pair

    tiles = depth // tile
    partial = call(
        functools.partial(shrink_kernel, tile, flips, pairs, slots),
        jax.ShapeDtypeStruct((rank, rows), jnp.float32),
        [ANYWHERE, VECTOR] + [ANYWHERE] * slots,
        [
            pltpu.VMEM((tiles, rows, tile), jnp.bfloat16),
            pltpu.VMEM((tiles, slots * rank, tile), jnp.bfloat16),
            pltpu.VMEM((rows, slots * rank), jnp.float32),
            pltpu.SemaphoreType.DMA((1 + slots, tiles)),
        ],
    )(tokens, stored, *downs)
    far[0], fetched_up, partial = chained(far[0], fetched_up, partial)
    swapped_up = swap(fetched_up)
    ups = [up] + single_up
    for pair in zip(fetched_up, swapped_up):
        ups += pair
    near = across(0)
    total = products(far_places(0), far[0], total)
    flip = 1
    while flip < tensors // 2:
        received = flipped(partial, "tensor", flip)
        if flip == 1:
            received, total = chained(received, total)
        partial += received
        flip *= 2
    more = flipped(partial.astype(jnp.bfloat16), "tensor", flip)
    total, partial = chained(total, partial)
    total = products(near_places(0), near, total)
    far[1], ups, total = chained(far[1], ups, total)
    near = across(1)
    places = far_places(1)
    total, spread, stacked = call(
        functools.partial(spread_kernel, tile, depth, places, flips, pairs, slots),
        [
            jax.ShapeDtypeStruct((rows, columns), jnp.float32),
            jax.ShapeDtypeStruct((slots * rank, rows), jnp.bfloat16),
            jax.ShapeDtypeStruct((slots * rank, columns), jnp.bfloat16),
        ],
        [ANYWHERE] * (1 + len(places)) + [VECTOR] * 2 + [ANYWHERE] * (2 + slots),
        [pltpu.VMEM((rank, rows), jnp.float32), pltpu.VMEM((rank, rows), jnp.bfloat16)]
        + tile_scratch(tile, rows, places, columns)
        + [pltpu.SemaphoreType.DMA((2 + slots,))],
        [VECTOR] * 3,
    )(frozen_projection_weight, *far[1], total, stored, partial, more, *ups)
    near, total = chained(near, total)
    return call(
        functools.partial(last_kernel, depth, near_places(1)),
        jax.ShapeDtypeStruct((rows, columns), jnp.bfloat16),
        [VECTOR] * (len(near) + 4),
        [pltpu.VMEM((rows, columns), jnp.float32)],
    )(frozen_projection_weight, *near, total, spread, stacked)


def solution(mesh):
    placed = (
        P(("parts", "adapter"), "tensor"),
        P(("parts", "adapter"), None),
        P(),
        P(None, "tensor"),
        P("adapter", None, "tensor"),
        P("adapter", None, "tensor"),
    )
    return jax.shard_map(
        body,
        mesh=mesh,
        in_specs=placed,
        out_specs=P(("parts", "adapter"), "tensor"),
        check_vma=False,
    )
```
